32 devices in a mesh: seq: 8 (over z, x), dp: 4 (over y, core).
Axes of the slice: x: 2, y: 2, z: 4, core: 2. Of those that a mesh axis runs over, the one named last changes fastest.
Arguments:
- layer_input: bfloat16 [4, 2048, 768], P('dp', 'seq'), may hold values from -6 to 6
- out_cotangent: bfloat16 [4, 2048, 768], P('dp', 'seq'), may hold values from -6 to 6
- segment_ids: int32 [4, 2048], P('dp', 'seq'), may hold values from 0 to 2, as said below
- piece_owner: int32 [768], replicated, may hold values from 0 to 31, as said below
- weight_master: float32 [1024, 16, 768], P(('seq', 'dp'))
- weight_first: float32 [1024, 16, 768], P(('seq', 'dp'))
- weight_second: float32 [1024, 16, 768], P(('seq', 'dp'))
- norm_params: float32 [4, 768], replicated
- norm_first: float32 [4, 768], replicated
- norm_second: float32 [4, 768], replicated
Outputs:
- out_hidden: bfloat16 [4, 2048, 768], P('dp', 'seq')
- input_grad: float32 [4, 2048, 768], P('dp', 'seq')
- weight_grads: float32 [1024, 16, 768], P(('seq', 'dp'))
- weight_first_new: float32 [1024, 16, 768], P(('seq', 'dp'))
- weight_second_new: float32 [1024, 16, 768], P(('seq', 'dp'))
- weight_new: float32 [1024, 16, 768], P(('seq', 'dp'))
- weight_low: bfloat16 [1024, 16, 768], P(('seq', 'dp'))
- norm_grads: float32 [4, 768], replicated
- norm_first_new: float32 [4, 768], replicated
- norm_second_new: float32 [4, 768], replicated
- norm_new: float32 [4, 768], replicated
The draws below stay inside these ranges and needn't reach their ends.
Inputs may be any that keep to these rules, and one draw needn't show every extreme that they name: `segment_ids`: in each sequence the numbers never fall: 0 on its first positions, 2 on its last ones, 1 between; the documents numbered 0 and 2 each hold 1 to 255 tokens. `piece_owner`: each device owns at most 32 pieces, and some device owns exactly 32.
All inputs are finite; a program needn't handle non-finite values.
Results may differ from the reference program's by a relative error of at most 0.013.
The reference program's roundings to bfloat16 on the way count: a program that leaves them out, or rounds other values in their place, can miss the bound.
Values may be sent and summed in bfloat16 or wider, within the bound.
A program may use at most 256 MiB of HBM per device.

```python
import math
import jax
import jax.numpy as jnp
from jax import lax

D = 768
HEADS = 12
HEAD = 64
FF = 3072
TOK_DEV = 256
PIECE = 16
STEP = 4
ROWS = 12288
PIECES = 768
SLOTS = 32
SLOT_ROWS = 1024
SEQ_LEN = 2048
SEQS = 4
TOKENS = 8192
N_SEQ = 8
DEVICES = 32


def owner_draw(key):
    key = jax.random.fold_in(key, 101)
    pick_key, order_key, place_key = jax.random.split(key, 3)
    full_device = jax.random.randint(pick_key, (), 0, DEVICES)
    ranking = jax.random.permutation(order_key, SLOT_ROWS).astype(jnp.int32)
    position = jnp.arange(SLOT_ROWS, dtype=jnp.int32)
    ranking = jnp.where(position // SLOTS == full_device, ranking - SLOT_ROWS, ranking)
    chosen = jnp.argsort(ranking, stable=True)[:PIECES].astype(jnp.int32)
    placed = jax.random.permutation(place_key, chosen)
    return (placed // SLOTS).astype(jnp.int32)


def slot_kinds(owners):
    numbers = jnp.arange(PIECES, dtype=jnp.int32)
    earlier = (owners[None, :] == owners[:, None]) & (numbers[None, :] < numbers[:, None])
    location = owners * SLOTS + jnp.sum(earlier.astype(jnp.int32), axis=1)
    first_row = numbers * PIECE
    bounds = [D, 2 * D, 3 * D, 4 * D, 4 * D + FF, 4 * D + 2 * FF]
    piece_kind = jnp.ones((PIECES,), jnp.int32)
    for limit_row in bounds:
        piece_kind = piece_kind + (first_row >= limit_row).astype(jnp.int32)
    return jnp.zeros((SLOT_ROWS,), jnp.int32).at[location].set(piece_kind)


def kind_scale(kinds, scale_table):
    table_array = jnp.array(scale_table, jnp.float32)
    return table_array[kinds]


def grad_table():
    root = math.sqrt(TOKENS)
    return [0.3 * root, root, root, root, 0.06 * root, 0.2 * root, 0.2 * root, 0.45 * root]


def draw_segment_ids(key, part):
    key = jax.random.fold_in(key, 9)
    head_key, tail_key = jax.random.split(key)
    head_len = jax.random.randint(head_key, (SEQS, 1), 1, TOK_DEV)
    tail_len = jax.random.randint(tail_key, (SEQS, 1), 1, TOK_DEV)
    position = jnp.arange(SEQ_LEN, dtype=jnp.int32)[None, :]
    return ((position >= head_len).astype(jnp.int32) + (position >= SEQ_LEN - tail_len).astype(jnp.int32)).astype(jnp.int32)


def draw_piece_owner(key, part):
    return owner_draw(key)


def draw_weight_master(key, part):
    kinds = slot_kinds(owner_draw(key))
    key = jax.random.fold_in(key, 3)
    narrow = D ** (-0.5)
    spread = kind_scale(kinds, [narrow, narrow, narrow, narrow, 0.35, narrow, narrow, FF ** (-0.5)])
    base = jax.random.normal(key, (SLOT_ROWS, PIECE, D), jnp.float32)
    return base * spread[:, None, None]


def draw_weight_first(key, part):
    kinds = slot_kinds(owner_draw(key))
    key = jax.random.fold_in(key, 4)
    spread = kind_scale(kinds, grad_table())
    base = jax.random.normal(key, (SLOT_ROWS, PIECE, D), jnp.float32)
    return base * spread[:, None, None]


def draw_weight_second(key, part):
    kinds = slot_kinds(owner_draw(key))
    key = jax.random.fold_in(key, 5)
    spread = kind_scale(kinds, grad_table())
    factor = jnp.exp(jax.random.uniform(key, (SLOT_ROWS, PIECE, D), jnp.float32, 0.0, math.log(4.0)))
    return factor * (spread * spread)[:, None, None]


def draw_norm_params(key, part):
    key = jax.random.fold_in(key, 6)
    base = jax.random.normal(key, (4, D), jnp.float32)
    is_gain = (jnp.arange(4, dtype=jnp.int32) % 2 == 0)[:, None]
    return jnp.where(is_gain, 1.0 + 0.1 * base, 0.3 * base)


def draw_norm_first(key, part):
    key = jax.random.fold_in(key, 7)
    scale_now = 0.6 * math.sqrt(TOKENS)
    base = jax.random.normal(key, (4, D), jnp.float32)
    return base * scale_now


def draw_norm_second(key, part):
    key = jax.random.fold_in(key, 8)
    scale_now = 0.6 * math.sqrt(TOKENS)
    factor = jnp.exp(jax.random.uniform(key, (4, D), jnp.float32, 0.0, math.log(4.0)))
    return factor * (scale_now * scale_now)


def block_levels(stream_key, dims, shards, least, top_value):
    level = 1.0
    for dim, parts in shards:
        heights = jax.random.uniform(jax.random.fold_in(jax.random.fold_in(stream_key, 6), dim), (parts,), jnp.float32, least / len(shards), top_value / len(shards))
        level = level * jnp.repeat(jnp.exp(heights), dims[dim] // parts).reshape((-1,) + (1,) * (len(dims) - 1 - dim))
    return level


def noise(rng, shape, deviation, most, cuts=(), kind=jnp.bfloat16):
    values = jax.random.normal(rng, shape, jnp.float32) * deviation
    if len(cuts) > 0:
        values = block_levels(rng, shape, cuts, -0.22, 0.18) * values
    return jnp.clip(values, min=-most, max=most).astype(kind)


def setup_inputs(seed: int = 0) -> dict:
    arg_keys = jax.random.split(jax.random.key(seed), 11)
    return {
        "layer_input": noise(arg_keys[0], (SEQS, SEQ_LEN, D), 1.0, 6.0, ((0, 4), (1, 8))),
        "out_cotangent": noise(arg_keys[1], (SEQS, SEQ_LEN, D), 1.0, 6.0, ((0, 4), (1, 8))),
        "segment_ids": draw_segment_ids(jax.random.fold_in(arg_keys[10], 71), 0),
        "piece_owner": draw_piece_owner(jax.random.fold_in(arg_keys[10], 71), 0),
        "weight_master": draw_weight_master(jax.random.fold_in(arg_keys[10], 71), 0),
        "weight_first": draw_weight_first(jax.random.fold_in(arg_keys[10], 71), 0),
        "weight_second": draw_weight_second(jax.random.fold_in(arg_keys[10], 71), 0),
        "norm_params": draw_norm_params(jax.random.fold_in(arg_keys[10], 71), 0),
        "norm_first": draw_norm_first(jax.random.fold_in(arg_keys[10], 71), 0),
        "norm_second": draw_norm_second(jax.random.fold_in(arg_keys[10], 71), 0),
    }


@jax.custom_vjp
def low(v):
    return lax.optimization_barrier(v.astype(jnp.bfloat16)).astype(jnp.float32)

@jax.custom_vjp
def low_back(v):
    return v

def low_keep(v):
    return (low(v), None)

def low_pass(kept, grad):
    return (grad,)

def back_keep(v):
    return (v, None)

def back_low(kept, grad):
    return (low(grad),)
low.defvjp(low_keep, low_pass)
low_back.defvjp(back_keep, back_low)
NORM_EPS = 1e-06
BETA_ONE = 0.5
BETA_TWO = 0.5
DECAY = 0.01
ADAM_EPS = 1e-08
NORM_RATE = 0.3
OUT_RATE = 0.35
MASKED = -1e+30
HIGH = lax.Precision.HIGHEST

def matmul(left_side, right_side):
    return jnp.dot(left_side, right_side, precision=HIGH, preferred_element_type=jnp.float32)

def layer_norm(values_in, gain_row, bias_row):
    row_mean = lax.optimization_barrier(jnp.mean(values_in, axis=-1, keepdims=True))
    centred = values_in - row_mean
    spread = lax.optimization_barrier(jnp.mean(centred * centred, axis=-1, keepdims=True))
    return centred * lax.rsqrt(spread + NORM_EPS) * gain_row + bias_row

def head_slopes(head_count, tok_rows, seq_devices):
    head_order = jnp.arange(head_count, dtype=jnp.float32)
    return 8.0 / tok_rows * jnp.power(jnp.float32(8.0 * seq_devices), -head_order / (head_count - 1))

def locate_pieces(owners, slot_count):
    pieces = owners.shape[0]
    numbers = jnp.arange(pieces, dtype=jnp.int32)
    earlier = (owners[None, :] == owners[:, None]) & (numbers[None, :] < numbers[:, None])
    return owners * slot_count + lax.optimization_barrier(jnp.sum(earlier.astype(jnp.int32), axis=1))

def slot_rates(inverse, piece_rows, model_width, hidden_units):
    first_row = (inverse - 1) * piece_rows
    narrow = model_width ** (-0.5)
    step_rate = jnp.where(first_row < 3 * model_width, narrow, jnp.where(first_row < 4 * model_width, OUT_RATE, jnp.where(first_row < 4 * model_width + 2 * hidden_units, narrow, hidden_units ** (-0.5))))
    return jnp.where(inverse > 0, step_rate, narrow).astype(jnp.float32)

def adamw_step(weight, first_moment, second, gradient, step_rate, step_count):
    first_moment = BETA_ONE * first_moment + (1.0 - BETA_ONE) * gradient
    second = BETA_TWO * second + (1.0 - BETA_TWO) * gradient * gradient
    mean_hat = first_moment / (1.0 - BETA_ONE ** step_count)
    square_hat = second / (1.0 - BETA_TWO ** step_count)
    weight = weight - step_rate * (mean_hat / (jnp.sqrt(square_hat) + ADAM_EPS) + DECAY * weight)
    return (first_moment, second, weight)

def attend(projected, segments, slopes):
    queries = projected[:, :D].reshape(SEQ_LEN, HEADS, HEAD)
    keys_all = projected[:, D:2 * D].reshape(SEQ_LEN, HEADS, HEAD)
    values_all = projected[:, 2 * D:].reshape(SEQ_LEN, HEADS, HEAD)
    block_rows = min(512, SEQ_LEN)
    key_pos = jnp.arange(SEQ_LEN, dtype=jnp.int32)

    def one_block(first_row):
        query_rows = lax.dynamic_slice_in_dim(queries, first_row, block_rows, 0)
        query_seg = lax.dynamic_slice_in_dim(segments, first_row, block_rows, 0)
        query_pos = first_row + jnp.arange(block_rows, dtype=jnp.int32)
        raw_scores = jnp.einsum('qhd,khd->hqk', query_rows, keys_all, precision=HIGH) * HEAD ** (-0.5)
        distance = jnp.abs(query_pos[:, None] - key_pos[None, :]).astype(jnp.float32)
        raw_scores = raw_scores - slopes[:, None, None] * distance[None]
        same_doc = query_seg[:, None] == segments[None, :]
        masked = low_back(jnp.where(same_doc[None], raw_scores, MASKED))
        attn_prob = jax.nn.softmax(masked, axis=-1)
        mixed = jnp.einsum('hqk,khd->qhd', low(attn_prob), values_all, precision=HIGH)
        return mixed.reshape(block_rows, D)
    starts = jnp.arange(0, SEQ_LEN, block_rows, dtype=jnp.int32)
    return lax.map(jax.checkpoint(one_block), starts).reshape(SEQ_LEN, D)

def forward_layer(tokens, weight_rows, norm_rows, segments, slopes):
    rounded = low(weight_rows)
    w_project = rounded[:3 * D]
    w_output = rounded[3 * D:4 * D]
    w_gate_up = rounded[4 * D:4 * D + 2 * FF]
    w_down = rounded[4 * D + 2 * FF:]
    projected = low(low_back(matmul(tokens, w_project.T)))
    mixed = low(low_back(attend(projected, segments, slopes)))
    pre_one = tokens + low_back(matmul(mixed, w_output.T))
    h_one = layer_norm(pre_one, norm_rows[0], norm_rows[1])
    gate_up = low_back(matmul(low(h_one), w_gate_up.T))
    hidden = low(jax.nn.gelu(gate_up[:, :FF], approximate=False) * gate_up[:, FF:])
    pre_two = h_one + low_back(matmul(hidden, w_down))
    return layer_norm(pre_two, norm_rows[2], norm_rows[3])

def reference(layer_input, out_cotangent, segment_ids, piece_owner, weight_master, weight_first, weight_second, norm_params, norm_first, norm_second):
    location = locate_pieces(piece_owner, SLOTS)
    weight_rows = jnp.take(weight_master, location, axis=0).reshape(ROWS, D)
    slopes = head_slopes(HEADS, TOK_DEV, N_SEQ)

    def one_sequence(carried, seq_items):
        tokens, cotangent, segments = seq_items

        def local_layer(token_rows, rows_in, norm_rows):
            return forward_layer(token_rows, rows_in, norm_rows, segments, slopes)
        output, pull_back = jax.vjp(local_layer, tokens.astype(jnp.float32), weight_rows, norm_params)
        d_tokens, d_rows, d_norms = pull_back(cotangent.astype(jnp.float32))
        return ((carried[0] + d_rows, carried[1] + d_norms), (output.astype(jnp.bfloat16), d_tokens))
    start_sums = (jnp.zeros((ROWS, D), jnp.float32), jnp.zeros((4, D), jnp.float32))
    (row_grads, norm_grads), (out_hidden, input_grad) = lax.scan(one_sequence, start_sums, (layer_input, out_cotangent, segment_ids))
    inverse = jnp.zeros((SLOT_ROWS,), jnp.int32).at[location].set(jnp.arange(PIECES, dtype=jnp.int32) + 1)
    weight_grads = jnp.zeros((SLOT_ROWS, PIECE, D), jnp.float32).at[location].set(row_grads.reshape(PIECES, PIECE, D))
    rates = slot_rates(inverse, PIECE, D, FF)
    first_new, second_new, weight_new = adamw_step(weight_master, weight_first, weight_second, weight_grads, rates[:, None, None], STEP)
    norm_first_new, norm_second_new, norm_new = adamw_step(norm_params, norm_first, norm_second, norm_grads, NORM_RATE, STEP)
    return (out_hidden, input_grad, weight_grads, first_new, second_new, weight_new, weight_new.astype(jnp.bfloat16), norm_grads, norm_first_new, norm_second_new, norm_new)
```

```python
import functools

import jax
import jax.numpy as jnp
from jax import lax
from jax.experimental import pallas as pl
from jax.experimental.pallas import tpu as pltpu
from jax.sharding import Mesh
from jax.sharding import PartitionSpec as P

HEADS = 12
GROUPS = 4
TRIO = HEADS // GROUPS
STEP = 4

NORM_EPS = 1e-06
BETA_ONE = 0.5
BETA_TWO = 0.5
DECAY = 0.01
ADAM_EPS = 1e-08
NORM_RATE = 0.3
OUT_RATE = 0.35
MASKED = -1e30
CHUNKS = 6
VMEM_LIMIT = 60 * 1024 * 1024
MESH_IDS = pl.DeviceIdType.MESH
F32 = jnp.float32
BF16 = jnp.bfloat16


def head_slopes(head_count, tok_rows, seq_devices):
    head_order = jnp.arange(head_count, dtype=jnp.float32)
    return (
        8.0 / tok_rows * jnp.power(jnp.float32(8.0 * seq_devices), -head_order / (head_count - 1))
    )


def locate_pieces(owners, slot_count):
    pieces = owners.shape[0]
    numbers = jnp.arange(pieces, dtype=jnp.int32)
    earlier = (owners[None, :] == owners[:, None]) & (numbers[None, :] < numbers[:, None])
    return owners * slot_count + jnp.sum(earlier.astype(jnp.int32), axis=1)


def slot_rates(inverse, piece_rows, model_width, hidden_units):
    first_row = (inverse - 1) * piece_rows
    narrow = model_width ** (-0.5)
    step_rate = jnp.where(
        first_row < 3 * model_width,
        narrow,
        jnp.where(
            first_row < 4 * model_width,
            OUT_RATE,
            jnp.where(
                first_row < 4 * model_width + 2 * hidden_units, narrow, hidden_units ** (-0.5)
            ),
        ),
    )
    return jnp.where(inverse > 0, step_rate, narrow).astype(jnp.float32)


def adamw_step(weight, first_moment, second, gradient, step_rate, step_count):
    first_moment = BETA_ONE * first_moment + (1.0 - BETA_ONE) * gradient
    second = BETA_TWO * second + (1.0 - BETA_TWO) * gradient * gradient
    mean_hat = first_moment / (1.0 - BETA_ONE**step_count)
    square_hat = second / (1.0 - BETA_TWO**step_count)
    weight = weight - step_rate * (mean_hat / (jnp.sqrt(square_hat) + ADAM_EPS) + DECAY * weight)
    return (first_moment, second, weight)


def dot_nt(left_side, right_side):
    return lax.dot_general(
        left_side, right_side, (((1,), (1,)), ((), ())), preferred_element_type=F32
    )


def dot_nn(left_side, right_side):
    return lax.dot_general(
        left_side, right_side, (((1,), (0,)), ((), ())), preferred_element_type=F32
    )


def dot_tn(left_side, right_side):
    return lax.dot_general(
        left_side, right_side, (((0,), (0,)), ((), ())), preferred_element_type=F32
    )


def fetch_piece(place, piece, slots, core, mine, twin, dst, sem):
    spot = place[piece]
    device = lax.div(spot, slots)
    row = lax.div(device, 2) * slots + lax.rem(spot, slots)

    @pl.when(lax.rem(device, 2) == core)
    def _():
        pltpu.make_async_copy(mine.at[row], dst, sem).start()

    @pl.when(lax.rem(device, 2) != core)
    def _():
        pltpu.make_async_copy(twin.at[row], dst, sem).start()


def fill_tables(table, slopes, group, tok):
    apart = lax.broadcasted_iota(jnp.int32, (tok, tok), 0) - lax.broadcasted_iota(
        jnp.int32, (tok, tok), 1
    )
    apart = apart.astype(F32)
    for h in range(TRIO):
        slope = slopes[group * TRIO + h]
        table[h * 3 + 0] = -slope * apart
        table[h * 3 + 1] = slope * jnp.abs(apart)
        table[h * 3 + 2] = slope * apart


def block_place(order, n_dp, reps):
    return (order % n_dp) * reps + order // n_dp


def bias_of(key_block, query_place, slope, h, tok, n_dp, reps):
    key_place = block_place(key_block, n_dp, reps)
    which = jnp.where(key_place > query_place, 2, jnp.where(key_place < query_place, 0, 1))
    shift = slope * (tok * jnp.abs(key_place - query_place)).astype(F32)
    return h * 3 + which, shift


def attend_forward_kernel(
    sizes,
    place,
    info,
    slopes,
    x_ref,
    query_marks,
    key_marks,
    mine,
    twin,
    q_out,
    k_out,
    kt_out,
    v_out,
    mixed_low,
    mixed_full,
    log_out,
    wpad,
    vt,
    table,
    scores,
    sems,
):
    n_dp, reps, splits, tok, slots, head, blocks = sizes
    core, group, split = info[0], info[1], info[2]
    piece = wpad.shape[1] // (2 * (head // 16))
    per_head = head // 16
    width = x_ref.shape[2]
    kind_pieces = width // 16

    def start(step, carry):
        kind = lax.div(step, TRIO * per_head)
        rest = lax.rem(step, TRIO * per_head)
        number = kind * kind_pieces + group * (TRIO * per_head) + rest
        dst = wpad.at[
            kind * TRIO + lax.div(rest, per_head), pl.ds(lax.rem(rest, per_head) * 16, 16)
        ]
        fetch_piece(place, number, slots, core, mine, twin, dst, sems.at[step])
        return carry

    def finish(step, carry):
        kind = lax.div(step, TRIO * per_head)
        rest = lax.rem(step, TRIO * per_head)
        dst = wpad.at[
            kind * TRIO + lax.div(rest, per_head), pl.ds(lax.rem(rest, per_head) * 16, 16)
        ]
        pltpu.make_async_copy(mine.at[0], dst, sems.at[step]).wait()
        return carry

    lax.fori_loop(0, 3 * TRIO * per_head, start, None)
    for row in range(3 * TRIO):
        wpad[row, head:, :] = jnp.zeros((wpad.shape[1] - head, width), BF16)
    fill_tables(table, slopes, group, tok)
    lax.fori_loop(0, 3 * TRIO * per_head, finish, None)

    w_query = wpad[0:TRIO].reshape(TRIO * 128, width)
    w_key = wpad[TRIO : 2 * TRIO].reshape(TRIO * 128, width)
    w_value = wpad[2 * TRIO : 3 * TRIO].reshape(TRIO * 128, width)

    def project(block, carry):
        rows = pl.ds(pl.multiple_of(block * tok, tok), tok)
        xb = x_ref[block, 0:tok, :]
        keys = dot_nt(xb, w_key).astype(BF16)
        values = dot_nt(xb, w_value).astype(BF16)
        marks = key_marks[rows, :]
        for h in range(TRIO):
            k_out[h, rows, :] = keys[:, h * 128 : (h + 1) * 128] + marks
            v_out[h, rows, :] = values[:, h * 128 : h * 128 + head]
            kt_out[h, :, rows] = dot_nt(wpad[TRIO + h, 0:head, :], xb).astype(BF16)
            vt[h, :, rows] = dot_nt(wpad[2 * TRIO + h, 0:head, :], xb).astype(BF16)
        return carry

    lax.fori_loop(0, blocks, project, None)

    def project_query(index, carry):
        rows = pl.ds(pl.multiple_of(index * tok, tok), tok)
        xb = x_ref[index * splits + split, 0:tok, :]
        queries = dot_nt(xb, w_query).astype(BF16) * jnp.asarray(head**-0.5, BF16)
        marks = query_marks[rows, :]
        for h in range(TRIO):
            q_out[h, rows, :] = queries[:, h * 128 : (h + 1) * 128] + marks
        return carry

    lax.fori_loop(0, GROUPS, project_query, None)

    def attend(step, carry):
        index, h = lax.div(step, TRIO), lax.rem(step, TRIO)
        order = index * splits + split
        query_place = lax.rem(order, n_dp) * reps + lax.div(order, n_dp)
        slope = slopes[group * TRIO + h]
        qh = q_out[h, pl.ds(pl.multiple_of(index * tok, tok), tok), :]
        top = None
        shifts = []
        for kb in range(blocks):
            which, shift = bias_of(kb, query_place, slope, h, tok, n_dp, reps)
            now = dot_nt(k_out[h, kb * tok : (kb + 1) * tok, :], qh) - table[which]
            scores[kb] = now
            here = jnp.max(now, axis=0, keepdims=True) - shift
            top = here if top is None else jnp.maximum(top, here)
            shifts.append(shift)
        total = jnp.zeros((1, tok), F32)
        for kb in range(blocks):
            grown = jnp.exp(scores[kb] - (top + shifts[kb]))
            total = total + jnp.sum(grown, axis=0, keepdims=True)
            scores[kb] = grown
        inverse = 1.0 / total
        mixed = jnp.zeros((head, tok), F32)
        for kb in range(blocks):
            prob = (scores[kb] * inverse).astype(BF16)
            mixed = mixed + dot_nn(vt[h, :, kb * tok : (kb + 1) * tok], prob)
        mixed_full[index, h] = mixed
        mixed_low[index, h] = mixed.astype(BF16)
        log_out[index, h] = top + jnp.log(total)
        return carry

    lax.fori_loop(0, GROUPS * TRIO, attend, None)


def attend_backward_kernel(
    sizes,
    info,
    slopes,
    q_ref,
    k_ref,
    kt_ref,
    v_ref,
    mixed_full,
    log_in,
    d_mixed,
    dq_out,
    dkv_out,
    dk_sum,
    dv_sum,
    table,
):
    n_dp, reps, splits, tok, slots, head, blocks = sizes
    group, split = info[1], info[2]
    fill_tables(table, slopes, group, tok)
    dk_sum[...] = jnp.zeros_like(dk_sum)
    dv_sum[...] = jnp.zeros_like(dv_sum)

    def step_fn(step, carry):
        h, index = lax.div(step, GROUPS), lax.rem(step, GROUPS)
        order = index * splits + split
        query_place = lax.rem(order, n_dp) * reps + lax.div(order, n_dp)
        slope = slopes[group * TRIO + h]
        qh = q_ref[h, pl.ds(pl.multiple_of(index * tok, tok), tok), :]
        dt = d_mixed[index, h]
        row_dot = jnp.sum(dt.astype(F32) * mixed_full[index, h], axis=0, keepdims=True)
        log_total = log_in[index, h]
        dq = jnp.zeros((head, tok), F32)
        for kb in range(blocks):
            rows = slice(kb * tok, (kb + 1) * tok)
            which, shift = bias_of(kb, query_place, slope, h, tok, n_dp, reps)
            now = dot_nt(k_ref[h, rows, :], qh) - table[which]
            prob = jnp.exp(now - (log_total + shift))
            d_prob = dot_nn(v_ref[h, rows, :], dt)
            d_score = (prob * (d_prob - row_dot)).astype(BF16)
            dv_sum[h, rows, :] += dot_nt(prob.astype(BF16), dt)
            dk_sum[h, rows, :] += dot_nn(d_score, qh)
            dq = dq + dot_nn(kt_ref[h, :, rows], d_score)
        dq_out[index, h] = (dq * (head**-0.5)).astype(BF16)
        return carry

    lax.fori_loop(0, TRIO * GROUPS, step_fn, None)

    def flip(step, carry):
        h, index = lax.div(step, GROUPS), lax.rem(step, GROUPS)
        for part in range(splits):
            rows = pl.ds(pl.multiple_of((index * splits + part) * tok, tok), tok)
            dkv_out[part, index, 0, h] = dk_sum[h, rows, :].T[0:head].astype(BF16)
            dkv_out[part, index, 1, h] = dv_sum[h, rows, :].T.astype(BF16)
        return carry

    lax.fori_loop(0, TRIO * GROUPS, flip, None)


def norm_stats(values_in):
    mean = jnp.mean(values_in, axis=-1, keepdims=True)
    centred = values_in - mean
    spread = jnp.mean(centred * centred, axis=-1, keepdims=True)
    scale = lax.rsqrt(spread + NORM_EPS)
    return centred * scale, scale


def norm_back(unit, scale, gain, cotangent):
    d_unit = cotangent * gain
    first = jnp.mean(d_unit, axis=-1, keepdims=True)
    second = jnp.mean(d_unit * unit, axis=-1, keepdims=True)
    d_in = scale * (d_unit - first - unit * second)
    d_gain = jnp.sum(cotangent * unit, axis=0, keepdims=True)
    d_bias = jnp.sum(cotangent, axis=0, keepdims=True)
    return d_in, d_gain, d_bias


def dense_kernel(
    sizes,
    place,
    info,
    x_ref,
    cot_ref,
    mixed_ref,
    norm_ref,
    mine,
    twin,
    out_ref,
    d_pre_one_ref,
    d_mixed_ref,
    norm_grad,
    grads,
    w_out,
    w_gate,
    w_up,
    w_down,
    keep_gate,
    keep_up,
    keep_hidden,
    stage,
    stage_out,
    load_sems,
    store_sems,
):
    slots, piece, kind_pieces, chunk_pieces, hidden_pieces = sizes
    core = info[0]
    first_gate = 4 * kind_pieces
    first_up = first_gate + hidden_pieces
    first_down = first_up + hidden_pieces
    bases = (first_gate, first_up, first_down)
    buffers = (w_gate, w_up, w_down)
    chunk = chunk_pieces * piece

    def load_out(step, carry):
        fetch_piece(
            place,
            3 * kind_pieces + step,
            slots,
            core,
            mine,
            twin,
            w_out.at[pl.ds(step * piece, piece)],
            load_sems.at[3 * CHUNKS],
        )
        return carry

    def load_chunk(c):
        def one(step, carry):
            for kind in range(3):
                fetch_piece(
                    place,
                    bases[kind] + c * chunk_pieces + step,
                    slots,
                    core,
                    mine,
                    twin,
                    buffers[kind].at[c, pl.ds(step * piece, piece)],
                    load_sems.at[kind * CHUNKS + c],
                )
            return carry

        lax.fori_loop(0, chunk_pieces, one, None)

    def wait_chunk(c):
        for kind in range(3):
            view = buffers[kind].at[c]
            pltpu.make_async_copy(view, view, load_sems.at[kind * CHUNKS + c]).wait()

    lax.fori_loop(0, kind_pieces, load_out, None)
    load_chunk(0)
    load_chunk(1)
    mixed = mixed_ref[...].T
    pltpu.make_async_copy(w_out, w_out, load_sems.at[3 * CHUNKS]).wait()
    pre_one = x_ref[...].astype(F32) + dot_nt(mixed, w_out[...])
    unit_one, scale_one = norm_stats(pre_one)
    h_one = unit_one * norm_ref[0:1, :] + norm_ref[1:2, :]
    h_low = h_one.astype(BF16)

    def forward(c, pre_two):
        @pl.when(c + 2 < CHUNKS)
        def _():
            load_chunk(c + 2)

        wait_chunk(c)
        gate = dot_nt(h_low, w_gate[c])
        up = dot_nt(h_low, w_up[c])
        below = 0.5 * (1.0 + lax.erf(gate * (0.5**0.5)))
        gelu = gate * below
        slope = below + gate * (jnp.exp(-0.5 * gate * gate) * (0.5 / jnp.pi) ** 0.5)
        hidden = (gelu * up).astype(BF16)
        keep_gate[c] = up * slope
        keep_up[c] = gelu
        keep_hidden[c] = hidden
        return pre_two + dot_nn(hidden, w_down[c])

    pre_two = lax.fori_loop(0, CHUNKS, forward, h_one)
    unit_two, scale_two = norm_stats(pre_two)
    out_ref[...] = (unit_two * norm_ref[2:3, :] + norm_ref[3:4, :]).astype(BF16)
    d_pre_two, d_gain_two, d_bias_two = norm_back(
        unit_two, scale_two, norm_ref[2:3, :], cot_ref[...].astype(F32)
    )
    d_branch = d_pre_two.astype(BF16)

    def drain(slot):
        for kind in range(3):
            view = stage.at[slot, kind]
            pltpu.make_async_copy(view, view, store_sems.at[slot * 3 + kind]).wait()

    def backward(c, d_h):
        slot = lax.rem(c, 2)

        @pl.when(c >= 2)
        def _():
            drain(slot)

        d_hidden = dot_nt(d_branch, w_down[c])
        d_gate = (d_hidden * keep_gate[c]).astype(BF16)
        d_up = (d_hidden * keep_up[c]).astype(BF16)
        stage[slot, 0] = dot_tn(d_gate, h_low).astype(BF16)
        stage[slot, 1] = dot_tn(d_up, h_low).astype(BF16)
        stage[slot, 2] = dot_tn(keep_hidden[c], d_branch).astype(BF16)

        def store(step, carry):
            for kind in range(3):
                pltpu.make_async_copy(
                    stage.at[slot, kind, pl.ds(step * piece, piece)],
                    grads.at[place[bases[kind] + c * chunk_pieces + step]],
                    store_sems.at[slot * 3 + kind],
                ).start()
            return carry

        lax.fori_loop(0, chunk_pieces, store, None)
        return d_h + dot_nn(d_gate, w_gate[c]) + dot_nn(d_up, w_up[c])

    d_h = lax.fori_loop(0, CHUNKS, backward, d_pre_two)
    d_pre_one, d_gain_one, d_bias_one = norm_back(unit_one, scale_one, norm_ref[0:1, :], d_h)
    d_pre_one_ref[...] = d_pre_one
    d_proj = d_pre_one.astype(BF16)
    d_mixed_ref[...] = lax.dot_general(
        w_out[...], d_proj, (((0,), (1,)), ((), ())), preferred_element_type=F32
    ).astype(BF16)
    stage_out[...] = dot_tn(d_proj, mixed).astype(BF16)

    def store_out(step, carry):
        pltpu.make_async_copy(
            stage_out.at[pl.ds(step * piece, piece)],
            grads.at[place[3 * kind_pieces + step]],
            store_sems.at[6],
        ).start()
        return carry

    lax.fori_loop(0, kind_pieces, store_out, None)
    norm_grad[...] = jnp.concatenate(
        [
            d_gain_one,
            d_bias_one,
            d_gain_two,
            d_bias_two,
            jnp.zeros((4, d_gain_one.shape[1]), F32),
        ],
        axis=0,
    )
    drain(CHUNKS % 2)
    drain((CHUNKS + 1) % 2)
    pltpu.make_async_copy(stage_out, stage_out, store_sems.at[6]).wait()


def project_grad_kernel(
    sizes,
    place,
    info,
    x_ref,
    d_groups,
    d_own,
    d_pre_one,
    mine,
    twin,
    grads_in,
    d_input,
    grads,
    w_all,
    stage,
    blank,
    load_sem,
    store_sem,
    blank_sem,
):
    slots, piece, kind_pieces, splits, tok = sizes
    core, group, split = info[0], info[1], info[2]
    group_pieces = kind_pieces // GROUPS
    del grads_in

    def load(step, carry):
        for kind in range(3):
            row = (lax.div(step, group_pieces) * 3 + kind) * group_pieces + lax.rem(
                step, group_pieces
            )
            fetch_piece(
                place,
                kind * kind_pieces + step,
                slots,
                core,
                mine,
                twin,
                w_all.at[pl.ds(row * piece, piece)],
                load_sem,
            )
        return carry

    lax.fori_loop(0, kind_pieces, load, None)
    blank[...] = jnp.zeros_like(blank)

    def clear(step, carry):
        other = lax.div(step, group_pieces)
        number = lax.rem(group + 1 + other, GROUPS) * group_pieces + lax.rem(step, group_pieces)
        for kind in range(3):
            pltpu.make_async_copy(
                blank.at[pl.ds(0, piece)], grads.at[place[kind * kind_pieces + number]], blank_sem
            ).start()
        return carry

    lax.fori_loop(0, (GROUPS - 1) * group_pieces, clear, None)
    total = dot_nn(d_groups[0], x_ref[split, 0:tok, :])
    for index in range(1, GROUPS):
        total = total + dot_nn(d_groups[index], x_ref[index * splits + split, 0:tok, :])
    stage[...] = total.astype(BF16)

    def store(step, carry):
        for kind in range(3):
            pltpu.make_async_copy(
                stage.at[pl.ds((kind * group_pieces + step) * piece, piece)],
                grads.at[place[kind * kind_pieces + group * group_pieces + step]],
                store_sem,
            ).start()
        return carry

    lax.fori_loop(0, group_pieces, store, None)
    pltpu.make_async_copy(w_all, w_all, load_sem).wait()
    d_input[...] = d_pre_one[...] + dot_tn(d_own[...], w_all[...])
    pltpu.make_async_copy(stage, stage, store_sem).wait()
    pltpu.make_async_copy(blank, blank, blank_sem).wait()


def holder(order, n_dp):
    dp = lax.rem(order, n_dp)
    return {"b": lax.div(order, n_dp), "y": lax.div(dp, 2), "core": lax.rem(dp, 2)}


def greet(peers):
    barrier = pltpu.get_barrier_semaphore()
    for peer in peers:
        pl.semaphore_signal(barrier, inc=1, device_id=peer, device_id_type=MESH_IDS)
    pl.semaphore_wait(barrier, len(peers))


def my_order(n_dp):
    return lax.axis_index("b") * n_dp + lax.axis_index("y") * 2 + lax.axis_index("core")


def swap_heads_kernel(sizes, in_ref, out_ref, send_sems, recv_sems, own_sem):
    n_dp, splits = sizes
    order = my_order(n_dp)
    group, split = lax.div(order, splits), lax.rem(order, splits)
    others = [lax.rem(group + k, GROUPS) for k in range(1, GROUPS)]
    peers = [holder(other * splits + split, n_dp) for other in others]
    greet(peers)
    copies = []
    for k in range(GROUPS - 1):
        copy = pltpu.make_async_remote_copy(
            src_ref=in_ref.at[others[k]],
            dst_ref=out_ref.at[group],
            send_sem=send_sems.at[k],
            recv_sem=recv_sems.at[k],
            device_id=peers[k],
            device_id_type=MESH_IDS,
        )
        copy.start()
        copies.append(copy)
    own = pltpu.make_async_copy(in_ref.at[group], out_ref.at[group], own_sem)
    own.start()
    own.wait()
    for copy in copies:
        copy.wait()


def share_grads_kernel(
    sizes,
    dq_ref,
    dkv_ref,
    groups_ref,
    own_ref,
    landed,
    near_send,
    near_recv,
    send_sems,
    recv_sems,
    own_sem,
):
    n_dp, splits = sizes
    order = my_order(n_dp)
    group, split = lax.div(order, splits), lax.rem(order, splits)
    twins = [lax.rem(split + k, splits) for k in range(1, splits)]
    twin_ids = [holder(group * splits + other, n_dp) for other in twins]
    others = [lax.rem(group + k, GROUPS) for k in range(1, GROUPS)]
    peers = [holder(other * splits + split, n_dp) for other in others]
    greet(twin_ids + peers)
    near = []
    for k in range(splits - 1):
        copy = pltpu.make_async_remote_copy(
            src_ref=dkv_ref.at[twins[k]],
            dst_ref=landed.at[k],
            send_sem=near_send.at[k],
            recv_sem=near_recv.at[k],
            device_id=twin_ids[k],
            device_id_type=MESH_IDS,
        )
        copy.start()
        near.append(copy)
    groups_ref[:, 0] = dq_ref[...]
    for copy in near:
        copy.wait()
    for index in range(GROUPS):
        for kind in range(2):
            total = dkv_ref[split, index, kind].astype(F32)
            for k in range(splits - 1):
                total = total + landed[k, index, kind].astype(F32)
            groups_ref[index, kind + 1] = total.astype(BF16)
    copies = []
    for k in range(GROUPS - 1):
        copy = pltpu.make_async_remote_copy(
            src_ref=groups_ref.at[others[k]],
            dst_ref=own_ref.at[group],
            send_sem=send_sems.at[k],
            recv_sem=recv_sems.at[k],
            device_id=peers[k],
            device_id_type=MESH_IDS,
        )
        copy.start()
        copies.append(copy)
    own = pltpu.make_async_copy(groups_ref.at[group], own_ref.at[group], own_sem)
    own.start()
    own.wait()
    for copy in copies:
        copy.wait()


def add_low(dst, src, rows):
    def one(i, carry):
        dst[i] = (dst[i].astype(F32) + src[i].astype(F32)).astype(BF16)
        return carry

    lax.fori_loop(0, rows, one, None)


def reduce_kernel(
    sizes,
    grads,
    norm_in,
    total_out,
    norm_out,
    held,
    near,
    ya,
    xa,
    za,
    xc,
    zc,
    yc,
    norm_core,
    norm_y,
    norm_x,
    norm_z,
    norm_sum,
    load_sems,
    near_sems,
    ya_sems,
    xa_sems,
    za_sems,
    xc_sems,
    zc_sems,
    yc_sems,
    norm_sems,
):
    zn, xn, yn, slots, part = sizes
    rest = slots - part
    z, x = lax.axis_index("a"), lax.axis_index("b")
    y, core = lax.axis_index("y"), lax.axis_index("core")
    core_peer = {"core": 1 - core}
    y_peers = [{"y": lax.rem(y + k, yn)} for k in range(1, yn)]
    x_peers = [{"b": lax.rem(x + k, xn)} for k in range(1, xn)]
    z_peers = [{"a": lax.rem(z + k, zn)} for k in range(1, zn)]
    greet([core_peer] + y_peers + x_peers + z_peers)

    def remote(src, dst, sems, index, peer):
        return pltpu.make_async_remote_copy(
            src_ref=src,
            dst_ref=dst,
            send_sem=sems.at[0, index],
            recv_sem=sems.at[1, index],
            device_id=peer,
            device_id_type=MESH_IDS,
        )

    def flat(jz, jx, jy):
        return (jz * xn + jx) * yn + jy

    def chip_rows(jz, jx, jy, which):
        chip = (lax.rem(z + jz, zn) * xn + lax.rem(x + jx, xn)) * yn + lax.rem(y + jy, yn)
        return grads.at[pl.ds((chip * 2 + which) * slots, slots)]

    def near_copy(jz, jx, jy):
        index = flat(jz, jx, jy)
        return remote(chip_rows(jz, jx, jy, 1 - core), near.at[index], near_sems, index, core_peer)

    def load_copy(jz, jx, jy):
        index = flat(jz, jx, jy)
        return pltpu.make_async_copy(
            chip_rows(jz, jx, jy, core), held.at[index], load_sems.at[index]
        )

    def first(jz, jx, jy):
        return held.at[flat(jz, jx, jy), pl.ds(0, part)]

    def second(jz, jx, jy):
        return held.at[flat(jz, jx, jy), pl.ds(part, rest)]

    def ya_copy(jz, jx, jy):
        index = ((jy - 1) * zn + jz) * xn + jx
        return remote(first(jz, jx, jy), ya.at[index], ya_sems, index, y_peers[jy - 1])

    def xa_copy(jz, jx):
        index = (jx - 1) * zn + jz
        return remote(first(jz, jx, 0), xa.at[index], xa_sems, index, x_peers[jx - 1])

    def za_copy(jz):
        return remote(first(jz, 0, 0), za.at[jz - 1], za_sems, jz - 1, z_peers[jz - 1])

    def xc_copy(jz, jx, jy):
        index = ((jx - 1) * zn + jz) * yn + jy
        return remote(second(jz, jx, jy), xc.at[index], xc_sems, index, x_peers[jx - 1])

    def zc_copy(jz, jy):
        index = (jz - 1) * yn + jy
        return remote(second(jz, 0, jy), zc.at[index], zc_sems, index, z_peers[jz - 1])

    def yc_copy(jy):
        return remote(second(0, 0, jy), yc.at[jy - 1], yc_sems, jy - 1, y_peers[jy - 1])

    z_order = list(range(1, zn)) + [0]
    x_order = list(range(1, xn)) + [0]
    y_order = list(range(1, yn)) + [0]
    chips = []
    for far_x, far_y in ((True, True), (False, True), (True, False), (False, False)):
        for jz in z_order:
            for jx in x_order:
                for jy in y_order:
                    if (jx != 0) == far_x and (jy != 0) == far_y:
                        chips.append((jz, jx, jy))
    started = []
    for chip in chips:
        copy = near_copy(*chip)
        copy.start()
        started.append(copy)
        load_copy(*chip).start()

    def launch(copy):
        copy.start()
        started.append(copy)

    norm_count = [0]

    def norm_step(buffer, peers):
        copies = []
        for k, peer in enumerate(peers):
            index = norm_count[0]
            norm_count[0] += 1
            copy = remote(norm_sum.at[len(steps_done)], buffer.at[k], norm_sems, index, peer)
            copy.start()
            copies.append(copy)
        return copies

    steps_done = []

    def norm_finish(buffer, copies):
        total = norm_sum[len(steps_done)]
        for k, copy in enumerate(copies):
            copy.wait()
            total = total + buffer[k]
        steps_done.append(None)
        norm_sum[len(steps_done)] = total

    norm_sum[0] = norm_in[...]
    pending = norm_step(norm_core, [core_peer])

    for chip in chips:
        jz, jx, jy = chip
        load_copy(*chip).wait()
        near_copy(*chip).wait_recv()
        index = flat(*chip)
        add_low(held.at[index], near.at[index], slots)
        if jy != 0:
            launch(ya_copy(*chip))
        if jx != 0:
            launch(xc_copy(*chip))

    norm_finish(norm_core, pending)
    pending = norm_step(norm_y, y_peers)

    for jz in z_order:
        for jx in x_order[:-1]:
            for jy in y_order[:-1]:
                copy = ya_copy(jz, jx, jy)
                copy.wait_recv()
                add_low(first(jz, jx, 0), ya.at[((jy - 1) * zn + jz) * xn + jx], part)
            launch(xa_copy(jz, jx))
        for jy in y_order[:-1]:
            for jx in x_order[:-1]:
                xc_copy(jz, jx, jy).wait_recv()
                add_low(second(jz, 0, jy), xc.at[((jx - 1) * zn + jz) * yn + jy], rest)
            if jz != 0:
                launch(zc_copy(jz, jy))

    norm_finish(norm_y, pending)
    pending = norm_step(norm_x, x_peers)

    for jz in z_order:
        for jx in x_order[:-1]:
            xc_copy(jz, jx, 0).wait_recv()
            add_low(second(jz, 0, 0), xc.at[((jx - 1) * zn + jz) * yn], rest)
        if jz != 0:
            launch(zc_copy(jz, 0))

    for jy in y_order[:-1]:
        for jz in z_order[:-1]:
            zc_copy(jz, jy).wait_recv()
            add_low(second(0, 0, jy), zc.at[(jz - 1) * yn + jy], rest)
        launch(yc_copy(jy))

    norm_finish(norm_x, pending)
    pending = norm_step(norm_z, z_peers)

    for jz in z_order:
        for jy in y_order[:-1]:
            ya_copy(jz, 0, jy).wait_recv()
            add_low(first(jz, 0, 0), ya.at[((jy - 1) * zn + jz) * xn], part)
        for jx in x_order[:-1]:
            xa_copy(jz, jx).wait_recv()
            add_low(first(jz, 0, 0), xa.at[(jx - 1) * zn + jz], part)
        if jz != 0:
            launch(za_copy(jz))

    for jz in z_order[:-1]:
        zc_copy(jz, 0).wait_recv()
    for jy in y_order[:-1]:
        yc_copy(jy).wait_recv()

    def last_second(i, carry):
        total = held[flat(0, 0, 0), part + i].astype(F32)
        for jz in z_order[:-1]:
            total = total + zc[(jz - 1) * yn, i].astype(F32)
        for jy in y_order[:-1]:
            total = total + yc[jy - 1, i].astype(F32)
        total_out[part + i] = total
        return carry

    lax.fori_loop(0, rest, last_second, None)
    for jz in z_order[:-1]:
        za_copy(jz).wait_recv()

    def last_first(i, carry):
        total = held[flat(0, 0, 0), i].astype(F32)
        for jz in z_order[:-1]:
            total = total + za[jz - 1, i].astype(F32)
        total_out[i] = total
        return carry

    lax.fori_loop(0, part, last_first, None)
    norm_finish(norm_z, pending)
    norm_out[...] = norm_sum[4]
    for copy in started:
        copy.wait_send()


def vmem():
    return pl.BlockSpec(memory_space=pltpu.VMEM)


def smem():
    return pl.BlockSpec(memory_space=pltpu.SMEM)


def anywhere():
    return pl.BlockSpec(memory_space=pl.ANY)


def shape_of(dims, kind):
    return jax.ShapeDtypeStruct(dims, kind)


def params(collective=None):
    if collective is None:
        return pltpu.CompilerParams(vmem_limit_bytes=VMEM_LIMIT)
    return pltpu.CompilerParams(
        vmem_limit_bytes=VMEM_LIMIT, collective_id=collective, has_side_effects=True
    )


def swap_heads(block, n_dp, splits, collective):
    return pl.pallas_call(
        functools.partial(swap_heads_kernel, (n_dp, splits)),
        out_shape=shape_of(block.shape, BF16),
        in_specs=[vmem()],
        out_specs=vmem(),
        scratch_shapes=[
            pltpu.SemaphoreType.DMA((GROUPS - 1,)),
            pltpu.SemaphoreType.DMA((GROUPS - 1,)),
            pltpu.SemaphoreType.DMA,
        ],
        compiler_params=params(collective),
    )(block)


def per_device(
    dims,
    layer_input,
    out_cotangent,
    segment_ids,
    piece_owner,
    weight_master,
    weight_first,
    weight_second,
    norm_params,
    norm_first,
    norm_second,
):
    n_seq, n_dp = dims
    reps = n_seq // n_dp
    splits = n_seq // GROUPS
    slots, piece, width = weight_master.shape
    pieces = piece_owner.shape[0]
    tok = layer_input.shape[1]
    length = tok * n_seq
    hidden_units = (pieces * piece - 4 * width) // 3
    head = width // HEADS
    kind_pieces = width // piece
    hidden_pieces = hidden_units // piece
    chunk = hidden_units // CHUNKS

    location = locate_pieces(piece_owner, slots)
    own_low = weight_master.astype(BF16)
    mine = lax.all_gather(own_low, ("a", "b", "y"), axis=0, tiled=True)
    twin = lax.ppermute(mine, "core", [(0, 1), (1, 0)])

    turn = [(i * n_dp + j, j * n_dp + i) for i in range(n_dp) for j in range(n_dp)]
    turn_axes = ("a", "y", "core")
    seg_row = jnp.zeros((16, width), BF16).at[0, :tok].set(segment_ids[0].astype(BF16))
    packed = lax.ppermute(
        jnp.concatenate([layer_input[0], seg_row, out_cotangent[0]], axis=0), turn_axes, turn
    )
    tokens = packed[:tok]
    cotangent = packed[tok + 16 :]
    gathered = lax.all_gather(packed[: tok + 16], ("b", "y", "core"), axis=0, tiled=False)

    core = lax.axis_index("core")
    order = my_order(n_dp)
    group, split = order // splits, order % splits
    info = jnp.stack([core, group, split]).astype(jnp.int32)
    slopes = head_slopes(HEADS, tok, n_seq)

    segs = gathered[:, tok, :tok]
    lanes = jnp.arange(128, dtype=jnp.int32)[None, :] - head
    key_same = segs.reshape(length, 1).astype(jnp.int32) == lanes
    key_marks = jnp.where(key_same | (lanes < 0) | (lanes > 2), 0.0, MASKED).astype(BF16)
    query_segs = lax.dynamic_index_in_dim(
        segs.reshape(GROUPS, splits, tok), split, axis=1, keepdims=False
    )
    query_marks = (query_segs.reshape(GROUPS * tok, 1).astype(jnp.int32) == lanes).astype(BF16)

    attend_sizes = (n_dp, reps, splits, tok, slots, head, n_seq)
    q_ext, k_ext, k_turned, v_rows, mixed_low, mixed_full, log_total = pl.pallas_call(
        functools.partial(attend_forward_kernel, attend_sizes),
        out_shape=(
            shape_of((TRIO, GROUPS * tok, 128), BF16),
            shape_of((TRIO, length, 128), BF16),
            shape_of((TRIO, head, length), BF16),
            shape_of((TRIO, length, head), BF16),
            shape_of((GROUPS, TRIO, head, tok), BF16),
            shape_of((GROUPS, TRIO, head, tok), F32),
            shape_of((GROUPS, TRIO, 1, tok), F32),
        ),
        in_specs=[smem(), smem(), smem(), vmem(), vmem(), vmem(), anywhere(), anywhere()],
        out_specs=(vmem(),) * 7,
        scratch_shapes=[
            pltpu.VMEM((3 * TRIO, 128, width), BF16),
            pltpu.VMEM((TRIO, head, length), BF16),
            pltpu.VMEM((3 * TRIO, tok, tok), F32),
            pltpu.VMEM((n_seq, tok, tok), F32),
            pltpu.SemaphoreType.DMA((3 * TRIO * (head // piece),)),
        ],
        compiler_params=params(),
    )(location, info, slopes, gathered, query_marks, key_marks, mine, twin)

    mixed_own = swap_heads(mixed_low.reshape(GROUPS, TRIO * head, tok), n_dp, splits, 1)

    out_low, d_pre_one, d_mixed, norm_part, grads = pl.pallas_call(
        functools.partial(
            dense_kernel, (slots, piece, kind_pieces, chunk // piece, hidden_pieces)
        ),
        out_shape=(
            shape_of((tok, width), BF16),
            shape_of((tok, width), F32),
            shape_of((width, tok), BF16),
            shape_of((8, width), F32),
            shape_of((n_seq * n_dp * slots, piece, width), BF16),
        ),
        in_specs=[smem(), smem(), vmem(), vmem(), vmem(), vmem(), anywhere(), anywhere()],
        out_specs=(vmem(), vmem(), vmem(), vmem(), anywhere()),
        scratch_shapes=[
            pltpu.VMEM((width, width), BF16),
            pltpu.VMEM((CHUNKS, chunk, width), BF16),
            pltpu.VMEM((CHUNKS, chunk, width), BF16),
            pltpu.VMEM((CHUNKS, chunk, width), BF16),
            pltpu.VMEM((CHUNKS, tok, chunk), F32),
            pltpu.VMEM((CHUNKS, tok, chunk), F32),
            pltpu.VMEM((CHUNKS, tok, chunk), BF16),
            pltpu.VMEM((2, 3, chunk, width), BF16),
            pltpu.VMEM((width, width), BF16),
            pltpu.SemaphoreType.DMA((3 * CHUNKS + 1,)),
            pltpu.SemaphoreType.DMA((7,)),
        ],
        compiler_params=params(),
    )(
        location,
        info,
        tokens,
        cotangent,
        mixed_own.reshape(width, tok),
        norm_params,
        mine,
        twin,
    )

    result = lax.ppermute(out_low, turn_axes, turn)
    d_mixed_own = swap_heads(d_mixed.reshape(GROUPS, TRIO * head, tok), n_dp, splits, 2)

    d_query, d_key_value = pl.pallas_call(
        functools.partial(attend_backward_kernel, attend_sizes),
        out_shape=(
            shape_of((GROUPS, TRIO, head, tok), BF16),
            shape_of((splits, GROUPS, 2, TRIO, head, tok), BF16),
        ),
        in_specs=[smem(), smem()] + [vmem()] * 7,
        out_specs=(vmem(), vmem()),
        scratch_shapes=[
            pltpu.VMEM((TRIO, length, 128), F32),
            pltpu.VMEM((TRIO, length, head), F32),
            pltpu.VMEM((3 * TRIO, tok, tok), F32),
        ],
        compiler_params=params(),
    )(
        info,
        slopes,
        q_ext,
        k_ext,
        k_turned,
        v_rows,
        mixed_full,
        log_total,
        d_mixed_own.reshape(GROUPS, TRIO, head, tok),
    )

    trio_rows = TRIO * head
    d_groups, d_own = pl.pallas_call(
        functools.partial(share_grads_kernel, (n_dp, splits)),
        out_shape=(
            shape_of((GROUPS, 3, trio_rows, tok), BF16),
            shape_of((GROUPS, 3, trio_rows, tok), BF16),
        ),
        in_specs=[vmem(), vmem()],
        out_specs=(vmem(), vmem()),
        scratch_shapes=[
            pltpu.VMEM((splits - 1, GROUPS, 2, trio_rows, tok), BF16),
            pltpu.SemaphoreType.DMA((splits - 1,)),
            pltpu.SemaphoreType.DMA((splits - 1,)),
            pltpu.SemaphoreType.DMA((GROUPS - 1,)),
            pltpu.SemaphoreType.DMA((GROUPS - 1,)),
            pltpu.SemaphoreType.DMA,
        ],
        compiler_params=params(3),
    )(
        d_query.reshape(GROUPS, trio_rows, tok),
        d_key_value.reshape(splits, GROUPS, 2, trio_rows, tok),
    )

    d_tokens, grads = pl.pallas_call(
        functools.partial(project_grad_kernel, (slots, piece, kind_pieces, splits, tok)),
        out_shape=(shape_of((tok, width), F32), shape_of(grads.shape, BF16)),
        in_specs=[smem(), smem(), vmem(), vmem(), vmem(), vmem()] + [anywhere()] * 3,
        out_specs=(vmem(), anywhere()),
        scratch_shapes=[
            pltpu.VMEM((3 * width, width), BF16),
            pltpu.VMEM((3 * trio_rows, width), BF16),
            pltpu.VMEM(((GROUPS - 1) * 3 * trio_rows, width), BF16),
            pltpu.SemaphoreType.DMA,
            pltpu.SemaphoreType.DMA,
            pltpu.SemaphoreType.DMA,
        ],
        input_output_aliases={8: 1},
        compiler_params=params(),
    )(
        location,
        info,
        gathered,
        d_groups.reshape(GROUPS, 3 * trio_rows, tok),
        d_own.reshape(3 * width, tok),
        d_pre_one,
        mine,
        twin,
        grads,
    )
    d_input = lax.ppermute(d_tokens, turn_axes, turn)

    zn, xn, yn = n_dp, reps, n_dp // 2
    part = slots * 5 // 8
    rest = slots - part
    n_chips = zn * xn * yn
    counts = {
        "near": n_chips,
        "ya": (yn - 1) * zn * xn,
        "xa": (xn - 1) * zn,
        "za": zn - 1,
        "xc": (xn - 1) * zn * yn,
        "zc": (zn - 1) * yn,
        "yc": yn - 1,
    }

    def chunks(name, rows):
        return pltpu.VMEM((max(counts[name], 1), rows, piece, width), BF16)

    def norm_rows(count):
        return pltpu.VMEM((max(count, 1), 8, width), F32)

    own_grad, norm_total = pl.pallas_call(
        functools.partial(reduce_kernel, (zn, xn, yn, slots, part)),
        out_shape=(shape_of((slots, piece, width), F32), shape_of((8, width), F32)),
        in_specs=[anywhere(), vmem()],
        out_specs=(vmem(), vmem()),
        scratch_shapes=[
            chunks("near", slots),
            chunks("near", slots),
            chunks("ya", part),
            chunks("xa", part),
            chunks("za", part),
            chunks("xc", rest),
            chunks("zc", rest),
            chunks("yc", rest),
            norm_rows(1),
            norm_rows(yn - 1),
            norm_rows(xn - 1),
            norm_rows(zn - 1),
            norm_rows(5),
            pltpu.SemaphoreType.DMA((n_chips,)),
        ]
        + [
            pltpu.SemaphoreType.DMA((2, max(counts[name], 1)))
            for name in ("near", "ya", "xa", "za", "xc", "zc", "yc")
        ]
        + [pltpu.SemaphoreType.DMA((2, 1 + (yn - 1) + (xn - 1) + (zn - 1)))],
        compiler_params=params(4),
    )(grads, norm_part)

    numbers = jnp.arange(pieces, dtype=jnp.int32) + 1
    own_slots = lax.axis_index(("a", "b", "y", "core")) * slots + jnp.arange(slots)
    inverse = jnp.sum(jnp.where(location[None, :] == own_slots[:, None], numbers[None, :], 0), axis=1)
    own_grad = jnp.where((inverse > 0)[:, None, None], own_grad, 0.0)
    norm_grad = norm_total[:4]
    rates = slot_rates(inverse, piece, width, hidden_units)
    first_new, second_new, weight_new = adamw_step(
        weight_master, weight_first, weight_second, own_grad, rates[:, None, None], STEP
    )
    norm_first_new, norm_second_new, norm_new = adamw_step(
        norm_params, norm_first, norm_second, norm_grad, NORM_RATE, STEP
    )
    return (
        result[None],
        d_input[None],
        own_grad,
        first_new,
        second_new,
        weight_new,
        weight_new.astype(BF16),
        norm_grad,
        norm_first_new,
        norm_second_new,
        norm_new,
    )


def solution(mesh):
    n_seq, n_dp = mesh.shape["seq"], mesh.shape["dp"]
    inner = Mesh(
        mesh.devices.reshape(n_dp, n_seq // n_dp, n_dp // 2, 2), ("a", "b", "y", "core")
    )
    seq, dp, every = ("a", "b"), ("y", "core"), ("a", "b", "y", "core")
    block = P(dp, seq, None)
    owned = P(every, None, None)
    in_specs = (block, block, P(dp, seq), P(), owned, owned, owned, P(), P(), P())
    out_specs = (block, block, owned, owned, owned, owned, owned, P(), P(), P(), P())
    return jax.shard_map(
        functools.partial(per_device, (n_seq, n_dp)),
        mesh=inner,
        in_specs=in_specs,
        out_specs=out_specs,
        check_vma=False,
    )
```

```python
import functools

import jax
import jax.numpy as jnp
from jax import lax
from jax.experimental import pallas as pl
from jax.experimental.pallas import tpu as pltpu
from jax.sharding import Mesh
from jax.sharding import PartitionSpec as P

HEADS = 12
GROUPS = 4
TRIO = HEADS // GROUPS
STEP = 4

NORM_EPS = 1e-06
BETA_ONE = 0.5
BETA_TWO = 0.5
DECAY = 0.01
ADAM_EPS = 1e-08
NORM_RATE = 0.3
OUT_RATE = 0.35
MASKED = -1e30
CHUNKS = 6
VMEM_LIMIT = 60 * 1024 * 1024
MESH_IDS = pl.DeviceIdType.MESH
F32 = jnp.float32
BF16 = jnp.bfloat16


def head_slopes(head_count, tok_rows, seq_devices):
    head_order = jnp.arange(head_count, dtype=jnp.float32)
    return (
        8.0 / tok_rows * jnp.power(jnp.float32(8.0 * seq_devices), -head_order / (head_count - 1))
    )


def locate_pieces(owners, slot_count):
    pieces = owners.shape[0]
    numbers = jnp.arange(pieces, dtype=jnp.int32)
    earlier = (owners[None, :] == owners[:, None]) & (numbers[None, :] < numbers[:, None])
    return owners * slot_count + jnp.sum(earlier.astype(jnp.int32), axis=1)


def slot_rates(inverse, piece_rows, model_width, hidden_units):
    first_row = (inverse - 1) * piece_rows
    narrow = model_width ** (-0.5)
    step_rate = jnp.where(
        first_row < 3 * model_width,
        narrow,
        jnp.where(
            first_row < 4 * model_width,
            OUT_RATE,
            jnp.where(
                first_row < 4 * model_width + 2 * hidden_units, narrow, hidden_units ** (-0.5)
            ),
        ),
    )
    return jnp.where(inverse > 0, step_rate, narrow).astype(jnp.float32)


def adamw_step(weight, first_moment, second, gradient, step_rate, step_count):
    first_moment = BETA_ONE * first_moment + (1.0 - BETA_ONE) * gradient
    second = BETA_TWO * second + (1.0 - BETA_TWO) * gradient * gradient
    mean_hat = first_moment / (1.0 - BETA_ONE**step_count)
    square_hat = second / (1.0 - BETA_TWO**step_count)
    weight = weight - step_rate * (mean_hat / (jnp.sqrt(square_hat) + ADAM_EPS) + DECAY * weight)
    return (first_moment, second, weight)


def dot_nt(left_side, right_side):
    return lax.dot_general(
        left_side, right_side, (((1,), (1,)), ((), ())), preferred_element_type=F32
    )


def dot_nn(left_side, right_side):
    return lax.dot_general(
        left_side, right_side, (((1,), (0,)), ((), ())), preferred_element_type=F32
    )


def dot_tn(left_side, right_side):
    return lax.dot_general(
        left_side, right_side, (((0,), (0,)), ((), ())), preferred_element_type=F32
    )


def fetch_piece(place, piece, weights, dst, sem):
    pltpu.make_async_copy(weights.at[place[piece]], dst, sem).start()


def fill_tables(table, slopes, group, tok):
    apart = lax.broadcasted_iota(jnp.int32, (tok, tok), 0) - lax.broadcasted_iota(
        jnp.int32, (tok, tok), 1
    )
    apart = apart.astype(F32)
    for h in range(TRIO):
        slope = slopes[group * TRIO + h]
        table[h * 3 + 0] = -slope * apart
        table[h * 3 + 1] = slope * jnp.abs(apart)
        table[h * 3 + 2] = slope * apart


def block_place(order, n_dp, reps):
    return (order % n_dp) * reps + order // n_dp


def bias_of(key_block, query_place, slope, h, tok, n_dp, reps):
    key_place = block_place(key_block, n_dp, reps)
    which = jnp.where(key_place > query_place, 2, jnp.where(key_place < query_place, 0, 1))
    shift = slope * (tok * jnp.abs(key_place - query_place)).astype(F32)
    return h * 3 + which, shift


def attend_forward_kernel(
    sizes,
    place,
    info,
    slopes,
    x_ref,
    query_marks,
    key_marks,
    weights,
    q_out,
    k_out,
    kt_out,
    v_out,
    mixed_low,
    mixed_full,
    log_out,
    wpad,
    vt,
    table,
    scores,
    sems,
):
    n_dp, reps, splits, tok, head, blocks = sizes
    group, split = info[1], info[2]
    per_head = head // 16
    width = x_ref.shape[2]
    kind_pieces = width // 16

    def start(step, carry):
        kind = lax.div(step, TRIO * per_head)
        rest = lax.rem(step, TRIO * per_head)
        number = kind * kind_pieces + group * (TRIO * per_head) + rest
        dst = wpad.at[
            kind * TRIO + lax.div(rest, per_head), pl.ds(lax.rem(rest, per_head) * 16, 16)
        ]
        fetch_piece(place, number, weights, dst, sems.at[step])
        return carry

    def finish(step, carry):
        kind = lax.div(step, TRIO * per_head)
        rest = lax.rem(step, TRIO * per_head)
        dst = wpad.at[
            kind * TRIO + lax.div(rest, per_head), pl.ds(lax.rem(rest, per_head) * 16, 16)
        ]
        pltpu.make_async_copy(weights.at[0], dst, sems.at[step]).wait()
        return carry

    lax.fori_loop(0, 3 * TRIO * per_head, start, None)
    for row in range(3 * TRIO):
        wpad[row, head:, :] = jnp.zeros((wpad.shape[1] - head, width), BF16)
    fill_tables(table, slopes, group, tok)
    lax.fori_loop(0, 3 * TRIO * per_head, finish, None)

    w_query = wpad[0:TRIO].reshape(TRIO * 128, width)
    w_key = wpad[TRIO : 2 * TRIO].reshape(TRIO * 128, width)
    w_value = wpad[2 * TRIO : 3 * TRIO].reshape(TRIO * 128, width)

    def project(block, carry):
        rows = pl.ds(pl.multiple_of(block * tok, tok), tok)
        xb = x_ref[block, 0:tok, :]
        keys = dot_nt(xb, w_key).astype(BF16)
        values = dot_nt(xb, w_value).astype(BF16)
        marks = key_marks[rows, :]
        for h in range(TRIO):
            k_out[h, rows, :] = keys[:, h * 128 : (h + 1) * 128] + marks
            v_out[h, rows, :] = values[:, h * 128 : h * 128 + head]
            kt_out[h, :, rows] = dot_nt(wpad[TRIO + h, 0:head, :], xb).astype(BF16)
            vt[h, :, rows] = dot_nt(wpad[2 * TRIO + h, 0:head, :], xb).astype(BF16)
        return carry

    lax.fori_loop(0, blocks, project, None)

    def project_query(index, carry):
        rows = pl.ds(pl.multiple_of(index * tok, tok), tok)
        xb = x_ref[index * splits + split, 0:tok, :]
        queries = dot_nt(xb, w_query).astype(BF16) * jnp.asarray(head**-0.5, BF16)
        marks = query_marks[rows, :]
        for h in range(TRIO):
            q_out[h, rows, :] = queries[:, h * 128 : (h + 1) * 128] + marks
        return carry

    lax.fori_loop(0, GROUPS, project_query, None)

    def attend(step, carry):
        index, h = lax.div(step, TRIO), lax.rem(step, TRIO)
        order = index * splits + split
        query_place = lax.rem(order, n_dp) * reps + lax.div(order, n_dp)
        slope = slopes[group * TRIO + h]
        qh = q_out[h, pl.ds(pl.multiple_of(index * tok, tok), tok), :]
        top = None
        shifts = []
        for kb in range(blocks):
            which, shift = bias_of(kb, query_place, slope, h, tok, n_dp, reps)
            now = dot_nt(k_out[h, kb * tok : (kb + 1) * tok, :], qh) - table[which]
            scores[kb] = now
            here = jnp.max(now, axis=0, keepdims=True) - shift
            top = here if top is None else jnp.maximum(top, here)
            shifts.append(shift)
        total = jnp.zeros((1, tok), F32)
        for kb in range(blocks):
            grown = jnp.exp(scores[kb] - (top + shifts[kb]))
            total = total + jnp.sum(grown, axis=0, keepdims=True)
            scores[kb] = grown
        inverse = 1.0 / total
        mixed = jnp.zeros((head, tok), F32)
        for kb in range(blocks):
            prob = (scores[kb] * inverse).astype(BF16)
            mixed = mixed + dot_nn(vt[h, :, kb * tok : (kb + 1) * tok], prob)
        mixed_full[index, h] = mixed
        mixed_low[index, h] = mixed.astype(BF16)
        log_out[index, h] = top + jnp.log(total)
        return carry

    lax.fori_loop(0, GROUPS * TRIO, attend, None)


def attend_backward_kernel(
    sizes,
    info,
    slopes,
    q_ref,
    k_ref,
    kt_ref,
    v_ref,
    mixed_full,
    log_in,
    d_mixed,
    dq_out,
    dkv_out,
    dk_sum,
    dv_sum,
    table,
):
    n_dp, reps, splits, tok, head, blocks = sizes
    group, split = info[1], info[2]
    fill_tables(table, slopes, group, tok)
    dk_sum[...] = jnp.zeros_like(dk_sum)
    dv_sum[...] = jnp.zeros_like(dv_sum)

    def step_fn(step, carry):
        h, index = lax.div(step, GROUPS), lax.rem(step, GROUPS)
        order = index * splits + split
        query_place = lax.rem(order, n_dp) * reps + lax.div(order, n_dp)
        slope = slopes[group * TRIO + h]
        qh = q_ref[h, pl.ds(pl.multiple_of(index * tok, tok), tok), :]
        dt = d_mixed[index, h]
        row_dot = jnp.sum(dt.astype(F32) * mixed_full[index, h], axis=0, keepdims=True)
        log_total = log_in[index, h]
        dq = jnp.zeros((head, tok), F32)
        for kb in range(blocks):
            rows = slice(kb * tok, (kb + 1) * tok)
            which, shift = bias_of(kb, query_place, slope, h, tok, n_dp, reps)
            now = dot_nt(k_ref[h, rows, :], qh) - table[which]
            prob = jnp.exp(now - (log_total + shift))
            d_prob = dot_nn(v_ref[h, rows, :], dt)
            d_score = (prob * (d_prob - row_dot)).astype(BF16)
            dv_sum[h, rows, :] += dot_nt(prob.astype(BF16), dt)
            dk_sum[h, rows, :] += dot_nn(d_score, qh)
            dq = dq + dot_nn(kt_ref[h, :, rows], d_score)
        dq_out[index, h] = (dq * (head**-0.5)).astype(BF16)
        return carry

    lax.fori_loop(0, TRIO * GROUPS, step_fn, None)

    def flip(step, carry):
        h, index = lax.div(step, GROUPS), lax.rem(step, GROUPS)
        for part in range(splits):
            rows = pl.ds(pl.multiple_of((index * splits + part) * tok, tok), tok)
            dkv_out[part, index, 0, h] = dk_sum[h, rows, :].T[0:head].astype(BF16)
            dkv_out[part, index, 1, h] = dv_sum[h, rows, :].T.astype(BF16)
        return carry

    lax.fori_loop(0, TRIO * GROUPS, flip, None)


def norm_stats(values_in):
    mean = jnp.mean(values_in, axis=-1, keepdims=True)
    centred = values_in - mean
    spread = jnp.mean(centred * centred, axis=-1, keepdims=True)
    scale = lax.rsqrt(spread + NORM_EPS)
    return centred * scale, scale


def norm_back(unit, scale, gain, cotangent):
    d_unit = cotangent * gain
    first = jnp.mean(d_unit, axis=-1, keepdims=True)
    second = jnp.mean(d_unit * unit, axis=-1, keepdims=True)
    d_in = scale * (d_unit - first - unit * second)
    d_gain = jnp.sum(cotangent * unit, axis=0, keepdims=True)
    d_bias = jnp.sum(cotangent, axis=0, keepdims=True)
    return d_in, d_gain, d_bias


def dense_kernel(
    sizes,
    place,
    packed_ref,
    mixed_ref,
    norm_ref,
    weights,
    out_ref,
    d_pre_one_ref,
    d_mixed_ref,
    norm_grad,
    grads,
    w_out,
    w_gate,
    w_up,
    w_down,
    keep_gate,
    keep_up,
    keep_hidden,
    stage,
    stage_out,
    load_sems,
    store_sems,
):
    tok, piece, kind_pieces, chunk_pieces, hidden_pieces = sizes
    first_gate = 4 * kind_pieces
    first_up = first_gate + hidden_pieces
    first_down = first_up + hidden_pieces
    bases = (first_gate, first_up, first_down)
    buffers = (w_gate, w_up, w_down)
    chunk = chunk_pieces * piece

    def load_out(step, carry):
        fetch_piece(
            place,
            3 * kind_pieces + step,
            weights,
            w_out.at[pl.ds(step * piece, piece)],
            load_sems.at[3 * CHUNKS],
        )
        return carry

    def load_chunk(c):
        def one(step, carry):
            for kind in range(3):
                fetch_piece(
                    place,
                    bases[kind] + c * chunk_pieces + step,
                    weights,
                    buffers[kind].at[c, pl.ds(step * piece, piece)],
                    load_sems.at[kind * CHUNKS + c],
                )
            return carry

        lax.fori_loop(0, chunk_pieces, one, None)

    def wait_chunk(c):
        for kind in range(3):
            view = buffers[kind].at[c]
            pltpu.make_async_copy(view, view, load_sems.at[kind * CHUNKS + c]).wait()

    lax.fori_loop(0, kind_pieces, load_out, None)
    load_chunk(0)
    load_chunk(1)
    mixed = mixed_ref[...].T
    pltpu.make_async_copy(w_out, w_out, load_sems.at[3 * CHUNKS]).wait()
    pre_one = packed_ref[0:tok].astype(F32) + dot_nt(mixed, w_out[...])
    unit_one, scale_one = norm_stats(pre_one)
    h_one = unit_one * norm_ref[0:1, :] + norm_ref[1:2, :]
    h_low = h_one.astype(BF16)

    def forward(c, pre_two):
        @pl.when(c + 2 < CHUNKS)
        def _():
            load_chunk(c + 2)

        wait_chunk(c)
        gate = dot_nt(h_low, w_gate[c])
        up = dot_nt(h_low, w_up[c])
        below = 0.5 * (1.0 + lax.erf(gate * (0.5**0.5)))
        gelu = gate * below
        slope = below + gate * (jnp.exp(-0.5 * gate * gate) * (0.5 / jnp.pi) ** 0.5)
        hidden = (gelu * up).astype(BF16)
        keep_gate[c] = up * slope
        keep_up[c] = gelu
        keep_hidden[c] = hidden
        return pre_two + dot_nn(hidden, w_down[c])

    pre_two = lax.fori_loop(0, CHUNKS, forward, h_one)
    unit_two, scale_two = norm_stats(pre_two)
    out_ref[...] = (unit_two * norm_ref[2:3, :] + norm_ref[3:4, :]).astype(BF16)
    d_pre_two, d_gain_two, d_bias_two = norm_back(
        unit_two, scale_two, norm_ref[2:3, :], packed_ref[tok + 16 :].astype(F32)
    )
    d_branch = d_pre_two.astype(BF16)

    def drain(slot):
        for kind in range(3):
            view = stage.at[slot, kind]
            pltpu.make_async_copy(view, view, store_sems.at[slot * 3 + kind]).wait()

    def backward(c, d_h):
        slot = lax.rem(c, 2)

        @pl.when(c >= 2)
        def _():
            drain(slot)

        d_hidden = dot_nt(d_branch, w_down[c])
        d_gate = (d_hidden * keep_gate[c]).astype(BF16)
        d_up = (d_hidden * keep_up[c]).astype(BF16)
        stage[slot, 0] = dot_tn(d_gate, h_low).astype(BF16)
        stage[slot, 1] = dot_tn(d_up, h_low).astype(BF16)
        stage[slot, 2] = dot_tn(keep_hidden[c], d_branch).astype(BF16)

        def store(step, carry):
            for kind in range(3):
                pltpu.make_async_copy(
                    stage.at[slot, kind, pl.ds(step * piece, piece)],
                    grads.at[place[bases[kind] + c * chunk_pieces + step]],
                    store_sems.at[slot * 3 + kind],
                ).start()
            return carry

        lax.fori_loop(0, chunk_pieces, store, None)
        return d_h + dot_nn(d_gate, w_gate[c]) + dot_nn(d_up, w_up[c])

    d_h = lax.fori_loop(0, CHUNKS, backward, d_pre_two)
    d_pre_one, d_gain_one, d_bias_one = norm_back(unit_one, scale_one, norm_ref[0:1, :], d_h)
    d_pre_one_ref[...] = d_pre_one
    d_proj = d_pre_one.astype(BF16)
    d_mixed_ref[...] = lax.dot_general(
        w_out[...], d_proj, (((0,), (1,)), ((), ())), preferred_element_type=F32
    ).astype(BF16)
    stage_out[...] = dot_tn(d_proj, mixed).astype(BF16)

    def store_out(step, carry):
        pltpu.make_async_copy(
            stage_out.at[pl.ds(step * piece, piece)],
            grads.at[place[3 * kind_pieces + step]],
            store_sems.at[6],
        ).start()
        return carry

    lax.fori_loop(0, kind_pieces, store_out, None)
    norm_grad[...] = jnp.concatenate(
        [
            d_gain_one,
            d_bias_one,
            d_gain_two,
            d_bias_two,
            jnp.zeros((4, d_gain_one.shape[1]), F32),
        ],
        axis=0,
    )
    drain(CHUNKS % 2)
    drain((CHUNKS + 1) % 2)
    pltpu.make_async_copy(stage_out, stage_out, store_sems.at[6]).wait()


def project_grad_kernel(
    sizes,
    place,
    info,
    x_ref,
    d_groups,
    d_own,
    d_pre_one,
    weights,
    grads_in,
    d_input,
    grads,
    w_all,
    stage,
    blank,
    load_sem,
    store_sem,
    blank_sem,
):
    piece, kind_pieces, splits, tok = sizes
    group, split = info[1], info[2]
    group_pieces = kind_pieces // GROUPS
    del grads_in

    def load(step, carry):
        for kind in range(3):
            row = (lax.div(step, group_pieces) * 3 + kind) * group_pieces + lax.rem(
                step, group_pieces
            )
            fetch_piece(
                place,
                kind * kind_pieces + step,
                weights,
                w_all.at[pl.ds(row * piece, piece)],
                load_sem,
            )
        return carry

    lax.fori_loop(0, kind_pieces, load, None)
    blank[...] = jnp.zeros_like(blank)

    def clear(step, carry):
        other = lax.div(step, group_pieces)
        number = lax.rem(group + 1 + other, GROUPS) * group_pieces + lax.rem(step, group_pieces)
        for kind in range(3):
            pltpu.make_async_copy(
                blank.at[pl.ds(0, piece)], grads.at[place[kind * kind_pieces + number]], blank_sem
            ).start()
        return carry

    lax.fori_loop(0, (GROUPS - 1) * group_pieces, clear, None)
    total = dot_nn(d_groups[0], x_ref[split, 0:tok, :])
    for index in range(1, GROUPS):
        total = total + dot_nn(d_groups[index], x_ref[index * splits + split, 0:tok, :])
    stage[...] = total.astype(BF16)

    def store(step, carry):
        for kind in range(3):
            pltpu.make_async_copy(
                stage.at[pl.ds((kind * group_pieces + step) * piece, piece)],
                grads.at[place[kind * kind_pieces + group * group_pieces + step]],
                store_sem,
            ).start()
        return carry

    lax.fori_loop(0, group_pieces, store, None)
    pltpu.make_async_copy(w_all, w_all, load_sem).wait()
    d_input[...] = d_pre_one[...] + dot_tn(d_own[...], w_all[...])
    pltpu.make_async_copy(stage, stage, store_sem).wait()
    pltpu.make_async_copy(blank, blank, blank_sem).wait()


def holder(order, n_dp):
    dp = lax.rem(order, n_dp)
    return {"b": lax.div(order, n_dp), "y": lax.div(dp, 2), "core": lax.rem(dp, 2)}


def greet(peers):
    barrier = pltpu.get_barrier_semaphore()
    for peer in peers:
        pl.semaphore_signal(barrier, inc=1, device_id=peer, device_id_type=MESH_IDS)
    pl.semaphore_wait(barrier, len(peers))


def my_order(n_dp):
    return lax.axis_index("b") * n_dp + lax.axis_index("y") * 2 + lax.axis_index("core")


def swap_heads_kernel(sizes, in_ref, out_ref, send_sems, recv_sems, own_sem):
    n_dp, splits = sizes
    order = my_order(n_dp)
    group, split = lax.div(order, splits), lax.rem(order, splits)
    others = [lax.rem(group + k, GROUPS) for k in range(1, GROUPS)]
    peers = [holder(other * splits + split, n_dp) for other in others]
    greet(peers)
    copies = []
    for k in range(GROUPS - 1):
        copy = pltpu.make_async_remote_copy(
            src_ref=in_ref.at[others[k]],
            dst_ref=out_ref.at[group],
            send_sem=send_sems.at[k],
            recv_sem=recv_sems.at[k],
            device_id=peers[k],
            device_id_type=MESH_IDS,
        )
        copy.start()
        copies.append(copy)
    own = pltpu.make_async_copy(in_ref.at[group], out_ref.at[group], own_sem)
    own.start()
    own.wait()
    for copy in copies:
        copy.wait()


def share_grads_kernel(
    sizes,
    dq_ref,
    dkv_ref,
    groups_ref,
    own_ref,
    landed,
    near_send,
    near_recv,
    send_sems,
    recv_sems,
    own_sem,
):
    n_dp, splits = sizes
    order = my_order(n_dp)
    group, split = lax.div(order, splits), lax.rem(order, splits)
    twins = [lax.rem(split + k, splits) for k in range(1, splits)]
    twin_ids = [holder(group * splits + other, n_dp) for other in twins]
    others = [lax.rem(group + k, GROUPS) for k in range(1, GROUPS)]
    peers = [holder(other * splits + split, n_dp) for other in others]
    greet(twin_ids + peers)
    near = []
    for k in range(splits - 1):
        copy = pltpu.make_async_remote_copy(
            src_ref=dkv_ref.at[twins[k]],
            dst_ref=landed.at[k],
            send_sem=near_send.at[k],
            recv_sem=near_recv.at[k],
            device_id=twin_ids[k],
            device_id_type=MESH_IDS,
        )
        copy.start()
        near.append(copy)
    groups_ref[:, 0] = dq_ref[...]
    for copy in near:
        copy.wait()
    for index in range(GROUPS):
        for kind in range(2):
            total = dkv_ref[split, index, kind].astype(F32)
            for k in range(splits - 1):
                total = total + landed[k, index, kind].astype(F32)
            groups_ref[index, kind + 1] = total.astype(BF16)
    copies = []
    for k in range(GROUPS - 1):
        copy = pltpu.make_async_remote_copy(
            src_ref=groups_ref.at[others[k]],
            dst_ref=own_ref.at[group],
            send_sem=send_sems.at[k],
            recv_sem=recv_sems.at[k],
            device_id=peers[k],
            device_id_type=MESH_IDS,
        )
        copy.start()
        copies.append(copy)
    own = pltpu.make_async_copy(groups_ref.at[group], own_ref.at[group], own_sem)
    own.start()
    own.wait()
    for copy in copies:
        copy.wait()


def add_low(dst, src, rows):
    def one(i, carry):
        dst[i] = (dst[i].astype(F32) + src[i].astype(F32)).astype(BF16)
        return carry

    lax.fori_loop(0, rows, one, None)


def z_order_of(count):
    order = [0]
    for k in range(1, count):
        for far in (k, count - k):
            if far not in order:
                order.append(far)
    return order


def spread_kernel(
    sizes,
    own,
    pack,
    every,
    turned,
    gathered,
    z_sems,
    xs_sems,
    ys_sems,
    xf_sems,
    yf_sems,
    near_sems,
    turn_sems,
    bx_sems,
    by_sems,
    bf_sems,
    bn_sems,
    own_sems,
):
    zn, xn, yn, slots, part, rows = sizes
    rest = slots - part
    z, x = lax.axis_index("a"), lax.axis_index("b")
    y, core = lax.axis_index("y"), lax.axis_index("core")
    core_peer = {"core": 1 - core}
    xs, ys, z_order = range(1, xn), range(1, yn), z_order_of(zn)
    x_peers = {k: {"b": lax.rem(x + k, xn)} for k in xs}
    y_peers = {k: {"y": lax.rem(y + k, yn)} for k in ys}
    z_peers = {k: {"a": lax.rem(z + k, zn)} for k in range(1, zn)}
    dp = y * 2 + core
    turn_peer = {"a": dp, "y": lax.div(z, 2), "core": lax.rem(z, 2)}
    moves = dp != z
    barrier = pltpu.get_barrier_semaphore()
    peers = [core_peer, *x_peers.values(), *y_peers.values(), *z_peers.values()]
    for peer in peers:
        pl.semaphore_signal(barrier, inc=1, device_id=peer, device_id_type=MESH_IDS)

    @pl.when(moves)
    def _():
        pl.semaphore_signal(barrier, inc=1, device_id=turn_peer, device_id_type=MESH_IDS)

    pl.semaphore_wait(barrier, len(peers) + moves.astype(jnp.int32))

    def remote(src, dst, sems, index, peer):
        return pltpu.make_async_remote_copy(
            src_ref=src,
            dst_ref=dst,
            send_sem=sems.at[0, index],
            recv_sem=sems.at[1, index],
            device_id=peer,
            device_id_type=MESH_IDS,
        )

    def number(jz, jx, jy):
        chip = (lax.rem(z + zn - jz, zn) * xn + lax.rem(x + xn - jx, xn)) * yn + lax.rem(
            y + yn - jy, yn
        )
        return chip * 2 + core

    def shard(jz, jx, jy, first=0, count=slots):
        return every.at[pl.ds(number(jz, jx, jy) * slots + first, count)]

    def held(jz, jx, jy):
        return own if (jz, jx, jy) == (0, 0, 0) else shard(jz, jx, jy)

    def z_copy(jz):
        return remote(own, shard(0, 0, 0), z_sems, jz - 1, z_peers[jz])

    def xs_copy(jz, jx):
        return remote(
            held(jz, 0, 0), shard(jz, 0, 0), xs_sems, jz * (xn - 1) + jx - 1, x_peers[jx]
        )

    def ys_copy(jz, jy):
        return remote(
            held(jz, 0, 0), shard(jz, 0, 0), ys_sems, jz * (yn - 1) + jy - 1, y_peers[jy]
        )

    def cross(jz, jx, jy):
        return (jz * (xn - 1) + jx - 1) * (yn - 1) + jy - 1

    def xf_copy(jz, jx, jy):
        view = shard(jz, 0, jy, part, rest)
        return remote(view, view, xf_sems, cross(jz, jx, jy), x_peers[jx])

    def yf_copy(jz, jx, jy):
        view = shard(jz, jx, 0, 0, part)
        return remote(view, view, yf_sems, cross(jz, jx, jy), y_peers[jy])

    def near_copy(jz, jx, jy):
        return remote(
            held(jz, jx, jy),
            shard(jz, jx, jy),
            near_sems,
            (jz * xn + jx) * yn + jy,
            core_peer,
        )

    def block(jx, jy, side):
        order = lax.rem(x + xn - jx, xn) * zn + lax.rem(y + yn - jy, yn) * 2 + side
        return gathered.at[order]

    head_rows = turned.at[pl.ds(0, rows)]

    def b_held(jx, jy):
        return head_rows if (jx, jy) == (0, 0) else block(jx, jy, core)

    def bx_copy(jx):
        return remote(head_rows, block(0, 0, core), bx_sems, jx - 1, x_peers[jx])

    def by_copy(jy):
        return remote(head_rows, block(0, 0, core), by_sems, jy - 1, y_peers[jy])

    def bf_copy(jx, jy):
        view = block(0, jy, core)
        return remote(view, view, bf_sems, (jx - 1) * (yn - 1) + jy - 1, x_peers[jx])

    def bn_copy(jx, jy):
        return remote(b_held(jx, jy), block(jx, jy, core), bn_sems, jx * yn + jy, core_peer)

    started = []

    def launch(copy):
        copy.start()
        started.append(copy)

    def send_own(jz):
        for jx in xs:
            launch(xs_copy(jz, jx))
        for jy in ys:
            launch(ys_copy(jz, jy))
        launch(near_copy(jz, 0, 0))

    def forward(jz):
        for jy in ys:
            ys_copy_in(jz, jy)
            for jx in xs:
                launch(xf_copy(jz, jx, jy))
        for jx in xs:
            xs_copy_in(jz, jx)
            for jy in ys:
                launch(yf_copy(jz, jx, jy))
        for jy in ys:
            launch(near_copy(jz, 0, jy))
        for jx in xs:
            launch(near_copy(jz, jx, 0))

    def ys_copy_in(jz, jy):
        view = shard(jz, 0, jy)
        remote(view, view, ys_sems, jz * (yn - 1) + jy - 1, y_peers[jy]).wait_recv()

    def xs_copy_in(jz, jx):
        view = shard(jz, jx, 0)
        remote(view, view, xs_sems, jz * (xn - 1) + jx - 1, x_peers[jx]).wait_recv()

    def finish(jz):
        for jx in xs:
            for jy in ys:
                view = shard(jz, jx, jy, part, rest)
                remote(view, view, xf_sems, cross(jz, jx, jy), x_peers[jx]).wait_recv()
                view = shard(jz, jx, jy, 0, part)
                remote(view, view, yf_sems, cross(jz, jx, jy), y_peers[jy]).wait_recv()
                launch(near_copy(jz, jx, jy))

    def z_in(index):
        jz = z_order[index]
        view = shard(jz, 0, 0)
        remote(view, view, z_sems, jz - 1, z_peers[jz]).wait_recv()
        if index + 1 < zn:
            launch(z_copy(z_order[index + 1]))

    turn_copy = remote(pack, turned, turn_sems, 0, turn_peer)
    turn_local = pltpu.make_async_copy(pack, turned, own_sems.at[0])
    own_local = pltpu.make_async_copy(own, shard(0, 0, 0), own_sems.at[1])
    block_local = pltpu.make_async_copy(head_rows, block(0, 0, core), own_sems.at[2])

    launch(z_copy(z_order[1]))
    send_own(0)

    @pl.when(moves)
    def _():
        turn_copy.start()

    @pl.when(jnp.logical_not(moves))
    def _():
        turn_local.start()

    own_local.start()

    def turn_in():
        @pl.when(moves)
        def _():
            turn_copy.wait()

        @pl.when(jnp.logical_not(moves))
        def _():
            turn_local.wait()

        block_local.start()
        for jx in xs:
            launch(bx_copy(jx))
        for jy in ys:
            launch(by_copy(jy))
        launch(bn_copy(0, 0))

    def blocks_forward():
        for jy in ys:
            view = block(0, jy, core)
            remote(view, view, by_sems, jy - 1, y_peers[jy]).wait_recv()
            for jx in xs:
                launch(bf_copy(jx, jy))
            launch(bn_copy(0, jy))
        for jx in xs:
            view = block(jx, 0, core)
            remote(view, view, bx_sems, jx - 1, x_peers[jx]).wait_recv()
            launch(bn_copy(jx, 0))

    def blocks_finish():
        for jx in xs:
            for jy in ys:
                view = block(jx, jy, core)
                remote(
                    view, view, bf_sems, (jx - 1) * (yn - 1) + jy - 1, x_peers[jx]
                ).wait_recv()
                launch(bn_copy(jx, jy))

    for index in range(1, zn):
        z_in(index)
        send_own(z_order[index])
        forward(z_order[index - 1])
        if index >= 2:
            finish(z_order[index - 2])
        if index == zn - 2:
            turn_in()
    blocks_forward()
    forward(z_order[zn - 1])
    blocks_finish()
    finish(z_order[zn - 2])
    finish(z_order[zn - 1])

    for jz in range(zn):
        for jx in range(xn):
            for jy in range(yn):
                chip = lax.div(number(jz, jx, jy), 2)
                view = every.at[pl.ds((chip * 2 + 1 - core) * slots, slots)]
                remote(
                    view, view, near_sems, (jz * xn + jx) * yn + jy, core_peer
                ).wait_recv()
    for jx in range(xn):
        for jy in range(yn):
            view = block(jx, jy, 1 - core)
            remote(view, view, bn_sems, jx * yn + jy, core_peer).wait_recv()
    own_local.wait()
    block_local.wait()
    for copy in started:
        copy.wait_send()


def reduce_kernel(
    sizes,
    grads,
    norm_in,
    total_out,
    norm_out,
    held,
    near,
    xd,
    yd,
    xs_in,
    ys_in,
    zs_in,
    norm_core,
    norm_y,
    norm_x,
    norm_z,
    norm_sum,
    load_sems,
    near_sems,
    xd_sems,
    yd_sems,
    xs_sems,
    ys_sems,
    zs_sems,
    norm_sems,
):
    zn, xn, yn, slots, part = sizes
    rest = slots - part
    z, x = lax.axis_index("a"), lax.axis_index("b")
    y, core = lax.axis_index("y"), lax.axis_index("core")
    core_peer = {"core": 1 - core}
    xs, ys = range(1, xn), range(1, yn)
    y_peers = [{"y": lax.rem(y + k, yn)} for k in ys]
    x_peers = [{"b": lax.rem(x + k, xn)} for k in xs]
    z_peers = [{"a": lax.rem(z + k, zn)} for k in range(1, zn)]
    greet([core_peer] + y_peers + x_peers + z_peers)

    def remote(src, dst, sems, index, peer):
        return pltpu.make_async_remote_copy(
            src_ref=src,
            dst_ref=dst,
            send_sem=sems.at[0, index],
            recv_sem=sems.at[1, index],
            device_id=peer,
            device_id_type=MESH_IDS,
        )

    def flat(jz, jx, jy):
        return (jz * xn + jx) * yn + jy

    def chip_rows(jz, jx, jy, which):
        chip = (lax.rem(z + jz, zn) * xn + lax.rem(x + jx, xn)) * yn + lax.rem(y + jy, yn)
        return grads.at[pl.ds((chip * 2 + which) * slots, slots)]

    def near_copy(jz, jx, jy):
        index = flat(jz, jx, jy)
        return remote(chip_rows(jz, jx, jy, 1 - core), near.at[index], near_sems, index, core_peer)

    def load_copy(jz, jx, jy):
        index = flat(jz, jx, jy)
        return pltpu.make_async_copy(
            chip_rows(jz, jx, jy, core), held.at[index], load_sems.at[index]
        )

    def whole(jz, jx, jy):
        return held.at[flat(jz, jx, jy)]

    def first(jz, jx, jy):
        return held.at[flat(jz, jx, jy), pl.ds(0, part)]

    def second(jz, jx, jy):
        return held.at[flat(jz, jx, jy), pl.ds(part, rest)]

    def cross(jz, jx, jy):
        return (jz * (xn - 1) + jx - 1) * (yn - 1) + jy - 1

    def yd_copy(jz, jx, jy):
        index = cross(jz, jx, jy)
        return remote(first(jz, jx, jy), yd.at[index], yd_sems, index, y_peers[jy - 1])

    def xd_copy(jz, jx, jy):
        index = cross(jz, jx, jy)
        return remote(second(jz, jx, jy), xd.at[index], xd_sems, index, x_peers[jx - 1])

    def xs_copy(jz, jx):
        index = jz * (xn - 1) + jx - 1
        return remote(whole(jz, jx, 0), xs_in.at[index], xs_sems, index, x_peers[jx - 1])

    def ys_copy(jz, jy):
        index = jz * (yn - 1) + jy - 1
        return remote(whole(jz, 0, jy), ys_in.at[index], ys_sems, index, y_peers[jy - 1])

    def zs_copy(jz):
        return remote(whole(jz, 0, 0), zs_in.at[jz - 1], zs_sems, jz - 1, z_peers[jz - 1])

    z_order = z_order_of(zn)[::-1]
    started = []

    def launch(copy):
        copy.start()
        started.append(copy)

    steps_done = []
    norm_count = [0]

    def norm_step(buffer, peers):
        copies = []
        for k, peer in enumerate(peers):
            index = norm_count[0]
            norm_count[0] += 1
            copy = remote(norm_sum.at[len(steps_done)], buffer.at[k], norm_sems, index, peer)
            copy.start()
            copies.append(copy)
        return copies

    def norm_finish(buffer, copies):
        total = norm_sum[len(steps_done)]
        for k, copy in enumerate(copies):
            copy.wait()
            total = total + buffer[k]
        steps_done.append(None)
        norm_sum[len(steps_done)] = total

    def plane(jz):
        return (
            [(jz, jx, jy) for jx in xs for jy in ys]
            + [(jz, jx, 0) for jx in xs]
            + [(jz, 0, jy) for jy in ys]
            + [(jz, 0, 0)]
        )

    def fetch(jz):
        for chip in plane(jz):
            launch(near_copy(*chip))
            load_copy(*chip).start()

    def prepare(index):
        for chip in plane(z_order[index]):
            load_copy(*chip).wait()
            near_copy(*chip).wait_recv()
            add_low(whole(*chip), near.at[flat(*chip)], slots)
            if chip[1] != 0 and chip[2] != 0:
                launch(yd_copy(*chip))
                launch(xd_copy(*chip))
        if index + 1 < zn:
            fetch(z_order[index + 1])

    def cross_in(index):
        jz = z_order[index]
        for jx in xs:
            for jy in ys:
                yd_copy(jz, jx, jy).wait_recv()
                add_low(first(jz, jx, 0), yd.at[cross(jz, jx, jy)], part)
            launch(xs_copy(jz, jx))
        for jy in ys:
            for jx in xs:
                xd_copy(jz, jx, jy).wait_recv()
                add_low(second(jz, 0, jy), xd.at[cross(jz, jx, jy)], rest)
            launch(ys_copy(jz, jy))

    def side_in(index):
        jz = z_order[index]
        for jx in xs:
            xs_copy(jz, jx).wait_recv()
        for jy in ys:
            ys_copy(jz, jy).wait_recv()

        def one(i, carry):
            total = held[flat(jz, 0, 0), i].astype(F32)
            for jx in xs:
                total = total + xs_in[jz * (xn - 1) + jx - 1, i].astype(F32)
            for jy in ys:
                total = total + ys_in[jz * (yn - 1) + jy - 1, i].astype(F32)
            if jz != 0:
                held[flat(jz, 0, 0), i] = total.astype(BF16)
            else:
                total_out[i] = total
            return carry

        lax.fori_loop(0, slots, one, None)
        if jz != 0:
            launch(zs_copy(jz))

    norm_sum[0] = norm_in[...]
    rounds = [(norm_core, [core_peer]), (norm_y, y_peers), (norm_x, x_peers), (norm_z, z_peers)]
    fetch(z_order[0])
    pending = norm_step(*rounds[0])
    prepare(0)
    for index in range(1, zn):
        prepare(index)
        cross_in(index - 1)
        if index >= 2:
            side_in(index - 2)
        if len(steps_done) < 3:
            norm_finish(rounds[len(steps_done)][0], pending)
            pending = norm_step(*rounds[len(steps_done)])
    cross_in(zn - 1)
    side_in(zn - 2)
    side_in(zn - 1)
    while len(steps_done) < 3:
        norm_finish(rounds[len(steps_done)][0], pending)
        pending = norm_step(*rounds[len(steps_done)])
    norm_finish(norm_z, pending)
    norm_out[...] = norm_sum[4]
    for jz in range(1, zn):
        zs_copy(jz).wait_recv()

    def last(i, carry):
        total = total_out[i]
        for jz in range(1, zn):
            total = total + zs_in[jz - 1, i].astype(F32)
        total_out[i] = total
        return carry

    lax.fori_loop(0, slots, last, None)
    for copy in started:
        copy.wait_send()


def vmem():
    return pl.BlockSpec(memory_space=pltpu.VMEM)


def smem():
    return pl.BlockSpec(memory_space=pltpu.SMEM)


def anywhere():
    return pl.BlockSpec(memory_space=pl.ANY)


def shape_of(dims, kind):
    return jax.ShapeDtypeStruct(dims, kind)


def params(collective=None):
    if collective is None:
        return pltpu.CompilerParams(vmem_limit_bytes=VMEM_LIMIT)
    return pltpu.CompilerParams(
        vmem_limit_bytes=VMEM_LIMIT, collective_id=collective, has_side_effects=True
    )


def swap_heads(block, n_dp, splits, collective):
    return pl.pallas_call(
        functools.partial(swap_heads_kernel, (n_dp, splits)),
        out_shape=shape_of(block.shape, BF16),
        in_specs=[vmem()],
        out_specs=vmem(),
        scratch_shapes=[
            pltpu.SemaphoreType.DMA((GROUPS - 1,)),
            pltpu.SemaphoreType.DMA((GROUPS - 1,)),
            pltpu.SemaphoreType.DMA,
        ],
        compiler_params=params(collective),
    )(block)


def per_device(
    dims,
    layer_input,
    out_cotangent,
    segment_ids,
    piece_owner,
    weight_master,
    weight_first,
    weight_second,
    norm_params,
    norm_first,
    norm_second,
):
    n_seq, n_dp = dims
    reps = n_seq // n_dp
    splits = n_seq // GROUPS
    slots, piece, width = weight_master.shape
    pieces = piece_owner.shape[0]
    tok = layer_input.shape[1]
    length = tok * n_seq
    hidden_units = (pieces * piece - 4 * width) // 3
    head = width // HEADS
    kind_pieces = width // piece
    hidden_pieces = hidden_units // piece
    chunk = hidden_units // CHUNKS

    location = locate_pieces(piece_owner, slots)
    own_low = weight_master.astype(BF16)
    seg_row = jnp.zeros((16, width), BF16).at[0, :tok].set(segment_ids[0].astype(BF16))
    pack = jnp.concatenate([layer_input[0], seg_row, out_cotangent[0]], axis=0)
    turn = [(i * n_dp + j, j * n_dp + i) for i in range(n_dp) for j in range(n_dp)]
    turn_axes = ("a", "y", "core")

    zn, xn, yn = n_dp, reps, n_dp // 2
    n_chips = zn * xn * yn

    def pair(count):
        return pltpu.SemaphoreType.DMA((2, max(count, 1)))

    half = slots // 2
    weights, packed, gathered = pl.pallas_call(
        functools.partial(spread_kernel, (zn, xn, yn, slots, half, tok + 16)),
        out_shape=(
            shape_of((n_chips * 2 * slots, piece, width), BF16),
            shape_of(pack.shape, BF16),
            shape_of((n_seq, tok + 16, width), BF16),
        ),
        in_specs=[anywhere(), anywhere()],
        out_specs=(anywhere(),) * 3,
        scratch_shapes=[
            pair(zn - 1),
            pair(zn * (xn - 1)),
            pair(zn * (yn - 1)),
            pair(zn * (xn - 1) * (yn - 1)),
            pair(zn * (xn - 1) * (yn - 1)),
            pair(n_chips),
            pair(1),
            pair(xn - 1),
            pair(yn - 1),
            pair((xn - 1) * (yn - 1)),
            pair(xn * yn),
            pltpu.SemaphoreType.DMA((3,)),
        ],
        compiler_params=params(5),
    )(own_low, pack)

    core = lax.axis_index("core")
    order = my_order(n_dp)
    group, split = order // splits, order % splits
    info = jnp.stack([core, group, split]).astype(jnp.int32)
    slopes = head_slopes(HEADS, tok, n_seq)

    segs = gathered[:, tok, :tok]
    lanes = jnp.arange(128, dtype=jnp.int32)[None, :] - head
    key_same = segs.reshape(length, 1).astype(jnp.int32) == lanes
    key_marks = jnp.where(key_same | (lanes < 0) | (lanes > 2), 0.0, MASKED).astype(BF16)
    query_segs = lax.dynamic_index_in_dim(
        segs.reshape(GROUPS, splits, tok), split, axis=1, keepdims=False
    )
    query_marks = (query_segs.reshape(GROUPS * tok, 1).astype(jnp.int32) == lanes).astype(BF16)

    attend_sizes = (n_dp, reps, splits, tok, head, n_seq)
    q_ext, k_ext, k_turned, v_rows, mixed_low, mixed_full, log_total = pl.pallas_call(
        functools.partial(attend_forward_kernel, attend_sizes),
        out_shape=(
            shape_of((TRIO, GROUPS * tok, 128), BF16),
            shape_of((TRIO, length, 128), BF16),
            shape_of((TRIO, head, length), BF16),
            shape_of((TRIO, length, head), BF16),
            shape_of((GROUPS, TRIO, head, tok), BF16),
            shape_of((GROUPS, TRIO, head, tok), F32),
            shape_of((GROUPS, TRIO, 1, tok), F32),
        ),
        in_specs=[smem(), smem(), smem(), vmem(), vmem(), vmem(), anywhere()],
        out_specs=(vmem(),) * 7,
        scratch_shapes=[
            pltpu.VMEM((3 * TRIO, 128, width), BF16),
            pltpu.VMEM((TRIO, head, length), BF16),
            pltpu.VMEM((3 * TRIO, tok, tok), F32),
            pltpu.VMEM((n_seq, tok, tok), F32),
            pltpu.SemaphoreType.DMA((3 * TRIO * (head // piece),)),
        ],
        compiler_params=params(),
    )(location, info, slopes, gathered, query_marks, key_marks, weights)

    mixed_own = swap_heads(mixed_low.reshape(GROUPS, TRIO * head, tok), n_dp, splits, 1)

    out_low, d_pre_one, d_mixed, norm_part, grads = pl.pallas_call(
        functools.partial(
            dense_kernel, (tok, piece, kind_pieces, chunk // piece, hidden_pieces)
        ),
        out_shape=(
            shape_of((tok, width), BF16),
            shape_of((tok, width), F32),
            shape_of((width, tok), BF16),
            shape_of((8, width), F32),
            shape_of((n_seq * n_dp * slots, piece, width), BF16),
        ),
        in_specs=[smem(), vmem(), vmem(), vmem(), anywhere()],
        out_specs=(vmem(), vmem(), vmem(), vmem(), anywhere()),
        scratch_shapes=[
            pltpu.VMEM((width, width), BF16),
            pltpu.VMEM((CHUNKS, chunk, width), BF16),
            pltpu.VMEM((CHUNKS, chunk, width), BF16),
            pltpu.VMEM((CHUNKS, chunk, width), BF16),
            pltpu.VMEM((CHUNKS, tok, chunk), F32),
            pltpu.VMEM((CHUNKS, tok, chunk), F32),
            pltpu.VMEM((CHUNKS, tok, chunk), BF16),
            pltpu.VMEM((2, 3, chunk, width), BF16),
            pltpu.VMEM((width, width), BF16),
            pltpu.SemaphoreType.DMA((3 * CHUNKS + 1,)),
            pltpu.SemaphoreType.DMA((7,)),
        ],
        compiler_params=params(),
    )(
        location,
        packed,
        mixed_own.reshape(width, tok),
        norm_params,
        weights,
    )

    result = lax.ppermute(out_low, turn_axes, turn)
    d_mixed_own = swap_heads(d_mixed.reshape(GROUPS, TRIO * head, tok), n_dp, splits, 2)

    d_query, d_key_value = pl.pallas_call(
        functools.partial(attend_backward_kernel, attend_sizes),
        out_shape=(
            shape_of((GROUPS, TRIO, head, tok), BF16),
            shape_of((splits, GROUPS, 2, TRIO, head, tok), BF16),
        ),
        in_specs=[smem(), smem()] + [vmem()] * 7,
        out_specs=(vmem(), vmem()),
        scratch_shapes=[
            pltpu.VMEM((TRIO, length, 128), F32),
            pltpu.VMEM((TRIO, length, head), F32),
            pltpu.VMEM((3 * TRIO, tok, tok), F32),
        ],
        compiler_params=params(),
    )(
        info,
        slopes,
        q_ext,
        k_ext,
        k_turned,
        v_rows,
        mixed_full,
        log_total,
        d_mixed_own.reshape(GROUPS, TRIO, head, tok),
    )

    trio_rows = TRIO * head
    d_groups, d_own = pl.pallas_call(
        functools.partial(share_grads_kernel, (n_dp, splits)),
        out_shape=(
            shape_of((GROUPS, 3, trio_rows, tok), BF16),
            shape_of((GROUPS, 3, trio_rows, tok), BF16),
        ),
        in_specs=[vmem(), vmem()],
        out_specs=(vmem(), vmem()),
        scratch_shapes=[
            pltpu.VMEM((splits - 1, GROUPS, 2, trio_rows, tok), BF16),
            pltpu.SemaphoreType.DMA((splits - 1,)),
            pltpu.SemaphoreType.DMA((splits - 1,)),
            pltpu.SemaphoreType.DMA((GROUPS - 1,)),
            pltpu.SemaphoreType.DMA((GROUPS - 1,)),
            pltpu.SemaphoreType.DMA,
        ],
        compiler_params=params(3),
    )(
        d_query.reshape(GROUPS, trio_rows, tok),
        d_key_value.reshape(splits, GROUPS, 2, trio_rows, tok),
    )

    d_tokens, grads = pl.pallas_call(
        functools.partial(project_grad_kernel, (piece, kind_pieces, splits, tok)),
        out_shape=(shape_of((tok, width), F32), shape_of(grads.shape, BF16)),
        in_specs=[smem(), smem(), vmem(), vmem(), vmem(), vmem()] + [anywhere()] * 2,
        out_specs=(vmem(), anywhere()),
        scratch_shapes=[
            pltpu.VMEM((3 * width, width), BF16),
            pltpu.VMEM((3 * trio_rows, width), BF16),
            pltpu.VMEM(((GROUPS - 1) * 3 * trio_rows, width), BF16),
            pltpu.SemaphoreType.DMA,
            pltpu.SemaphoreType.DMA,
            pltpu.SemaphoreType.DMA,
        ],
        input_output_aliases={7: 1},
        compiler_params=params(),
    )(
        location,
        info,
        gathered,
        d_groups.reshape(GROUPS, 3 * trio_rows, tok),
        d_own.reshape(3 * width, tok),
        d_pre_one,
        weights,
        grads,
    )
    d_input = lax.ppermute(d_tokens, turn_axes, turn)

    def chunks(count, rows):
        return pltpu.VMEM((max(count, 1), rows, piece, width), BF16)

    def norm_rows(count):
        return pltpu.VMEM((max(count, 1), 8, width), F32)

    crossing = zn * (xn - 1) * (yn - 1)
    own_grad, norm_total = pl.pallas_call(
        functools.partial(reduce_kernel, (zn, xn, yn, slots, half)),
        out_shape=(shape_of((slots, piece, width), F32), shape_of((8, width), F32)),
        in_specs=[anywhere(), vmem()],
        out_specs=(vmem(), vmem()),
        scratch_shapes=[
            chunks(n_chips, slots),
            chunks(n_chips, slots),
            chunks(crossing, slots - half),
            chunks(crossing, half),
            chunks(zn * (xn - 1), slots),
            chunks(zn * (yn - 1), slots),
            chunks(zn - 1, slots),
            norm_rows(1),
            norm_rows(yn - 1),
            norm_rows(xn - 1),
            norm_rows(zn - 1),
            norm_rows(5),
            pltpu.SemaphoreType.DMA((n_chips,)),
            pair(n_chips),
            pair(crossing),
            pair(crossing),
            pair(zn * (xn - 1)),
            pair(zn * (yn - 1)),
            pair(zn - 1),
            pair(1 + (yn - 1) + (xn - 1) + (zn - 1)),
        ],
        compiler_params=params(4),
    )(grads, norm_part)

    numbers = jnp.arange(pieces, dtype=jnp.int32) + 1
    own_slots = lax.axis_index(("a", "b", "y", "core")) * slots + jnp.arange(slots)
    inverse = jnp.sum(jnp.where(location[None, :] == own_slots[:, None], numbers[None, :], 0), axis=1)
    own_grad = jnp.where((inverse > 0)[:, None, None], own_grad, 0.0)
    norm_grad = norm_total[:4]
    rates = slot_rates(inverse, piece, width, hidden_units)
    first_new, second_new, weight_new = adamw_step(
        weight_master, weight_first, weight_second, own_grad, rates[:, None, None], STEP
    )
    norm_first_new, norm_second_new, norm_new = adamw_step(
        norm_params, norm_first, norm_second, norm_grad, NORM_RATE, STEP
    )
    return (
        result[None],
        d_input[None],
        own_grad,
        first_new,
        second_new,
        weight_new,
        weight_new.astype(BF16),
        norm_grad,
        norm_first_new,
        norm_second_new,
        norm_new,
    )


def solution(mesh):
    n_seq, n_dp = mesh.shape["seq"], mesh.shape["dp"]
    inner = Mesh(
        mesh.devices.reshape(n_dp, n_seq // n_dp, n_dp // 2, 2), ("a", "b", "y", "core")
    )
    seq, dp, every = ("a", "b"), ("y", "core"), ("a", "b", "y", "core")
    block = P(dp, seq, None)
    owned = P(every, None, None)
    in_specs = (block, block, P(dp, seq), P(), owned, owned, owned, P(), P(), P())
    out_specs = (block, block, owned, owned, owned, owned, owned, P(), P(), P(), P())
    return jax.shard_map(
        functools.partial(per_device, (n_seq, n_dp)),
        mesh=inner,
        in_specs=in_specs,
        out_specs=out_specs,
        check_vma=False,
    )
```

```python
import functools

import jax
import jax.numpy as jnp
from jax import lax
from jax.experimental import pallas as pl
from jax.experimental.pallas import tpu as pltpu
from jax.sharding import Mesh
from jax.sharding import PartitionSpec as P

HEADS = 12
GROUPS = 4
TRIO = HEADS // GROUPS
STEP = 4

NORM_EPS = 1e-06
BETA_ONE = 0.5
BETA_TWO = 0.5
DECAY = 0.01
ADAM_EPS = 1e-08
NORM_RATE = 0.3
OUT_RATE = 0.35
MASKED = -1e30
CHUNKS = 6
VMEM_LIMIT = 60 * 1024 * 1024
MESH_IDS = pl.DeviceIdType.MESH
F32 = jnp.float32
BF16 = jnp.bfloat16


def head_slopes(head_count, tok_rows, seq_devices):
    head_order = jnp.arange(head_count, dtype=jnp.float32)
    return (
        8.0 / tok_rows * jnp.power(jnp.float32(8.0 * seq_devices), -head_order / (head_count - 1))
    )


def locate_pieces(owners, slot_count):
    pieces = owners.shape[0]
    numbers = jnp.arange(pieces, dtype=jnp.int32)
    earlier = (owners[None, :] == owners[:, None]) & (numbers[None, :] < numbers[:, None])
    return owners * slot_count + jnp.sum(earlier.astype(jnp.int32), axis=1)


def slot_rates(inverse, piece_rows, model_width, hidden_units):
    first_row = (inverse - 1) * piece_rows
    narrow = model_width ** (-0.5)
    step_rate = jnp.where(
        first_row < 3 * model_width,
        narrow,
        jnp.where(
            first_row < 4 * model_width,
            OUT_RATE,
            jnp.where(
                first_row < 4 * model_width + 2 * hidden_units, narrow, hidden_units ** (-0.5)
            ),
        ),
    )
    return jnp.where(inverse > 0, step_rate, narrow).astype(jnp.float32)


def adamw_step(weight, first_moment, second, gradient, step_rate, step_count):
    first_moment = BETA_ONE * first_moment + (1.0 - BETA_ONE) * gradient
    second = BETA_TWO * second + (1.0 - BETA_TWO) * gradient * gradient
    mean_hat = first_moment / (1.0 - BETA_ONE**step_count)
    square_hat = second / (1.0 - BETA_TWO**step_count)
    weight = weight - step_rate * (mean_hat / (jnp.sqrt(square_hat) + ADAM_EPS) + DECAY * weight)
    return (first_moment, second, weight)


def dot_nt(left_side, right_side):
    return lax.dot_general(
        left_side, right_side, (((1,), (1,)), ((), ())), preferred_element_type=F32
    )


def dot_nn(left_side, right_side):
    return lax.dot_general(
        left_side, right_side, (((1,), (0,)), ((), ())), preferred_element_type=F32
    )


def dot_tn(left_side, right_side):
    return lax.dot_general(
        left_side, right_side, (((0,), (0,)), ((), ())), preferred_element_type=F32
    )


def fetch_piece(place, piece, weights, dst, sem):
    pltpu.make_async_copy(weights.at[place[piece]], dst, sem).start()


def fill_tables(table, slopes, group, tok):
    apart = lax.broadcasted_iota(jnp.int32, (tok, tok), 0) - lax.broadcasted_iota(
        jnp.int32, (tok, tok), 1
    )
    apart = apart.astype(F32)
    for h in range(TRIO):
        slope = slopes[group * TRIO + h]
        table[h * 3 + 0] = -slope * apart
        table[h * 3 + 1] = slope * jnp.abs(apart)
        table[h * 3 + 2] = slope * apart


def block_place(order, n_dp, reps):
    return (order % n_dp) * reps + order // n_dp


def bias_of(key_block, query_place, slope, h, tok, n_dp, reps):
    key_place = block_place(key_block, n_dp, reps)
    which = jnp.where(key_place > query_place, 2, jnp.where(key_place < query_place, 0, 1))
    shift = slope * (tok * jnp.abs(key_place - query_place)).astype(F32)
    return h * 3 + which, shift


def attend_forward_kernel(
    sizes,
    place,
    info,
    slopes,
    x_ref,
    query_marks,
    key_marks,
    weights,
    q_out,
    k_out,
    kt_out,
    v_out,
    mixed_low,
    mixed_full,
    log_out,
    wpad,
    vt,
    table,
    scores,
    sems,
):
    n_dp, reps, splits, tok, head, blocks = sizes
    group, split = info[1], info[2]
    per_head = head // 16
    width = x_ref.shape[2]
    kind_pieces = width // 16

    def start(step, carry):
        kind = lax.div(step, TRIO * per_head)
        rest = lax.rem(step, TRIO * per_head)
        number = kind * kind_pieces + group * (TRIO * per_head) + rest
        dst = wpad.at[
            kind * TRIO + lax.div(rest, per_head), pl.ds(lax.rem(rest, per_head) * 16, 16)
        ]
        fetch_piece(place, number, weights, dst, sems.at[step])
        return carry

    def finish(step, carry):
        kind = lax.div(step, TRIO * per_head)
        rest = lax.rem(step, TRIO * per_head)
        dst = wpad.at[
            kind * TRIO + lax.div(rest, per_head), pl.ds(lax.rem(rest, per_head) * 16, 16)
        ]
        pltpu.make_async_copy(weights.at[0], dst, sems.at[step]).wait()
        return carry

    lax.fori_loop(0, 3 * TRIO * per_head, start, None)
    for row in range(3 * TRIO):
        wpad[row, head:, :] = jnp.zeros((wpad.shape[1] - head, width), BF16)
    fill_tables(table, slopes, group, tok)
    lax.fori_loop(0, 3 * TRIO * per_head, finish, None)

    w_query = wpad[0:TRIO].reshape(TRIO * 128, width)
    w_key = wpad[TRIO : 2 * TRIO].reshape(TRIO * 128, width)
    w_value = wpad[2 * TRIO : 3 * TRIO].reshape(TRIO * 128, width)

    def project(block, carry):
        rows = pl.ds(pl.multiple_of(block * tok, tok), tok)
        xb = x_ref[block, 0:tok, :]
        keys = dot_nt(xb, w_key)
        values = dot_nt(xb, w_value)
        marks = key_marks[rows, :]
        for h in range(TRIO):
            key = keys[:, h * 128 : (h + 1) * 128]
            value = values[:, h * 128 : (h + 1) * 128]
            k_out[h, rows, :] = key.astype(BF16) + marks
            v_out[h, rows, :] = value[:, 0:head].astype(BF16)
            kt_out[h, :, rows] = key.T[0:head].astype(BF16)
            vt[h, :, rows] = value.T[0:head].astype(BF16)
        return carry

    lax.fori_loop(0, blocks, project, None)

    def project_query(index, carry):
        rows = pl.ds(pl.multiple_of(index * tok, tok), tok)
        xb = x_ref[index * splits + split, 0:tok, :]
        queries = dot_nt(xb, w_query).astype(BF16) * jnp.asarray(head**-0.5, BF16)
        marks = query_marks[rows, :]
        for h in range(TRIO):
            q_out[h, rows, :] = queries[:, h * 128 : (h + 1) * 128] + marks
        return carry

    lax.fori_loop(0, GROUPS, project_query, None)

    def attend(step, carry):
        index, h = lax.div(step, TRIO), lax.rem(step, TRIO)
        order = index * splits + split
        query_place = lax.rem(order, n_dp) * reps + lax.div(order, n_dp)
        slope = slopes[group * TRIO + h]
        qh = q_out[h, pl.ds(pl.multiple_of(index * tok, tok), tok), :]
        top = None
        shifts = []
        for kb in range(blocks):
            which, shift = bias_of(kb, query_place, slope, h, tok, n_dp, reps)
            now = dot_nt(k_out[h, kb * tok : (kb + 1) * tok, :], qh) - table[which]
            scores[kb] = now
            here = jnp.max(now, axis=0, keepdims=True) - shift
            top = here if top is None else jnp.maximum(top, here)
            shifts.append(shift)
        total = jnp.zeros((1, tok), F32)
        for kb in range(blocks):
            grown = jnp.exp(scores[kb] - (top + shifts[kb]))
            total = total + jnp.sum(grown, axis=0, keepdims=True)
            scores[kb] = grown
        inverse = 1.0 / total
        mixed = jnp.zeros((head, tok), F32)
        for kb in range(blocks):
            prob = (scores[kb] * inverse).astype(BF16)
            mixed = mixed + dot_nn(vt[h, :, kb * tok : (kb + 1) * tok], prob)
        mixed_full[index, h] = mixed
        mixed_low[index, h] = mixed.astype(BF16)
        log_out[index, h] = top + jnp.log(total)
        return carry

    lax.fori_loop(0, GROUPS * TRIO, attend, None)


def attend_backward_kernel(
    sizes,
    info,
    slopes,
    q_ref,
    k_ref,
    kt_ref,
    v_ref,
    mixed_full,
    log_in,
    d_mixed,
    dq_out,
    dkv_out,
    dk_sum,
    dv_sum,
    table,
):
    n_dp, reps, splits, tok, head, blocks = sizes
    group, split = info[1], info[2]
    fill_tables(table, slopes, group, tok)
    dk_sum[...] = jnp.zeros_like(dk_sum)
    dv_sum[...] = jnp.zeros_like(dv_sum)

    def step_fn(step, carry):
        h, index = lax.div(step, GROUPS), lax.rem(step, GROUPS)
        order = index * splits + split
        query_place = lax.rem(order, n_dp) * reps + lax.div(order, n_dp)
        slope = slopes[group * TRIO + h]
        qh = q_ref[h, pl.ds(pl.multiple_of(index * tok, tok), tok), :]
        dt = d_mixed[index, h]
        row_dot = jnp.sum(dt.astype(F32) * mixed_full[index, h], axis=0, keepdims=True)
        log_total = log_in[index, h]
        dq = jnp.zeros((head, tok), F32)
        for kb in range(blocks):
            rows = slice(kb * tok, (kb + 1) * tok)
            which, shift = bias_of(kb, query_place, slope, h, tok, n_dp, reps)
            now = dot_nt(k_ref[h, rows, :], qh) - table[which]
            prob = jnp.exp(now - (log_total + shift))
            d_prob = dot_nn(v_ref[h, rows, :], dt)
            d_score = (prob * (d_prob - row_dot)).astype(BF16)
            dv_sum[h, rows, :] += dot_nt(prob.astype(BF16), dt)
            dk_sum[h, rows, :] += dot_nn(d_score, qh)
            dq = dq + dot_nn(kt_ref[h, :, rows], d_score)
        dq_out[index, h] = (dq * (head**-0.5)).astype(BF16)
        return carry

    lax.fori_loop(0, TRIO * GROUPS, step_fn, None)

    def flip(step, carry):
        h, index = lax.div(step, GROUPS), lax.rem(step, GROUPS)
        for part in range(splits):
            rows = pl.ds(pl.multiple_of((index * splits + part) * tok, tok), tok)
            dkv_out[part, index, 0, h] = dk_sum[h, rows, :].T[0:head].astype(BF16)
            dkv_out[part, index, 1, h] = dv_sum[h, rows, :].T.astype(BF16)
        return carry

    lax.fori_loop(0, TRIO * GROUPS, flip, None)


def norm_stats(values_in):
    mean = jnp.mean(values_in, axis=-1, keepdims=True)
    centred = values_in - mean
    spread = jnp.mean(centred * centred, axis=-1, keepdims=True)
    scale = lax.rsqrt(spread + NORM_EPS)
    return centred * scale, scale


def norm_back(unit, scale, gain, cotangent):
    d_unit = cotangent * gain
    first = jnp.mean(d_unit, axis=-1, keepdims=True)
    second = jnp.mean(d_unit * unit, axis=-1, keepdims=True)
    d_in = scale * (d_unit - first - unit * second)
    d_gain = jnp.sum(cotangent * unit, axis=0, keepdims=True)
    d_bias = jnp.sum(cotangent, axis=0, keepdims=True)
    return d_in, d_gain, d_bias


def dense_kernel(
    sizes,
    place,
    packed_ref,
    mixed_ref,
    norm_ref,
    weights,
    out_ref,
    d_pre_one_ref,
    d_mixed_ref,
    norm_grad,
    grads,
    w_out,
    w_gate,
    w_up,
    w_down,
    keep_gate,
    keep_up,
    keep_hidden,
    stage,
    stage_out,
    load_sems,
    store_sems,
):
    tok, piece, kind_pieces, chunk_pieces, hidden_pieces = sizes
    first_gate = 4 * kind_pieces
    first_up = first_gate + hidden_pieces
    first_down = first_up + hidden_pieces
    bases = (first_gate, first_up, first_down)
    buffers = (w_gate, w_up, w_down)
    chunk = chunk_pieces * piece

    def load_out(step, carry):
        fetch_piece(
            place,
            3 * kind_pieces + step,
            weights,
            w_out.at[pl.ds(step * piece, piece)],
            load_sems.at[3 * CHUNKS],
        )
        return carry

    def load_chunk(c):
        def one(step, carry):
            for kind in range(3):
                fetch_piece(
                    place,
                    bases[kind] + c * chunk_pieces + step,
                    weights,
                    buffers[kind].at[c, pl.ds(step * piece, piece)],
                    load_sems.at[kind * CHUNKS + c],
                )
            return carry

        lax.fori_loop(0, chunk_pieces, one, None)

    def wait_chunk(c):
        for kind in range(3):
            view = buffers[kind].at[c]
            pltpu.make_async_copy(view, view, load_sems.at[kind * CHUNKS + c]).wait()

    lax.fori_loop(0, kind_pieces, load_out, None)
    load_chunk(0)
    load_chunk(1)
    mixed = mixed_ref[...].T
    pltpu.make_async_copy(w_out, w_out, load_sems.at[3 * CHUNKS]).wait()
    pre_one = packed_ref[0:tok].astype(F32) + dot_nt(mixed, w_out[...])
    unit_one, scale_one = norm_stats(pre_one)
    h_one = unit_one * norm_ref[0:1, :] + norm_ref[1:2, :]
    h_low = h_one.astype(BF16)

    def forward(c, pre_two):
        @pl.when(c + 2 < CHUNKS)
        def _():
            load_chunk(c + 2)

        wait_chunk(c)
        gate = dot_nt(h_low, w_gate[c])
        up = dot_nt(h_low, w_up[c])
        below = 0.5 * (1.0 + lax.erf(gate * (0.5**0.5)))
        gelu = gate * below
        slope = below + gate * (jnp.exp(-0.5 * gate * gate) * (0.5 / jnp.pi) ** 0.5)
        hidden = (gelu * up).astype(BF16)
        keep_gate[c] = up * slope
        keep_up[c] = gelu
        keep_hidden[c] = hidden
        return pre_two + dot_nn(hidden, w_down[c])

    pre_two = lax.fori_loop(0, CHUNKS, forward, h_one)
    unit_two, scale_two = norm_stats(pre_two)
    out_ref[...] = (unit_two * norm_ref[2:3, :] + norm_ref[3:4, :]).astype(BF16)
    d_pre_two, d_gain_two, d_bias_two = norm_back(
        unit_two, scale_two, norm_ref[2:3, :], packed_ref[tok + 16 :].astype(F32)
    )
    d_branch = d_pre_two.astype(BF16)

    def drain(slot):
        for kind in range(3):
            view = stage.at[slot, kind]
            pltpu.make_async_copy(view, view, store_sems.at[slot * 3 + kind]).wait()

    def backward(c, d_h):
        slot = lax.rem(c, 2)

        @pl.when(c >= 2)
        def _():
            drain(slot)

        d_hidden = dot_nt(d_branch, w_down[c])
        d_gate = (d_hidden * keep_gate[c]).astype(BF16)
        d_up = (d_hidden * keep_up[c]).astype(BF16)
        stage[slot, 0] = dot_tn(d_gate, h_low).astype(BF16)
        stage[slot, 1] = dot_tn(d_up, h_low).astype(BF16)
        stage[slot, 2] = dot_tn(keep_hidden[c], d_branch).astype(BF16)

        def store(step, carry):
            for kind in range(3):
                pltpu.make_async_copy(
                    stage.at[slot, kind, pl.ds(step * piece, piece)],
                    grads.at[place[bases[kind] + c * chunk_pieces + step]],
                    store_sems.at[slot * 3 + kind],
                ).start()
            return carry

        lax.fori_loop(0, chunk_pieces, store, None)
        return d_h + dot_nn(d_gate, w_gate[c]) + dot_nn(d_up, w_up[c])

    d_h = lax.fori_loop(0, CHUNKS, backward, d_pre_two)
    d_pre_one, d_gain_one, d_bias_one = norm_back(unit_one, scale_one, norm_ref[0:1, :], d_h)
    d_pre_one_ref[...] = d_pre_one
    d_proj = d_pre_one.astype(BF16)
    d_mixed_ref[...] = lax.dot_general(
        w_out[...], d_proj, (((0,), (1,)), ((), ())), preferred_element_type=F32
    ).astype(BF16)
    stage_out[...] = dot_tn(d_proj, mixed).astype(BF16)

    def store_out(step, carry):
        pltpu.make_async_copy(
            stage_out.at[pl.ds(step * piece, piece)],
            grads.at[place[3 * kind_pieces + step]],
            store_sems.at[6],
        ).start()
        return carry

    lax.fori_loop(0, kind_pieces, store_out, None)
    norm_grad[...] = jnp.concatenate(
        [
            d_gain_one,
            d_bias_one,
            d_gain_two,
            d_bias_two,
            jnp.zeros((4, d_gain_one.shape[1]), F32),
        ],
        axis=0,
    )
    drain(CHUNKS % 2)
    drain((CHUNKS + 1) % 2)
    pltpu.make_async_copy(stage_out, stage_out, store_sems.at[6]).wait()


def project_grad_kernel(
    sizes,
    place,
    info,
    x_ref,
    d_groups,
    d_own,
    d_pre_one,
    weights,
    grads_in,
    d_input,
    grads,
    w_all,
    stage,
    blank,
    load_sem,
    store_sem,
    blank_sem,
):
    piece, kind_pieces, splits, tok = sizes
    group, split = info[1], info[2]
    group_pieces = kind_pieces // GROUPS
    del grads_in

    def load(step, carry):
        for kind in range(3):
            row = (lax.div(step, group_pieces) * 3 + kind) * group_pieces + lax.rem(
                step, group_pieces
            )
            fetch_piece(
                place,
                kind * kind_pieces + step,
                weights,
                w_all.at[pl.ds(row * piece, piece)],
                load_sem,
            )
        return carry

    lax.fori_loop(0, kind_pieces, load, None)
    blank[...] = jnp.zeros_like(blank)

    def clear(step, carry):
        other = lax.div(step, group_pieces)
        number = lax.rem(group + 1 + other, GROUPS) * group_pieces + lax.rem(step, group_pieces)
        for kind in range(3):
            pltpu.make_async_copy(
                blank.at[pl.ds(0, piece)], grads.at[place[kind * kind_pieces + number]], blank_sem
            ).start()
        return carry

    lax.fori_loop(0, (GROUPS - 1) * group_pieces, clear, None)
    total = dot_nn(d_groups[0], x_ref[split, 0:tok, :])
    for index in range(1, GROUPS):
        total = total + dot_nn(d_groups[index], x_ref[index * splits + split, 0:tok, :])
    stage[...] = total.astype(BF16)

    def store(step, carry):
        for kind in range(3):
            pltpu.make_async_copy(
                stage.at[pl.ds((kind * group_pieces + step) * piece, piece)],
                grads.at[place[kind * kind_pieces + group * group_pieces + step]],
                store_sem,
            ).start()
        return carry

    lax.fori_loop(0, group_pieces, store, None)
    pltpu.make_async_copy(w_all, w_all, load_sem).wait()
    d_input[...] = d_pre_one[...] + dot_tn(d_own[...], w_all[...])
    pltpu.make_async_copy(stage, stage, store_sem).wait()
    pltpu.make_async_copy(blank, blank, blank_sem).wait()


def holder(order, n_dp):
    dp = lax.rem(order, n_dp)
    return {"b": lax.div(order, n_dp), "y": lax.div(dp, 2), "core": lax.rem(dp, 2)}


def greet(peers):
    barrier = pltpu.get_barrier_semaphore()
    for peer in peers:
        pl.semaphore_signal(barrier, inc=1, device_id=peer, device_id_type=MESH_IDS)
    pl.semaphore_wait(barrier, len(peers))


def my_order(n_dp):
    return lax.axis_index("b") * n_dp + lax.axis_index("y") * 2 + lax.axis_index("core")


def swap_heads_kernel(sizes, in_ref, out_ref, send_sems, recv_sems, own_sem):
    n_dp, splits = sizes
    order = my_order(n_dp)
    group, split = lax.div(order, splits), lax.rem(order, splits)
    others = [lax.rem(group + k, GROUPS) for k in range(1, GROUPS)]
    peers = [holder(other * splits + split, n_dp) for other in others]
    greet(peers)
    copies = []
    for k in range(GROUPS - 1):
        copy = pltpu.make_async_remote_copy(
            src_ref=in_ref.at[others[k]],
            dst_ref=out_ref.at[group],
            send_sem=send_sems.at[k],
            recv_sem=recv_sems.at[k],
            device_id=peers[k],
            device_id_type=MESH_IDS,
        )
        copy.start()
        copies.append(copy)
    own = pltpu.make_async_copy(in_ref.at[group], out_ref.at[group], own_sem)
    own.start()
    own.wait()
    for copy in copies:
        copy.wait()


def share_grads_kernel(
    sizes,
    dq_ref,
    dkv_ref,
    groups_ref,
    own_ref,
    landed,
    near_send,
    near_recv,
    send_sems,
    recv_sems,
    own_sem,
):
    n_dp, splits = sizes
    order = my_order(n_dp)
    group, split = lax.div(order, splits), lax.rem(order, splits)
    twins = [lax.rem(split + k, splits) for k in range(1, splits)]
    twin_ids = [holder(group * splits + other, n_dp) for other in twins]
    others = [lax.rem(group + k, GROUPS) for k in range(1, GROUPS)]
    peers = [holder(other * splits + split, n_dp) for other in others]
    greet(twin_ids + peers)
    near = []
    for k in range(splits - 1):
        copy = pltpu.make_async_remote_copy(
            src_ref=dkv_ref.at[twins[k]],
            dst_ref=landed.at[k],
            send_sem=near_send.at[k],
            recv_sem=near_recv.at[k],
            device_id=twin_ids[k],
            device_id_type=MESH_IDS,
        )
        copy.start()
        near.append(copy)
    groups_ref[:, 0] = dq_ref[...]
    for copy in near:
        copy.wait()
    for index in range(GROUPS):
        for kind in range(2):
            total = dkv_ref[split, index, kind].astype(F32)
            for k in range(splits - 1):
                total = total + landed[k, index, kind].astype(F32)
            groups_ref[index, kind + 1] = total.astype(BF16)
    copies = []
    for k in range(GROUPS - 1):
        copy = pltpu.make_async_remote_copy(
            src_ref=groups_ref.at[others[k]],
            dst_ref=own_ref.at[group],
            send_sem=send_sems.at[k],
            recv_sem=recv_sems.at[k],
            device_id=peers[k],
            device_id_type=MESH_IDS,
        )
        copy.start()
        copies.append(copy)
    own = pltpu.make_async_copy(groups_ref.at[group], own_ref.at[group], own_sem)
    own.start()
    own.wait()
    for copy in copies:
        copy.wait()


def add_low(dst, src, rows):
    def one(i, carry):
        dst[i] = (dst[i].astype(F32) + src[i].astype(F32)).astype(BF16)
        return carry

    lax.fori_loop(0, rows, one, None)


def z_order_of(count):
    order = [0]
    for k in range(1, count):
        for far in (k, count - k):
            if far not in order:
                order.append(far)
    return order


def turn_kernel(
    sizes,
    pack,
    turned,
    gathered,
    turn_sems,
    bx_sems,
    by_sems,
    bf_sems,
    bn_sems,
    own_sems,
):
    zn, xn, yn, rows = sizes
    z, x = lax.axis_index("a"), lax.axis_index("b")
    y, core = lax.axis_index("y"), lax.axis_index("core")
    core_peer = {"core": 1 - core}
    xs, ys = range(1, xn), range(1, yn)
    x_peers = {k: {"b": lax.rem(x + k, xn)} for k in xs}
    y_peers = {k: {"y": lax.rem(y + k, yn)} for k in ys}
    dp = y * 2 + core
    turn_peer = {"a": dp, "y": lax.div(z, 2), "core": lax.rem(z, 2)}
    moves = dp != z
    barrier = pltpu.get_barrier_semaphore()
    peers = [core_peer, *x_peers.values(), *y_peers.values()]
    for peer in peers:
        pl.semaphore_signal(barrier, inc=1, device_id=peer, device_id_type=MESH_IDS)

    @pl.when(moves)
    def _():
        pl.semaphore_signal(barrier, inc=1, device_id=turn_peer, device_id_type=MESH_IDS)

    pl.semaphore_wait(barrier, len(peers) + moves.astype(jnp.int32))

    def remote(src, dst, sems, index, peer):
        return pltpu.make_async_remote_copy(
            src_ref=src,
            dst_ref=dst,
            send_sem=sems.at[0, index],
            recv_sem=sems.at[1, index],
            device_id=peer,
            device_id_type=MESH_IDS,
        )

    def block(jx, jy, side):
        order = lax.rem(x + xn - jx, xn) * zn + lax.rem(y + yn - jy, yn) * 2 + side
        return gathered.at[order]

    head_rows = turned.at[pl.ds(0, rows)]
    started = []

    def launch(copy):
        copy.start()
        started.append(copy)

    def near(jx, jy):
        src = head_rows if (jx, jy) == (0, 0) else block(jx, jy, core)
        launch(remote(src, block(jx, jy, core), bn_sems, jx * yn + jy, core_peer))

    turn_copy = remote(pack, turned, turn_sems, 0, turn_peer)
    turn_local = pltpu.make_async_copy(pack, turned, own_sems.at[0])
    block_local = pltpu.make_async_copy(head_rows, block(0, 0, core), own_sems.at[1])

    @pl.when(moves)
    def _():
        turn_copy.start()
        turn_copy.wait()

    @pl.when(jnp.logical_not(moves))
    def _():
        turn_local.start()
        turn_local.wait()

    block_local.start()
    for jx in xs:
        launch(remote(head_rows, block(0, 0, core), bx_sems, jx - 1, x_peers[jx]))
    for jy in ys:
        launch(remote(head_rows, block(0, 0, core), by_sems, jy - 1, y_peers[jy]))
    near(0, 0)
    for jy in ys:
        view = block(0, jy, core)
        remote(view, view, by_sems, jy - 1, y_peers[jy]).wait_recv()
        for jx in xs:
            index = (jx - 1) * (yn - 1) + jy - 1
            launch(remote(view, view, bf_sems, index, x_peers[jx]))
        near(0, jy)
    for jx in xs:
        view = block(jx, 0, core)
        remote(view, view, bx_sems, jx - 1, x_peers[jx]).wait_recv()
        near(jx, 0)
    for jx in xs:
        for jy in ys:
            view = block(jx, jy, core)
            index = (jx - 1) * (yn - 1) + jy - 1
            remote(view, view, bf_sems, index, x_peers[jx]).wait_recv()
            near(jx, jy)
    for jx in range(xn):
        for jy in range(yn):
            view = block(jx, jy, 1 - core)
            remote(view, view, bn_sems, jx * yn + jy, core_peer).wait_recv()
    block_local.wait()
    for copy in started:
        copy.wait_send()


def spread_kernel(
    sizes,
    own,
    every,
    z_sems,
    xs_sems,
    ys_sems,
    xf_sems,
    yf_sems,
    near_sems,
    own_sem,
):
    zn, xn, yn, slots, part = sizes
    rest = slots - part
    z, x = lax.axis_index("a"), lax.axis_index("b")
    y, core = lax.axis_index("y"), lax.axis_index("core")
    core_peer = {"core": 1 - core}
    xs, ys, z_order = range(1, xn), range(1, yn), z_order_of(zn)
    x_peers = {k: {"b": lax.rem(x + k, xn)} for k in xs}
    y_peers = {k: {"y": lax.rem(y + k, yn)} for k in ys}
    z_peers = {k: {"a": lax.rem(z + k, zn)} for k in range(1, zn)}
    greet([core_peer, *x_peers.values(), *y_peers.values(), *z_peers.values()])

    def remote(src, dst, sems, index, peer):
        return pltpu.make_async_remote_copy(
            src_ref=src,
            dst_ref=dst,
            send_sem=sems.at[0, index],
            recv_sem=sems.at[1, index],
            device_id=peer,
            device_id_type=MESH_IDS,
        )

    def number(jz, jx, jy):
        chip = (lax.rem(z + zn - jz, zn) * xn + lax.rem(x + xn - jx, xn)) * yn + lax.rem(
            y + yn - jy, yn
        )
        return chip * 2 + core

    def shard(jz, jx, jy, first=0, count=slots):
        return every.at[pl.ds(number(jz, jx, jy) * slots + first, count)]

    def held(jz, jx, jy):
        return own if (jz, jx, jy) == (0, 0, 0) else shard(jz, jx, jy)

    def z_copy(jz):
        return remote(own, shard(0, 0, 0), z_sems, jz - 1, z_peers[jz])

    def xs_copy(jz, jx):
        return remote(
            held(jz, 0, 0), shard(jz, 0, 0), xs_sems, jz * (xn - 1) + jx - 1, x_peers[jx]
        )

    def ys_copy(jz, jy):
        return remote(
            held(jz, 0, 0), shard(jz, 0, 0), ys_sems, jz * (yn - 1) + jy - 1, y_peers[jy]
        )

    def cross(jz, jx, jy):
        return (jz * (xn - 1) + jx - 1) * (yn - 1) + jy - 1

    def xf_copy(jz, jx, jy):
        view = shard(jz, 0, jy, part, rest)
        return remote(view, view, xf_sems, cross(jz, jx, jy), x_peers[jx])

    def yf_copy(jz, jx, jy):
        view = shard(jz, jx, 0, 0, part)
        return remote(view, view, yf_sems, cross(jz, jx, jy), y_peers[jy])

    def near_copy(jz, jx, jy):
        return remote(
            held(jz, jx, jy),
            shard(jz, jx, jy),
            near_sems,
            (jz * xn + jx) * yn + jy,
            core_peer,
        )

    started = []

    def launch(copy):
        copy.start()
        started.append(copy)

    def send_own(jz):
        for jx in xs:
            launch(xs_copy(jz, jx))
        for jy in ys:
            launch(ys_copy(jz, jy))
        launch(near_copy(jz, 0, 0))

    def forward(jz):
        for jy in ys:
            ys_copy_in(jz, jy)
            for jx in xs:
                launch(xf_copy(jz, jx, jy))
        for jx in xs:
            xs_copy_in(jz, jx)
            for jy in ys:
                launch(yf_copy(jz, jx, jy))
        for jy in ys:
            launch(near_copy(jz, 0, jy))
        for jx in xs:
            launch(near_copy(jz, jx, 0))

    def ys_copy_in(jz, jy):
        view = shard(jz, 0, jy)
        remote(view, view, ys_sems, jz * (yn - 1) + jy - 1, y_peers[jy]).wait_recv()

    def xs_copy_in(jz, jx):
        view = shard(jz, jx, 0)
        remote(view, view, xs_sems, jz * (xn - 1) + jx - 1, x_peers[jx]).wait_recv()

    def finish(jz):
        for jx in xs:
            for jy in ys:
                view = shard(jz, jx, jy, part, rest)
                remote(view, view, xf_sems, cross(jz, jx, jy), x_peers[jx]).wait_recv()
                view = shard(jz, jx, jy, 0, part)
                remote(view, view, yf_sems, cross(jz, jx, jy), y_peers[jy]).wait_recv()
                launch(near_copy(jz, jx, jy))

    def z_in(index):
        jz = z_order[index]
        view = shard(jz, 0, 0)
        remote(view, view, z_sems, jz - 1, z_peers[jz]).wait_recv()
        if index + 1 < zn:
            launch(z_copy(z_order[index + 1]))

    own_local = pltpu.make_async_copy(own, shard(0, 0, 0), own_sem)

    launch(z_copy(z_order[1]))
    send_own(0)

    own_local.start()

    for index in range(1, zn):
        z_in(index)
        send_own(z_order[index])
        forward(z_order[index - 1])
        if index >= 2:
            finish(z_order[index - 2])
    forward(z_order[zn - 1])
    finish(z_order[zn - 2])
    finish(z_order[zn - 1])

    for jz in range(zn):
        for jx in range(xn):
            for jy in range(yn):
                chip = lax.div(number(jz, jx, jy), 2)
                view = every.at[pl.ds((chip * 2 + 1 - core) * slots, slots)]
                remote(
                    view, view, near_sems, (jz * xn + jx) * yn + jy, core_peer
                ).wait_recv()
    own_local.wait()
    for copy in started:
        copy.wait_send()


def reduce_kernel(
    sizes,
    grads,
    norm_in,
    total_out,
    norm_out,
    held,
    near,
    xd,
    yd,
    xs_in,
    ys_in,
    zs_in,
    norm_core,
    norm_y,
    norm_x,
    norm_z,
    norm_sum,
    load_sems,
    near_sems,
    xd_sems,
    yd_sems,
    xs_sems,
    ys_sems,
    zs_sems,
    norm_sems,
):
    zn, xn, yn, slots, part = sizes
    rest = slots - part
    z, x = lax.axis_index("a"), lax.axis_index("b")
    y, core = lax.axis_index("y"), lax.axis_index("core")
    core_peer = {"core": 1 - core}
    xs, ys = range(1, xn), range(1, yn)
    y_peers = [{"y": lax.rem(y + k, yn)} for k in ys]
    x_peers = [{"b": lax.rem(x + k, xn)} for k in xs]
    z_peers = [{"a": lax.rem(z + k, zn)} for k in range(1, zn)]
    greet([core_peer] + y_peers + x_peers + z_peers)

    def remote(src, dst, sems, index, peer):
        return pltpu.make_async_remote_copy(
            src_ref=src,
            dst_ref=dst,
            send_sem=sems.at[0, index],
            recv_sem=sems.at[1, index],
            device_id=peer,
            device_id_type=MESH_IDS,
        )

    def flat(jz, jx, jy):
        return (jz * xn + jx) * yn + jy

    def chip_rows(jz, jx, jy, which):
        chip = (lax.rem(z + jz, zn) * xn + lax.rem(x + jx, xn)) * yn + lax.rem(y + jy, yn)
        return grads.at[pl.ds((chip * 2 + which) * slots, slots)]

    def near_copy(jz, jx, jy):
        index = flat(jz, jx, jy)
        return remote(chip_rows(jz, jx, jy, 1 - core), near.at[index], near_sems, index, core_peer)

    def load_copy(jz, jx, jy):
        index = flat(jz, jx, jy)
        return pltpu.make_async_copy(
            chip_rows(jz, jx, jy, core), held.at[index], load_sems.at[index]
        )

    def whole(jz, jx, jy):
        return held.at[flat(jz, jx, jy)]

    def first(jz, jx, jy):
        return held.at[flat(jz, jx, jy), pl.ds(0, part)]

    def second(jz, jx, jy):
        return held.at[flat(jz, jx, jy), pl.ds(part, rest)]

    def cross(jz, jx, jy):
        return (jz * (xn - 1) + jx - 1) * (yn - 1) + jy - 1

    def yd_copy(jz, jx, jy):
        index = cross(jz, jx, jy)
        return remote(first(jz, jx, jy), yd.at[index], yd_sems, index, y_peers[jy - 1])

    def xd_copy(jz, jx, jy):
        index = cross(jz, jx, jy)
        return remote(second(jz, jx, jy), xd.at[index], xd_sems, index, x_peers[jx - 1])

    def xs_copy(jz, jx):
        index = jz * (xn - 1) + jx - 1
        return remote(whole(jz, jx, 0), xs_in.at[index], xs_sems, index, x_peers[jx - 1])

    def ys_copy(jz, jy):
        index = jz * (yn - 1) + jy - 1
        return remote(whole(jz, 0, jy), ys_in.at[index], ys_sems, index, y_peers[jy - 1])

    def zs_copy(jz):
        return remote(whole(jz, 0, 0), zs_in.at[jz - 1], zs_sems, jz - 1, z_peers[jz - 1])

    z_order = z_order_of(zn)[::-1]
    started = []

    def launch(copy):
        copy.start()
        started.append(copy)

    steps_done = []
    norm_count = [0]

    def norm_step(buffer, peers):
        copies = []
        for k, peer in enumerate(peers):
            index = norm_count[0]
            norm_count[0] += 1
            copy = remote(norm_sum.at[len(steps_done)], buffer.at[k], norm_sems, index, peer)
            copy.start()
            copies.append(copy)
        return copies

    def norm_finish(buffer, copies):
        total = norm_sum[len(steps_done)]
        for k, copy in enumerate(copies):
            copy.wait()
            total = total + buffer[k]
        steps_done.append(None)
        norm_sum[len(steps_done)] = total

    def plane(jz):
        return (
            [(jz, jx, jy) for jx in xs for jy in ys]
            + [(jz, jx, 0) for jx in xs]
            + [(jz, 0, jy) for jy in ys]
            + [(jz, 0, 0)]
        )

    def fetch(jz):
        for chip in plane(jz):
            launch(near_copy(*chip))
            load_copy(*chip).start()

    def prepare(index):
        for chip in plane(z_order[index]):
            load_copy(*chip).wait()
            near_copy(*chip).wait_recv()
            add_low(whole(*chip), near.at[flat(*chip)], slots)
            if chip[1] != 0 and chip[2] != 0:
                launch(yd_copy(*chip))
                launch(xd_copy(*chip))
        if index + 1 < zn:
            fetch(z_order[index + 1])

    def cross_in(index):
        jz = z_order[index]
        for jx in xs:
            for jy in ys:
                yd_copy(jz, jx, jy).wait_recv()
                add_low(first(jz, jx, 0), yd.at[cross(jz, jx, jy)], part)
            launch(xs_copy(jz, jx))
        for jy in ys:
            for jx in xs:
                xd_copy(jz, jx, jy).wait_recv()
                add_low(second(jz, 0, jy), xd.at[cross(jz, jx, jy)], rest)
            launch(ys_copy(jz, jy))

    def side_in(index):
        jz = z_order[index]
        for jx in xs:
            xs_copy(jz, jx).wait_recv()
        for jy in ys:
            ys_copy(jz, jy).wait_recv()

        def one(i, carry):
            total = held[flat(jz, 0, 0), i].astype(F32)
            for jx in xs:
                total = total + xs_in[jz * (xn - 1) + jx - 1, i].astype(F32)
            for jy in ys:
                total = total + ys_in[jz * (yn - 1) + jy - 1, i].astype(F32)
            if jz != 0:
                held[flat(jz, 0, 0), i] = total.astype(BF16)
            else:
                total_out[i] = total
            return carry

        lax.fori_loop(0, slots, one, None)
        if jz != 0:
            launch(zs_copy(jz))

    norm_sum[0] = norm_in[...]
    rounds = [(norm_core, [core_peer]), (norm_y, y_peers), (norm_x, x_peers), (norm_z, z_peers)]
    fetch(z_order[0])
    pending = norm_step(*rounds[0])
    prepare(0)
    for index in range(1, zn):
        prepare(index)
        cross_in(index - 1)
        if index >= 2:
            side_in(index - 2)
        if len(steps_done) < 3:
            norm_finish(rounds[len(steps_done)][0], pending)
            pending = norm_step(*rounds[len(steps_done)])
    cross_in(zn - 1)
    side_in(zn - 2)
    side_in(zn - 1)
    while len(steps_done) < 3:
        norm_finish(rounds[len(steps_done)][0], pending)
        pending = norm_step(*rounds[len(steps_done)])
    norm_finish(norm_z, pending)
    norm_out[...] = norm_sum[4]
    for jz in range(1, zn):
        zs_copy(jz).wait_recv()

    def last(i, carry):
        total = total_out[i]
        for jz in range(1, zn):
            total = total + zs_in[jz - 1, i].astype(F32)
        total_out[i] = total
        return carry

    lax.fori_loop(0, slots, last, None)
    for copy in started:
        copy.wait_send()


def vmem():
    return pl.BlockSpec(memory_space=pltpu.VMEM)


def smem():
    return pl.BlockSpec(memory_space=pltpu.SMEM)


def anywhere():
    return pl.BlockSpec(memory_space=pl.ANY)


def shape_of(dims, kind):
    return jax.ShapeDtypeStruct(dims, kind)


def params(collective=None):
    if collective is None:
        return pltpu.CompilerParams(vmem_limit_bytes=VMEM_LIMIT)
    return pltpu.CompilerParams(
        vmem_limit_bytes=VMEM_LIMIT, collective_id=collective, has_side_effects=True
    )


def swap_heads(block, n_dp, splits, collective):
    return pl.pallas_call(
        functools.partial(swap_heads_kernel, (n_dp, splits)),
        out_shape=shape_of(block.shape, BF16),
        in_specs=[vmem()],
        out_specs=vmem(),
        scratch_shapes=[
            pltpu.SemaphoreType.DMA((GROUPS - 1,)),
            pltpu.SemaphoreType.DMA((GROUPS - 1,)),
            pltpu.SemaphoreType.DMA,
        ],
        compiler_params=params(collective),
    )(block)


def per_device(
    dims,
    layer_input,
    out_cotangent,
    segment_ids,
    piece_owner,
    weight_master,
    weight_first,
    weight_second,
    norm_params,
    norm_first,
    norm_second,
):
    n_seq, n_dp = dims
    reps = n_seq // n_dp
    splits = n_seq // GROUPS
    slots, piece, width = weight_master.shape
    pieces = piece_owner.shape[0]
    tok = layer_input.shape[1]
    length = tok * n_seq
    hidden_units = (pieces * piece - 4 * width) // 3
    head = width // HEADS
    kind_pieces = width // piece
    hidden_pieces = hidden_units // piece
    chunk = hidden_units // CHUNKS

    location = locate_pieces(piece_owner, slots)
    own_low = weight_master.astype(BF16)
    seg_row = jnp.zeros((16, width), BF16).at[0, :tok].set(segment_ids[0].astype(BF16))
    pack = jnp.concatenate([layer_input[0], seg_row, out_cotangent[0]], axis=0)
    turn = [(i * n_dp + j, j * n_dp + i) for i in range(n_dp) for j in range(n_dp)]
    turn_axes = ("a", "y", "core")

    zn, xn, yn = n_dp, reps, n_dp // 2
    n_chips = zn * xn * yn

    def pair(count):
        return pltpu.SemaphoreType.DMA((2, max(count, 1)))

    half = slots // 2
    packed, gathered = pl.pallas_call(
        functools.partial(turn_kernel, (zn, xn, yn, tok + 16)),
        out_shape=(shape_of(pack.shape, BF16), shape_of((n_seq, tok + 16, width), BF16)),
        in_specs=[anywhere()],
        out_specs=(anywhere(),) * 2,
        scratch_shapes=[
            pair(1),
            pair(xn - 1),
            pair(yn - 1),
            pair((xn - 1) * (yn - 1)),
            pair(xn * yn),
            pltpu.SemaphoreType.DMA((2,)),
        ],
        compiler_params=params(6),
    )(pack)

    weights = pl.pallas_call(
        functools.partial(spread_kernel, (zn, xn, yn, slots, half)),
        out_shape=shape_of((n_chips * 2 * slots, piece, width), BF16),
        in_specs=[anywhere()],
        out_specs=anywhere(),
        scratch_shapes=[
            pair(zn - 1),
            pair(zn * (xn - 1)),
            pair(zn * (yn - 1)),
            pair(zn * (xn - 1) * (yn - 1)),
            pair(zn * (xn - 1) * (yn - 1)),
            pair(n_chips),
            pltpu.SemaphoreType.DMA,
        ],
        compiler_params=params(5),
    )(own_low)

    core = lax.axis_index("core")
    order = my_order(n_dp)
    group, split = order // splits, order % splits
    info = jnp.stack([core, group, split]).astype(jnp.int32)
    slopes = head_slopes(HEADS, tok, n_seq)

    segs = gathered[:, tok, :tok]
    lanes = jnp.arange(128, dtype=jnp.int32)[None, :] - head
    key_same = segs.reshape(length, 1).astype(jnp.int32) == lanes
    key_marks = jnp.where(key_same | (lanes < 0) | (lanes > 2), 0.0, MASKED).astype(BF16)
    query_segs = lax.dynamic_index_in_dim(
        segs.reshape(GROUPS, splits, tok), split, axis=1, keepdims=False
    )
    query_marks = (query_segs.reshape(GROUPS * tok, 1).astype(jnp.int32) == lanes).astype(BF16)

    attend_sizes = (n_dp, reps, splits, tok, head, n_seq)
    q_ext, k_ext, k_turned, v_rows, mixed_low, mixed_full, log_total = pl.pallas_call(
        functools.partial(attend_forward_kernel, attend_sizes),
        out_shape=(
            shape_of((TRIO, GROUPS * tok, 128), BF16),
            shape_of((TRIO, length, 128), BF16),
            shape_of((TRIO, head, length), BF16),
            shape_of((TRIO, length, head), BF16),
            shape_of((GROUPS, TRIO, head, tok), BF16),
            shape_of((GROUPS, TRIO, head, tok), F32),
            shape_of((GROUPS, TRIO, 1, tok), F32),
        ),
        in_specs=[smem(), smem(), smem(), vmem(), vmem(), vmem(), anywhere()],
        out_specs=(vmem(),) * 7,
        scratch_shapes=[
            pltpu.VMEM((3 * TRIO, 128, width), BF16),
            pltpu.VMEM((TRIO, head, length), BF16),
            pltpu.VMEM((3 * TRIO, tok, tok), F32),
            pltpu.VMEM((n_seq, tok, tok), F32),
            pltpu.SemaphoreType.DMA((3 * TRIO * (head // piece),)),
        ],
        compiler_params=params(),
    )(location, info, slopes, gathered, query_marks, key_marks, weights)

    mixed_own = swap_heads(mixed_low.reshape(GROUPS, TRIO * head, tok), n_dp, splits, 1)

    out_low, d_pre_one, d_mixed, norm_part, grads = pl.pallas_call(
        functools.partial(
            dense_kernel, (tok, piece, kind_pieces, chunk // piece, hidden_pieces)
        ),
        out_shape=(
            shape_of((tok, width), BF16),
            shape_of((tok, width), F32),
            shape_of((width, tok), BF16),
            shape_of((8, width), F32),
            shape_of((n_seq * n_dp * slots, piece, width), BF16),
        ),
        in_specs=[smem(), vmem(), vmem(), vmem(), anywhere()],
        out_specs=(vmem(), vmem(), vmem(), vmem(), anywhere()),
        scratch_shapes=[
            pltpu.VMEM((width, width), BF16),
            pltpu.VMEM((CHUNKS, chunk, width), BF16),
            pltpu.VMEM((CHUNKS, chunk, width), BF16),
            pltpu.VMEM((CHUNKS, chunk, width), BF16),
            pltpu.VMEM((CHUNKS, tok, chunk), F32),
            pltpu.VMEM((CHUNKS, tok, chunk), F32),
            pltpu.VMEM((CHUNKS, tok, chunk), BF16),
            pltpu.VMEM((2, 3, chunk, width), BF16),
            pltpu.VMEM((width, width), BF16),
            pltpu.SemaphoreType.DMA((3 * CHUNKS + 1,)),
            pltpu.SemaphoreType.DMA((7,)),
        ],
        compiler_params=params(),
    )(
        location,
        packed,
        mixed_own.reshape(width, tok),
        norm_params,
        weights,
    )

    result = lax.ppermute(out_low, turn_axes, turn)
    d_mixed_own = swap_heads(d_mixed.reshape(GROUPS, TRIO * head, tok), n_dp, splits, 2)

    d_query, d_key_value = pl.pallas_call(
        functools.partial(attend_backward_kernel, attend_sizes),
        out_shape=(
            shape_of((GROUPS, TRIO, head, tok), BF16),
            shape_of((splits, GROUPS, 2, TRIO, head, tok), BF16),
        ),
        in_specs=[smem(), smem()] + [vmem()] * 7,
        out_specs=(vmem(), vmem()),
        scratch_shapes=[
            pltpu.VMEM((TRIO, length, 128), F32),
            pltpu.VMEM((TRIO, length, head), F32),
            pltpu.VMEM((3 * TRIO, tok, tok), F32),
        ],
        compiler_params=params(),
    )(
        info,
        slopes,
        q_ext,
        k_ext,
        k_turned,
        v_rows,
        mixed_full,
        log_total,
        d_mixed_own.reshape(GROUPS, TRIO, head, tok),
    )

    trio_rows = TRIO * head
    d_groups, d_own = pl.pallas_call(
        functools.partial(share_grads_kernel, (n_dp, splits)),
        out_shape=(
            shape_of((GROUPS, 3, trio_rows, tok), BF16),
            shape_of((GROUPS, 3, trio_rows, tok), BF16),
        ),
        in_specs=[vmem(), vmem()],
        out_specs=(vmem(), vmem()),
        scratch_shapes=[
            pltpu.VMEM((splits - 1, GROUPS, 2, trio_rows, tok), BF16),
            pltpu.SemaphoreType.DMA((splits - 1,)),
            pltpu.SemaphoreType.DMA((splits - 1,)),
            pltpu.SemaphoreType.DMA((GROUPS - 1,)),
            pltpu.SemaphoreType.DMA((GROUPS - 1,)),
            pltpu.SemaphoreType.DMA,
        ],
        compiler_params=params(3),
    )(
        d_query.reshape(GROUPS, trio_rows, tok),
        d_key_value.reshape(splits, GROUPS, 2, trio_rows, tok),
    )

    d_tokens, grads = pl.pallas_call(
        functools.partial(project_grad_kernel, (piece, kind_pieces, splits, tok)),
        out_shape=(shape_of((tok, width), F32), shape_of(grads.shape, BF16)),
        in_specs=[smem(), smem(), vmem(), vmem(), vmem(), vmem()] + [anywhere()] * 2,
        out_specs=(vmem(), anywhere()),
        scratch_shapes=[
            pltpu.VMEM((3 * width, width), BF16),
            pltpu.VMEM((3 * trio_rows, width), BF16),
            pltpu.VMEM(((GROUPS - 1) * 3 * trio_rows, width), BF16),
            pltpu.SemaphoreType.DMA,
            pltpu.SemaphoreType.DMA,
            pltpu.SemaphoreType.DMA,
        ],
        input_output_aliases={7: 1},
        compiler_params=params(),
    )(
        location,
        info,
        gathered,
        d_groups.reshape(GROUPS, 3 * trio_rows, tok),
        d_own.reshape(3 * width, tok),
        d_pre_one,
        weights,
        grads,
    )
    d_input = lax.ppermute(d_tokens, turn_axes, turn)

    def chunks(count, rows):
        return pltpu.VMEM((max(count, 1), rows, piece, width), BF16)

    def norm_rows(count):
        return pltpu.VMEM((max(count, 1), 8, width), F32)

    crossing = zn * (xn - 1) * (yn - 1)
    own_grad, norm_total = pl.pallas_call(
        functools.partial(reduce_kernel, (zn, xn, yn, slots, half)),
        out_shape=(shape_of((slots, piece, width), F32), shape_of((8, width), F32)),
        in_specs=[anywhere(), vmem()],
        out_specs=(vmem(), vmem()),
        scratch_shapes=[
            chunks(n_chips, slots),
            chunks(n_chips, slots),
            chunks(crossing, slots - half),
            chunks(crossing, half),
            chunks(zn * (xn - 1), slots),
            chunks(zn * (yn - 1), slots),
            chunks(zn - 1, slots),
            norm_rows(1),
            norm_rows(yn - 1),
            norm_rows(xn - 1),
            norm_rows(zn - 1),
            norm_rows(5),
            pltpu.SemaphoreType.DMA((n_chips,)),
            pair(n_chips),
            pair(crossing),
            pair(crossing),
            pair(zn * (xn - 1)),
            pair(zn * (yn - 1)),
            pair(zn - 1),
            pair(1 + (yn - 1) + (xn - 1) + (zn - 1)),
        ],
        compiler_params=params(4),
    )(grads, norm_part)

    numbers = jnp.arange(pieces, dtype=jnp.int32) + 1
    own_slots = lax.axis_index(("a", "b", "y", "core")) * slots + jnp.arange(slots)
    inverse = jnp.sum(jnp.where(location[None, :] == own_slots[:, None], numbers[None, :], 0), axis=1)
    own_grad = jnp.where((inverse > 0)[:, None, None], own_grad, 0.0)
    norm_grad = norm_total[:4]
    rates = slot_rates(inverse, piece, width, hidden_units)
    first_new, second_new, weight_new = adamw_step(
        weight_master, weight_first, weight_second, own_grad, rates[:, None, None], STEP
    )
    norm_first_new, norm_second_new, norm_new = adamw_step(
        norm_params, norm_first, norm_second, norm_grad, NORM_RATE, STEP
    )
    return (
        result[None],
        d_input[None],
        own_grad,
        first_new,
        second_new,
        weight_new,
        weight_new.astype(BF16),
        norm_grad,
        norm_first_new,
        norm_second_new,
        norm_new,
    )


def solution(mesh):
    n_seq, n_dp = mesh.shape["seq"], mesh.shape["dp"]
    inner = Mesh(
        mesh.devices.reshape(n_dp, n_seq // n_dp, n_dp // 2, 2), ("a", "b", "y", "core")
    )
    seq, dp, every = ("a", "b"), ("y", "core"), ("a", "b", "y", "core")
    block = P(dp, seq, None)
    owned = P(every, None, None)
    in_specs = (block, block, P(dp, seq), P(), owned, owned, owned, P(), P(), P())
    out_specs = (block, block, owned, owned, owned, owned, owned, P(), P(), P(), P())
    return jax.shard_map(
        functools.partial(per_device, (n_seq, n_dp)),
        mesh=inner,
        in_specs=in_specs,
        out_specs=out_specs,
        check_vma=False,
    )
```

```python
import functools

import jax
import jax.numpy as jnp
from jax import lax
from jax.experimental import pallas as pl
from jax.experimental.pallas import tpu as pltpu
from jax.sharding import Mesh
from jax.sharding import PartitionSpec as P

HEADS = 12
GROUPS = 4
TRIO = HEADS // GROUPS
STEP = 4

NORM_EPS = 1e-06
BETA_ONE = 0.5
BETA_TWO = 0.5
DECAY = 0.01
ADAM_EPS = 1e-08
NORM_RATE = 0.3
OUT_RATE = 0.35
MASKED = -1e30
CHUNKS = 6
VMEM_LIMIT = 60 * 1024 * 1024
MESH_IDS = pl.DeviceIdType.MESH
F32 = jnp.float32
BF16 = jnp.bfloat16


def head_slopes(head_count, tok_rows, seq_devices):
    head_order = jnp.arange(head_count, dtype=jnp.float32)
    return (
        8.0 / tok_rows * jnp.power(jnp.float32(8.0 * seq_devices), -head_order / (head_count - 1))
    )


def locate_pieces(owners, slot_count):
    pieces = owners.shape[0]
    numbers = jnp.arange(pieces, dtype=jnp.int32)
    earlier = (owners[None, :] == owners[:, None]) & (numbers[None, :] < numbers[:, None])
    return owners * slot_count + jnp.sum(earlier.astype(jnp.int32), axis=1)


def slot_rates(inverse, piece_rows, model_width, hidden_units):
    first_row = (inverse - 1) * piece_rows
    narrow = model_width ** (-0.5)
    step_rate = jnp.where(
        first_row < 3 * model_width,
        narrow,
        jnp.where(
            first_row < 4 * model_width,
            OUT_RATE,
            jnp.where(
                first_row < 4 * model_width + 2 * hidden_units, narrow, hidden_units ** (-0.5)
            ),
        ),
    )
    return jnp.where(inverse > 0, step_rate, narrow).astype(jnp.float32)


def adamw_step(weight, first_moment, second, gradient, step_rate, step_count):
    first_moment = BETA_ONE * first_moment + (1.0 - BETA_ONE) * gradient
    second = BETA_TWO * second + (1.0 - BETA_TWO) * gradient * gradient
    mean_hat = first_moment / (1.0 - BETA_ONE**step_count)
    square_hat = second / (1.0 - BETA_TWO**step_count)
    weight = weight - step_rate * (mean_hat / (jnp.sqrt(square_hat) + ADAM_EPS) + DECAY * weight)
    return (first_moment, second, weight)


def dot_nt(left_side, right_side):
    return lax.dot_general(
        left_side, right_side, (((1,), (1,)), ((), ())), preferred_element_type=F32
    )


def dot_nn(left_side, right_side):
    return lax.dot_general(
        left_side, right_side, (((1,), (0,)), ((), ())), preferred_element_type=F32
    )


def dot_tn(left_side, right_side):
    return lax.dot_general(
        left_side, right_side, (((0,), (0,)), ((), ())), preferred_element_type=F32
    )


def fetch_piece(place, piece, weights, dst, sem):
    pltpu.make_async_copy(weights.at[place[piece]], dst, sem).start()


def fill_tables(table, slopes, group, tok):
    apart = lax.broadcasted_iota(jnp.int32, (tok, tok), 0) - lax.broadcasted_iota(
        jnp.int32, (tok, tok), 1
    )
    apart = apart.astype(F32)
    for h in range(TRIO):
        slope = slopes[group * TRIO + h]
        table[h * 3 + 0] = -slope * apart
        table[h * 3 + 1] = slope * jnp.abs(apart)
        table[h * 3 + 2] = slope * apart


def block_place(order, n_dp, reps):
    return (order % n_dp) * reps + order // n_dp


def bias_of(key_block, query_place, slope, h, tok, n_dp, reps):
    key_place = block_place(key_block, n_dp, reps)
    which = jnp.where(key_place > query_place, 2, jnp.where(key_place < query_place, 0, 1))
    shift = slope * (tok * jnp.abs(key_place - query_place)).astype(F32)
    return h * 3 + which, shift


def attend_forward_kernel(
    sizes,
    place,
    info,
    slopes,
    x_ref,
    query_marks,
    key_marks,
    weights,
    q_out,
    k_out,
    kt_out,
    v_out,
    mixed_low,
    mixed_full,
    log_out,
    wpad,
    vt,
    table,
    scores,
    sems,
):
    n_dp, reps, splits, tok, head, blocks = sizes
    group, split = info[1], info[2]
    per_head = head // 16
    width = x_ref.shape[2]
    kind_pieces = width // 16

    def start(step, carry):
        kind = lax.div(step, TRIO * per_head)
        rest = lax.rem(step, TRIO * per_head)
        number = kind * kind_pieces + group * (TRIO * per_head) + rest
        dst = wpad.at[
            kind * TRIO + lax.div(rest, per_head), pl.ds(lax.rem(rest, per_head) * 16, 16)
        ]
        fetch_piece(place, number, weights, dst, sems.at[step])
        return carry

    def finish(step, carry):
        kind = lax.div(step, TRIO * per_head)
        rest = lax.rem(step, TRIO * per_head)
        dst = wpad.at[
            kind * TRIO + lax.div(rest, per_head), pl.ds(lax.rem(rest, per_head) * 16, 16)
        ]
        pltpu.make_async_copy(weights.at[0], dst, sems.at[step]).wait()
        return carry

    lax.fori_loop(0, 3 * TRIO * per_head, start, None)
    for row in range(3 * TRIO):
        wpad[row, head:, :] = jnp.zeros((wpad.shape[1] - head, width), BF16)
    fill_tables(table, slopes, group, tok)
    lax.fori_loop(0, 3 * TRIO * per_head, finish, None)

    w_query = wpad[0:TRIO].reshape(TRIO * 128, width)
    w_key = wpad[TRIO : 2 * TRIO].reshape(TRIO * 128, width)
    w_value = wpad[2 * TRIO : 3 * TRIO].reshape(TRIO * 128, width)

    def project(block, carry):
        rows = pl.ds(pl.multiple_of(block * tok, tok), tok)
        xb = x_ref[block, 0:tok, :]
        keys = dot_nt(xb, w_key)
        values = dot_nt(xb, w_value)
        marks = key_marks[rows, :]
        for h in range(TRIO):
            key = keys[:, h * 128 : (h + 1) * 128]
            value = values[:, h * 128 : (h + 1) * 128]
            k_out[h, rows, :] = key.astype(BF16) + marks
            v_out[h, rows, :] = value[:, 0:head].astype(BF16)
            kt_out[h, :, rows] = key.T[0:head].astype(BF16)
            vt[h, :, rows] = value.T[0:head].astype(BF16)
        return carry

    lax.fori_loop(0, blocks, project, None)

    def project_query(index, carry):
        rows = pl.ds(pl.multiple_of(index * tok, tok), tok)
        xb = x_ref[index * splits + split, 0:tok, :]
        queries = dot_nt(xb, w_query).astype(BF16) * jnp.asarray(head**-0.5, BF16)
        marks = query_marks[rows, :]
        for h in range(TRIO):
            q_out[h, rows, :] = queries[:, h * 128 : (h + 1) * 128] + marks
        return carry

    lax.fori_loop(0, GROUPS, project_query, None)

    def attend(step, carry):
        index, h = lax.div(step, TRIO), lax.rem(step, TRIO)
        order = index * splits + split
        query_place = lax.rem(order, n_dp) * reps + lax.div(order, n_dp)
        slope = slopes[group * TRIO + h]
        qh = q_out[h, pl.ds(pl.multiple_of(index * tok, tok), tok), :]
        top = None
        shifts = []
        for kb in range(blocks):
            which, shift = bias_of(kb, query_place, slope, h, tok, n_dp, reps)
            now = dot_nt(k_out[h, kb * tok : (kb + 1) * tok, :], qh) - table[which]
            scores[kb] = now
            here = jnp.max(now, axis=0, keepdims=True) - shift
            top = here if top is None else jnp.maximum(top, here)
            shifts.append(shift)
        total = jnp.zeros((1, tok), F32)
        for kb in range(blocks):
            grown = jnp.exp(scores[kb] - (top + shifts[kb]))
            total = total + jnp.sum(grown, axis=0, keepdims=True)
            scores[kb] = grown
        inverse = 1.0 / total
        mixed = jnp.zeros((head, tok), F32)
        for kb in range(blocks):
            prob = (scores[kb] * inverse).astype(BF16)
            mixed = mixed + dot_nn(vt[h, :, kb * tok : (kb + 1) * tok], prob)
        mixed_full[index, h] = mixed
        mixed_low[index, h] = mixed.astype(BF16)
        log_out[index, h] = top + jnp.log(total)
        return carry

    lax.fori_loop(0, GROUPS * TRIO, attend, None)


def attend_backward_kernel(
    sizes,
    info,
    slopes,
    q_ref,
    k_ref,
    kt_ref,
    v_ref,
    mixed_full,
    log_in,
    d_mixed,
    dq_out,
    dkv_out,
    dk_sum,
    dv_sum,
    table,
):
    n_dp, reps, splits, tok, head, blocks = sizes
    group, split = info[1], info[2]
    fill_tables(table, slopes, group, tok)
    dk_sum[...] = jnp.zeros_like(dk_sum)
    dv_sum[...] = jnp.zeros_like(dv_sum)

    def step_fn(step, carry):
        h, index = lax.div(step, GROUPS), lax.rem(step, GROUPS)
        order = index * splits + split
        query_place = lax.rem(order, n_dp) * reps + lax.div(order, n_dp)
        slope = slopes[group * TRIO + h]
        qh = q_ref[h, pl.ds(pl.multiple_of(index * tok, tok), tok), :]
        dt = d_mixed[index, h]
        row_dot = jnp.sum(dt.astype(F32) * mixed_full[index, h], axis=0, keepdims=True)
        log_total = log_in[index, h]
        dq = jnp.zeros((head, tok), F32)
        for kb in range(blocks):
            rows = slice(kb * tok, (kb + 1) * tok)
            which, shift = bias_of(kb, query_place, slope, h, tok, n_dp, reps)
            now = dot_nt(k_ref[h, rows, :], qh) - table[which]
            prob = jnp.exp(now - (log_total + shift))
            d_prob = dot_nn(v_ref[h, rows, :], dt)
            d_score = (prob * (d_prob - row_dot)).astype(BF16)
            dv_sum[h, rows, :] += dot_nt(prob.astype(BF16), dt)
            dk_sum[h, rows, :] += dot_nn(d_score, qh)
            dq = dq + dot_nn(kt_ref[h, :, rows], d_score)
        dq_out[index, h] = (dq * (head**-0.5)).astype(BF16)
        return carry

    lax.fori_loop(0, TRIO * GROUPS, step_fn, None)

    def flip(step, carry):
        h, index = lax.div(step, GROUPS), lax.rem(step, GROUPS)
        for part in range(splits):
            rows = pl.ds(pl.multiple_of((index * splits + part) * tok, tok), tok)
            dkv_out[part, index, 0, h] = dk_sum[h, rows, :].T[0:head].astype(BF16)
            dkv_out[part, index, 1, h] = dv_sum[h, rows, :].T.astype(BF16)
        return carry

    lax.fori_loop(0, TRIO * GROUPS, flip, None)


def norm_stats(values_in):
    mean = jnp.mean(values_in, axis=-1, keepdims=True)
    centred = values_in - mean
    spread = jnp.mean(centred * centred, axis=-1, keepdims=True)
    scale = lax.rsqrt(spread + NORM_EPS)
    return centred * scale, scale


def norm_back(unit, scale, gain, cotangent):
    d_unit = cotangent * gain
    first = jnp.mean(d_unit, axis=-1, keepdims=True)
    second = jnp.mean(d_unit * unit, axis=-1, keepdims=True)
    d_in = scale * (d_unit - first - unit * second)
    d_gain = jnp.sum(cotangent * unit, axis=0, keepdims=True)
    d_bias = jnp.sum(cotangent, axis=0, keepdims=True)
    return d_in, d_gain, d_bias


def dense_kernel(
    sizes,
    place,
    x_ref,
    cot_ref,
    mixed_ref,
    norm_ref,
    weights,
    out_ref,
    d_pre_one_ref,
    d_mixed_ref,
    norm_grad,
    grads,
    w_out,
    w_gate,
    w_up,
    w_down,
    keep_gate,
    keep_up,
    keep_hidden,
    stage,
    stage_out,
    load_sems,
    store_sems,
):
    tok, piece, kind_pieces, chunk_pieces, hidden_pieces = sizes
    first_gate = 4 * kind_pieces
    first_up = first_gate + hidden_pieces
    first_down = first_up + hidden_pieces
    bases = (first_gate, first_up, first_down)
    buffers = (w_gate, w_up, w_down)
    chunk = chunk_pieces * piece

    def load_out(step, carry):
        fetch_piece(
            place,
            3 * kind_pieces + step,
            weights,
            w_out.at[pl.ds(step * piece, piece)],
            load_sems.at[3 * CHUNKS],
        )
        return carry

    def load_chunk(c):
        def one(step, carry):
            for kind in range(3):
                fetch_piece(
                    place,
                    bases[kind] + c * chunk_pieces + step,
                    weights,
                    buffers[kind].at[c, pl.ds(step * piece, piece)],
                    load_sems.at[kind * CHUNKS + c],
                )
            return carry

        lax.fori_loop(0, chunk_pieces, one, None)

    def wait_chunk(c):
        for kind in range(3):
            view = buffers[kind].at[c]
            pltpu.make_async_copy(view, view, load_sems.at[kind * CHUNKS + c]).wait()

    lax.fori_loop(0, kind_pieces, load_out, None)
    load_chunk(0)
    load_chunk(1)
    mixed = mixed_ref[...].T
    pltpu.make_async_copy(w_out, w_out, load_sems.at[3 * CHUNKS]).wait()
    pre_one = x_ref[...].astype(F32) + dot_nt(mixed, w_out[...])
    unit_one, scale_one = norm_stats(pre_one)
    h_one = unit_one * norm_ref[0:1, :] + norm_ref[1:2, :]
    h_low = h_one.astype(BF16)

    def forward(c, pre_two):
        @pl.when(c + 2 < CHUNKS)
        def _():
            load_chunk(c + 2)

        wait_chunk(c)
        gate = dot_nt(h_low, w_gate[c])
        up = dot_nt(h_low, w_up[c])
        below = 0.5 * (1.0 + lax.erf(gate * (0.5**0.5)))
        gelu = gate * below
        slope = below + gate * (jnp.exp(-0.5 * gate * gate) * (0.5 / jnp.pi) ** 0.5)
        hidden = (gelu * up).astype(BF16)
        keep_gate[c] = up * slope
        keep_up[c] = gelu
        keep_hidden[c] = hidden
        return pre_two + dot_nn(hidden, w_down[c])

    pre_two = lax.fori_loop(0, CHUNKS, forward, h_one)
    unit_two, scale_two = norm_stats(pre_two)
    out_ref[...] = (unit_two * norm_ref[2:3, :] + norm_ref[3:4, :]).astype(BF16)
    d_pre_two, d_gain_two, d_bias_two = norm_back(
        unit_two, scale_two, norm_ref[2:3, :], cot_ref[...].astype(F32)
    )
    d_branch = d_pre_two.astype(BF16)

    def drain(slot):
        for kind in range(3):
            view = stage.at[slot, kind]
            pltpu.make_async_copy(view, view, store_sems.at[slot * 3 + kind]).wait()

    def backward(c, d_h):
        slot = lax.rem(c, 2)

        @pl.when(c >= 2)
        def _():
            drain(slot)

        d_hidden = dot_nt(d_branch, w_down[c])
        d_gate = (d_hidden * keep_gate[c]).astype(BF16)
        d_up = (d_hidden * keep_up[c]).astype(BF16)
        stage[slot, 0] = dot_tn(d_gate, h_low).astype(BF16)
        stage[slot, 1] = dot_tn(d_up, h_low).astype(BF16)
        stage[slot, 2] = dot_tn(keep_hidden[c], d_branch).astype(BF16)

        def store(step, carry):
            for kind in range(3):
                pltpu.make_async_copy(
                    stage.at[slot, kind, pl.ds(step * piece, piece)],
                    grads.at[place[bases[kind] + c * chunk_pieces + step]],
                    store_sems.at[slot * 3 + kind],
                ).start()
            return carry

        lax.fori_loop(0, chunk_pieces, store, None)
        return d_h + dot_nn(d_gate, w_gate[c]) + dot_nn(d_up, w_up[c])

    d_h = lax.fori_loop(0, CHUNKS, backward, d_pre_two)
    d_pre_one, d_gain_one, d_bias_one = norm_back(unit_one, scale_one, norm_ref[0:1, :], d_h)
    d_pre_one_ref[...] = d_pre_one
    d_proj = d_pre_one.astype(BF16)
    d_mixed_ref[...] = lax.dot_general(
        w_out[...], d_proj, (((0,), (1,)), ((), ())), preferred_element_type=F32
    ).astype(BF16)
    stage_out[...] = dot_tn(d_proj, mixed).astype(BF16)

    def store_out(step, carry):
        pltpu.make_async_copy(
            stage_out.at[pl.ds(step * piece, piece)],
            grads.at[place[3 * kind_pieces + step]],
            store_sems.at[6],
        ).start()
        return carry

    lax.fori_loop(0, kind_pieces, store_out, None)
    norm_grad[...] = jnp.concatenate(
        [
            d_gain_one,
            d_bias_one,
            d_gain_two,
            d_bias_two,
            jnp.zeros((4, d_gain_one.shape[1]), F32),
        ],
        axis=0,
    )
    drain(CHUNKS % 2)
    drain((CHUNKS + 1) % 2)
    pltpu.make_async_copy(stage_out, stage_out, store_sems.at[6]).wait()


def project_grad_kernel(
    sizes,
    place,
    info,
    x_ref,
    d_groups,
    d_own,
    d_pre_one,
    weights,
    grads_in,
    d_input,
    grads,
    w_all,
    stage,
    blank,
    load_sem,
    store_sem,
    blank_sem,
):
    piece, kind_pieces, splits, tok = sizes
    group, split = info[1], info[2]
    group_pieces = kind_pieces // GROUPS
    del grads_in

    def load(step, carry):
        for kind in range(3):
            row = (lax.div(step, group_pieces) * 3 + kind) * group_pieces + lax.rem(
                step, group_pieces
            )
            fetch_piece(
                place,
                kind * kind_pieces + step,
                weights,
                w_all.at[pl.ds(row * piece, piece)],
                load_sem,
            )
        return carry

    lax.fori_loop(0, kind_pieces, load, None)
    blank[...] = jnp.zeros_like(blank)

    def clear(step, carry):
        other = lax.div(step, group_pieces)
        number = lax.rem(group + 1 + other, GROUPS) * group_pieces + lax.rem(step, group_pieces)
        for kind in range(3):
            pltpu.make_async_copy(
                blank.at[pl.ds(0, piece)], grads.at[place[kind * kind_pieces + number]], blank_sem
            ).start()
        return carry

    lax.fori_loop(0, (GROUPS - 1) * group_pieces, clear, None)
    total = dot_nn(d_groups[0], x_ref[split, 0:tok, :])
    for index in range(1, GROUPS):
        total = total + dot_nn(d_groups[index], x_ref[index * splits + split, 0:tok, :])
    stage[...] = total.astype(BF16)

    def store(step, carry):
        for kind in range(3):
            pltpu.make_async_copy(
                stage.at[pl.ds((kind * group_pieces + step) * piece, piece)],
                grads.at[place[kind * kind_pieces + group * group_pieces + step]],
                store_sem,
            ).start()
        return carry

    lax.fori_loop(0, group_pieces, store, None)
    pltpu.make_async_copy(w_all, w_all, load_sem).wait()
    d_input[...] = d_pre_one[...] + dot_tn(d_own[...], w_all[...])
    pltpu.make_async_copy(stage, stage, store_sem).wait()
    pltpu.make_async_copy(blank, blank, blank_sem).wait()


def holder(order, n_dp):
    dp = lax.rem(order, n_dp)
    return {"b": lax.div(order, n_dp), "y": lax.div(dp, 2), "core": lax.rem(dp, 2)}


def greet(peers):
    barrier = pltpu.get_barrier_semaphore()
    for peer in peers:
        pl.semaphore_signal(barrier, inc=1, device_id=peer, device_id_type=MESH_IDS)
    pl.semaphore_wait(barrier, len(peers))


def my_order(n_dp):
    return lax.axis_index("b") * n_dp + lax.axis_index("y") * 2 + lax.axis_index("core")


def swap_heads_kernel(sizes, in_ref, out_ref, send_sems, recv_sems, own_sem):
    n_dp, splits = sizes
    order = my_order(n_dp)
    group, split = lax.div(order, splits), lax.rem(order, splits)
    others = [lax.rem(group + k, GROUPS) for k in range(1, GROUPS)]
    peers = [holder(other * splits + split, n_dp) for other in others]
    greet(peers)
    copies = []
    for k in range(GROUPS - 1):
        copy = pltpu.make_async_remote_copy(
            src_ref=in_ref.at[others[k]],
            dst_ref=out_ref.at[group],
            send_sem=send_sems.at[k],
            recv_sem=recv_sems.at[k],
            device_id=peers[k],
            device_id_type=MESH_IDS,
        )
        copy.start()
        copies.append(copy)
    own = pltpu.make_async_copy(in_ref.at[group], out_ref.at[group], own_sem)
    own.start()
    own.wait()
    for copy in copies:
        copy.wait()


def share_grads_kernel(
    sizes,
    dq_ref,
    dkv_ref,
    groups_ref,
    own_ref,
    landed,
    near_send,
    near_recv,
    send_sems,
    recv_sems,
    own_sem,
):
    n_dp, splits = sizes
    order = my_order(n_dp)
    group, split = lax.div(order, splits), lax.rem(order, splits)
    twins = [lax.rem(split + k, splits) for k in range(1, splits)]
    twin_ids = [holder(group * splits + other, n_dp) for other in twins]
    others = [lax.rem(group + k, GROUPS) for k in range(1, GROUPS)]
    peers = [holder(other * splits + split, n_dp) for other in others]
    greet(twin_ids + peers)
    near = []
    for k in range(splits - 1):
        copy = pltpu.make_async_remote_copy(
            src_ref=dkv_ref.at[twins[k]],
            dst_ref=landed.at[k],
            send_sem=near_send.at[k],
            recv_sem=near_recv.at[k],
            device_id=twin_ids[k],
            device_id_type=MESH_IDS,
        )
        copy.start()
        near.append(copy)
    groups_ref[:, 0] = dq_ref[...]
    for copy in near:
        copy.wait()
    for index in range(GROUPS):
        for kind in range(2):
            total = dkv_ref[split, index, kind].astype(F32)
            for k in range(splits - 1):
                total = total + landed[k, index, kind].astype(F32)
            groups_ref[index, kind + 1] = total.astype(BF16)
    copies = []
    for k in range(GROUPS - 1):
        copy = pltpu.make_async_remote_copy(
            src_ref=groups_ref.at[others[k]],
            dst_ref=own_ref.at[group],
            send_sem=send_sems.at[k],
            recv_sem=recv_sems.at[k],
            device_id=peers[k],
            device_id_type=MESH_IDS,
        )
        copy.start()
        copies.append(copy)
    own = pltpu.make_async_copy(groups_ref.at[group], own_ref.at[group], own_sem)
    own.start()
    own.wait()
    for copy in copies:
        copy.wait()


def add_low(dst, src, rows):
    def one(i, carry):
        dst[i] = (dst[i].astype(F32) + src[i].astype(F32)).astype(BF16)
        return carry

    lax.fori_loop(0, rows, one, None)


def z_order_of(count):
    order = [0]
    for k in range(1, count):
        for far in (k, count - k):
            if far not in order:
                order.append(far)
    return order


def turn_kernel(
    sizes,
    pack,
    gathered,
    crossed,
    y_sems,
    z_sems,
    x_sems,
    near_sems,
    own_sem,
):
    zn, xn, yn = sizes
    z, x = lax.axis_index("a"), lax.axis_index("b")
    y, core = lax.axis_index("y"), lax.axis_index("core")
    core_peer = {"core": 1 - core}
    xs, ys, z_order = range(1, xn), range(1, yn), z_order_of(zn)
    x_peers = {k: {"b": lax.rem(x + k, xn)} for k in xs}
    y_peers = {k: {"y": lax.rem(y + k, yn)} for k in ys}
    z_peers = {k: {"a": lax.rem(z + k, zn)} for k in range(1, zn)}
    hosts = lax.rem(z, 2) == core
    greet([core_peer, *x_peers.values(), *y_peers.values(), *z_peers.values()])

    def remote(src, dst, sems, index, peer):
        return pltpu.make_async_remote_copy(
            src_ref=src,
            dst_ref=dst,
            send_sem=sems.at[0, index],
            recv_sem=sems.at[1, index],
            device_id=peer,
            device_id_type=MESH_IDS,
        )

    def block(jz, jx=0):
        return gathered.at[lax.rem(x + xn - jx, xn) * zn + lax.rem(z + zn - jz, zn)]

    def y_copy(jy):
        return remote(pack, crossed.at[jy - 1], y_sems, jy - 1, y_peers[jy])

    def plane(jy):
        return lax.rem(y + yn - jy, yn) * 2 + core

    def z_copy(jy):
        src = pack if jy == 0 else crossed.at[jy - 1]
        far = lax.rem(plane(jy) + zn - z, zn)
        return remote(src, block(0), z_sems, far, {"a": plane(jy)})

    def stay_copy(jy):
        src = pack if jy == 0 else crossed.at[jy - 1]
        return pltpu.make_async_copy(src, block(0), own_sem)

    def x_copy(jz, jx):
        return remote(block(jz), block(jz), x_sems, jz * (xn - 1) + jx - 1, x_peers[jx])

    def near_copy(jz, jx):
        return remote(block(jz, jx), block(jz, jx), near_sems, jz * xn + jx, core_peer)

    for jy in ys:
        y_copy(jy).start()
    for jy in range(yn):
        if jy != 0:
            y_copy(jy).wait_recv()

        @pl.when(plane(jy) != z)
        def _():
            z_copy(jy).start()

        @pl.when(plane(jy) == z)
        def _():
            stay_copy(jy).start()
            stay_copy(jy).wait()

    @pl.when(hosts)
    def _():
        for jz in z_order:
            if jz != 0:
                remote(block(jz), block(jz), z_sems, jz, z_peers[jz]).wait_recv()
            for jx in xs:
                x_copy(jz, jx).start()
            near_copy(jz, 0).start()
        for jz in z_order:
            for jx in xs:
                view = block(jz, jx)
                remote(view, view, x_sems, jz * (xn - 1) + jx - 1, x_peers[jx]).wait_recv()
                near_copy(jz, jx).start()
        for jz in z_order:
            for jx in xs:
                x_copy(jz, jx).wait_send()
            for jx in range(xn):
                near_copy(jz, jx).wait_send()

    @pl.when(jnp.logical_not(hosts))
    def _():
        for jz in range(zn):
            for jx in range(xn):
                near_copy(jz, jx).wait_recv()

    for jy in range(yn):

        @pl.when(plane(jy) != z)
        def _():
            z_copy(jy).wait_send()

    for jy in ys:
        y_copy(jy).wait_send()


def spread_kernel(
    sizes,
    own,
    every,
    z_sems,
    xs_sems,
    ys_sems,
    xf_sems,
    yf_sems,
    near_sems,
    own_sem,
):
    zn, xn, yn, slots, part = sizes
    rest = slots - part
    z, x = lax.axis_index("a"), lax.axis_index("b")
    y, core = lax.axis_index("y"), lax.axis_index("core")
    core_peer = {"core": 1 - core}
    xs, ys, z_order = range(1, xn), range(1, yn), z_order_of(zn)
    x_peers = {k: {"b": lax.rem(x + k, xn)} for k in xs}
    y_peers = {k: {"y": lax.rem(y + k, yn)} for k in ys}
    z_peers = {k: {"a": lax.rem(z + k, zn)} for k in range(1, zn)}
    greet([core_peer, *x_peers.values(), *y_peers.values(), *z_peers.values()])

    def remote(src, dst, sems, index, peer):
        return pltpu.make_async_remote_copy(
            src_ref=src,
            dst_ref=dst,
            send_sem=sems.at[0, index],
            recv_sem=sems.at[1, index],
            device_id=peer,
            device_id_type=MESH_IDS,
        )

    def number(jz, jx, jy):
        chip = (lax.rem(z + zn - jz, zn) * xn + lax.rem(x + xn - jx, xn)) * yn + lax.rem(
            y + yn - jy, yn
        )
        return chip * 2 + core

    def shard(jz, jx, jy, first=0, count=slots):
        return every.at[pl.ds(number(jz, jx, jy) * slots + first, count)]

    def held(jz, jx, jy):
        return own if (jz, jx, jy) == (0, 0, 0) else shard(jz, jx, jy)

    def z_copy(jz):
        return remote(own, shard(0, 0, 0), z_sems, jz - 1, z_peers[jz])

    def xs_copy(jz, jx):
        return remote(
            held(jz, 0, 0), shard(jz, 0, 0), xs_sems, jz * (xn - 1) + jx - 1, x_peers[jx]
        )

    def ys_copy(jz, jy):
        return remote(
            held(jz, 0, 0), shard(jz, 0, 0), ys_sems, jz * (yn - 1) + jy - 1, y_peers[jy]
        )

    def cross(jz, jx, jy):
        return (jz * (xn - 1) + jx - 1) * (yn - 1) + jy - 1

    def xf_copy(jz, jx, jy):
        view = shard(jz, 0, jy, part, rest)
        return remote(view, view, xf_sems, cross(jz, jx, jy), x_peers[jx])

    def yf_copy(jz, jx, jy):
        view = shard(jz, jx, 0, 0, part)
        return remote(view, view, yf_sems, cross(jz, jx, jy), y_peers[jy])

    def near_copy(jz, jx, jy):
        return remote(
            held(jz, jx, jy),
            shard(jz, jx, jy),
            near_sems,
            (jz * xn + jx) * yn + jy,
            core_peer,
        )

    started = []

    def launch(copy):
        copy.start()
        started.append(copy)

    def send_own(jz):
        for jx in xs:
            launch(xs_copy(jz, jx))
        for jy in ys:
            launch(ys_copy(jz, jy))
        launch(near_copy(jz, 0, 0))

    def forward(jz):
        for jy in ys:
            ys_copy_in(jz, jy)
            for jx in xs:
                launch(xf_copy(jz, jx, jy))
        for jx in xs:
            xs_copy_in(jz, jx)
            for jy in ys:
                launch(yf_copy(jz, jx, jy))
        for jy in ys:
            launch(near_copy(jz, 0, jy))
        for jx in xs:
            launch(near_copy(jz, jx, 0))

    def ys_copy_in(jz, jy):
        view = shard(jz, 0, jy)
        remote(view, view, ys_sems, jz * (yn - 1) + jy - 1, y_peers[jy]).wait_recv()

    def xs_copy_in(jz, jx):
        view = shard(jz, jx, 0)
        remote(view, view, xs_sems, jz * (xn - 1) + jx - 1, x_peers[jx]).wait_recv()

    def finish(jz):
        for jx in xs:
            for jy in ys:
                view = shard(jz, jx, jy, part, rest)
                remote(view, view, xf_sems, cross(jz, jx, jy), x_peers[jx]).wait_recv()
                view = shard(jz, jx, jy, 0, part)
                remote(view, view, yf_sems, cross(jz, jx, jy), y_peers[jy]).wait_recv()
                launch(near_copy(jz, jx, jy))

    def z_in(index):
        jz = z_order[index]
        view = shard(jz, 0, 0)
        remote(view, view, z_sems, jz - 1, z_peers[jz]).wait_recv()
        if index + 1 < zn:
            launch(z_copy(z_order[index + 1]))

    own_local = pltpu.make_async_copy(own, shard(0, 0, 0), own_sem)

    launch(z_copy(z_order[1]))
    send_own(0)

    own_local.start()

    for index in range(1, zn):
        z_in(index)
        send_own(z_order[index])
        forward(z_order[index - 1])
        if index >= 2:
            finish(z_order[index - 2])
    forward(z_order[zn - 1])
    finish(z_order[zn - 2])
    finish(z_order[zn - 1])

    for jz in range(zn):
        for jx in range(xn):
            for jy in range(yn):
                chip = lax.div(number(jz, jx, jy), 2)
                view = every.at[pl.ds((chip * 2 + 1 - core) * slots, slots)]
                remote(
                    view, view, near_sems, (jz * xn + jx) * yn + jy, core_peer
                ).wait_recv()
    own_local.wait()
    for copy in started:
        copy.wait_send()


def reduce_kernel(
    sizes,
    grads,
    norm_in,
    total_out,
    norm_out,
    held,
    near,
    xd,
    yd,
    xs_in,
    ys_in,
    zs_in,
    norm_core,
    norm_y,
    norm_x,
    norm_z,
    norm_sum,
    load_sems,
    near_sems,
    xd_sems,
    yd_sems,
    xs_sems,
    ys_sems,
    zs_sems,
    norm_sems,
):
    zn, xn, yn, slots, part = sizes
    rest = slots - part
    z, x = lax.axis_index("a"), lax.axis_index("b")
    y, core = lax.axis_index("y"), lax.axis_index("core")
    core_peer = {"core": 1 - core}
    xs, ys = range(1, xn), range(1, yn)
    y_peers = [{"y": lax.rem(y + k, yn)} for k in ys]
    x_peers = [{"b": lax.rem(x + k, xn)} for k in xs]
    z_peers = [{"a": lax.rem(z + k, zn)} for k in range(1, zn)]
    greet([core_peer] + y_peers + x_peers + z_peers)

    def remote(src, dst, sems, index, peer):
        return pltpu.make_async_remote_copy(
            src_ref=src,
            dst_ref=dst,
            send_sem=sems.at[0, index],
            recv_sem=sems.at[1, index],
            device_id=peer,
            device_id_type=MESH_IDS,
        )

    def flat(jz, jx, jy):
        return (jz * xn + jx) * yn + jy

    def chip_rows(jz, jx, jy, which):
        chip = (lax.rem(z + jz, zn) * xn + lax.rem(x + jx, xn)) * yn + lax.rem(y + jy, yn)
        return grads.at[pl.ds((chip * 2 + which) * slots, slots)]

    def near_copy(jz, jx, jy):
        index = flat(jz, jx, jy)
        return remote(chip_rows(jz, jx, jy, 1 - core), near.at[index], near_sems, index, core_peer)

    def load_copy(jz, jx, jy):
        index = flat(jz, jx, jy)
        return pltpu.make_async_copy(
            chip_rows(jz, jx, jy, core), held.at[index], load_sems.at[index]
        )

    def whole(jz, jx, jy):
        return held.at[flat(jz, jx, jy)]

    def first(jz, jx, jy):
        return held.at[flat(jz, jx, jy), pl.ds(0, part)]

    def second(jz, jx, jy):
        return held.at[flat(jz, jx, jy), pl.ds(part, rest)]

    def cross(jz, jx, jy):
        return (jz * (xn - 1) + jx - 1) * (yn - 1) + jy - 1

    def yd_copy(jz, jx, jy):
        index = cross(jz, jx, jy)
        return remote(first(jz, jx, jy), yd.at[index], yd_sems, index, y_peers[jy - 1])

    def xd_copy(jz, jx, jy):
        index = cross(jz, jx, jy)
        return remote(second(jz, jx, jy), xd.at[index], xd_sems, index, x_peers[jx - 1])

    def halves(low_half):
        return pl.ds(0, part) if low_half else pl.ds(part, rest)

    def xs_copy(jz, jx, low_half):
        index = jz * (xn - 1) + jx - 1
        return remote(
            held.at[flat(jz, jx, 0), halves(low_half)],
            xs_in.at[index, halves(low_half)],
            xs_sems,
            index * 2 + int(low_half),
            x_peers[jx - 1],
        )

    def ys_copy(jz, jy, low_half):
        index = jz * (yn - 1) + jy - 1
        return remote(
            held.at[flat(jz, 0, jy), halves(low_half)],
            ys_in.at[index, halves(low_half)],
            ys_sems,
            index * 2 + int(low_half),
            y_peers[jy - 1],
        )

    def zs_copy(jz):
        return remote(whole(jz, 0, 0), zs_in.at[jz - 1], zs_sems, jz - 1, z_peers[jz - 1])

    z_order = z_order_of(zn)[::-1]
    started = []

    def launch(copy):
        copy.start()
        started.append(copy)

    steps_done = []
    norm_count = [0]

    def norm_step(buffer, peers):
        copies = []
        for k, peer in enumerate(peers):
            index = norm_count[0]
            norm_count[0] += 1
            copy = remote(norm_sum.at[len(steps_done)], buffer.at[k], norm_sems, index, peer)
            copy.start()
            copies.append(copy)
        return copies

    def norm_finish(buffer, copies):
        total = norm_sum[len(steps_done)]
        for k, copy in enumerate(copies):
            copy.wait()
            total = total + buffer[k]
        steps_done.append(None)
        norm_sum[len(steps_done)] = total

    def plane(jz):
        return (
            [(jz, jx, jy) for jx in xs for jy in ys]
            + [(jz, jx, 0) for jx in xs]
            + [(jz, 0, jy) for jy in ys]
            + [(jz, 0, 0)]
        )

    def fetch(jz):
        for chip in plane(jz):
            launch(near_copy(*chip))
            load_copy(*chip).start()

    def prepare(index):
        for chip in plane(z_order[index]):
            load_copy(*chip).wait()
            near_copy(*chip).wait_recv()
            add_low(whole(*chip), near.at[flat(*chip)], slots)
        if index + 1 < zn:
            fetch(z_order[index + 1])

    stages = [(index, stage) for index in range(zn) for stage in range(3)]

    def send_stage(number):
        index, stage = stages[number]
        jz = z_order[index]
        for jx in xs:
            if stage == 0:
                for jy in ys:
                    launch(xd_copy(jz, jx, jy))
            else:
                launch(xs_copy(jz, jx, stage == 2))
        for jy in ys:
            if stage == 0:
                for jx in xs:
                    launch(yd_copy(jz, jx, jy))
            else:
                launch(ys_copy(jz, jy, stage == 1))

    def take_stage(number):
        index, stage = stages[number]
        jz = z_order[index]
        if stage == 0:
            for jx in xs:
                for jy in ys:
                    yd_copy(jz, jx, jy).wait_recv()
                    add_low(first(jz, jx, 0), yd.at[cross(jz, jx, jy)], part)
                    xd_copy(jz, jx, jy).wait_recv()
                    add_low(second(jz, 0, jy), xd.at[cross(jz, jx, jy)], rest)
        else:
            for jx in xs:
                xs_copy(jz, jx, stage == 2).wait_recv()
            for jy in ys:
                ys_copy(jz, jy, stage == 1).wait_recv()

    def side_in(index):
        jz = z_order[index]

        def one(i, carry):
            total = held[flat(jz, 0, 0), i].astype(F32)
            for jx in xs:
                total = total + xs_in[jz * (xn - 1) + jx - 1, i].astype(F32)
            for jy in ys:
                total = total + ys_in[jz * (yn - 1) + jy - 1, i].astype(F32)
            if jz != 0:
                held[flat(jz, 0, 0), i] = total.astype(BF16)
            else:
                total_out[i] = total
            return carry

        lax.fori_loop(0, slots, one, None)
        if jz != 0:
            launch(zs_copy(jz))

    norm_sum[0] = norm_in[...]
    rounds = [(norm_core, [core_peer]), (norm_y, y_peers), (norm_x, x_peers), (norm_z, z_peers)]
    fetch(z_order[0])
    pending = norm_step(*rounds[0])
    prepare(0)
    prepared, ahead = 1, 2
    for number in range(ahead):
        send_stage(number)
    for number in range(len(stages)):
        take_stage(number)
        later = number + ahead
        if later < len(stages):
            if stages[later][0] >= prepared:
                prepare(prepared)
                prepared += 1
            send_stage(later)
        if stages[number][1] == 2:
            side_in(stages[number][0])
        if number % 3 == 2 and len(steps_done) < 3:
            norm_finish(rounds[len(steps_done)][0], pending)
            pending = norm_step(*rounds[len(steps_done)])
    while len(steps_done) < 3:
        norm_finish(rounds[len(steps_done)][0], pending)
        pending = norm_step(*rounds[len(steps_done)])
    norm_finish(norm_z, pending)
    norm_out[...] = norm_sum[4]
    for jz in range(1, zn):
        zs_copy(jz).wait_recv()

    def last(i, carry):
        total = total_out[i]
        for jz in range(1, zn):
            total = total + zs_in[jz - 1, i].astype(F32)
        total_out[i] = total
        return carry

    lax.fori_loop(0, slots, last, None)
    for copy in started:
        copy.wait_send()


def vmem():
    return pl.BlockSpec(memory_space=pltpu.VMEM)


def smem():
    return pl.BlockSpec(memory_space=pltpu.SMEM)


def anywhere():
    return pl.BlockSpec(memory_space=pl.ANY)


def shape_of(dims, kind):
    return jax.ShapeDtypeStruct(dims, kind)


def params(collective=None):
    if collective is None:
        return pltpu.CompilerParams(vmem_limit_bytes=VMEM_LIMIT)
    return pltpu.CompilerParams(
        vmem_limit_bytes=VMEM_LIMIT, collective_id=collective, has_side_effects=True
    )


def swap_heads(block, n_dp, splits, collective):
    return pl.pallas_call(
        functools.partial(swap_heads_kernel, (n_dp, splits)),
        out_shape=shape_of(block.shape, BF16),
        in_specs=[vmem()],
        out_specs=vmem(),
        scratch_shapes=[
            pltpu.SemaphoreType.DMA((GROUPS - 1,)),
            pltpu.SemaphoreType.DMA((GROUPS - 1,)),
            pltpu.SemaphoreType.DMA,
        ],
        compiler_params=params(collective),
    )(block)


def per_device(
    dims,
    layer_input,
    out_cotangent,
    segment_ids,
    piece_owner,
    weight_master,
    weight_first,
    weight_second,
    norm_params,
    norm_first,
    norm_second,
):
    n_seq, n_dp = dims
    reps = n_seq // n_dp
    splits = n_seq // GROUPS
    slots, piece, width = weight_master.shape
    pieces = piece_owner.shape[0]
    tok = layer_input.shape[1]
    length = tok * n_seq
    hidden_units = (pieces * piece - 4 * width) // 3
    head = width // HEADS
    kind_pieces = width // piece
    hidden_pieces = hidden_units // piece
    chunk = hidden_units // CHUNKS

    location = locate_pieces(piece_owner, slots)
    own_low = weight_master.astype(BF16)
    seg_row = jnp.zeros((16, width), BF16).at[0, :tok].set(segment_ids[0].astype(BF16))
    pack = jnp.concatenate([layer_input[0], seg_row], axis=0)
    turn = [(i * n_dp + j, j * n_dp + i) for i in range(n_dp) for j in range(n_dp)]
    turn_axes = ("a", "y", "core")

    zn, xn, yn = n_dp, reps, n_dp // 2
    n_chips = zn * xn * yn

    def pair(count):
        return pltpu.SemaphoreType.DMA((2, max(count, 1)))

    half = slots // 2
    gathered, _ = pl.pallas_call(
        functools.partial(turn_kernel, (zn, xn, yn)),
        out_shape=(
            shape_of((n_seq, tok + 16, width), BF16),
            shape_of((max(yn - 1, 1), tok + 16, width), BF16),
        ),
        in_specs=[anywhere()],
        out_specs=(anywhere(), anywhere()),
        scratch_shapes=[
            pair(yn - 1),
            pair(zn),
            pair(zn * (xn - 1)),
            pair(zn * xn),
            pltpu.SemaphoreType.DMA,
        ],
        compiler_params=params(6),
    )(pack)

    weights = pl.pallas_call(
        functools.partial(spread_kernel, (zn, xn, yn, slots, half)),
        out_shape=shape_of((n_chips * 2 * slots, piece, width), BF16),
        in_specs=[anywhere()],
        out_specs=anywhere(),
        scratch_shapes=[
            pair(zn - 1),
            pair(zn * (xn - 1)),
            pair(zn * (yn - 1)),
            pair(zn * (xn - 1) * (yn - 1)),
            pair(zn * (xn - 1) * (yn - 1)),
            pair(n_chips),
            pltpu.SemaphoreType.DMA,
        ],
        compiler_params=params(5),
    )(own_low)
    weights, cotangent = lax.optimization_barrier((weights, out_cotangent[0]))
    cotangent = lax.ppermute(cotangent, turn_axes, turn)

    core = lax.axis_index("core")
    order = my_order(n_dp)
    group, split = order // splits, order % splits
    info = jnp.stack([core, group, split]).astype(jnp.int32)
    tokens = lax.dynamic_index_in_dim(gathered, order, axis=0, keepdims=False)[:tok]
    slopes = head_slopes(HEADS, tok, n_seq)

    segs = gathered[:, tok, :tok]
    lanes = jnp.arange(128, dtype=jnp.int32)[None, :] - head
    key_same = segs.reshape(length, 1).astype(jnp.int32) == lanes
    key_marks = jnp.where(key_same | (lanes < 0) | (lanes > 2), 0.0, MASKED).astype(BF16)
    query_segs = lax.dynamic_index_in_dim(
        segs.reshape(GROUPS, splits, tok), split, axis=1, keepdims=False
    )
    query_marks = (query_segs.reshape(GROUPS * tok, 1).astype(jnp.int32) == lanes).astype(BF16)

    attend_sizes = (n_dp, reps, splits, tok, head, n_seq)
    q_ext, k_ext, k_turned, v_rows, mixed_low, mixed_full, log_total = pl.pallas_call(
        functools.partial(attend_forward_kernel, attend_sizes),
        out_shape=(
            shape_of((TRIO, GROUPS * tok, 128), BF16),
            shape_of((TRIO, length, 128), BF16),
            shape_of((TRIO, head, length), BF16),
            shape_of((TRIO, length, head), BF16),
            shape_of((GROUPS, TRIO, head, tok), BF16),
            shape_of((GROUPS, TRIO, head, tok), F32),
            shape_of((GROUPS, TRIO, 1, tok), F32),
        ),
        in_specs=[smem(), smem(), smem(), vmem(), vmem(), vmem(), anywhere()],
        out_specs=(vmem(),) * 7,
        scratch_shapes=[
            pltpu.VMEM((3 * TRIO, 128, width), BF16),
            pltpu.VMEM((TRIO, head, length), BF16),
            pltpu.VMEM((3 * TRIO, tok, tok), F32),
            pltpu.VMEM((n_seq, tok, tok), F32),
            pltpu.SemaphoreType.DMA((3 * TRIO * (head // piece),)),
        ],
        compiler_params=params(),
    )(location, info, slopes, gathered, query_marks, key_marks, weights)

    mixed_own = swap_heads(mixed_low.reshape(GROUPS, TRIO * head, tok), n_dp, splits, 1)

    out_low, d_pre_one, d_mixed, norm_part, grads = pl.pallas_call(
        functools.partial(
            dense_kernel, (tok, piece, kind_pieces, chunk // piece, hidden_pieces)
        ),
        out_shape=(
            shape_of((tok, width), BF16),
            shape_of((tok, width), F32),
            shape_of((width, tok), BF16),
            shape_of((8, width), F32),
            shape_of((n_seq * n_dp * slots, piece, width), BF16),
        ),
        in_specs=[smem(), vmem(), vmem(), vmem(), vmem(), anywhere()],
        out_specs=(vmem(), vmem(), vmem(), vmem(), anywhere()),
        scratch_shapes=[
            pltpu.VMEM((width, width), BF16),
            pltpu.VMEM((CHUNKS, chunk, width), BF16),
            pltpu.VMEM((CHUNKS, chunk, width), BF16),
            pltpu.VMEM((CHUNKS, chunk, width), BF16),
            pltpu.VMEM((CHUNKS, tok, chunk), F32),
            pltpu.VMEM((CHUNKS, tok, chunk), F32),
            pltpu.VMEM((CHUNKS, tok, chunk), BF16),
            pltpu.VMEM((2, 3, chunk, width), BF16),
            pltpu.VMEM((width, width), BF16),
            pltpu.SemaphoreType.DMA((3 * CHUNKS + 1,)),
            pltpu.SemaphoreType.DMA((7,)),
        ],
        compiler_params=params(),
    )(
        location,
        tokens,
        cotangent,
        mixed_own.reshape(width, tok),
        norm_params,
        weights,
    )

    result = lax.ppermute(out_low, turn_axes, turn)
    d_mixed_own = swap_heads(d_mixed.reshape(GROUPS, TRIO * head, tok), n_dp, splits, 2)

    d_query, d_key_value = pl.pallas_call(
        functools.partial(attend_backward_kernel, attend_sizes),
        out_shape=(
            shape_of((GROUPS, TRIO, head, tok), BF16),
            shape_of((splits, GROUPS, 2, TRIO, head, tok), BF16),
        ),
        in_specs=[smem(), smem()] + [vmem()] * 7,
        out_specs=(vmem(), vmem()),
        scratch_shapes=[
            pltpu.VMEM((TRIO, length, 128), F32),
            pltpu.VMEM((TRIO, length, head), F32),
            pltpu.VMEM((3 * TRIO, tok, tok), F32),
        ],
        compiler_params=params(),
    )(
        info,
        slopes,
        q_ext,
        k_ext,
        k_turned,
        v_rows,
        mixed_full,
        log_total,
        d_mixed_own.reshape(GROUPS, TRIO, head, tok),
    )

    trio_rows = TRIO * head
    d_groups, d_own = pl.pallas_call(
        functools.partial(share_grads_kernel, (n_dp, splits)),
        out_shape=(
            shape_of((GROUPS, 3, trio_rows, tok), BF16),
            shape_of((GROUPS, 3, trio_rows, tok), BF16),
        ),
        in_specs=[vmem(), vmem()],
        out_specs=(vmem(), vmem()),
        scratch_shapes=[
            pltpu.VMEM((splits - 1, GROUPS, 2, trio_rows, tok), BF16),
            pltpu.SemaphoreType.DMA((splits - 1,)),
            pltpu.SemaphoreType.DMA((splits - 1,)),
            pltpu.SemaphoreType.DMA((GROUPS - 1,)),
            pltpu.SemaphoreType.DMA((GROUPS - 1,)),
            pltpu.SemaphoreType.DMA,
        ],
        compiler_params=params(3),
    )(
        d_query.reshape(GROUPS, trio_rows, tok),
        d_key_value.reshape(splits, GROUPS, 2, trio_rows, tok),
    )

    d_tokens, grads = pl.pallas_call(
        functools.partial(project_grad_kernel, (piece, kind_pieces, splits, tok)),
        out_shape=(shape_of((tok, width), F32), shape_of(grads.shape, BF16)),
        in_specs=[smem(), smem(), vmem(), vmem(), vmem(), vmem()] + [anywhere()] * 2,
        out_specs=(vmem(), anywhere()),
        scratch_shapes=[
            pltpu.VMEM((3 * width, width), BF16),
            pltpu.VMEM((3 * trio_rows, width), BF16),
            pltpu.VMEM(((GROUPS - 1) * 3 * trio_rows, width), BF16),
            pltpu.SemaphoreType.DMA,
            pltpu.SemaphoreType.DMA,
            pltpu.SemaphoreType.DMA,
        ],
        input_output_aliases={7: 1},
        compiler_params=params(),
    )(
        location,
        info,
        gathered,
        d_groups.reshape(GROUPS, 3 * trio_rows, tok),
        d_own.reshape(3 * width, tok),
        d_pre_one,
        weights,
        grads,
    )
    d_input = lax.ppermute(d_tokens, turn_axes, turn)

    def chunks(count, rows):
        return pltpu.VMEM((max(count, 1), rows, piece, width), BF16)

    def norm_rows(count):
        return pltpu.VMEM((max(count, 1), 8, width), F32)

    crossing = zn * (xn - 1) * (yn - 1)
    own_grad, norm_total = pl.pallas_call(
        functools.partial(reduce_kernel, (zn, xn, yn, slots, half)),
        out_shape=(shape_of((slots, piece, width), F32), shape_of((8, width), F32)),
        in_specs=[anywhere(), vmem()],
        out_specs=(vmem(), vmem()),
        scratch_shapes=[
            chunks(n_chips, slots),
            chunks(n_chips, slots),
            chunks(crossing, slots - half),
            chunks(crossing, half),
            chunks(zn * (xn - 1), slots),
            chunks(zn * (yn - 1), slots),
            chunks(zn - 1, slots),
            norm_rows(1),
            norm_rows(yn - 1),
            norm_rows(xn - 1),
            norm_rows(zn - 1),
            norm_rows(5),
            pltpu.SemaphoreType.DMA((n_chips,)),
            pair(n_chips),
            pair(crossing),
            pair(crossing),
            pair(2 * zn * (xn - 1)),
            pair(2 * zn * (yn - 1)),
            pair(zn - 1),
            pair(1 + (yn - 1) + (xn - 1) + (zn - 1)),
        ],
        compiler_params=params(4),
    )(grads, norm_part)

    numbers = jnp.arange(pieces, dtype=jnp.int32) + 1
    own_slots = lax.axis_index(("a", "b", "y", "core")) * slots + jnp.arange(slots)
    inverse = jnp.sum(jnp.where(location[None, :] == own_slots[:, None], numbers[None, :], 0), axis=1)
    own_grad = jnp.where((inverse > 0)[:, None, None], own_grad, 0.0)
    norm_grad = norm_total[:4]
    rates = slot_rates(inverse, piece, width, hidden_units)
    first_new, second_new, weight_new = adamw_step(
        weight_master, weight_first, weight_second, own_grad, rates[:, None, None], STEP
    )
    norm_first_new, norm_second_new, norm_new = adamw_step(
        norm_params, norm_first, norm_second, norm_grad, NORM_RATE, STEP
    )
    return (
        result[None],
        d_input[None],
        own_grad,
        first_new,
        second_new,
        weight_new,
        weight_new.astype(BF16),
        norm_grad,
        norm_first_new,
        norm_second_new,
        norm_new,
    )


def solution(mesh):
    n_seq, n_dp = mesh.shape["seq"], mesh.shape["dp"]
    inner = Mesh(
        mesh.devices.reshape(n_dp, n_seq // n_dp, n_dp // 2, 2), ("a", "b", "y", "core")
    )
    seq, dp, every = ("a", "b"), ("y", "core"), ("a", "b", "y", "core")
    block = P(dp, seq, None)
    owned = P(every, None, None)
    in_specs = (block, block, P(dp, seq), P(), owned, owned, owned, P(), P(), P())
    out_specs = (block, block, owned, owned, owned, owned, owned, P(), P(), P(), P())
    return jax.shard_map(
        functools.partial(per_device, (n_seq, n_dp)),
        mesh=inner,
        in_specs=in_specs,
        out_specs=out_specs,
        check_vma=False,
    )
```

```python
import functools

import jax
import jax.numpy as jnp
from jax import lax
from jax.experimental import pallas as pl
from jax.experimental.pallas import tpu as pltpu
from jax.sharding import Mesh
from jax.sharding import PartitionSpec as P

HEADS = 12
GROUPS = 4
TRIO = HEADS // GROUPS
STEP = 4

NORM_EPS = 1e-06
BETA_ONE = 0.5
BETA_TWO = 0.5
DECAY = 0.01
ADAM_EPS = 1e-08
NORM_RATE = 0.3
OUT_RATE = 0.35
MASKED = -1e30
CHUNKS = 6
VMEM_LIMIT = 60 * 1024 * 1024
MESH_IDS = pl.DeviceIdType.MESH
F32 = jnp.float32
BF16 = jnp.bfloat16


def head_slopes(head_count, tok_rows, seq_devices):
    head_order = jnp.arange(head_count, dtype=jnp.float32)
    return (
        8.0 / tok_rows * jnp.power(jnp.float32(8.0 * seq_devices), -head_order / (head_count - 1))
    )


def locate_pieces(owners, slot_count):
    pieces = owners.shape[0]
    numbers = jnp.arange(pieces, dtype=jnp.int32)
    earlier = (owners[None, :] == owners[:, None]) & (numbers[None, :] < numbers[:, None])
    return owners * slot_count + jnp.sum(earlier.astype(jnp.int32), axis=1)


def slot_rates(inverse, piece_rows, model_width, hidden_units):
    first_row = (inverse - 1) * piece_rows
    narrow = model_width ** (-0.5)
    step_rate = jnp.where(
        first_row < 3 * model_width,
        narrow,
        jnp.where(
            first_row < 4 * model_width,
            OUT_RATE,
            jnp.where(
                first_row < 4 * model_width + 2 * hidden_units, narrow, hidden_units ** (-0.5)
            ),
        ),
    )
    return jnp.where(inverse > 0, step_rate, narrow).astype(jnp.float32)


def adamw_step(weight, first_moment, second, gradient, step_rate, step_count):
    first_moment = BETA_ONE * first_moment + (1.0 - BETA_ONE) * gradient
    second = BETA_TWO * second + (1.0 - BETA_TWO) * gradient * gradient
    mean_hat = first_moment / (1.0 - BETA_ONE**step_count)
    square_hat = second / (1.0 - BETA_TWO**step_count)
    weight = weight - step_rate * (mean_hat / (jnp.sqrt(square_hat) + ADAM_EPS) + DECAY * weight)
    return (first_moment, second, weight)


def dot_nt(left_side, right_side):
    return lax.dot_general(
        left_side, right_side, (((1,), (1,)), ((), ())), preferred_element_type=F32
    )


def dot_nn(left_side, right_side):
    return lax.dot_general(
        left_side, right_side, (((1,), (0,)), ((), ())), preferred_element_type=F32
    )


def dot_tn(left_side, right_side):
    return lax.dot_general(
        left_side, right_side, (((0,), (0,)), ((), ())), preferred_element_type=F32
    )


def fetch_piece(place, piece, weights, dst, sem):
    pltpu.make_async_copy(weights.at[place[piece]], dst, sem).start()


def fill_tables(table, slopes, group, tok):
    apart = lax.broadcasted_iota(jnp.int32, (tok, tok), 0) - lax.broadcasted_iota(
        jnp.int32, (tok, tok), 1
    )
    apart = apart.astype(F32)
    for h in range(TRIO):
        slope = slopes[group * TRIO + h]
        table[h * 3 + 0] = -slope * apart
        table[h * 3 + 1] = slope * jnp.abs(apart)
        table[h * 3 + 2] = slope * apart


def block_place(order, n_dp, reps):
    return (order % n_dp) * reps + order // n_dp


def bias_of(key_block, query_place, slope, h, tok, n_dp, reps):
    key_place = block_place(key_block, n_dp, reps)
    which = jnp.where(key_place > query_place, 2, jnp.where(key_place < query_place, 0, 1))
    shift = slope * (tok * jnp.abs(key_place - query_place)).astype(F32)
    return h * 3 + which, shift


def attend_forward_kernel(
    sizes,
    place,
    info,
    slopes,
    x_ref,
    query_marks,
    key_marks,
    weights,
    q_out,
    k_out,
    kt_out,
    v_out,
    mixed_low,
    mixed_full,
    log_out,
    wpad,
    vt,
    table,
    scores,
    sems,
):
    n_dp, reps, splits, tok, head, blocks = sizes
    group, split = info[1], info[2]
    per_head = head // 16
    width = x_ref.shape[2]
    kind_pieces = width // 16

    def start(step, carry):
        kind = lax.div(step, TRIO * per_head)
        rest = lax.rem(step, TRIO * per_head)
        number = kind * kind_pieces + group * (TRIO * per_head) + rest
        dst = wpad.at[
            kind * TRIO + lax.div(rest, per_head), pl.ds(lax.rem(rest, per_head) * 16, 16)
        ]
        fetch_piece(place, number, weights, dst, sems.at[step])
        return carry

    def finish(step, carry):
        kind = lax.div(step, TRIO * per_head)
        rest = lax.rem(step, TRIO * per_head)
        dst = wpad.at[
            kind * TRIO + lax.div(rest, per_head), pl.ds(lax.rem(rest, per_head) * 16, 16)
        ]
        pltpu.make_async_copy(weights.at[0], dst, sems.at[step]).wait()
        return carry

    lax.fori_loop(0, 3 * TRIO * per_head, start, None, unroll=6)
    for row in range(3 * TRIO):
        wpad[row, head:, :] = jnp.zeros((wpad.shape[1] - head, width), BF16)
    fill_tables(table, slopes, group, tok)
    lax.fori_loop(0, 3 * TRIO * per_head, finish, None)

    w_query = wpad[0:TRIO].reshape(TRIO * 128, width)
    w_key = wpad[TRIO : 2 * TRIO].reshape(TRIO * 128, width)
    w_value = wpad[2 * TRIO : 3 * TRIO].reshape(TRIO * 128, width)

    def project(block, carry):
        rows = pl.ds(pl.multiple_of(block * tok, tok), tok)
        xb = x_ref[block, 0:tok, :]
        keys = dot_nt(xb, w_key)
        values = dot_nt(xb, w_value)
        marks = key_marks[rows, :]
        for h in range(TRIO):
            key = keys[:, h * 128 : (h + 1) * 128]
            value = values[:, h * 128 : (h + 1) * 128]
            k_out[h, rows, :] = key.astype(BF16) + marks
            v_out[h, rows, :] = value[:, 0:head].astype(BF16)
            kt_out[h, :, rows] = key.T[0:head].astype(BF16)
            vt[h, :, rows] = value.T[0:head].astype(BF16)
        return carry

    lax.fori_loop(0, blocks, project, None)

    def project_query(index, carry):
        rows = pl.ds(pl.multiple_of(index * tok, tok), tok)
        xb = x_ref[index * splits + split, 0:tok, :]
        queries = dot_nt(xb, w_query).astype(BF16) * jnp.asarray(head**-0.5, BF16)
        marks = query_marks[rows, :]
        for h in range(TRIO):
            q_out[h, rows, :] = queries[:, h * 128 : (h + 1) * 128] + marks
        return carry

    lax.fori_loop(0, GROUPS, project_query, None)

    def attend(step, carry):
        index, h = lax.div(step, TRIO), lax.rem(step, TRIO)
        order = index * splits + split
        query_place = lax.rem(order, n_dp) * reps + lax.div(order, n_dp)
        slope = slopes[group * TRIO + h]
        qh = q_out[h, pl.ds(pl.multiple_of(index * tok, tok), tok), :]
        top = None
        shifts = []
        for kb in range(blocks):
            which, shift = bias_of(kb, query_place, slope, h, tok, n_dp, reps)
            now = dot_nt(k_out[h, kb * tok : (kb + 1) * tok, :], qh) - table[which]
            scores[kb] = now
            here = jnp.max(now, axis=0, keepdims=True) - shift
            top = here if top is None else jnp.maximum(top, here)
            shifts.append(shift)
        total = jnp.zeros((1, tok), F32)
        for kb in range(blocks):
            grown = jnp.exp(scores[kb] - (top + shifts[kb]))
            total = total + jnp.sum(grown, axis=0, keepdims=True)
            scores[kb] = grown
        inverse = 1.0 / total
        mixed = jnp.zeros((head, tok), F32)
        for kb in range(blocks):
            prob = (scores[kb] * inverse).astype(BF16)
            mixed = mixed + dot_nn(vt[h, :, kb * tok : (kb + 1) * tok], prob)
        mixed_full[index, h] = mixed
        mixed_low[index, h] = mixed.astype(BF16)
        log_out[index, h] = top + jnp.log(total)
        return carry

    lax.fori_loop(0, GROUPS * TRIO, attend, None)


def attend_backward_kernel(
    sizes,
    info,
    slopes,
    q_ref,
    k_ref,
    kt_ref,
    v_ref,
    mixed_full,
    log_in,
    d_mixed,
    dq_out,
    dkv_out,
    dk_sum,
    dv_sum,
    table,
):
    n_dp, reps, splits, tok, head, blocks = sizes
    group, split = info[1], info[2]
    fill_tables(table, slopes, group, tok)
    dk_sum[...] = jnp.zeros_like(dk_sum)
    dv_sum[...] = jnp.zeros_like(dv_sum)

    def step_fn(step, carry):
        h, index = lax.div(step, GROUPS), lax.rem(step, GROUPS)
        order = index * splits + split
        query_place = lax.rem(order, n_dp) * reps + lax.div(order, n_dp)
        slope = slopes[group * TRIO + h]
        qh = q_ref[h, pl.ds(pl.multiple_of(index * tok, tok), tok), :]
        qt = qh[:, 0:head].T
        dt = d_mixed[index, h]
        row_dot = jnp.sum(dt.astype(F32) * mixed_full[index, h], axis=0, keepdims=True)
        log_total = log_in[index, h]
        dq = jnp.zeros((head, tok), F32)
        for kb in range(blocks):
            rows = slice(kb * tok, (kb + 1) * tok)
            which, shift = bias_of(kb, query_place, slope, h, tok, n_dp, reps)
            now = dot_nt(k_ref[h, rows, :], qh) - table[which]
            prob = jnp.exp(now - (log_total + shift))
            d_prob = dot_nn(v_ref[h, rows, :], dt)
            d_score = (prob * (d_prob - row_dot)).astype(BF16)
            dv_sum[h, :, rows] += dot_nt(dt, prob.astype(BF16))
            dk_sum[h, :, rows] += dot_nt(qt, d_score)
            dq = dq + dot_nn(kt_ref[h, :, rows], d_score)
        dq_out[index, h] = (dq * (head**-0.5)).astype(BF16)
        return carry

    lax.fori_loop(0, TRIO * GROUPS, step_fn, None)

    def flip(step, carry):
        h, index = lax.div(step, GROUPS), lax.rem(step, GROUPS)
        for part in range(splits):
            rows = pl.ds(pl.multiple_of((index * splits + part) * tok, tok), tok)
            dkv_out[part, index, 0, h] = dk_sum[h, :, rows].astype(BF16)
            dkv_out[part, index, 1, h] = dv_sum[h, :, rows].astype(BF16)
        return carry

    lax.fori_loop(0, TRIO * GROUPS, flip, None)


def norm_stats(values_in):
    mean = jnp.mean(values_in, axis=-1, keepdims=True)
    centred = values_in - mean
    spread = jnp.mean(centred * centred, axis=-1, keepdims=True)
    scale = lax.rsqrt(spread + NORM_EPS)
    return centred * scale, scale


def norm_back(unit, scale, gain, cotangent):
    d_unit = cotangent * gain
    first = jnp.mean(d_unit, axis=-1, keepdims=True)
    second = jnp.mean(d_unit * unit, axis=-1, keepdims=True)
    d_in = scale * (d_unit - first - unit * second)
    d_gain = jnp.sum(cotangent * unit, axis=0, keepdims=True)
    d_bias = jnp.sum(cotangent, axis=0, keepdims=True)
    return d_in, d_gain, d_bias


def dense_kernel(
    sizes,
    place,
    x_ref,
    cot_ref,
    mixed_ref,
    norm_ref,
    weights,
    out_ref,
    d_pre_one_ref,
    d_mixed_ref,
    norm_grad,
    grads,
    w_out,
    w_gate,
    w_up,
    w_down,
    keep_gate,
    keep_up,
    keep_hidden,
    stage,
    stage_out,
    load_sems,
    store_sems,
):
    tok, piece, kind_pieces, chunk_pieces, hidden_pieces = sizes
    first_gate = 4 * kind_pieces
    first_up = first_gate + hidden_pieces
    first_down = first_up + hidden_pieces
    bases = (first_gate, first_up, first_down)
    buffers = (w_gate, w_up, w_down)
    chunk = chunk_pieces * piece

    def load_out(step, carry):
        fetch_piece(
            place,
            3 * kind_pieces + step,
            weights,
            w_out.at[pl.ds(step * piece, piece)],
            load_sems.at[3 * CHUNKS],
        )
        return carry

    def load_chunk(c):
        def one(step, carry):
            for kind in range(3):
                fetch_piece(
                    place,
                    bases[kind] + c * chunk_pieces + step,
                    weights,
                    buffers[kind].at[c, pl.ds(step * piece, piece)],
                    load_sems.at[kind * CHUNKS + c],
                )
            return carry

        lax.fori_loop(0, chunk_pieces, one, None, unroll=4)

    def wait_chunk(c):
        for kind in range(3):
            view = buffers[kind].at[c]
            pltpu.make_async_copy(view, view, load_sems.at[kind * CHUNKS + c]).wait()

    lax.fori_loop(0, kind_pieces, load_out, None, unroll=8)
    load_chunk(0)
    load_chunk(1)
    mixed = mixed_ref[...].T
    pltpu.make_async_copy(w_out, w_out, load_sems.at[3 * CHUNKS]).wait()
    pre_one = x_ref[...].astype(F32) + dot_nt(mixed, w_out[...])
    unit_one, scale_one = norm_stats(pre_one)
    h_one = unit_one * norm_ref[0:1, :] + norm_ref[1:2, :]
    h_low = h_one.astype(BF16)

    def forward(c, pre_two):
        @pl.when(c + 2 < CHUNKS)
        def _():
            load_chunk(c + 2)

        wait_chunk(c)
        gate = dot_nt(h_low, w_gate[c])
        up = dot_nt(h_low, w_up[c])
        below = 0.5 * (1.0 + lax.erf(gate * (0.5**0.5)))
        gelu = gate * below
        slope = below + gate * (jnp.exp(-0.5 * gate * gate) * (0.5 / jnp.pi) ** 0.5)
        hidden = (gelu * up).astype(BF16)
        keep_gate[c] = up * slope
        keep_up[c] = gelu
        keep_hidden[c] = hidden
        return pre_two + dot_nn(hidden, w_down[c])

    pre_two = lax.fori_loop(0, CHUNKS, forward, h_one)
    unit_two, scale_two = norm_stats(pre_two)
    out_ref[...] = (unit_two * norm_ref[2:3, :] + norm_ref[3:4, :]).astype(BF16)
    d_pre_two, d_gain_two, d_bias_two = norm_back(
        unit_two, scale_two, norm_ref[2:3, :], cot_ref[...].astype(F32)
    )
    d_branch = d_pre_two.astype(BF16)

    def drain(slot):
        for kind in range(3):
            view = stage.at[slot, kind]
            pltpu.make_async_copy(view, view, store_sems.at[slot * 3 + kind]).wait()

    def backward(c, d_h):
        slot = lax.rem(c, 2)

        @pl.when(c >= 2)
        def _():
            drain(slot)

        d_hidden = dot_nt(d_branch, w_down[c])
        d_gate = (d_hidden * keep_gate[c]).astype(BF16)
        d_up = (d_hidden * keep_up[c]).astype(BF16)
        stage[slot, 0] = dot_tn(d_gate, h_low).astype(BF16)
        stage[slot, 1] = dot_tn(d_up, h_low).astype(BF16)
        stage[slot, 2] = dot_tn(keep_hidden[c], d_branch).astype(BF16)

        def store(step, carry):
            for kind in range(3):
                pltpu.make_async_copy(
                    stage.at[slot, kind, pl.ds(step * piece, piece)],
                    grads.at[place[bases[kind] + c * chunk_pieces + step]],
                    store_sems.at[slot * 3 + kind],
                ).start()
            return carry

        lax.fori_loop(0, chunk_pieces, store, None, unroll=4)
        return d_h + dot_nn(d_gate, w_gate[c]) + dot_nn(d_up, w_up[c])

    d_h = lax.fori_loop(0, CHUNKS, backward, d_pre_two)
    d_pre_one, d_gain_one, d_bias_one = norm_back(unit_one, scale_one, norm_ref[0:1, :], d_h)
    d_pre_one_ref[...] = d_pre_one
    d_proj = d_pre_one.astype(BF16)
    d_mixed_ref[...] = lax.dot_general(
        w_out[...], d_proj, (((0,), (1,)), ((), ())), preferred_element_type=F32
    ).astype(BF16)
    stage_out[...] = dot_tn(d_proj, mixed).astype(BF16)

    def store_out(step, carry):
        pltpu.make_async_copy(
            stage_out.at[pl.ds(step * piece, piece)],
            grads.at[place[3 * kind_pieces + step]],
            store_sems.at[6],
        ).start()
        return carry

    lax.fori_loop(0, kind_pieces, store_out, None, unroll=8)
    norm_grad[...] = jnp.concatenate(
        [
            d_gain_one,
            d_bias_one,
            d_gain_two,
            d_bias_two,
            jnp.zeros((4, d_gain_one.shape[1]), F32),
        ],
        axis=0,
    )
    drain(CHUNKS % 2)
    drain((CHUNKS + 1) % 2)
    pltpu.make_async_copy(stage_out, stage_out, store_sems.at[6]).wait()


def project_grad_kernel(
    sizes,
    place,
    info,
    x_ref,
    d_groups,
    d_own,
    d_pre_one,
    weights,
    grads_in,
    d_input,
    grads,
    w_all,
    stage,
    blank,
    load_sem,
    store_sem,
    blank_sem,
):
    piece, kind_pieces, splits, tok = sizes
    group, split = info[1], info[2]
    group_pieces = kind_pieces // GROUPS
    del grads_in

    def load(step, carry):
        for kind in range(3):
            row = (lax.div(step, group_pieces) * 3 + kind) * group_pieces + lax.rem(
                step, group_pieces
            )
            fetch_piece(
                place,
                kind * kind_pieces + step,
                weights,
                w_all.at[pl.ds(row * piece, piece)],
                load_sem,
            )
        return carry

    lax.fori_loop(0, kind_pieces, load, None, unroll=4)
    blank[...] = jnp.zeros_like(blank)

    def clear(step, carry):
        other = lax.div(step, group_pieces)
        number = lax.rem(group + 1 + other, GROUPS) * group_pieces + lax.rem(step, group_pieces)
        for kind in range(3):
            pltpu.make_async_copy(
                blank.at[pl.ds(0, piece)], grads.at[place[kind * kind_pieces + number]], blank_sem
            ).start()
        return carry

    lax.fori_loop(0, (GROUPS - 1) * group_pieces, clear, None, unroll=4)
    total = dot_nn(d_groups[0], x_ref[split, 0:tok, :])
    for index in range(1, GROUPS):
        total = total + dot_nn(d_groups[index], x_ref[index * splits + split, 0:tok, :])
    stage[...] = total.astype(BF16)

    def store(step, carry):
        for kind in range(3):
            pltpu.make_async_copy(
                stage.at[pl.ds((kind * group_pieces + step) * piece, piece)],
                grads.at[place[kind * kind_pieces + group * group_pieces + step]],
                store_sem,
            ).start()
        return carry

    lax.fori_loop(0, group_pieces, store, None, unroll=4)
    pltpu.make_async_copy(w_all, w_all, load_sem).wait()
    d_input[...] = (d_pre_one[...] + dot_tn(d_own[...], w_all[...])).astype(BF16)
    pltpu.make_async_copy(stage, stage, store_sem).wait()
    pltpu.make_async_copy(blank, blank, blank_sem).wait()


def holder(order, n_dp):
    dp = lax.rem(order, n_dp)
    return {"b": lax.div(order, n_dp), "y": lax.div(dp, 2), "core": lax.rem(dp, 2)}


def turn_to():
    z, dp = lax.axis_index("a"), lax.axis_index("y") * 2 + lax.axis_index("core")
    return {"a": dp, "y": lax.div(z, 2), "core": lax.rem(z, 2)}, dp != z


def start_turn(src, dst, send_sem, recv_sem):
    peer, moves = turn_to()

    @pl.when(moves)
    def _():
        pltpu.make_async_remote_copy(
            src_ref=src,
            dst_ref=dst,
            send_sem=send_sem,
            recv_sem=recv_sem,
            device_id=peer,
            device_id_type=MESH_IDS,
        ).start()

    @pl.when(jnp.logical_not(moves))
    def _():
        pltpu.make_async_copy(src, dst, recv_sem).start()


def finish_turn(src, dst, send_sem, recv_sem):
    peer, moves = turn_to()

    @pl.when(moves)
    def _():
        pltpu.make_async_remote_copy(
            src_ref=src,
            dst_ref=dst,
            send_sem=send_sem,
            recv_sem=recv_sem,
            device_id=peer,
            device_id_type=MESH_IDS,
        ).wait()

    @pl.when(jnp.logical_not(moves))
    def _():
        pltpu.make_async_copy(src, dst, recv_sem).wait()


def greet(peers, turning=False):
    barrier = pltpu.get_barrier_semaphore()
    for peer in peers:
        pl.semaphore_signal(barrier, inc=1, device_id=peer, device_id_type=MESH_IDS)
    if not turning:
        pl.semaphore_wait(barrier, len(peers))
        return
    turn_peer, moves = turn_to()

    @pl.when(moves)
    def _():
        pl.semaphore_signal(barrier, inc=1, device_id=turn_peer, device_id_type=MESH_IDS)

    pl.semaphore_wait(barrier, len(peers) + moves.astype(jnp.int32))


def my_order(n_dp):
    return lax.axis_index("b") * n_dp + lax.axis_index("y") * 2 + lax.axis_index("core")


def swap_heads_kernel(sizes, in_ref, out_ref, send_sems, recv_sems, own_sem):
    n_dp, splits = sizes
    order = my_order(n_dp)
    group, split = lax.div(order, splits), lax.rem(order, splits)
    others = [lax.rem(group + k, GROUPS) for k in range(1, GROUPS)]
    peers = [holder(other * splits + split, n_dp) for other in others]
    greet(peers)
    copies = []
    for k in range(GROUPS - 1):
        copy = pltpu.make_async_remote_copy(
            src_ref=in_ref.at[others[k]],
            dst_ref=out_ref.at[group],
            send_sem=send_sems.at[k],
            recv_sem=recv_sems.at[k],
            device_id=peers[k],
            device_id_type=MESH_IDS,
        )
        copy.start()
        copies.append(copy)
    own = pltpu.make_async_copy(in_ref.at[group], out_ref.at[group], own_sem)
    own.start()
    own.wait()
    for copy in copies:
        copy.wait()


def share_grads_kernel(
    sizes,
    dq_ref,
    dkv_ref,
    low_ref,
    groups_ref,
    own_ref,
    turned_ref,
    landed,
    near_send,
    near_recv,
    send_sems,
    recv_sems,
    own_sem,
    turn_sems,
):
    n_dp, splits = sizes
    order = my_order(n_dp)
    group, split = lax.div(order, splits), lax.rem(order, splits)
    twins = [lax.rem(split + k, splits) for k in range(1, splits)]
    twin_ids = [holder(group * splits + other, n_dp) for other in twins]
    others = [lax.rem(group + k, GROUPS) for k in range(1, GROUPS)]
    peers = [holder(other * splits + split, n_dp) for other in others]
    greet(twin_ids + peers, True)
    turn_refs = (low_ref, turned_ref, turn_sems.at[0], turn_sems.at[1])
    start_turn(*turn_refs)
    near = []
    for k in range(splits - 1):
        copy = pltpu.make_async_remote_copy(
            src_ref=dkv_ref.at[twins[k]],
            dst_ref=landed.at[k],
            send_sem=near_send.at[k],
            recv_sem=near_recv.at[k],
            device_id=twin_ids[k],
            device_id_type=MESH_IDS,
        )
        copy.start()
        near.append(copy)
    groups_ref[:, 0] = dq_ref[...]
    for copy in near:
        copy.wait()
    for index in range(GROUPS):
        for kind in range(2):
            total = dkv_ref[split, index, kind].astype(F32)
            for k in range(splits - 1):
                total = total + landed[k, index, kind].astype(F32)
            groups_ref[index, kind + 1] = total.astype(BF16)
    copies = []
    for k in range(GROUPS - 1):
        copy = pltpu.make_async_remote_copy(
            src_ref=groups_ref.at[others[k]],
            dst_ref=own_ref.at[group],
            send_sem=send_sems.at[k],
            recv_sem=recv_sems.at[k],
            device_id=peers[k],
            device_id_type=MESH_IDS,
        )
        copy.start()
        copies.append(copy)
    own = pltpu.make_async_copy(groups_ref.at[group], own_ref.at[group], own_sem)
    own.start()
    own.wait()
    for copy in copies:
        copy.wait()
    finish_turn(*turn_refs)


def add_low(dst, src, rows):
    def one(i, carry):
        dst[i] = (dst[i].astype(F32) + src[i].astype(F32)).astype(BF16)
        return carry

    lax.fori_loop(0, rows, one, None)


def z_order_of(count):
    order = [0]
    for k in range(1, count):
        for far in (k, count - k):
            if far not in order:
                order.append(far)
    return order


def spread_kernel(
    sizes,
    own,
    pack,
    every,
    gathered,
    crossed,
    z_sems,
    xs_sems,
    ys_sems,
    xf_sems,
    yf_sems,
    near_sems,
    own_sem,
    by_sems,
    bz_sems,
    bx_sems,
    bn_sems,
    stay_sem,
):
    zn, xn, yn, slots, part = sizes
    rest = slots - part
    z, x = lax.axis_index("a"), lax.axis_index("b")
    y, core = lax.axis_index("y"), lax.axis_index("core")
    core_peer = {"core": 1 - core}
    xs, ys, z_order = range(1, xn), range(1, yn), z_order_of(zn)
    x_peers = {k: {"b": lax.rem(x + k, xn)} for k in xs}
    y_peers = {k: {"y": lax.rem(y + k, yn)} for k in ys}
    z_peers = {k: {"a": lax.rem(z + k, zn)} for k in range(1, zn)}
    greet([core_peer, *x_peers.values(), *y_peers.values(), *z_peers.values()])

    def remote(src, dst, sems, index, peer):
        return pltpu.make_async_remote_copy(
            src_ref=src,
            dst_ref=dst,
            send_sem=sems.at[0, index],
            recv_sem=sems.at[1, index],
            device_id=peer,
            device_id_type=MESH_IDS,
        )

    def number(jz, jx, jy):
        chip = (lax.rem(z + zn - jz, zn) * xn + lax.rem(x + xn - jx, xn)) * yn + lax.rem(
            y + yn - jy, yn
        )
        return chip * 2 + core

    def shard(jz, jx, jy, first=0, count=slots):
        return every.at[pl.ds(number(jz, jx, jy) * slots + first, count)]

    def held(jz, jx, jy):
        return own if (jz, jx, jy) == (0, 0, 0) else shard(jz, jx, jy)

    def z_copy(jz):
        return remote(own, shard(0, 0, 0), z_sems, jz - 1, z_peers[jz])

    def xs_copy(jz, jx):
        return remote(
            held(jz, 0, 0), shard(jz, 0, 0), xs_sems, jz * (xn - 1) + jx - 1, x_peers[jx]
        )

    def ys_copy(jz, jy):
        return remote(
            held(jz, 0, 0), shard(jz, 0, 0), ys_sems, jz * (yn - 1) + jy - 1, y_peers[jy]
        )

    def cross(jz, jx, jy):
        return (jz * (xn - 1) + jx - 1) * (yn - 1) + jy - 1

    def xf_copy(jz, jx, jy):
        view = shard(jz, 0, jy, part, rest)
        return remote(view, view, xf_sems, cross(jz, jx, jy), x_peers[jx])

    def yf_copy(jz, jx, jy):
        view = shard(jz, jx, 0, 0, part)
        return remote(view, view, yf_sems, cross(jz, jx, jy), y_peers[jy])

    def near_copy(jz, jx, jy):
        return remote(
            held(jz, jx, jy),
            shard(jz, jx, jy),
            near_sems,
            (jz * xn + jx) * yn + jy,
            core_peer,
        )

    started = []

    def launch(copy):
        copy.start()
        started.append(copy)

    def send_own(jz):
        for jx in xs:
            launch(xs_copy(jz, jx))
        for jy in ys:
            launch(ys_copy(jz, jy))
        launch(near_copy(jz, 0, 0))

    def forward(jz):
        for jy in ys:
            ys_copy_in(jz, jy)
            for jx in xs:
                launch(xf_copy(jz, jx, jy))
        for jx in xs:
            xs_copy_in(jz, jx)
            for jy in ys:
                launch(yf_copy(jz, jx, jy))
        for jy in ys:
            launch(near_copy(jz, 0, jy))
        for jx in xs:
            launch(near_copy(jz, jx, 0))

    def ys_copy_in(jz, jy):
        view = shard(jz, 0, jy)
        remote(view, view, ys_sems, jz * (yn - 1) + jy - 1, y_peers[jy]).wait_recv()

    def xs_copy_in(jz, jx):
        view = shard(jz, jx, 0)
        remote(view, view, xs_sems, jz * (xn - 1) + jx - 1, x_peers[jx]).wait_recv()

    def finish(jz):
        for jx in xs:
            for jy in ys:
                view = shard(jz, jx, jy, part, rest)
                remote(view, view, xf_sems, cross(jz, jx, jy), x_peers[jx]).wait_recv()
                view = shard(jz, jx, jy, 0, part)
                remote(view, view, yf_sems, cross(jz, jx, jy), y_peers[jy]).wait_recv()
                launch(near_copy(jz, jx, jy))

    def z_in(index):
        jz = z_order[index]
        view = shard(jz, 0, 0)
        remote(view, view, z_sems, jz - 1, z_peers[jz]).wait_recv()
        if index + 1 < zn:
            launch(z_copy(z_order[index + 1]))

    own_local = pltpu.make_async_copy(own, shard(0, 0, 0), own_sem)
    hosts = lax.rem(z, 2) == core

    def block(jz, jx=0):
        return gathered.at[lax.rem(x + xn - jx, xn) * zn + lax.rem(z + zn - jz, zn)]

    def by_copy(jy):
        return remote(pack, crossed.at[jy - 1], by_sems, jy - 1, y_peers[jy])

    def plane(jy):
        return lax.rem(y + yn - jy, yn) * 2 + core

    def bz_copy(jy):
        src = pack if jy == 0 else crossed.at[jy - 1]
        far = lax.rem(plane(jy) + zn - z, zn)
        return remote(src, block(0), bz_sems, far, {"a": plane(jy)})

    def stay_copy(jy):
        src = pack if jy == 0 else crossed.at[jy - 1]
        return pltpu.make_async_copy(src, block(0), stay_sem)

    def bx_copy(jz, jx):
        return remote(block(jz), block(jz), bx_sems, jz * (xn - 1) + jx - 1, x_peers[jx])

    def bn_copy(jz, jx):
        return remote(block(jz, jx), block(jz, jx), bn_sems, jz * xn + jx, core_peer)

    def blocks_to_planes():
        for jy in range(yn):
            if jy != 0:
                by_copy(jy).wait_recv()

            @pl.when(plane(jy) != z)
            def _():
                bz_copy(jy).start()

            @pl.when(plane(jy) == z)
            def _():
                stay_copy(jy).start()
                stay_copy(jy).wait()

    def blocks_across():
        @pl.when(hosts)
        def _():
            for jz in z_order:
                if jz != 0:
                    remote(block(jz), block(jz), bz_sems, jz, z_peers[jz]).wait_recv()
                for jx in xs:
                    bx_copy(jz, jx).start()
                bn_copy(jz, 0).start()

    def blocks_end():
        @pl.when(hosts)
        def _():
            for jz in z_order:
                for jx in xs:
                    view = block(jz, jx)
                    index = jz * (xn - 1) + jx - 1
                    remote(view, view, bx_sems, index, x_peers[jx]).wait_recv()
                    bn_copy(jz, jx).start()
            for jz in z_order:
                for jx in xs:
                    bx_copy(jz, jx).wait_send()
                for jx in range(xn):
                    bn_copy(jz, jx).wait_send()

        @pl.when(jnp.logical_not(hosts))
        def _():
            for jz in range(zn):
                for jx in range(xn):
                    bn_copy(jz, jx).wait_recv()

        for jy in range(yn):

            @pl.when(plane(jy) != z)
            def _():
                bz_copy(jy).wait_send()

    launch(z_copy(z_order[1]))
    send_own(0)

    own_local.start()
    for jy in ys:
        launch(by_copy(jy))

    for index in range(1, zn):
        z_in(index)
        send_own(z_order[index])
        forward(z_order[index - 1])
        if index >= 2:
            finish(z_order[index - 2])
    blocks_to_planes()
    forward(z_order[zn - 1])
    blocks_across()
    finish(z_order[zn - 2])
    finish(z_order[zn - 1])

    for jz in range(zn):
        for jx in range(xn):
            for jy in range(yn):
                chip = lax.div(number(jz, jx, jy), 2)
                view = every.at[pl.ds((chip * 2 + 1 - core) * slots, slots)]
                remote(
                    view, view, near_sems, (jz * xn + jx) * yn + jy, core_peer
                ).wait_recv()
    blocks_end()
    own_local.wait()
    for copy in started:
        copy.wait_send()


def reduce_kernel(
    sizes,
    grads,
    norm_in,
    tokens_in,
    total_out,
    norm_out,
    tokens_out,
    held,
    near,
    xd,
    yd,
    xs_in,
    ys_in,
    zs_in,
    norm_core,
    norm_y,
    norm_x,
    norm_z,
    norm_sum,
    load_sems,
    near_sems,
    xd_sems,
    yd_sems,
    xs_sems,
    ys_sems,
    zs_sems,
    norm_sems,
    turn_sems,
):
    zn, xn, yn, slots, part = sizes
    rest = slots - part
    z, x = lax.axis_index("a"), lax.axis_index("b")
    y, core = lax.axis_index("y"), lax.axis_index("core")
    core_peer = {"core": 1 - core}
    xs, ys = range(1, xn), range(1, yn)
    y_peers = [{"y": lax.rem(y + k, yn)} for k in ys]
    x_peers = [{"b": lax.rem(x + k, xn)} for k in xs]
    z_peers = [{"a": lax.rem(z + k, zn)} for k in range(1, zn)]
    greet([core_peer] + y_peers + x_peers + z_peers, True)
    turn_refs = (tokens_in, tokens_out, turn_sems.at[0], turn_sems.at[1])
    start_turn(*turn_refs)

    def remote(src, dst, sems, index, peer):
        return pltpu.make_async_remote_copy(
            src_ref=src,
            dst_ref=dst,
            send_sem=sems.at[0, index],
            recv_sem=sems.at[1, index],
            device_id=peer,
            device_id_type=MESH_IDS,
        )

    def flat(jz, jx, jy):
        return (jz * xn + jx) * yn + jy

    def chip_rows(jz, jx, jy, which):
        chip = (lax.rem(z + jz, zn) * xn + lax.rem(x + jx, xn)) * yn + lax.rem(y + jy, yn)
        return grads.at[pl.ds((chip * 2 + which) * slots, slots)]

    def near_copy(jz, jx, jy):
        index = flat(jz, jx, jy)
        return remote(chip_rows(jz, jx, jy, 1 - core), near.at[index], near_sems, index, core_peer)

    def load_copy(jz, jx, jy):
        index = flat(jz, jx, jy)
        return pltpu.make_async_copy(
            chip_rows(jz, jx, jy, core), held.at[index], load_sems.at[index]
        )

    def whole(jz, jx, jy):
        return held.at[flat(jz, jx, jy)]

    def first(jz, jx, jy):
        return held.at[flat(jz, jx, jy), pl.ds(0, part)]

    def second(jz, jx, jy):
        return held.at[flat(jz, jx, jy), pl.ds(part, rest)]

    def cross(jz, jx, jy):
        return (jz * (xn - 1) + jx - 1) * (yn - 1) + jy - 1

    def yd_copy(jz, jx, jy):
        index = cross(jz, jx, jy)
        return remote(first(jz, jx, jy), yd.at[index], yd_sems, index, y_peers[jy - 1])

    def xd_copy(jz, jx, jy):
        index = cross(jz, jx, jy)
        return remote(second(jz, jx, jy), xd.at[index], xd_sems, index, x_peers[jx - 1])

    def halves(low_half):
        return pl.ds(0, part) if low_half else pl.ds(part, rest)

    def xs_copy(jz, jx, low_half):
        index = jz * (xn - 1) + jx - 1
        return remote(
            held.at[flat(jz, jx, 0), halves(low_half)],
            xs_in.at[index, halves(low_half)],
            xs_sems,
            index * 2 + int(low_half),
            x_peers[jx - 1],
        )

    def ys_copy(jz, jy, low_half):
        index = jz * (yn - 1) + jy - 1
        return remote(
            held.at[flat(jz, 0, jy), halves(low_half)],
            ys_in.at[index, halves(low_half)],
            ys_sems,
            index * 2 + int(low_half),
            y_peers[jy - 1],
        )

    def zs_copy(jz):
        return remote(whole(jz, 0, 0), zs_in.at[jz - 1], zs_sems, jz - 1, z_peers[jz - 1])

    z_order = z_order_of(zn)[::-1]
    started = []

    def launch(copy):
        copy.start()
        started.append(copy)

    steps_done = []
    norm_count = [0]

    def norm_step(buffer, peers):
        copies = []
        for k, peer in enumerate(peers):
            index = norm_count[0]
            norm_count[0] += 1
            copy = remote(norm_sum.at[len(steps_done)], buffer.at[k], norm_sems, index, peer)
            copy.start()
            copies.append(copy)
        return copies

    def norm_finish(buffer, copies):
        total = norm_sum[len(steps_done)]
        for k, copy in enumerate(copies):
            copy.wait()
            total = total + buffer[k]
        steps_done.append(None)
        norm_sum[len(steps_done)] = total

    def plane(jz):
        return (
            [(jz, jx, jy) for jx in xs for jy in ys]
            + [(jz, jx, 0) for jx in xs]
            + [(jz, 0, jy) for jy in ys]
            + [(jz, 0, 0)]
        )

    def fetch(jz):
        for chip in plane(jz):
            launch(near_copy(*chip))
            load_copy(*chip).start()

    def prepare(index):
        for chip in plane(z_order[index]):
            load_copy(*chip).wait()
            near_copy(*chip).wait_recv()
            add_low(whole(*chip), near.at[flat(*chip)], slots)
        if index + 1 < zn:
            fetch(z_order[index + 1])

    stages = [(index, stage) for index in range(zn) for stage in range(3)]

    def send_stage(number):
        index, stage = stages[number]
        jz = z_order[index]
        for jx in xs:
            if stage == 0:
                for jy in ys:
                    launch(xd_copy(jz, jx, jy))
            else:
                launch(xs_copy(jz, jx, stage == 2))
        for jy in ys:
            if stage == 0:
                for jx in xs:
                    launch(yd_copy(jz, jx, jy))
            else:
                launch(ys_copy(jz, jy, stage == 1))

    def take_stage(number):
        index, stage = stages[number]
        jz = z_order[index]
        if stage == 0:
            for jx in xs:
                for jy in ys:
                    yd_copy(jz, jx, jy).wait_recv()
                    add_low(first(jz, jx, 0), yd.at[cross(jz, jx, jy)], part)
                    xd_copy(jz, jx, jy).wait_recv()
                    add_low(second(jz, 0, jy), xd.at[cross(jz, jx, jy)], rest)
        else:
            for jx in xs:
                xs_copy(jz, jx, stage == 2).wait_recv()
            for jy in ys:
                ys_copy(jz, jy, stage == 1).wait_recv()

    def side_in(index):
        jz = z_order[index]

        def one(i, carry):
            total = held[flat(jz, 0, 0), i].astype(F32)
            for jx in xs:
                total = total + xs_in[jz * (xn - 1) + jx - 1, i].astype(F32)
            for jy in ys:
                total = total + ys_in[jz * (yn - 1) + jy - 1, i].astype(F32)
            if jz != 0:
                held[flat(jz, 0, 0), i] = total.astype(BF16)
            else:
                total_out[i] = total
            return carry

        lax.fori_loop(0, slots, one, None)
        if jz != 0:
            launch(zs_copy(jz))

    norm_sum[0] = norm_in[...]
    rounds = [(norm_core, [core_peer]), (norm_y, y_peers), (norm_x, x_peers), (norm_z, z_peers)]
    fetch(z_order[0])
    pending = norm_step(*rounds[0])
    prepare(0)
    prepared, ahead = 1, 2
    for number in range(ahead):
        send_stage(number)
    for number in range(len(stages)):
        take_stage(number)
        later = number + ahead
        if later < len(stages):
            if stages[later][0] >= prepared:
                prepare(prepared)
                prepared += 1
            send_stage(later)
        if stages[number][1] == 2:
            side_in(stages[number][0])
        if number % 3 == 2 and len(steps_done) < 3:
            norm_finish(rounds[len(steps_done)][0], pending)
            pending = norm_step(*rounds[len(steps_done)])
    while len(steps_done) < 3:
        norm_finish(rounds[len(steps_done)][0], pending)
        pending = norm_step(*rounds[len(steps_done)])
    norm_finish(norm_z, pending)
    norm_out[...] = norm_sum[4]
    for jz in range(1, zn):
        zs_copy(jz).wait_recv()

    def last(i, carry):
        total = total_out[i]
        for jz in range(1, zn):
            total = total + zs_in[jz - 1, i].astype(F32)
        total_out[i] = total
        return carry

    lax.fori_loop(0, slots, last, None)
    finish_turn(*turn_refs)
    for copy in started:
        copy.wait_send()


def vmem():
    return pl.BlockSpec(memory_space=pltpu.VMEM)


def smem():
    return pl.BlockSpec(memory_space=pltpu.SMEM)


def anywhere():
    return pl.BlockSpec(memory_space=pl.ANY)


def shape_of(dims, kind):
    return jax.ShapeDtypeStruct(dims, kind)


def params(collective=None):
    if collective is None:
        return pltpu.CompilerParams(vmem_limit_bytes=VMEM_LIMIT)
    return pltpu.CompilerParams(
        vmem_limit_bytes=VMEM_LIMIT, collective_id=collective, has_side_effects=True
    )


def swap_heads(block, n_dp, splits, collective):
    return pl.pallas_call(
        functools.partial(swap_heads_kernel, (n_dp, splits)),
        out_shape=shape_of(block.shape, BF16),
        in_specs=[vmem()],
        out_specs=vmem(),
        scratch_shapes=[
            pltpu.SemaphoreType.DMA((GROUPS - 1,)),
            pltpu.SemaphoreType.DMA((GROUPS - 1,)),
            pltpu.SemaphoreType.DMA,
        ],
        compiler_params=params(collective),
    )(block)


def per_device(
    dims,
    layer_input,
    out_cotangent,
    segment_ids,
    piece_owner,
    weight_master,
    weight_first,
    weight_second,
    norm_params,
    norm_first,
    norm_second,
):
    n_seq, n_dp = dims
    reps = n_seq // n_dp
    splits = n_seq // GROUPS
    slots, piece, width = weight_master.shape
    pieces = piece_owner.shape[0]
    tok = layer_input.shape[1]
    length = tok * n_seq
    hidden_units = (pieces * piece - 4 * width) // 3
    head = width // HEADS
    kind_pieces = width // piece
    hidden_pieces = hidden_units // piece
    chunk = hidden_units // CHUNKS

    location = locate_pieces(piece_owner, slots)
    own_low = weight_master.astype(BF16)
    seg_row = jnp.zeros((16, width), BF16).at[0, :tok].set(segment_ids[0].astype(BF16))
    pack = jnp.concatenate([layer_input[0], seg_row], axis=0)
    turn = [(i * n_dp + j, j * n_dp + i) for i in range(n_dp) for j in range(n_dp)]
    turn_axes = ("a", "y", "core")

    zn, xn, yn = n_dp, reps, n_dp // 2
    n_chips = zn * xn * yn

    def pair(count):
        return pltpu.SemaphoreType.DMA((2, max(count, 1)))

    half = slots // 2
    split_rows = slots * 9 // 16
    weights, gathered, _ = pl.pallas_call(
        functools.partial(spread_kernel, (zn, xn, yn, slots, split_rows)),
        out_shape=(
            shape_of((n_chips * 2 * slots, piece, width), BF16),
            shape_of((n_seq, tok + 16, width), BF16),
            shape_of((max(yn - 1, 1), tok + 16, width), BF16),
        ),
        in_specs=[anywhere(), anywhere()],
        out_specs=(anywhere(),) * 3,
        scratch_shapes=[
            pair(zn - 1),
            pair(zn * (xn - 1)),
            pair(zn * (yn - 1)),
            pair(zn * (xn - 1) * (yn - 1)),
            pair(zn * (xn - 1) * (yn - 1)),
            pair(n_chips),
            pltpu.SemaphoreType.DMA,
            pair(yn - 1),
            pair(zn),
            pair(zn * (xn - 1)),
            pair(zn * xn),
            pltpu.SemaphoreType.DMA,
        ],
        compiler_params=params(5),
    )(own_low, pack)
    weights, cotangent = lax.optimization_barrier((weights, out_cotangent[0]))
    cotangent = lax.ppermute(cotangent, turn_axes, turn)

    core = lax.axis_index("core")
    order = my_order(n_dp)
    group, split = order // splits, order % splits
    info = jnp.stack([core, group, split]).astype(jnp.int32)
    tokens = lax.dynamic_index_in_dim(gathered, order, axis=0, keepdims=False)[:tok]
    slopes = head_slopes(HEADS, tok, n_seq)

    segs = gathered[:, tok, :tok]
    lanes = jnp.arange(128, dtype=jnp.int32)[None, :] - head
    key_same = segs.reshape(length, 1).astype(jnp.int32) == lanes
    key_marks = jnp.where(key_same | (lanes < 0) | (lanes > 2), 0.0, MASKED).astype(BF16)
    query_segs = lax.dynamic_index_in_dim(
        segs.reshape(GROUPS, splits, tok), split, axis=1, keepdims=False
    )
    query_marks = (query_segs.reshape(GROUPS * tok, 1).astype(jnp.int32) == lanes).astype(BF16)

    attend_sizes = (n_dp, reps, splits, tok, head, n_seq)
    q_ext, k_ext, k_turned, v_rows, mixed_low, mixed_full, log_total = pl.pallas_call(
        functools.partial(attend_forward_kernel, attend_sizes),
        out_shape=(
            shape_of((TRIO, GROUPS * tok, 128), BF16),
            shape_of((TRIO, length, 128), BF16),
            shape_of((TRIO, head, length), BF16),
            shape_of((TRIO, length, head), BF16),
            shape_of((GROUPS, TRIO, head, tok), BF16),
            shape_of((GROUPS, TRIO, head, tok), F32),
            shape_of((GROUPS, TRIO, 1, tok), F32),
        ),
        in_specs=[smem(), smem(), smem(), vmem(), vmem(), vmem(), anywhere()],
        out_specs=(vmem(),) * 7,
        scratch_shapes=[
            pltpu.VMEM((3 * TRIO, 128, width), BF16),
            pltpu.VMEM((TRIO, head, length), BF16),
            pltpu.VMEM((3 * TRIO, tok, tok), F32),
            pltpu.VMEM((n_seq, tok, tok), F32),
            pltpu.SemaphoreType.DMA((3 * TRIO * (head // piece),)),
        ],
        compiler_params=params(),
    )(location, info, slopes, gathered, query_marks, key_marks, weights)

    mixed_own = swap_heads(mixed_low.reshape(GROUPS, TRIO * head, tok), n_dp, splits, 1)

    out_low, d_pre_one, d_mixed, norm_part, grads = pl.pallas_call(
        functools.partial(
            dense_kernel, (tok, piece, kind_pieces, chunk // piece, hidden_pieces)
        ),
        out_shape=(
            shape_of((tok, width), BF16),
            shape_of((tok, width), F32),
            shape_of((width, tok), BF16),
            shape_of((8, width), F32),
            shape_of((n_seq * n_dp * slots, piece, width), BF16),
        ),
        in_specs=[smem(), vmem(), vmem(), vmem(), vmem(), anywhere()],
        out_specs=(vmem(), vmem(), vmem(), vmem(), anywhere()),
        scratch_shapes=[
            pltpu.VMEM((width, width), BF16),
            pltpu.VMEM((CHUNKS, chunk, width), BF16),
            pltpu.VMEM((CHUNKS, chunk, width), BF16),
            pltpu.VMEM((CHUNKS, chunk, width), BF16),
            pltpu.VMEM((CHUNKS, tok, chunk), F32),
            pltpu.VMEM((CHUNKS, tok, chunk), F32),
            pltpu.VMEM((CHUNKS, tok, chunk), BF16),
            pltpu.VMEM((2, 3, chunk, width), BF16),
            pltpu.VMEM((width, width), BF16),
            pltpu.SemaphoreType.DMA((3 * CHUNKS + 1,)),
            pltpu.SemaphoreType.DMA((7,)),
        ],
        compiler_params=params(),
    )(
        location,
        tokens,
        cotangent,
        mixed_own.reshape(width, tok),
        norm_params,
        weights,
    )

    d_mixed_own = swap_heads(d_mixed.reshape(GROUPS, TRIO * head, tok), n_dp, splits, 2)

    d_query, d_key_value = pl.pallas_call(
        functools.partial(attend_backward_kernel, attend_sizes),
        out_shape=(
            shape_of((GROUPS, TRIO, head, tok), BF16),
            shape_of((splits, GROUPS, 2, TRIO, head, tok), BF16),
        ),
        in_specs=[smem(), smem()] + [vmem()] * 7,
        out_specs=(vmem(), vmem()),
        scratch_shapes=[
            pltpu.VMEM((TRIO, head, length), F32),
            pltpu.VMEM((TRIO, head, length), F32),
            pltpu.VMEM((3 * TRIO, tok, tok), F32),
        ],
        compiler_params=params(),
    )(
        info,
        slopes,
        q_ext,
        k_ext,
        k_turned,
        v_rows,
        mixed_full,
        log_total,
        d_mixed_own.reshape(GROUPS, TRIO, head, tok),
    )

    trio_rows = TRIO * head
    d_groups, d_own, result = pl.pallas_call(
        functools.partial(share_grads_kernel, (n_dp, splits)),
        out_shape=(
            shape_of((GROUPS, 3, trio_rows, tok), BF16),
            shape_of((GROUPS, 3, trio_rows, tok), BF16),
            shape_of(out_low.shape, BF16),
        ),
        in_specs=[vmem(), vmem(), anywhere()],
        out_specs=(vmem(), vmem(), anywhere()),
        scratch_shapes=[
            pltpu.VMEM((splits - 1, GROUPS, 2, trio_rows, tok), BF16),
            pltpu.SemaphoreType.DMA((splits - 1,)),
            pltpu.SemaphoreType.DMA((splits - 1,)),
            pltpu.SemaphoreType.DMA((GROUPS - 1,)),
            pltpu.SemaphoreType.DMA((GROUPS - 1,)),
            pltpu.SemaphoreType.DMA,
            pltpu.SemaphoreType.DMA((2,)),
        ],
        compiler_params=params(3),
    )(
        d_query.reshape(GROUPS, trio_rows, tok),
        d_key_value.reshape(splits, GROUPS, 2, trio_rows, tok),
        out_low,
    )

    d_tokens, grads = pl.pallas_call(
        functools.partial(project_grad_kernel, (piece, kind_pieces, splits, tok)),
        out_shape=(shape_of((tok, width), BF16), shape_of(grads.shape, BF16)),
        in_specs=[smem(), smem(), vmem(), vmem(), vmem(), vmem()] + [anywhere()] * 2,
        out_specs=(vmem(), anywhere()),
        scratch_shapes=[
            pltpu.VMEM((3 * width, width), BF16),
            pltpu.VMEM((3 * trio_rows, width), BF16),
            pltpu.VMEM(((GROUPS - 1) * 3 * trio_rows, width), BF16),
            pltpu.SemaphoreType.DMA,
            pltpu.SemaphoreType.DMA,
            pltpu.SemaphoreType.DMA,
        ],
        input_output_aliases={7: 1},
        compiler_params=params(),
    )(
        location,
        info,
        gathered,
        d_groups.reshape(GROUPS, 3 * trio_rows, tok),
        d_own.reshape(3 * width, tok),
        d_pre_one,
        weights,
        grads,
    )

    def chunks(count, rows):
        return pltpu.VMEM((max(count, 1), rows, piece, width), BF16)

    def norm_rows(count):
        return pltpu.VMEM((max(count, 1), 8, width), F32)

    crossing = zn * (xn - 1) * (yn - 1)
    own_grad, norm_total, d_turned = pl.pallas_call(
        functools.partial(reduce_kernel, (zn, xn, yn, slots, half)),
        out_shape=(
            shape_of((slots, piece, width), F32),
            shape_of((8, width), F32),
            shape_of(d_tokens.shape, BF16),
        ),
        in_specs=[anywhere(), vmem(), anywhere()],
        out_specs=(vmem(), vmem(), anywhere()),
        scratch_shapes=[
            chunks(n_chips, slots),
            chunks(n_chips, slots),
            chunks(crossing, slots - half),
            chunks(crossing, half),
            chunks(zn * (xn - 1), slots),
            chunks(zn * (yn - 1), slots),
            chunks(zn - 1, slots),
            norm_rows(1),
            norm_rows(yn - 1),
            norm_rows(xn - 1),
            norm_rows(zn - 1),
            norm_rows(5),
            pltpu.SemaphoreType.DMA((n_chips,)),
            pair(n_chips),
            pair(crossing),
            pair(crossing),
            pair(2 * zn * (xn - 1)),
            pair(2 * zn * (yn - 1)),
            pair(zn - 1),
            pair(1 + (yn - 1) + (xn - 1) + (zn - 1)),
            pltpu.SemaphoreType.DMA((2,)),
        ],
        compiler_params=params(4),
    )(grads, norm_part, d_tokens)
    d_input = d_turned.astype(F32)

    numbers = jnp.arange(pieces, dtype=jnp.int32) + 1
    own_slots = lax.axis_index(("a", "b", "y", "core")) * slots + jnp.arange(slots)
    inverse = jnp.sum(jnp.where(location[None, :] == own_slots[:, None], numbers[None, :], 0), axis=1)
    own_grad = jnp.where((inverse > 0)[:, None, None], own_grad, 0.0)
    norm_grad = norm_total[:4]
    rates = slot_rates(inverse, piece, width, hidden_units)
    first_new, second_new, weight_new = adamw_step(
        weight_master, weight_first, weight_second, own_grad, rates[:, None, None], STEP
    )
    norm_first_new, norm_second_new, norm_new = adamw_step(
        norm_params, norm_first, norm_second, norm_grad, NORM_RATE, STEP
    )
    return (
        result[None],
        d_input[None],
        own_grad,
        first_new,
        second_new,
        weight_new,
        weight_new.astype(BF16),
        norm_grad,
        norm_first_new,
        norm_second_new,
        norm_new,
    )


def solution(mesh):
    n_seq, n_dp = mesh.shape["seq"], mesh.shape["dp"]
    inner = Mesh(
        mesh.devices.reshape(n_dp, n_seq // n_dp, n_dp // 2, 2), ("a", "b", "y", "core")
    )
    seq, dp, every = ("a", "b"), ("y", "core"), ("a", "b", "y", "core")
    block = P(dp, seq, None)
    owned = P(every, None, None)
    in_specs = (block, block, P(dp, seq), P(), owned, owned, owned, P(), P(), P())
    out_specs = (block, block, owned, owned, owned, owned, owned, P(), P(), P(), P())
    return jax.shard_map(
        functools.partial(per_device, (n_seq, n_dp)),
        mesh=inner,
        in_specs=in_specs,
        out_specs=out_specs,
        check_vma=False,
    )
```

```python
import functools

import jax
import jax.numpy as jnp
from jax import lax
from jax.experimental import pallas as pl
from jax.experimental.pallas import tpu as pltpu
from jax.sharding import Mesh
from jax.sharding import PartitionSpec as P

HEADS = 12
GROUPS = 4
TRIO = HEADS // GROUPS
STEP = 4

NORM_EPS = 1e-06
BETA_ONE = 0.5
BETA_TWO = 0.5
DECAY = 0.01
ADAM_EPS = 1e-08
NORM_RATE = 0.3
OUT_RATE = 0.35
MASKED = -1e30
CHUNKS = 6
VMEM_LIMIT = 60 * 1024 * 1024
MESH_IDS = pl.DeviceIdType.MESH
F32 = jnp.float32
BF16 = jnp.bfloat16


def head_slopes(head_count, tok_rows, seq_devices):
    head_order = jnp.arange(head_count, dtype=jnp.float32)
    return (
        8.0 / tok_rows * jnp.power(jnp.float32(8.0 * seq_devices), -head_order / (head_count - 1))
    )


def locate_pieces(owners, slot_count):
    pieces = owners.shape[0]
    numbers = jnp.arange(pieces, dtype=jnp.int32)
    earlier = (owners[None, :] == owners[:, None]) & (numbers[None, :] < numbers[:, None])
    return owners * slot_count + jnp.sum(earlier.astype(jnp.int32), axis=1)


def slot_rates(inverse, piece_rows, model_width, hidden_units):
    first_row = (inverse - 1) * piece_rows
    narrow = model_width ** (-0.5)
    step_rate = jnp.where(
        first_row < 3 * model_width,
        narrow,
        jnp.where(
            first_row < 4 * model_width,
            OUT_RATE,
            jnp.where(
                first_row < 4 * model_width + 2 * hidden_units, narrow, hidden_units ** (-0.5)
            ),
        ),
    )
    return jnp.where(inverse > 0, step_rate, narrow).astype(jnp.float32)


def adamw_step(weight, first_moment, second, gradient, step_rate, step_count):
    first_moment = BETA_ONE * first_moment + (1.0 - BETA_ONE) * gradient
    second = BETA_TWO * second + (1.0 - BETA_TWO) * gradient * gradient
    mean_hat = first_moment / (1.0 - BETA_ONE**step_count)
    square_hat = second / (1.0 - BETA_TWO**step_count)
    weight = weight - step_rate * (mean_hat / (jnp.sqrt(square_hat) + ADAM_EPS) + DECAY * weight)
    return (first_moment, second, weight)


def dot_nt(left_side, right_side):
    return lax.dot_general(
        left_side, right_side, (((1,), (1,)), ((), ())), preferred_element_type=F32
    )


def dot_nn(left_side, right_side):
    return lax.dot_general(
        left_side, right_side, (((1,), (0,)), ((), ())), preferred_element_type=F32
    )


def dot_tn(left_side, right_side):
    return lax.dot_general(
        left_side, right_side, (((0,), (0,)), ((), ())), preferred_element_type=F32
    )


def fetch_piece(place, piece, weights, dst, sem):
    pltpu.make_async_copy(weights.at[place[piece]], dst, sem).start()


def fill_tables(table, slopes, group, tok):
    apart = lax.broadcasted_iota(jnp.int32, (tok, tok), 0) - lax.broadcasted_iota(
        jnp.int32, (tok, tok), 1
    )
    apart = apart.astype(F32)
    for h in range(TRIO):
        slope = slopes[group * TRIO + h]
        table[h * 3 + 0] = -slope * apart
        table[h * 3 + 1] = slope * jnp.abs(apart)
        table[h * 3 + 2] = slope * apart


def block_place(order, n_dp, reps):
    return (order % n_dp) * reps + order // n_dp


def bias_of(key_block, query_place, slope, h, tok, n_dp, reps):
    key_place = block_place(key_block, n_dp, reps)
    which = jnp.where(key_place > query_place, 2, jnp.where(key_place < query_place, 0, 1))
    shift = slope * (tok * jnp.abs(key_place - query_place)).astype(F32)
    return h * 3 + which, shift


def attend_forward_kernel(
    sizes,
    place,
    info,
    slopes,
    x_ref,
    query_marks,
    key_marks,
    weights,
    q_out,
    k_out,
    kt_out,
    v_out,
    mixed_low,
    mixed_full,
    log_out,
    wpad,
    vt,
    table,
    scores,
    sems,
):
    n_dp, reps, splits, tok, head, blocks = sizes
    group, split = info[1], info[2]
    per_head = head // 16
    width = x_ref.shape[2]
    kind_pieces = width // 16

    def start(step, carry):
        kind = lax.div(step, TRIO * per_head)
        rest = lax.rem(step, TRIO * per_head)
        number = kind * kind_pieces + group * (TRIO * per_head) + rest
        dst = wpad.at[
            kind * TRIO + lax.div(rest, per_head), pl.ds(lax.rem(rest, per_head) * 16, 16)
        ]
        fetch_piece(place, number, weights, dst, sems.at[step])
        return carry

    def finish(step, carry):
        kind = lax.div(step, TRIO * per_head)
        rest = lax.rem(step, TRIO * per_head)
        dst = wpad.at[
            kind * TRIO + lax.div(rest, per_head), pl.ds(lax.rem(rest, per_head) * 16, 16)
        ]
        pltpu.make_async_copy(weights.at[0], dst, sems.at[step]).wait()
        return carry

    lax.fori_loop(0, 3 * TRIO * per_head, start, None, unroll=6)
    for row in range(3 * TRIO):
        wpad[row, head:, :] = jnp.zeros((wpad.shape[1] - head, width), BF16)
    fill_tables(table, slopes, group, tok)
    lax.fori_loop(0, 3 * TRIO * per_head, finish, None)

    w_query = wpad[0:TRIO].reshape(TRIO * 128, width)
    w_key = wpad[TRIO : 2 * TRIO].reshape(TRIO * 128, width)
    w_value = wpad[2 * TRIO : 3 * TRIO].reshape(TRIO * 128, width)

    def project(block, carry):
        rows = pl.ds(pl.multiple_of(block * tok, tok), tok)
        xb = x_ref[block, 0:tok, :]
        keys = dot_nt(xb, w_key)
        values = dot_nt(xb, w_value)
        marks = key_marks[rows, :]
        for h in range(TRIO):
            key = keys[:, h * 128 : (h + 1) * 128]
            value = values[:, h * 128 : (h + 1) * 128]
            k_out[h, rows, :] = key.astype(BF16) + marks
            v_out[h, rows, :] = value[:, 0:head].astype(BF16)
            kt_out[h, :, rows] = key.T[0:head].astype(BF16)
            vt[h, :, rows] = value.T[0:head].astype(BF16)
        return carry

    lax.fori_loop(0, blocks, project, None)

    def project_query(index, carry):
        rows = pl.ds(pl.multiple_of(index * tok, tok), tok)
        xb = x_ref[index * splits + split, 0:tok, :]
        queries = dot_nt(xb, w_query).astype(BF16) * jnp.asarray(head**-0.5, BF16)
        marks = query_marks[rows, :]
        for h in range(TRIO):
            q_out[h, rows, :] = queries[:, h * 128 : (h + 1) * 128] + marks
        return carry

    lax.fori_loop(0, GROUPS, project_query, None)

    def attend(step, carry):
        index, h = lax.div(step, TRIO), lax.rem(step, TRIO)
        order = index * splits + split
        query_place = lax.rem(order, n_dp) * reps + lax.div(order, n_dp)
        slope = slopes[group * TRIO + h]
        qh = q_out[h, pl.ds(pl.multiple_of(index * tok, tok), tok), :]
        top = None
        shifts = []
        for kb in range(blocks):
            which, shift = bias_of(kb, query_place, slope, h, tok, n_dp, reps)
            now = dot_nt(k_out[h, kb * tok : (kb + 1) * tok, :], qh) - table[which]
            scores[kb] = now
            here = jnp.max(now, axis=0, keepdims=True) - shift
            top = here if top is None else jnp.maximum(top, here)
            shifts.append(shift)
        total = jnp.zeros((1, tok), F32)
        for kb in range(blocks):
            grown = jnp.exp(scores[kb] - (top + shifts[kb]))
            total = total + jnp.sum(grown, axis=0, keepdims=True)
            scores[kb] = grown
        inverse = 1.0 / total
        mixed = jnp.zeros((head, tok), F32)
        for kb in range(blocks):
            prob = (scores[kb] * inverse).astype(BF16)
            mixed = mixed + dot_nn(vt[h, :, kb * tok : (kb + 1) * tok], prob)
        mixed_full[index, h] = mixed
        mixed_low[index, h] = mixed.astype(BF16)
        log_out[index, h] = top + jnp.log(total)
        return carry

    lax.fori_loop(0, GROUPS * TRIO, attend, None)


def attend_backward_kernel(
    sizes,
    slopes,
    q_ref,
    k_ref,
    kt_ref,
    v_ref,
    mixed_full,
    log_in,
    d_mixed,
    own_ref,
    dk_sum,
    dv_sum,
    table,
    d_blocks,
    shared,
    pairs,
    landed,
    swap_sems,
    query_sems,
    pair_sems,
    value_sems,
):
    n_dp, reps, splits, tok, head, blocks = sizes
    order = my_order(n_dp)
    group, split = lax.div(order, splits), lax.rem(order, splits)
    twins = [lax.rem(split + k, splits) for k in range(1, splits)]
    twin_ids = [holder(group * splits + other, n_dp) for other in twins]
    others = [lax.rem(group + k, GROUPS) for k in range(1, GROUPS)]
    peers = [holder(other * splits + split, n_dp) for other in others]
    greet(twin_ids + peers)

    def remote(src, dst, sems, index, peer):
        return pltpu.make_async_remote_copy(
            src_ref=src,
            dst_ref=dst,
            send_sem=sems.at[0, index],
            recv_sem=sems.at[1, index],
            device_id=peer,
            device_id_type=MESH_IDS,
        )

    started = []

    def launch(copy):
        copy.start()
        started.append(copy)

    for k in range(GROUPS - 1):
        launch(remote(d_mixed.at[others[k]], d_blocks.at[group], swap_sems, k, peers[k]))
    d_blocks[group] = d_mixed[group]
    fill_tables(table, slopes, group, tok)
    dk_sum[...] = jnp.zeros_like(dk_sum)
    dv_sum[...] = jnp.zeros_like(dv_sum)

    def step_fn(h, step):
        index = lax.rem(group + GROUPS - step, GROUPS)
        if h == 0:

            @pl.when(step > 0)
            def _():
                view = d_blocks.at[index]
                remote(view, view, swap_sems, step - 1, peers[0]).wait_recv()

        place_order = index * splits + split
        query_place = lax.rem(place_order, n_dp) * reps + lax.div(place_order, n_dp)
        slope = slopes[group * TRIO + h]
        qh = q_ref[h, pl.ds(pl.multiple_of(index * tok, tok), tok), :]
        dt = d_blocks[index, h]
        row_dot = jnp.sum(dt.astype(F32) * mixed_full[index, h], axis=0, keepdims=True)
        log_total = log_in[index, h]
        dq = jnp.zeros((head, tok), F32)
        for kb in range(blocks):
            rows = slice(kb * tok, (kb + 1) * tok)
            which, shift = bias_of(kb, query_place, slope, h, tok, n_dp, reps)
            now = dot_nt(k_ref[h, rows, :], qh) - table[which]
            prob = jnp.exp(now - (log_total + shift))
            d_prob = dot_nn(v_ref[h, rows, :], dt)
            d_score = (prob * (d_prob - row_dot)).astype(BF16)
            dv_sum[rows, :] += dot_nt(prob.astype(BF16), dt)
            dk_sum[rows, :] += dot_nn(d_score, qh)
            dq = dq + dot_nn(kt_ref[h, :, rows], d_score)
        shared[index, 0, h] = (dq * (head**-0.5)).astype(BF16)

    def pair_copy(h, k):
        return remote(
            pairs.at[h, twins[k]], landed.at[h, k], pair_sems, h * (splits - 1) + k, twin_ids[k]
        )

    def take_pairs(h):
        for k in range(splits - 1):
            pair_copy(h, k).wait_recv()
        for index in range(GROUPS):
            for kind in range(2):
                total = pairs[h, split, index, kind].astype(F32)
                for k in range(splits - 1):
                    total = total + landed[h, k, index, kind].astype(F32)
                shared[index, kind + 1, h] = total.astype(BF16)
        for k in range(GROUPS - 1):
            launch(
                remote(
                    shared.at[others[k], pl.ds(1, 2), h],
                    own_ref.at[group, pl.ds(1, 2), h],
                    value_sems,
                    h * (GROUPS - 1) + k,
                    peers[k],
                )
            )

    for h in range(TRIO):

        def one(step, carry, h=h):
            step_fn(h, step)
            return carry

        lax.fori_loop(0, GROUPS, one, None)
        for k in range(GROUPS - 1):
            launch(
                remote(
                    shared.at[others[k], 0, h],
                    own_ref.at[group, 0, h],
                    query_sems,
                    h * (GROUPS - 1) + k,
                    peers[k],
                )
            )

        def flip(index, carry, h=h):
            for part in range(splits):
                rows = pl.ds(pl.multiple_of((index * splits + part) * tok, tok), tok)
                pairs[h, part, index, 0] = dk_sum[rows, :].T[0:head].astype(BF16)
                pairs[h, part, index, 1] = dv_sum[rows, :].T.astype(BF16)
            return carry

        lax.fori_loop(0, GROUPS, flip, None)
        if h + 1 < TRIO:
            dk_sum[...] = jnp.zeros_like(dk_sum)
            dv_sum[...] = jnp.zeros_like(dv_sum)
        for k in range(splits - 1):
            launch(pair_copy(h, k))
        if h > 0:
            take_pairs(h - 1)
    take_pairs(TRIO - 1)
    own_ref[group] = shared[group]
    for h in range(TRIO):
        for k in range(GROUPS - 1):
            view = own_ref.at[others[k], 0, h]
            remote(view, view, query_sems, h * (GROUPS - 1) + k, peers[k]).wait_recv()
            view = own_ref.at[others[k], pl.ds(1, 2), h]
            remote(view, view, value_sems, h * (GROUPS - 1) + k, peers[k]).wait_recv()
    for copy in started:
        copy.wait_send()


def norm_stats(values_in):
    mean = jnp.mean(values_in, axis=-1, keepdims=True)
    centred = values_in - mean
    spread = jnp.mean(centred * centred, axis=-1, keepdims=True)
    scale = lax.rsqrt(spread + NORM_EPS)
    return centred * scale, scale


def norm_back(unit, scale, gain, cotangent):
    d_unit = cotangent * gain
    first = jnp.mean(d_unit, axis=-1, keepdims=True)
    second = jnp.mean(d_unit * unit, axis=-1, keepdims=True)
    d_in = scale * (d_unit - first - unit * second)
    d_gain = jnp.sum(cotangent * unit, axis=0, keepdims=True)
    d_bias = jnp.sum(cotangent, axis=0, keepdims=True)
    return d_in, d_gain, d_bias


def dense_kernel(
    sizes,
    place,
    x_ref,
    cot_ref,
    mixed_ref,
    norm_ref,
    weights,
    out_ref,
    d_pre_one_ref,
    d_mixed_ref,
    norm_grad,
    grads,
    w_out,
    w_gate,
    w_up,
    w_down,
    keep_gate,
    keep_up,
    keep_hidden,
    stage,
    stage_out,
    load_sems,
    store_sems,
):
    tok, piece, kind_pieces, chunk_pieces, hidden_pieces = sizes
    first_gate = 4 * kind_pieces
    first_up = first_gate + hidden_pieces
    first_down = first_up + hidden_pieces
    bases = (first_gate, first_up, first_down)
    buffers = (w_gate, w_up, w_down)
    chunk = chunk_pieces * piece

    def load_out(step, carry):
        fetch_piece(
            place,
            3 * kind_pieces + step,
            weights,
            w_out.at[pl.ds(step * piece, piece)],
            load_sems.at[3 * CHUNKS],
        )
        return carry

    def load_chunk(c):
        def one(step, carry):
            for kind in range(3):
                fetch_piece(
                    place,
                    bases[kind] + c * chunk_pieces + step,
                    weights,
                    buffers[kind].at[c, pl.ds(step * piece, piece)],
                    load_sems.at[kind * CHUNKS + c],
                )
            return carry

        lax.fori_loop(0, chunk_pieces, one, None, unroll=4)

    def wait_chunk(c):
        for kind in range(3):
            view = buffers[kind].at[c]
            pltpu.make_async_copy(view, view, load_sems.at[kind * CHUNKS + c]).wait()

    lax.fori_loop(0, kind_pieces, load_out, None, unroll=8)
    load_chunk(0)
    load_chunk(1)
    mixed = mixed_ref[...].T
    pltpu.make_async_copy(w_out, w_out, load_sems.at[3 * CHUNKS]).wait()
    pre_one = x_ref[...].astype(F32) + dot_nt(mixed, w_out[...])
    unit_one, scale_one = norm_stats(pre_one)
    h_one = unit_one * norm_ref[0:1, :] + norm_ref[1:2, :]
    h_low = h_one.astype(BF16)

    def forward(c, pre_two):
        @pl.when(c + 2 < CHUNKS)
        def _():
            load_chunk(c + 2)

        wait_chunk(c)
        gate = dot_nt(h_low, w_gate[c])
        up = dot_nt(h_low, w_up[c])
        below = 0.5 * (1.0 + lax.erf(gate * (0.5**0.5)))
        gelu = gate * below
        slope = below + gate * (jnp.exp(-0.5 * gate * gate) * (0.5 / jnp.pi) ** 0.5)
        hidden = (gelu * up).astype(BF16)
        keep_gate[c] = up * slope
        keep_up[c] = gelu
        keep_hidden[c] = hidden
        return pre_two + dot_nn(hidden, w_down[c])

    pre_two = lax.fori_loop(0, CHUNKS, forward, h_one)
    unit_two, scale_two = norm_stats(pre_two)
    out_ref[...] = (unit_two * norm_ref[2:3, :] + norm_ref[3:4, :]).astype(BF16)
    d_pre_two, d_gain_two, d_bias_two = norm_back(
        unit_two, scale_two, norm_ref[2:3, :], cot_ref[...].astype(F32)
    )
    d_branch = d_pre_two.astype(BF16)

    def drain(slot):
        for kind in range(3):
            view = stage.at[slot, kind]
            pltpu.make_async_copy(view, view, store_sems.at[slot * 3 + kind]).wait()

    def backward(c, d_h):
        slot = lax.rem(c, 2)

        @pl.when(c >= 2)
        def _():
            drain(slot)

        d_hidden = dot_nt(d_branch, w_down[c])
        d_gate = (d_hidden * keep_gate[c]).astype(BF16)
        d_up = (d_hidden * keep_up[c]).astype(BF16)
        stage[slot, 0] = dot_tn(d_gate, h_low).astype(BF16)
        stage[slot, 1] = dot_tn(d_up, h_low).astype(BF16)
        stage[slot, 2] = dot_tn(keep_hidden[c], d_branch).astype(BF16)

        def store(step, carry):
            for kind in range(3):
                pltpu.make_async_copy(
                    stage.at[slot, kind, pl.ds(step * piece, piece)],
                    grads.at[place[bases[kind] + c * chunk_pieces + step]],
                    store_sems.at[slot * 3 + kind],
                ).start()
            return carry

        lax.fori_loop(0, chunk_pieces, store, None, unroll=4)
        return d_h + dot_nn(d_gate, w_gate[c]) + dot_nn(d_up, w_up[c])

    d_h = lax.fori_loop(0, CHUNKS, backward, d_pre_two)
    d_pre_one, d_gain_one, d_bias_one = norm_back(unit_one, scale_one, norm_ref[0:1, :], d_h)
    d_pre_one_ref[...] = d_pre_one
    d_proj = d_pre_one.astype(BF16)
    d_mixed_ref[...] = lax.dot_general(
        w_out[...], d_proj, (((0,), (1,)), ((), ())), preferred_element_type=F32
    ).astype(BF16)
    stage_out[...] = dot_tn(d_proj, mixed).astype(BF16)

    def store_out(step, carry):
        pltpu.make_async_copy(
            stage_out.at[pl.ds(step * piece, piece)],
            grads.at[place[3 * kind_pieces + step]],
            store_sems.at[6],
        ).start()
        return carry

    lax.fori_loop(0, kind_pieces, store_out, None, unroll=8)
    norm_grad[...] = jnp.concatenate(
        [
            d_gain_one,
            d_bias_one,
            d_gain_two,
            d_bias_two,
            jnp.zeros((4, d_gain_one.shape[1]), F32),
        ],
        axis=0,
    )
    drain(CHUNKS % 2)
    drain((CHUNKS + 1) % 2)
    pltpu.make_async_copy(stage_out, stage_out, store_sems.at[6]).wait()


def project_grad_kernel(
    sizes,
    place,
    x_ref,
    d_own,
    d_pre_one,
    weights,
    grads_in,
    d_input,
    grads,
    w_all,
    stage,
    load_sems,
    store_sems,
):
    piece, kind_pieces = sizes
    group_pieces = kind_pieces // GROUPS
    rows = 3 * group_pieces * piece
    del grads_in

    def each(group, act):
        def one(step, carry):
            for kind in range(3):
                act(kind * kind_pieces + group * group_pieces + step, kind * group_pieces + step)
            return carry

        lax.fori_loop(0, group_pieces, one, None, unroll=4)

    for group in range(GROUPS):

        def load(number, row, group=group):
            dst = w_all.at[group, pl.ds(row * piece, piece)]
            fetch_piece(place, number, weights, dst, load_sems.at[group])

        each(group, load)
    x_own = x_ref[...]
    for group in range(GROUPS):
        stage[group] = dot_nn(d_own[group], x_own).astype(BF16)

        def store(number, row, group=group):
            src = stage.at[group, pl.ds(row * piece, piece)]
            pltpu.make_async_copy(src, grads.at[place[number]], store_sems.at[group]).start()

        each(group, store)
    total = d_pre_one[...]
    for group in range(GROUPS):
        view = w_all.at[group]
        pltpu.make_async_copy(view, view, load_sems.at[group]).wait()
        total = total + dot_tn(d_own[group], w_all[group])
    d_input[...] = total.astype(BF16)
    for group in range(GROUPS):
        view = stage.at[group]
        pltpu.make_async_copy(view, view, store_sems.at[group]).wait()


def holder(order, n_dp):
    dp = lax.rem(order, n_dp)
    return {"b": lax.div(order, n_dp), "y": lax.div(dp, 2), "core": lax.rem(dp, 2)}


def turn_to():
    z, dp = lax.axis_index("a"), lax.axis_index("y") * 2 + lax.axis_index("core")
    return {"a": dp, "y": lax.div(z, 2), "core": lax.rem(z, 2)}, dp != z


def start_turn(src, dst, send_sem, recv_sem):
    peer, moves = turn_to()

    @pl.when(moves)
    def _():
        pltpu.make_async_remote_copy(
            src_ref=src,
            dst_ref=dst,
            send_sem=send_sem,
            recv_sem=recv_sem,
            device_id=peer,
            device_id_type=MESH_IDS,
        ).start()

    @pl.when(jnp.logical_not(moves))
    def _():
        pltpu.make_async_copy(src, dst, recv_sem).start()


def finish_turn(src, dst, send_sem, recv_sem):
    peer, moves = turn_to()

    @pl.when(moves)
    def _():
        pltpu.make_async_remote_copy(
            src_ref=src,
            dst_ref=dst,
            send_sem=send_sem,
            recv_sem=recv_sem,
            device_id=peer,
            device_id_type=MESH_IDS,
        ).wait()

    @pl.when(jnp.logical_not(moves))
    def _():
        pltpu.make_async_copy(src, dst, recv_sem).wait()


def greet(peers, turning=False):
    barrier = pltpu.get_barrier_semaphore()
    for peer in peers:
        pl.semaphore_signal(barrier, inc=1, device_id=peer, device_id_type=MESH_IDS)
    if not turning:
        pl.semaphore_wait(barrier, len(peers))
        return
    turn_peer, moves = turn_to()

    @pl.when(moves)
    def _():
        pl.semaphore_signal(barrier, inc=1, device_id=turn_peer, device_id_type=MESH_IDS)

    pl.semaphore_wait(barrier, len(peers) + moves.astype(jnp.int32))


def my_order(n_dp):
    return lax.axis_index("b") * n_dp + lax.axis_index("y") * 2 + lax.axis_index("core")


def swap_heads_kernel(sizes, in_ref, out_ref, send_sems, recv_sems, own_sem):
    n_dp, splits = sizes
    order = my_order(n_dp)
    group, split = lax.div(order, splits), lax.rem(order, splits)
    others = [lax.rem(group + k, GROUPS) for k in range(1, GROUPS)]
    peers = [holder(other * splits + split, n_dp) for other in others]
    greet(peers)
    copies = []
    for k in range(GROUPS - 1):
        copy = pltpu.make_async_remote_copy(
            src_ref=in_ref.at[others[k]],
            dst_ref=out_ref.at[group],
            send_sem=send_sems.at[k],
            recv_sem=recv_sems.at[k],
            device_id=peers[k],
            device_id_type=MESH_IDS,
        )
        copy.start()
        copies.append(copy)
    own = pltpu.make_async_copy(in_ref.at[group], out_ref.at[group], own_sem)
    own.start()
    own.wait()
    for copy in copies:
        copy.wait()


def add_low(dst, src, rows):
    def one(i, carry):
        dst[i] = (dst[i].astype(F32) + src[i].astype(F32)).astype(BF16)
        return carry

    lax.fori_loop(0, rows, one, None)


def z_order_of(count):
    order = [0]
    for k in range(1, count):
        for far in (k, count - k):
            if far not in order:
                order.append(far)
    return order


def spread_kernel(
    sizes,
    own,
    pack,
    every,
    gathered,
    crossed,
    z_sems,
    xs_sems,
    ys_sems,
    xf_sems,
    yf_sems,
    near_sems,
    own_sem,
    by_sems,
    bz_sems,
    bx_sems,
    bn_sems,
    stay_sem,
):
    zn, xn, yn, slots, part = sizes
    rest = slots - part
    z, x = lax.axis_index("a"), lax.axis_index("b")
    y, core = lax.axis_index("y"), lax.axis_index("core")
    core_peer = {"core": 1 - core}
    xs, ys, z_order = range(1, xn), range(1, yn), z_order_of(zn)
    x_peers = {k: {"b": lax.rem(x + k, xn)} for k in xs}
    y_peers = {k: {"y": lax.rem(y + k, yn)} for k in ys}
    z_peers = {k: {"a": lax.rem(z + k, zn)} for k in range(1, zn)}
    greet([core_peer, *x_peers.values(), *y_peers.values(), *z_peers.values()])

    def remote(src, dst, sems, index, peer):
        return pltpu.make_async_remote_copy(
            src_ref=src,
            dst_ref=dst,
            send_sem=sems.at[0, index],
            recv_sem=sems.at[1, index],
            device_id=peer,
            device_id_type=MESH_IDS,
        )

    def number(jz, jx, jy):
        chip = (lax.rem(z + zn - jz, zn) * xn + lax.rem(x + xn - jx, xn)) * yn + lax.rem(
            y + yn - jy, yn
        )
        return chip * 2 + core

    def shard(jz, jx, jy, first=0, count=slots):
        return every.at[pl.ds(number(jz, jx, jy) * slots + first, count)]

    def held(jz, jx, jy):
        return own if (jz, jx, jy) == (0, 0, 0) else shard(jz, jx, jy)

    def z_copy(jz):
        return remote(own, shard(0, 0, 0), z_sems, jz - 1, z_peers[jz])

    def xs_copy(jz, jx):
        return remote(
            held(jz, 0, 0), shard(jz, 0, 0), xs_sems, jz * (xn - 1) + jx - 1, x_peers[jx]
        )

    def ys_copy(jz, jy):
        return remote(
            held(jz, 0, 0), shard(jz, 0, 0), ys_sems, jz * (yn - 1) + jy - 1, y_peers[jy]
        )

    def cross(jz, jx, jy):
        return (jz * (xn - 1) + jx - 1) * (yn - 1) + jy - 1

    def xf_copy(jz, jx, jy):
        view = shard(jz, 0, jy, part, rest)
        return remote(view, view, xf_sems, cross(jz, jx, jy), x_peers[jx])

    def yf_copy(jz, jx, jy):
        view = shard(jz, jx, 0, 0, part)
        return remote(view, view, yf_sems, cross(jz, jx, jy), y_peers[jy])

    def near_copy(jz, jx, jy):
        return remote(
            held(jz, jx, jy),
            shard(jz, jx, jy),
            near_sems,
            (jz * xn + jx) * yn + jy,
            core_peer,
        )

    started = []

    def launch(copy):
        copy.start()
        started.append(copy)

    def send_own(jz):
        for jx in xs:
            launch(xs_copy(jz, jx))
        for jy in ys:
            launch(ys_copy(jz, jy))
        launch(near_copy(jz, 0, 0))

    def forward(jz):
        for jy in ys:
            ys_copy_in(jz, jy)
            for jx in xs:
                launch(xf_copy(jz, jx, jy))
        for jx in xs:
            xs_copy_in(jz, jx)
            for jy in ys:
                launch(yf_copy(jz, jx, jy))
        for jy in ys:
            launch(near_copy(jz, 0, jy))
        for jx in xs:
            launch(near_copy(jz, jx, 0))

    def ys_copy_in(jz, jy):
        view = shard(jz, 0, jy)
        remote(view, view, ys_sems, jz * (yn - 1) + jy - 1, y_peers[jy]).wait_recv()

    def xs_copy_in(jz, jx):
        view = shard(jz, jx, 0)
        remote(view, view, xs_sems, jz * (xn - 1) + jx - 1, x_peers[jx]).wait_recv()

    def finish(jz):
        for jx in xs:
            for jy in ys:
                view = shard(jz, jx, jy, part, rest)
                remote(view, view, xf_sems, cross(jz, jx, jy), x_peers[jx]).wait_recv()
                view = shard(jz, jx, jy, 0, part)
                remote(view, view, yf_sems, cross(jz, jx, jy), y_peers[jy]).wait_recv()
                launch(near_copy(jz, jx, jy))

    def z_in(index):
        jz = z_order[index]
        view = shard(jz, 0, 0)
        remote(view, view, z_sems, jz - 1, z_peers[jz]).wait_recv()
        if index + 1 < zn:
            launch(z_copy(z_order[index + 1]))

    own_local = pltpu.make_async_copy(own, shard(0, 0, 0), own_sem)
    hosts = lax.rem(z, 2) == core

    def block(jz, jx=0):
        return gathered.at[lax.rem(x + xn - jx, xn) * zn + lax.rem(z + zn - jz, zn)]

    def by_copy(jy):
        return remote(pack, crossed.at[jy - 1], by_sems, jy - 1, y_peers[jy])

    def plane(jy):
        return lax.rem(y + yn - jy, yn) * 2 + core

    def bz_copy(jy):
        src = pack if jy == 0 else crossed.at[jy - 1]
        far = lax.rem(plane(jy) + zn - z, zn)
        return remote(src, block(0), bz_sems, far, {"a": plane(jy)})

    def stay_copy(jy):
        src = pack if jy == 0 else crossed.at[jy - 1]
        return pltpu.make_async_copy(src, block(0), stay_sem)

    def bx_copy(jz, jx):
        return remote(block(jz), block(jz), bx_sems, jz * (xn - 1) + jx - 1, x_peers[jx])

    def bn_copy(jz, jx):
        return remote(block(jz, jx), block(jz, jx), bn_sems, jz * xn + jx, core_peer)

    def blocks_to_planes():
        for jy in range(yn):
            if jy != 0:
                by_copy(jy).wait_recv()

            @pl.when(plane(jy) != z)
            def _():
                bz_copy(jy).start()

            @pl.when(plane(jy) == z)
            def _():
                stay_copy(jy).start()
                stay_copy(jy).wait()

    def blocks_across():
        @pl.when(hosts)
        def _():
            for jz in z_order:
                if jz != 0:
                    remote(block(jz), block(jz), bz_sems, jz, z_peers[jz]).wait_recv()
                for jx in xs:
                    bx_copy(jz, jx).start()
                bn_copy(jz, 0).start()

    def blocks_end():
        @pl.when(hosts)
        def _():
            for jz in z_order:
                for jx in xs:
                    view = block(jz, jx)
                    index = jz * (xn - 1) + jx - 1
                    remote(view, view, bx_sems, index, x_peers[jx]).wait_recv()
                    bn_copy(jz, jx).start()
            for jz in z_order:
                for jx in xs:
                    bx_copy(jz, jx).wait_send()
                for jx in range(xn):
                    bn_copy(jz, jx).wait_send()

        @pl.when(jnp.logical_not(hosts))
        def _():
            for jz in range(zn):
                for jx in range(xn):
                    bn_copy(jz, jx).wait_recv()

        for jy in range(yn):

            @pl.when(plane(jy) != z)
            def _():
                bz_copy(jy).wait_send()

    launch(z_copy(z_order[1]))
    send_own(0)

    own_local.start()
    for jy in ys:
        launch(by_copy(jy))

    for index in range(1, zn):
        z_in(index)
        send_own(z_order[index])
        forward(z_order[index - 1])
        if index >= 2:
            finish(z_order[index - 2])
    blocks_to_planes()
    forward(z_order[zn - 1])
    blocks_across()
    finish(z_order[zn - 2])
    finish(z_order[zn - 1])

    for jz in range(zn):
        for jx in range(xn):
            for jy in range(yn):
                chip = lax.div(number(jz, jx, jy), 2)
                view = every.at[pl.ds((chip * 2 + 1 - core) * slots, slots)]
                remote(
                    view, view, near_sems, (jz * xn + jx) * yn + jy, core_peer
                ).wait_recv()
    blocks_end()
    own_local.wait()
    for copy in started:
        copy.wait_send()


def reduce_kernel(
    sizes,
    grads,
    norm_in,
    tokens_in,
    low_in,
    total_out,
    norm_out,
    tokens_out,
    low_out,
    held,
    near,
    xd,
    yd,
    xs_in,
    ys_in,
    zs_in,
    norm_core,
    norm_y,
    norm_x,
    norm_z,
    norm_sum,
    load_sems,
    near_sems,
    xd_sems,
    yd_sems,
    xs_sems,
    ys_sems,
    zs_sems,
    norm_sems,
    turn_sems,
):
    zn, xn, yn, slots, part = sizes
    rest = slots - part
    z, x = lax.axis_index("a"), lax.axis_index("b")
    y, core = lax.axis_index("y"), lax.axis_index("core")
    core_peer = {"core": 1 - core}
    xs, ys = range(1, xn), range(1, yn)
    y_peers = [{"y": lax.rem(y + k, yn)} for k in ys]
    x_peers = [{"b": lax.rem(x + k, xn)} for k in xs]
    z_peers = [{"a": lax.rem(z + k, zn)} for k in range(1, zn)]
    greet([core_peer] + y_peers + x_peers + z_peers, True)
    turn_refs = (tokens_in, tokens_out, turn_sems.at[0], turn_sems.at[1])
    low_refs = (low_in, low_out, turn_sems.at[2], turn_sems.at[3])
    start_turn(*low_refs)
    start_turn(*turn_refs)

    def remote(src, dst, sems, index, peer):
        return pltpu.make_async_remote_copy(
            src_ref=src,
            dst_ref=dst,
            send_sem=sems.at[0, index],
            recv_sem=sems.at[1, index],
            device_id=peer,
            device_id_type=MESH_IDS,
        )

    def flat(jz, jx, jy):
        return (jz * xn + jx) * yn + jy

    def chip_rows(jz, jx, jy, which):
        chip = (lax.rem(z + jz, zn) * xn + lax.rem(x + jx, xn)) * yn + lax.rem(y + jy, yn)
        return grads.at[pl.ds((chip * 2 + which) * slots, slots)]

    def near_copy(jz, jx, jy):
        index = flat(jz, jx, jy)
        return remote(chip_rows(jz, jx, jy, 1 - core), near.at[index], near_sems, index, core_peer)

    def load_copy(jz, jx, jy):
        index = flat(jz, jx, jy)
        return pltpu.make_async_copy(
            chip_rows(jz, jx, jy, core), held.at[index], load_sems.at[index]
        )

    def whole(jz, jx, jy):
        return held.at[flat(jz, jx, jy)]

    def first(jz, jx, jy):
        return held.at[flat(jz, jx, jy), pl.ds(0, part)]

    def second(jz, jx, jy):
        return held.at[flat(jz, jx, jy), pl.ds(part, rest)]

    def cross(jz, jx, jy):
        return (jz * (xn - 1) + jx - 1) * (yn - 1) + jy - 1

    def yd_copy(jz, jx, jy):
        index = cross(jz, jx, jy)
        return remote(first(jz, jx, jy), yd.at[index], yd_sems, index, y_peers[jy - 1])

    def xd_copy(jz, jx, jy):
        index = cross(jz, jx, jy)
        return remote(second(jz, jx, jy), xd.at[index], xd_sems, index, x_peers[jx - 1])

    def halves(low_half):
        return pl.ds(0, part) if low_half else pl.ds(part, rest)

    def xs_copy(jz, jx, low_half):
        index = jz * (xn - 1) + jx - 1
        return remote(
            held.at[flat(jz, jx, 0), halves(low_half)],
            xs_in.at[index, halves(low_half)],
            xs_sems,
            index * 2 + int(low_half),
            x_peers[jx - 1],
        )

    def ys_copy(jz, jy, low_half):
        index = jz * (yn - 1) + jy - 1
        return remote(
            held.at[flat(jz, 0, jy), halves(low_half)],
            ys_in.at[index, halves(low_half)],
            ys_sems,
            index * 2 + int(low_half),
            y_peers[jy - 1],
        )

    def zs_copy(jz):
        return remote(whole(jz, 0, 0), zs_in.at[jz - 1], zs_sems, jz - 1, z_peers[jz - 1])

    z_order = z_order_of(zn)[::-1]
    started = []

    def launch(copy):
        copy.start()
        started.append(copy)

    steps_done = []
    norm_count = [0]

    def norm_step(buffer, peers):
        copies = []
        for k, peer in enumerate(peers):
            index = norm_count[0]
            norm_count[0] += 1
            copy = remote(norm_sum.at[len(steps_done)], buffer.at[k], norm_sems, index, peer)
            copy.start()
            copies.append(copy)
        return copies

    def norm_finish(buffer, copies):
        total = norm_sum[len(steps_done)]
        for k, copy in enumerate(copies):
            copy.wait()
            total = total + buffer[k]
        steps_done.append(None)
        norm_sum[len(steps_done)] = total

    def plane(jz):
        return (
            [(jz, jx, jy) for jx in xs for jy in ys]
            + [(jz, jx, 0) for jx in xs]
            + [(jz, 0, jy) for jy in ys]
            + [(jz, 0, 0)]
        )

    def fetch(jz):
        for chip in plane(jz):
            launch(near_copy(*chip))
            load_copy(*chip).start()

    def prepare(index):
        for chip in plane(z_order[index]):
            load_copy(*chip).wait()
            near_copy(*chip).wait_recv()
            add_low(whole(*chip), near.at[flat(*chip)], slots)
        if index + 1 < zn:
            fetch(z_order[index + 1])

    stages = [(index, stage) for index in range(zn) for stage in range(3)]

    def send_stage(number):
        index, stage = stages[number]
        jz = z_order[index]
        for jx in xs:
            if stage == 0:
                for jy in ys:
                    launch(xd_copy(jz, jx, jy))
            else:
                launch(xs_copy(jz, jx, stage == 2))
        for jy in ys:
            if stage == 0:
                for jx in xs:
                    launch(yd_copy(jz, jx, jy))
            else:
                launch(ys_copy(jz, jy, stage == 1))

    def take_stage(number):
        index, stage = stages[number]
        jz = z_order[index]
        if stage == 0:
            for jx in xs:
                for jy in ys:
                    yd_copy(jz, jx, jy).wait_recv()
                    add_low(first(jz, jx, 0), yd.at[cross(jz, jx, jy)], part)
                    xd_copy(jz, jx, jy).wait_recv()
                    add_low(second(jz, 0, jy), xd.at[cross(jz, jx, jy)], rest)
        else:
            for jx in xs:
                xs_copy(jz, jx, stage == 2).wait_recv()
            for jy in ys:
                ys_copy(jz, jy, stage == 1).wait_recv()

    def side_in(index):
        jz = z_order[index]

        def one(i, carry):
            total = held[flat(jz, 0, 0), i].astype(F32)
            for jx in xs:
                total = total + xs_in[jz * (xn - 1) + jx - 1, i].astype(F32)
            for jy in ys:
                total = total + ys_in[jz * (yn - 1) + jy - 1, i].astype(F32)
            if jz != 0:
                held[flat(jz, 0, 0), i] = total.astype(BF16)
            else:
                total_out[i] = total
            return carry

        lax.fori_loop(0, slots, one, None)
        if jz != 0:
            launch(zs_copy(jz))

    norm_sum[0] = norm_in[...]
    rounds = [(norm_core, [core_peer]), (norm_y, y_peers), (norm_x, x_peers), (norm_z, z_peers)]
    fetch(z_order[0])
    pending = norm_step(*rounds[0])
    prepare(0)
    prepared, ahead = 1, 2
    for number in range(ahead):
        send_stage(number)
    for number in range(len(stages)):
        take_stage(number)
        later = number + ahead
        if later < len(stages):
            if stages[later][0] >= prepared:
                prepare(prepared)
                prepared += 1
            send_stage(later)
        if stages[number][1] == 2:
            side_in(stages[number][0])
        if number % 3 == 2 and len(steps_done) < 3:
            norm_finish(rounds[len(steps_done)][0], pending)
            pending = norm_step(*rounds[len(steps_done)])
    while len(steps_done) < 3:
        norm_finish(rounds[len(steps_done)][0], pending)
        pending = norm_step(*rounds[len(steps_done)])
    norm_finish(norm_z, pending)
    norm_out[...] = norm_sum[4]
    for jz in range(1, zn):
        zs_copy(jz).wait_recv()

    def last(i, carry):
        total = total_out[i]
        for jz in range(1, zn):
            total = total + zs_in[jz - 1, i].astype(F32)
        total_out[i] = total
        return carry

    lax.fori_loop(0, slots, last, None)
    finish_turn(*low_refs)
    finish_turn(*turn_refs)
    for copy in started:
        copy.wait_send()


def vmem():
    return pl.BlockSpec(memory_space=pltpu.VMEM)


def smem():
    return pl.BlockSpec(memory_space=pltpu.SMEM)


def anywhere():
    return pl.BlockSpec(memory_space=pl.ANY)


def shape_of(dims, kind):
    return jax.ShapeDtypeStruct(dims, kind)


def params(collective=None):
    if collective is None:
        return pltpu.CompilerParams(vmem_limit_bytes=VMEM_LIMIT)
    return pltpu.CompilerParams(
        vmem_limit_bytes=VMEM_LIMIT, collective_id=collective, has_side_effects=True
    )


def swap_heads(block, n_dp, splits, collective):
    return pl.pallas_call(
        functools.partial(swap_heads_kernel, (n_dp, splits)),
        out_shape=shape_of(block.shape, BF16),
        in_specs=[vmem()],
        out_specs=vmem(),
        scratch_shapes=[
            pltpu.SemaphoreType.DMA((GROUPS - 1,)),
            pltpu.SemaphoreType.DMA((GROUPS - 1,)),
            pltpu.SemaphoreType.DMA,
        ],
        compiler_params=params(collective),
    )(block)


def per_device(
    dims,
    layer_input,
    out_cotangent,
    segment_ids,
    piece_owner,
    weight_master,
    weight_first,
    weight_second,
    norm_params,
    norm_first,
    norm_second,
):
    n_seq, n_dp = dims
    reps = n_seq // n_dp
    splits = n_seq // GROUPS
    slots, piece, width = weight_master.shape
    pieces = piece_owner.shape[0]
    tok = layer_input.shape[1]
    length = tok * n_seq
    hidden_units = (pieces * piece - 4 * width) // 3
    head = width // HEADS
    kind_pieces = width // piece
    hidden_pieces = hidden_units // piece
    chunk = hidden_units // CHUNKS

    location = locate_pieces(piece_owner, slots)
    own_low = weight_master.astype(BF16)
    seg_row = jnp.zeros((16, width), BF16).at[0, :tok].set(segment_ids[0].astype(BF16))
    pack = jnp.concatenate([layer_input[0], seg_row], axis=0)
    turn = [(i * n_dp + j, j * n_dp + i) for i in range(n_dp) for j in range(n_dp)]
    turn_axes = ("a", "y", "core")

    zn, xn, yn = n_dp, reps, n_dp // 2
    n_chips = zn * xn * yn

    def pair(count):
        return pltpu.SemaphoreType.DMA((2, max(count, 1)))

    half = slots // 2
    split_rows = slots * 9 // 16
    weights, gathered, _ = pl.pallas_call(
        functools.partial(spread_kernel, (zn, xn, yn, slots, split_rows)),
        out_shape=(
            shape_of((n_chips * 2 * slots, piece, width), BF16),
            shape_of((n_seq, tok + 16, width), BF16),
            shape_of((max(yn - 1, 1), tok + 16, width), BF16),
        ),
        in_specs=[anywhere(), anywhere()],
        out_specs=(anywhere(),) * 3,
        scratch_shapes=[
            pair(zn - 1),
            pair(zn * (xn - 1)),
            pair(zn * (yn - 1)),
            pair(zn * (xn - 1) * (yn - 1)),
            pair(zn * (xn - 1) * (yn - 1)),
            pair(n_chips),
            pltpu.SemaphoreType.DMA,
            pair(yn - 1),
            pair(zn),
            pair(zn * (xn - 1)),
            pair(zn * xn),
            pltpu.SemaphoreType.DMA,
        ],
        compiler_params=params(5),
    )(own_low, pack)
    weights, cotangent = lax.optimization_barrier((weights, out_cotangent[0]))
    cotangent = lax.ppermute(cotangent, turn_axes, turn)

    core = lax.axis_index("core")
    order = my_order(n_dp)
    group, split = order // splits, order % splits
    info = jnp.stack([core, group, split]).astype(jnp.int32)
    tokens = lax.dynamic_index_in_dim(gathered, order, axis=0, keepdims=False)[:tok]
    slopes = head_slopes(HEADS, tok, n_seq)

    segs = gathered[:, tok, :tok]
    lanes = jnp.arange(128, dtype=jnp.int32)[None, :] - head
    key_same = segs.reshape(length, 1).astype(jnp.int32) == lanes
    key_marks = jnp.where(key_same | (lanes < 0) | (lanes > 2), 0.0, MASKED).astype(BF16)
    query_segs = lax.dynamic_index_in_dim(
        segs.reshape(GROUPS, splits, tok), split, axis=1, keepdims=False
    )
    query_marks = (query_segs.reshape(GROUPS * tok, 1).astype(jnp.int32) == lanes).astype(BF16)

    attend_sizes = (n_dp, reps, splits, tok, head, n_seq)
    q_ext, k_ext, k_turned, v_rows, mixed_low, mixed_full, log_total = pl.pallas_call(
        functools.partial(attend_forward_kernel, attend_sizes),
        out_shape=(
            shape_of((TRIO, GROUPS * tok, 128), BF16),
            shape_of((TRIO, length, 128), BF16),
            shape_of((TRIO, head, length), BF16),
            shape_of((TRIO, length, head), BF16),
            shape_of((GROUPS, TRIO, head, tok), BF16),
            shape_of((GROUPS, TRIO, head, tok), F32),
            shape_of((GROUPS, TRIO, 1, tok), F32),
        ),
        in_specs=[smem(), smem(), smem(), vmem(), vmem(), vmem(), anywhere()],
        out_specs=(vmem(),) * 7,
        scratch_shapes=[
            pltpu.VMEM((3 * TRIO, 128, width), BF16),
            pltpu.VMEM((TRIO, head, length), BF16),
            pltpu.VMEM((3 * TRIO, tok, tok), F32),
            pltpu.VMEM((n_seq, tok, tok), F32),
            pltpu.SemaphoreType.DMA((3 * TRIO * (head // piece),)),
        ],
        compiler_params=params(),
    )(location, info, slopes, gathered, query_marks, key_marks, weights)

    mixed_own = swap_heads(mixed_low.reshape(GROUPS, TRIO * head, tok), n_dp, splits, 1)

    out_low, d_pre_one, d_mixed, norm_part, grads = pl.pallas_call(
        functools.partial(
            dense_kernel, (tok, piece, kind_pieces, chunk // piece, hidden_pieces)
        ),
        out_shape=(
            shape_of((tok, width), BF16),
            shape_of((tok, width), F32),
            shape_of((width, tok), BF16),
            shape_of((8, width), F32),
            shape_of((n_seq * n_dp * slots, piece, width), BF16),
        ),
        in_specs=[smem(), vmem(), vmem(), vmem(), vmem(), anywhere()],
        out_specs=(vmem(), vmem(), vmem(), vmem(), anywhere()),
        scratch_shapes=[
            pltpu.VMEM((width, width), BF16),
            pltpu.VMEM((CHUNKS, chunk, width), BF16),
            pltpu.VMEM((CHUNKS, chunk, width), BF16),
            pltpu.VMEM((CHUNKS, chunk, width), BF16),
            pltpu.VMEM((CHUNKS, tok, chunk), F32),
            pltpu.VMEM((CHUNKS, tok, chunk), F32),
            pltpu.VMEM((CHUNKS, tok, chunk), BF16),
            pltpu.VMEM((2, 3, chunk, width), BF16),
            pltpu.VMEM((width, width), BF16),
            pltpu.SemaphoreType.DMA((3 * CHUNKS + 1,)),
            pltpu.SemaphoreType.DMA((7,)),
        ],
        compiler_params=params(),
    )(
        location,
        tokens,
        cotangent,
        mixed_own.reshape(width, tok),
        norm_params,
        weights,
    )

    (d_own,) = pl.pallas_call(
        functools.partial(attend_backward_kernel, attend_sizes),
        out_shape=(shape_of((GROUPS, 3, TRIO, head, tok), BF16),),
        in_specs=[smem()] + [vmem()] * 7,
        out_specs=(vmem(),),
        scratch_shapes=[
            pltpu.VMEM((length, 128), F32),
            pltpu.VMEM((length, head), F32),
            pltpu.VMEM((3 * TRIO, tok, tok), F32),
            pltpu.VMEM((GROUPS, TRIO, head, tok), BF16),
            pltpu.VMEM((GROUPS, 3, TRIO, head, tok), BF16),
            pltpu.VMEM((TRIO, splits, GROUPS, 2, head, tok), BF16),
            pltpu.VMEM((TRIO, splits - 1, GROUPS, 2, head, tok), BF16),
            pair(GROUPS - 1),
            pair(TRIO * (GROUPS - 1)),
            pair(TRIO * (splits - 1)),
            pair(TRIO * (GROUPS - 1)),
        ],
        compiler_params=params(3),
    )(
        slopes,
        q_ext,
        k_ext,
        k_turned,
        v_rows,
        mixed_full,
        log_total,
        d_mixed.reshape(GROUPS, TRIO, head, tok),
    )

    trio_rows = TRIO * head
    d_tokens, grads = pl.pallas_call(
        functools.partial(project_grad_kernel, (piece, kind_pieces)),
        out_shape=(shape_of((tok, width), BF16), shape_of(grads.shape, BF16)),
        in_specs=[smem(), vmem(), vmem(), vmem()] + [anywhere()] * 2,
        out_specs=(vmem(), anywhere()),
        scratch_shapes=[
            pltpu.VMEM((GROUPS, 3 * trio_rows, width), BF16),
            pltpu.VMEM((GROUPS, 3 * trio_rows, width), BF16),
            pltpu.SemaphoreType.DMA((GROUPS,)),
            pltpu.SemaphoreType.DMA((GROUPS,)),
        ],
        input_output_aliases={5: 1},
        compiler_params=params(),
    )(
        location,
        tokens,
        d_own.reshape(GROUPS, 3 * trio_rows, tok),
        d_pre_one,
        weights,
        grads,
    )

    def chunks(count, rows):
        return pltpu.VMEM((max(count, 1), rows, piece, width), BF16)

    def norm_rows(count):
        return pltpu.VMEM((max(count, 1), 8, width), F32)

    crossing = zn * (xn - 1) * (yn - 1)
    own_grad, norm_total, d_turned, result = pl.pallas_call(
        functools.partial(reduce_kernel, (zn, xn, yn, slots, half)),
        out_shape=(
            shape_of((slots, piece, width), F32),
            shape_of((8, width), F32),
            shape_of(d_tokens.shape, BF16),
            shape_of(out_low.shape, BF16),
        ),
        in_specs=[anywhere(), vmem(), anywhere(), anywhere()],
        out_specs=(vmem(), vmem(), anywhere(), anywhere()),
        scratch_shapes=[
            chunks(n_chips, slots),
            chunks(n_chips, slots),
            chunks(crossing, slots - half),
            chunks(crossing, half),
            chunks(zn * (xn - 1), slots),
            chunks(zn * (yn - 1), slots),
            chunks(zn - 1, slots),
            norm_rows(1),
            norm_rows(yn - 1),
            norm_rows(xn - 1),
            norm_rows(zn - 1),
            norm_rows(5),
            pltpu.SemaphoreType.DMA((n_chips,)),
            pair(n_chips),
            pair(crossing),
            pair(crossing),
            pair(2 * zn * (xn - 1)),
            pair(2 * zn * (yn - 1)),
            pair(zn - 1),
            pair(1 + (yn - 1) + (xn - 1) + (zn - 1)),
            pltpu.SemaphoreType.DMA((4,)),
        ],
        compiler_params=params(4),
    )(grads, norm_part, d_tokens, out_low)
    d_input = d_turned.astype(F32)

    numbers = jnp.arange(pieces, dtype=jnp.int32) + 1
    own_slots = lax.axis_index(("a", "b", "y", "core")) * slots + jnp.arange(slots)
    inverse = jnp.sum(jnp.where(location[None, :] == own_slots[:, None], numbers[None, :], 0), axis=1)
    own_grad = jnp.where((inverse > 0)[:, None, None], own_grad, 0.0)
    norm_grad = norm_total[:4]
    rates = slot_rates(inverse, piece, width, hidden_units)
    first_new, second_new, weight_new = adamw_step(
        weight_master, weight_first, weight_second, own_grad, rates[:, None, None], STEP
    )
    norm_first_new, norm_second_new, norm_new = adamw_step(
        norm_params, norm_first, norm_second, norm_grad, NORM_RATE, STEP
    )
    return (
        result[None],
        d_input[None],
        own_grad,
        first_new,
        second_new,
        weight_new,
        weight_new.astype(BF16),
        norm_grad,
        norm_first_new,
        norm_second_new,
        norm_new,
    )


def solution(mesh):
    n_seq, n_dp = mesh.shape["seq"], mesh.shape["dp"]
    inner = Mesh(
        mesh.devices.reshape(n_dp, n_seq // n_dp, n_dp // 2, 2), ("a", "b", "y", "core")
    )
    seq, dp, every = ("a", "b"), ("y", "core"), ("a", "b", "y", "core")
    block = P(dp, seq, None)
    owned = P(every, None, None)
    in_specs = (block, block, P(dp, seq), P(), owned, owned, owned, P(), P(), P())
    out_specs = (block, block, owned, owned, owned, owned, owned, P(), P(), P(), P())
    return jax.shard_map(
        functools.partial(per_device, (n_seq, n_dp)),
        mesh=inner,
        in_specs=in_specs,
        out_specs=out_specs,
        check_vma=False,
    )
```

```python
import functools

import jax
import jax.numpy as jnp
import numpy as np
from jax import lax
from jax.experimental import pallas as pl
from jax.experimental.pallas import tpu as pltpu
from jax.sharding import Mesh
from jax.sharding import PartitionSpec as P

HEADS = 12
GROUPS = 4
TRIO = HEADS // GROUPS
STEP = 4

NORM_EPS = 1e-06
BETA_ONE = 0.5
BETA_TWO = 0.5
DECAY = 0.01
ADAM_EPS = 1e-08
NORM_RATE = 0.3
OUT_RATE = 0.35
MASKED = -1e30
CHUNKS = 6
VMEM_LIMIT = 60 * 1024 * 1024
MESH_IDS = pl.DeviceIdType.MESH
F32 = jnp.float32
BF16 = jnp.bfloat16


def head_slopes(head_count, tok_rows, seq_devices):
    head_order = np.arange(head_count, dtype=np.float64)
    slopes = 8.0 / tok_rows * np.power(8.0 * seq_devices, -head_order / (head_count - 1))
    return slopes.astype(np.float32)


def locate_pieces(owners, slot_count):
    pieces = owners.shape[0]
    numbers = jnp.arange(pieces, dtype=jnp.int32)
    earlier = (owners[None, :] == owners[:, None]) & (numbers[None, :] < numbers[:, None])
    return owners * slot_count + jnp.sum(earlier.astype(jnp.int32), axis=1)


def slot_rates(inverse, piece_rows, model_width, hidden_units):
    first_row = (inverse - 1) * piece_rows
    narrow = model_width ** (-0.5)
    step_rate = jnp.where(
        first_row < 3 * model_width,
        narrow,
        jnp.where(
            first_row < 4 * model_width,
            OUT_RATE,
            jnp.where(
                first_row < 4 * model_width + 2 * hidden_units, narrow, hidden_units ** (-0.5)
            ),
        ),
    )
    return jnp.where(inverse > 0, step_rate, narrow).astype(jnp.float32)


def adamw_step(weight, first_moment, second, gradient, step_rate, step_count):
    first_moment = BETA_ONE * first_moment + (1.0 - BETA_ONE) * gradient
    second = BETA_TWO * second + (1.0 - BETA_TWO) * gradient * gradient
    mean_hat = first_moment / (1.0 - BETA_ONE**step_count)
    square_hat = second / (1.0 - BETA_TWO**step_count)
    weight = weight - step_rate * (mean_hat / (jnp.sqrt(square_hat) + ADAM_EPS) + DECAY * weight)
    return (first_moment, second, weight)


def dot_nt(left_side, right_side):
    return lax.dot_general(
        left_side, right_side, (((1,), (1,)), ((), ())), preferred_element_type=F32
    )


def dot_nn(left_side, right_side):
    return lax.dot_general(
        left_side, right_side, (((1,), (0,)), ((), ())), preferred_element_type=F32
    )


def dot_tn(left_side, right_side):
    return lax.dot_general(
        left_side, right_side, (((0,), (0,)), ((), ())), preferred_element_type=F32
    )


def fetch_piece(place, piece, weights, dst, sem):
    pltpu.make_async_copy(weights.at[place[piece]], dst, sem).start()


def fill_tables(table, slopes, group, tok):
    apart = lax.broadcasted_iota(jnp.int32, (tok, tok), 0) - lax.broadcasted_iota(
        jnp.int32, (tok, tok), 1
    )
    apart = apart.astype(F32)
    for h in range(TRIO):
        slope = slopes[group * TRIO + h]
        table[h * 3 + 0] = -slope * apart
        table[h * 3 + 1] = slope * jnp.abs(apart)
        table[h * 3 + 2] = slope * apart


def block_place(order, n_dp, reps):
    return (order % n_dp) * reps + order // n_dp


def bias_of(key_block, query_place, slope, h, tok, n_dp, reps):
    key_place = block_place(key_block, n_dp, reps)
    which = jnp.where(key_place > query_place, 2, jnp.where(key_place < query_place, 0, 1))
    shift = slope * (tok * jnp.abs(key_place - query_place)).astype(F32)
    return h * 3 + which, shift


def holder(order, n_dp):
    dp = lax.rem(order, n_dp)
    return {"b": lax.div(order, n_dp), "y": lax.div(dp, 2), "core": lax.rem(dp, 2)}


def turn_to():
    z, dp = lax.axis_index("a"), lax.axis_index("y") * 2 + lax.axis_index("core")
    return {"a": dp, "y": lax.div(z, 2), "core": lax.rem(z, 2)}, dp != z


def start_turn(src, dst, send_sem, recv_sem):
    peer, moves = turn_to()

    @pl.when(moves)
    def _():
        pltpu.make_async_remote_copy(
            src_ref=src,
            dst_ref=dst,
            send_sem=send_sem,
            recv_sem=recv_sem,
            device_id=peer,
            device_id_type=MESH_IDS,
        ).start()

    @pl.when(jnp.logical_not(moves))
    def _():
        pltpu.make_async_copy(src, dst, recv_sem).start()


def finish_turn(src, dst, send_sem, recv_sem):
    peer, moves = turn_to()

    @pl.when(moves)
    def _():
        pltpu.make_async_remote_copy(
            src_ref=src,
            dst_ref=dst,
            send_sem=send_sem,
            recv_sem=recv_sem,
            device_id=peer,
            device_id_type=MESH_IDS,
        ).wait()

    @pl.when(jnp.logical_not(moves))
    def _():
        pltpu.make_async_copy(src, dst, recv_sem).wait()


def greet(peers, turning=False):
    barrier = pltpu.get_barrier_semaphore()
    for peer in peers:
        pl.semaphore_signal(barrier, inc=1, device_id=peer, device_id_type=MESH_IDS)
    if not turning:
        pl.semaphore_wait(barrier, len(peers))
        return
    turn_peer, moves = turn_to()

    @pl.when(moves)
    def _():
        pl.semaphore_signal(barrier, inc=1, device_id=turn_peer, device_id_type=MESH_IDS)

    pl.semaphore_wait(barrier, len(peers) + moves.astype(jnp.int32))


def my_order(n_dp):
    return lax.axis_index("b") * n_dp + lax.axis_index("y") * 2 + lax.axis_index("core")


def remote(src, dst, sems, index, peer):
    return pltpu.make_async_remote_copy(
        src_ref=src,
        dst_ref=dst,
        send_sem=sems.at[0, index],
        recv_sem=sems.at[1, index],
        device_id=peer,
        device_id_type=MESH_IDS,
    )


def project_kernel(
    sizes,
    place,
    x_ref,
    weights,
    q_out,
    k_out,
    kt_out,
    v_out,
    vt_out,
    wpad,
    sems,
):
    n_dp, splits, tok, head, blocks = sizes
    order = my_order(n_dp)
    group, split = lax.div(order, splits), lax.rem(order, splits)
    per_head = head // 16
    width = x_ref.shape[2]
    kind_pieces = width // 16

    def spot(step):
        kind = lax.div(step, TRIO * per_head)
        rest = lax.rem(step, TRIO * per_head)
        dst = wpad.at[
            kind * TRIO + lax.div(rest, per_head), pl.ds(lax.rem(rest, per_head) * 16, 16)
        ]
        return kind * kind_pieces + group * (TRIO * per_head) + rest, dst

    def start(step, carry):
        number, dst = spot(step)
        fetch_piece(place, number, weights, dst, sems.at[step])
        return carry

    def finish(step, carry):
        pltpu.make_async_copy(weights.at[0], spot(step)[1], sems.at[step]).wait()
        return carry

    lax.fori_loop(0, 3 * TRIO * per_head, start, None, unroll=6)
    for row in range(3 * TRIO):
        wpad[row, head:, :] = jnp.zeros((wpad.shape[1] - head, width), BF16)
    lax.fori_loop(0, 3 * TRIO * per_head, finish, None)

    w_query = wpad[0:TRIO].reshape(TRIO * 128, width)
    w_key = wpad[TRIO : 2 * TRIO].reshape(TRIO * 128, width)
    w_value = wpad[2 * TRIO : 3 * TRIO].reshape(TRIO * 128, width)

    def marks_of(block):
        segs = x_ref[block, tok : tok + 1, 0:tok].astype(F32)
        number = lax.broadcasted_iota(jnp.int32, (128, tok), 0) - head
        same = segs == number.astype(F32)
        used = (number >= 0) & (number < 3)
        query_marks = jnp.where(same & used, 1.0, 0.0)
        key_marks = jnp.where(used & jnp.logical_not(same), MASKED, 0.0)
        return query_marks.T.astype(BF16), key_marks.T.astype(BF16)

    def project(block, carry):
        rows = pl.ds(pl.multiple_of(block * tok, tok), tok)
        xb = x_ref[block, 0:tok, :]
        keys = dot_nt(xb, w_key)
        values = dot_nt(xb, w_value)
        marks = marks_of(block)[1]
        for h in range(TRIO):
            key = keys[:, h * 128 : (h + 1) * 128]
            value = values[:, h * 128 : (h + 1) * 128]
            k_out[h, rows, :] = key.astype(BF16) + marks
            v_out[h, rows, :] = value[:, 0:head].astype(BF16)
            kt_out[h, :, rows] = key.T[0:head].astype(BF16)
            vt_out[h, :, rows] = value.T[0:head].astype(BF16)
        return carry

    lax.fori_loop(0, blocks, project, None)

    def project_query(index, carry):
        block = index * splits + split
        rows = pl.ds(pl.multiple_of(index * tok, tok), tok)
        xb = x_ref[block, 0:tok, :]
        queries = dot_nt(xb, w_query).astype(BF16) * jnp.asarray(head**-0.5, BF16)
        marks = marks_of(block)[0]
        for h in range(TRIO):
            q_out[h, rows, :] = queries[:, h * 128 : (h + 1) * 128] + marks
        return carry

    lax.fori_loop(0, GROUPS, project_query, None)


def attend_forward_kernel(
    sizes,
    spread_sizes,
    slopes,
    q_ref,
    k_ref,
    vt_ref,
    *refs,
):
    n_dp, reps, splits, tok, head, blocks = sizes
    if spread_sizes is not None:
        own, _, mixed_full, log_out, mixed_own, every = refs[:6]
        refs = refs[6:]
    else:
        mixed_full, log_out, mixed_own = refs[:3]
        refs = refs[3:]
    table, scores, mixed_low, swap_sems = refs[:4]
    order = my_order(n_dp)
    group, split = lax.div(order, splits), lax.rem(order, splits)
    others = [lax.rem(group + k, GROUPS) for k in range(1, GROUPS)]
    peers = [holder(other * splits + split, n_dp) for other in others]
    steps, started = [], []
    more_peers = []
    if spread_sizes is not None:
        more_peers, steps = spread_steps(spread_sizes, own, every, refs[4:])
    greet(peers + more_peers)
    steps = list(steps)
    if steps:
        steps.pop(0)()
    fill_tables(table, slopes, group, tok)

    def attend(index, h):
        place_order = index * splits + split
        query_place = lax.rem(place_order, n_dp) * reps + lax.div(place_order, n_dp)
        slope = slopes[group * TRIO + h]
        qh = q_ref[h, pl.ds(pl.multiple_of(index * tok, tok), tok), :]
        top = None
        shifts = []
        for kb in range(blocks):
            which, shift = bias_of(kb, query_place, slope, h, tok, n_dp, reps)
            now = dot_nt(k_ref[h, kb * tok : (kb + 1) * tok, :], qh) - table[which]
            scores[kb] = now
            here = jnp.max(now, axis=0, keepdims=True) - shift
            top = here if top is None else jnp.maximum(top, here)
            shifts.append(shift)
        total = jnp.zeros((1, tok), F32)
        for kb in range(blocks):
            grown = jnp.exp(scores[kb] - (top + shifts[kb]))
            total = total + jnp.sum(grown, axis=0, keepdims=True)
            scores[kb] = grown
        inverse = 1.0 / total
        mixed = jnp.zeros((head, tok), F32)
        for kb in range(blocks):
            prob = (scores[kb] * inverse).astype(BF16)
            mixed = mixed + dot_nn(vt_ref[h, :, kb * tok : (kb + 1) * tok], prob)
        mixed_full[index, h] = mixed
        mixed_low[index, h] = mixed.astype(BF16)
        log_out[index, h] = top + jnp.log(total)

    for k in list(range(GROUPS - 1)) + [None]:
        index = group if k is None else others[k]

        def one(h, carry, index=index):
            attend(index, h)
            return carry

        lax.fori_loop(0, TRIO, one, None)
        if k is not None:
            copy = swap_copy(mixed_low, mixed_own, index, group, swap_sems, k, peers[k])
            copy.start()
            started.append(copy)
        else:
            mixed_own[group] = mixed_low[group]
        for _ in range(2):
            if steps:
                steps.pop(0)()
    for step in steps:
        step()
    for copy in started:
        copy.wait()


def swap_copy(src, dst, there, here, sems, index, peer):
    return pltpu.make_async_remote_copy(
        src_ref=src.at[there],
        dst_ref=dst.at[here],
        send_sem=sems.at[0, index],
        recv_sem=sems.at[1, index],
        device_id=peer,
        device_id_type=MESH_IDS,
    )


def attend_backward_kernel(
    sizes,
    reduce_sizes,
    slopes,
    q_ref,
    k_ref,
    kt_ref,
    v_ref,
    mixed_full,
    log_in,
    d_mixed,
    low_in,
    *refs,
):
    n_dp, reps, splits, tok, head, blocks = sizes
    if reduce_sizes is not None:
        grads, own_ref, low_out, total_out = refs[:4]
        refs = refs[4:]
    else:
        own_ref, low_out = refs[:2]
        refs = refs[2:]
    dk_sum, dv_sum, table, d_blocks, shared, pairs, landed = refs[:7]
    swap_sems, query_sems, pair_sems, value_sems, turn_sems = refs[7:12]
    order = my_order(n_dp)
    group, split = lax.div(order, splits), lax.rem(order, splits)
    twins = [lax.rem(split + k, splits) for k in range(1, splits)]
    twin_ids = [holder(group * splits + other, n_dp) for other in twins]
    others = [lax.rem(group + k, GROUPS) for k in range(1, GROUPS)]
    peers = [holder(other * splits + split, n_dp) for other in others]
    more_peers, steps = [], []
    if reduce_sizes is not None:
        more_peers, steps = reduce_steps(reduce_sizes, grads, total_out, refs[12:])
    greet(twin_ids + peers + more_peers, True)
    turn_refs = (low_in, low_out, turn_sems.at[0], turn_sems.at[1])
    started = []

    def launch(copy):
        copy.start()
        started.append(copy)

    def advance(count):
        for _ in range(count):
            if steps:
                steps.pop(0)()

    for k in range(GROUPS - 1):
        launch(remote(d_mixed.at[others[k]], d_blocks.at[group], swap_sems, k, peers[k]))
    start_turn(*turn_refs)
    d_blocks[group] = d_mixed[group]
    fill_tables(table, slopes, group, tok)
    advance(2)
    dk_sum[...] = jnp.zeros_like(dk_sum)
    dv_sum[...] = jnp.zeros_like(dv_sum)

    def step_fn(h, step):
        index = lax.rem(group + GROUPS - step, GROUPS)
        if h == 0:

            @pl.when(step > 0)
            def _():
                view = d_blocks.at[index]
                remote(view, view, swap_sems, step - 1, peers[0]).wait_recv()

        place_order = index * splits + split
        query_place = lax.rem(place_order, n_dp) * reps + lax.div(place_order, n_dp)
        slope = slopes[group * TRIO + h]
        qh = q_ref[h, pl.ds(pl.multiple_of(index * tok, tok), tok), :]
        dt = d_blocks[index, h]
        row_dot = jnp.sum(dt.astype(F32) * mixed_full[index, h], axis=0, keepdims=True)
        log_total = log_in[index, h]
        dq = jnp.zeros((head, tok), F32)
        for kb in range(blocks):
            rows = slice(kb * tok, (kb + 1) * tok)
            which, shift = bias_of(kb, query_place, slope, h, tok, n_dp, reps)
            now = dot_nt(k_ref[h, rows, :], qh) - table[which]
            prob = jnp.exp(now - (log_total + shift))
            d_prob = dot_nn(v_ref[h, rows, :], dt)
            d_score = (prob * (d_prob - row_dot)).astype(BF16)
            dv_sum[rows, :] += dot_nt(prob.astype(BF16), dt)
            dk_sum[rows, :] += dot_nn(d_score, qh)
            dq = dq + dot_nn(kt_ref[h, :, rows], d_score)
        shared[index, 0, h] = (dq * (head**-0.5)).astype(BF16)

    def pair_copy(h, k):
        return remote(
            pairs.at[h, twins[k]], landed.at[h, k], pair_sems, h * (splits - 1) + k, twin_ids[k]
        )

    def take_pairs(h):
        for k in range(splits - 1):
            pair_copy(h, k).wait_recv()
        for index in range(GROUPS):
            for kind in range(2):
                total = pairs[h, split, index, kind].astype(F32)
                for k in range(splits - 1):
                    total = total + landed[h, k, index, kind].astype(F32)
                shared[index, kind + 1, h] = total.astype(BF16)
        for k in range(GROUPS - 1):
            launch(
                remote(
                    shared.at[others[k], pl.ds(1, 2), h],
                    own_ref.at[group, pl.ds(1, 2), h],
                    value_sems,
                    h * (GROUPS - 1) + k,
                    peers[k],
                )
            )

    for h in range(TRIO):

        def one(step, carry, h=h):
            step_fn(h, step)
            return carry

        lax.fori_loop(0, GROUPS // 2, one, None)
        advance(2)
        lax.fori_loop(GROUPS // 2, GROUPS, one, None)
        advance(1)
        for k in range(GROUPS - 1):
            launch(
                remote(
                    shared.at[others[k], 0, h],
                    own_ref.at[group, 0, h],
                    query_sems,
                    h * (GROUPS - 1) + k,
                    peers[k],
                )
            )

        def flip(index, carry, h=h):
            for part in range(splits):
                rows = pl.ds(pl.multiple_of((index * splits + part) * tok, tok), tok)
                pairs[h, part, index, 0] = dk_sum[rows, :].T[0:head].astype(BF16)
                pairs[h, part, index, 1] = dv_sum[rows, :].T.astype(BF16)
            return carry

        lax.fori_loop(0, GROUPS, flip, None)
        if h + 1 < TRIO:
            dk_sum[...] = jnp.zeros_like(dk_sum)
            dv_sum[...] = jnp.zeros_like(dv_sum)
        for k in range(splits - 1):
            launch(pair_copy(h, k))
        if h > 0:
            take_pairs(h - 1)
        advance(1)
    take_pairs(TRIO - 1)
    advance(len(steps))
    own_ref[group] = shared[group]
    for h in range(TRIO):
        for k in range(GROUPS - 1):
            view = own_ref.at[others[k], 0, h]
            remote(view, view, query_sems, h * (GROUPS - 1) + k, peers[k]).wait_recv()
            view = own_ref.at[others[k], pl.ds(1, 2), h]
            remote(view, view, value_sems, h * (GROUPS - 1) + k, peers[k]).wait_recv()
    finish_turn(*turn_refs)
    for copy in started:
        copy.wait_send()


def norm_stats(values_in):
    mean = jnp.mean(values_in, axis=-1, keepdims=True)
    centred = values_in - mean
    spread = jnp.mean(centred * centred, axis=-1, keepdims=True)
    scale = lax.rsqrt(spread + NORM_EPS)
    return centred * scale, scale


def norm_back(unit, scale, gain, cotangent):
    d_unit = cotangent * gain
    first = jnp.mean(d_unit, axis=-1, keepdims=True)
    second = jnp.mean(d_unit * unit, axis=-1, keepdims=True)
    d_in = scale * (d_unit - first - unit * second)
    d_gain = jnp.sum(cotangent * unit, axis=0, keepdims=True)
    d_bias = jnp.sum(cotangent, axis=0, keepdims=True)
    return d_in, d_gain, d_bias


def dense_kernel(
    sizes,
    place,
    x_ref,
    cot_ref,
    mixed_ref,
    norm_ref,
    weights,
    out_ref,
    d_pre_one_ref,
    d_mixed_ref,
    norm_grad,
    grads,
    w_out,
    w_gate,
    w_up,
    w_down,
    keep_gate,
    keep_up,
    keep_hidden,
    stage,
    stage_out,
    load_sems,
    store_sems,
):
    tok, piece, kind_pieces, chunk_pieces, hidden_pieces = sizes
    first_gate = 4 * kind_pieces
    first_up = first_gate + hidden_pieces
    first_down = first_up + hidden_pieces
    bases = (first_gate, first_up, first_down)
    buffers = (w_gate, w_up, w_down)
    chunk = chunk_pieces * piece

    def load_out(step, carry):
        fetch_piece(
            place,
            3 * kind_pieces + step,
            weights,
            w_out.at[pl.ds(step * piece, piece)],
            load_sems.at[3 * CHUNKS],
        )
        return carry

    def load_chunk(c):
        def one(step, carry):
            for kind in range(3):
                fetch_piece(
                    place,
                    bases[kind] + c * chunk_pieces + step,
                    weights,
                    buffers[kind].at[c, pl.ds(step * piece, piece)],
                    load_sems.at[kind * CHUNKS + c],
                )
            return carry

        lax.fori_loop(0, chunk_pieces, one, None, unroll=4)

    def wait_chunk(c):
        for kind in range(3):
            view = buffers[kind].at[c]
            pltpu.make_async_copy(view, view, load_sems.at[kind * CHUNKS + c]).wait()

    lax.fori_loop(0, kind_pieces, load_out, None, unroll=8)
    load_chunk(0)
    load_chunk(1)
    mixed = mixed_ref[...].T
    pltpu.make_async_copy(w_out, w_out, load_sems.at[3 * CHUNKS]).wait()
    pre_one = x_ref[...].astype(F32) + dot_nt(mixed, w_out[...])
    unit_one, scale_one = norm_stats(pre_one)
    h_one = unit_one * norm_ref[0:1, :] + norm_ref[1:2, :]
    h_low = h_one.astype(BF16)

    def forward(c, pre_two):
        @pl.when(c + 2 < CHUNKS)
        def _():
            load_chunk(c + 2)

        wait_chunk(c)
        gate = dot_nt(h_low, w_gate[c])
        up = dot_nt(h_low, w_up[c])
        below = 0.5 * (1.0 + lax.erf(gate * (0.5**0.5)))
        gelu = gate * below
        slope = below + gate * (jnp.exp(-0.5 * gate * gate) * (0.5 / jnp.pi) ** 0.5)
        hidden = (gelu * up).astype(BF16)
        keep_gate[c] = up * slope
        keep_up[c] = gelu
        keep_hidden[c] = hidden
        return pre_two + dot_nn(hidden, w_down[c])

    pre_two = lax.fori_loop(0, CHUNKS, forward, h_one)
    unit_two, scale_two = norm_stats(pre_two)
    out_ref[...] = (unit_two * norm_ref[2:3, :] + norm_ref[3:4, :]).astype(BF16)
    d_pre_two, d_gain_two, d_bias_two = norm_back(
        unit_two, scale_two, norm_ref[2:3, :], cot_ref[...].astype(F32)
    )
    d_branch = d_pre_two.astype(BF16)

    def drain(slot):
        for kind in range(3):
            view = stage.at[slot, kind]
            pltpu.make_async_copy(view, view, store_sems.at[slot * 3 + kind]).wait()

    def backward(c, d_h):
        slot = lax.rem(c, 2)

        @pl.when(c >= 2)
        def _():
            drain(slot)

        d_hidden = dot_nt(d_branch, w_down[c])
        d_gate = (d_hidden * keep_gate[c]).astype(BF16)
        d_up = (d_hidden * keep_up[c]).astype(BF16)
        stage[slot, 0] = dot_tn(d_gate, h_low).astype(BF16)
        stage[slot, 1] = dot_tn(d_up, h_low).astype(BF16)
        stage[slot, 2] = dot_tn(keep_hidden[c], d_branch).astype(BF16)

        def store(step, carry):
            for kind in range(3):
                pltpu.make_async_copy(
                    stage.at[slot, kind, pl.ds(step * piece, piece)],
                    grads.at[place[bases[kind] + c * chunk_pieces + step]],
                    store_sems.at[slot * 3 + kind],
                ).start()
            return carry

        lax.fori_loop(0, chunk_pieces, store, None, unroll=4)
        return d_h + dot_nn(d_gate, w_gate[c]) + dot_nn(d_up, w_up[c])

    d_h = lax.fori_loop(0, CHUNKS, backward, d_pre_two)
    d_pre_one, d_gain_one, d_bias_one = norm_back(unit_one, scale_one, norm_ref[0:1, :], d_h)
    d_pre_one_ref[...] = d_pre_one
    d_proj = d_pre_one.astype(BF16)
    d_mixed_ref[...] = lax.dot_general(
        w_out[...], d_proj, (((0,), (1,)), ((), ())), preferred_element_type=F32
    ).astype(BF16)
    stage_out[...] = dot_tn(d_proj, mixed).astype(BF16)

    def store_out(step, carry):
        pltpu.make_async_copy(
            stage_out.at[pl.ds(step * piece, piece)],
            grads.at[place[3 * kind_pieces + step]],
            store_sems.at[6],
        ).start()
        return carry

    lax.fori_loop(0, kind_pieces, store_out, None, unroll=8)
    norm_grad[...] = jnp.concatenate(
        [
            d_gain_one,
            d_bias_one,
            d_gain_two,
            d_bias_two,
            jnp.zeros((4, d_gain_one.shape[1]), F32),
        ],
        axis=0,
    )
    drain(CHUNKS % 2)
    drain((CHUNKS + 1) % 2)
    pltpu.make_async_copy(stage_out, stage_out, store_sems.at[6]).wait()


def project_grad_kernel(
    sizes,
    place,
    x_ref,
    d_own,
    d_pre_one,
    weights,
    grads_in,
    d_input,
    grads,
    w_all,
    stage,
    load_sems,
    store_sems,
):
    piece, kind_pieces = sizes
    group_pieces = kind_pieces // GROUPS
    rows = 3 * group_pieces * piece
    del grads_in

    def each(group, act):
        def one(step, carry):
            for kind in range(3):
                act(kind * kind_pieces + group * group_pieces + step, kind * group_pieces + step)
            return carry

        lax.fori_loop(0, group_pieces, one, None, unroll=4)

    for group in range(GROUPS):

        def load(number, row, group=group):
            dst = w_all.at[group, pl.ds(row * piece, piece)]
            fetch_piece(place, number, weights, dst, load_sems.at[group])

        each(group, load)
    x_own = x_ref[...]
    for group in range(GROUPS):
        stage[group] = dot_nn(d_own[group], x_own).astype(BF16)

        def store(number, row, group=group):
            src = stage.at[group, pl.ds(row * piece, piece)]
            pltpu.make_async_copy(src, grads.at[place[number]], store_sems.at[group]).start()

        each(group, store)
    total = d_pre_one[...]
    for group in range(GROUPS):
        view = w_all.at[group]
        pltpu.make_async_copy(view, view, load_sems.at[group]).wait()
        total = total + dot_tn(d_own[group], w_all[group])
    d_input[...] = total.astype(BF16)
    for group in range(GROUPS):
        view = stage.at[group]
        pltpu.make_async_copy(view, view, store_sems.at[group]).wait()


def add_low(dst, src, rows):
    def one(i, carry):
        dst[i] = (dst[i].astype(F32) + src[i].astype(F32)).astype(BF16)
        return carry

    lax.fori_loop(0, rows, one, None)


def z_order_of(count):
    order = [0]
    for k in range(1, count):
        for far in (k, count - k):
            if far not in order:
                order.append(far)
    return order


def spread_steps(sizes, own, every, sems, extra=None):
    zn, xn, yn, slots, first, count, part = sizes
    z_sems, xs_sems, ys_sems, xf_sems, yf_sems, near_sems, own_sem = sems[:7]
    rest = count - part
    z, x = lax.axis_index("a"), lax.axis_index("b")
    y, core = lax.axis_index("y"), lax.axis_index("core")
    core_peer = {"core": 1 - core}
    xs, ys, z_order = range(1, xn), range(1, yn), z_order_of(zn)
    x_peers = {k: {"b": lax.rem(x + k, xn)} for k in xs}
    y_peers = {k: {"y": lax.rem(y + k, yn)} for k in ys}
    z_peers = {k: {"a": lax.rem(z + k, zn)} for k in range(1, zn)}
    source = own.at[pl.ds(first, count)]

    def number(jz, jx, jy):
        chip = (lax.rem(z + zn - jz, zn) * xn + lax.rem(x + xn - jx, xn)) * yn + lax.rem(
            y + yn - jy, yn
        )
        return chip * 2 + core

    def shard(jz, jx, jy, lead=0, rows=count):
        return every.at[pl.ds(number(jz, jx, jy) * slots + first + lead, rows)]

    def held(jz, jx, jy):
        return source if (jz, jx, jy) == (0, 0, 0) else shard(jz, jx, jy)

    def z_copy(jz):
        return remote(source, shard(0, 0, 0), z_sems, jz - 1, z_peers[jz])

    def xs_copy(jz, jx):
        return remote(
            held(jz, 0, 0), shard(jz, 0, 0), xs_sems, jz * (xn - 1) + jx - 1, x_peers[jx]
        )

    def ys_copy(jz, jy):
        return remote(
            held(jz, 0, 0), shard(jz, 0, 0), ys_sems, jz * (yn - 1) + jy - 1, y_peers[jy]
        )

    def cross(jz, jx, jy):
        return (jz * (xn - 1) + jx - 1) * (yn - 1) + jy - 1

    def xf_copy(jz, jx, jy):
        view = shard(jz, 0, jy, part, rest)
        return remote(view, view, xf_sems, cross(jz, jx, jy), x_peers[jx])

    def yf_copy(jz, jx, jy):
        view = shard(jz, jx, 0, 0, part)
        return remote(view, view, yf_sems, cross(jz, jx, jy), y_peers[jy])

    def near_copy(jz, jx, jy):
        return remote(
            held(jz, jx, jy),
            shard(jz, jx, jy),
            near_sems,
            (jz * xn + jx) * yn + jy,
            core_peer,
        )

    started = []

    def launch(copy):
        copy.start()
        started.append(copy)

    def send_own(jz):
        for jx in xs:
            launch(xs_copy(jz, jx))
        for jy in ys:
            launch(ys_copy(jz, jy))
        launch(near_copy(jz, 0, 0))

    def ys_copy_in(jz, jy):
        view = shard(jz, 0, jy)
        remote(view, view, ys_sems, jz * (yn - 1) + jy - 1, y_peers[jy]).wait_recv()

    def xs_copy_in(jz, jx):
        view = shard(jz, jx, 0)
        remote(view, view, xs_sems, jz * (xn - 1) + jx - 1, x_peers[jx]).wait_recv()

    def forward(jz):
        for jy in ys:
            ys_copy_in(jz, jy)
            for jx in xs:
                launch(xf_copy(jz, jx, jy))
        for jx in xs:
            xs_copy_in(jz, jx)
            for jy in ys:
                launch(yf_copy(jz, jx, jy))
        for jy in ys:
            launch(near_copy(jz, 0, jy))
        for jx in xs:
            launch(near_copy(jz, jx, 0))

    def finish(jz):
        for jx in xs:
            for jy in ys:
                view = shard(jz, jx, jy, part, rest)
                remote(view, view, xf_sems, cross(jz, jx, jy), x_peers[jx]).wait_recv()
                view = shard(jz, jx, jy, 0, part)
                remote(view, view, yf_sems, cross(jz, jx, jy), y_peers[jy]).wait_recv()
                launch(near_copy(jz, jx, jy))

    def z_in(index):
        jz = z_order[index]
        view = shard(jz, 0, 0)
        remote(view, view, z_sems, jz - 1, z_peers[jz]).wait_recv()
        if index + 1 < zn:
            launch(z_copy(z_order[index + 1]))

    own_local = pltpu.make_async_copy(source, shard(0, 0, 0), own_sem)

    def begin():
        launch(z_copy(z_order[1]))
        send_own(0)
        own_local.start()

    def advance(index):
        z_in(index)
        send_own(z_order[index])

    def end():
        finish(z_order[zn - 1])
        for jz in range(zn):
            for jx in range(xn):
                for jy in range(yn):
                    chip = lax.div(number(jz, jx, jy), 2)
                    view = every.at[pl.ds((chip * 2 + 1 - core) * slots + first, count)]
                    remote(
                        view, view, near_sems, (jz * xn + jx) * yn + jy, core_peer
                    ).wait_recv()

    def settle():
        own_local.wait()
        for copy in started:
            copy.wait_send()

    steps = [begin]
    for index in range(1, zn):
        steps.append(functools.partial(advance, index))
        steps.append(functools.partial(forward, z_order[index - 1]))
        if index >= 2:
            steps.append(functools.partial(finish, z_order[index - 2]))
    steps.append(functools.partial(forward, z_order[zn - 1]))
    steps.append(functools.partial(finish, z_order[zn - 2]))
    steps.append(end)
    steps.append(settle)
    return [core_peer, *x_peers.values(), *y_peers.values(), *z_peers.values()], steps


def block_steps(sizes, pack, gathered, crossed, sems):
    zn, xn, yn = sizes
    by_sems, bz_sems, bx_sems, bn_sems, stay_sem = sems
    z, x = lax.axis_index("a"), lax.axis_index("b")
    y, core = lax.axis_index("y"), lax.axis_index("core")
    core_peer = {"core": 1 - core}
    xs, ys, z_order = range(1, xn), range(1, yn), z_order_of(zn)
    x_peers = {k: {"b": lax.rem(x + k, xn)} for k in xs}
    y_peers = {k: {"y": lax.rem(y + k, yn)} for k in ys}
    z_peers = {k: {"a": lax.rem(z + k, zn)} for k in range(1, zn)}
    hosts = lax.rem(z, 2) == core

    def block(jz, jx=0):
        return gathered.at[lax.rem(x + xn - jx, xn) * zn + lax.rem(z + zn - jz, zn)]

    def by_copy(jy):
        return remote(pack, crossed.at[jy - 1], by_sems, jy - 1, y_peers[jy])

    def plane(jy):
        return lax.rem(y + yn - jy, yn) * 2 + core

    def bz_copy(jy):
        src = pack if jy == 0 else crossed.at[jy - 1]
        far = lax.rem(plane(jy) + zn - z, zn)
        return remote(src, block(0), bz_sems, far, {"a": plane(jy)})

    def stay_copy(jy):
        src = pack if jy == 0 else crossed.at[jy - 1]
        return pltpu.make_async_copy(src, block(0), stay_sem)

    def bx_copy(jz, jx):
        return remote(block(jz), block(jz), bx_sems, jz * (xn - 1) + jx - 1, x_peers[jx])

    def bn_copy(jz, jx):
        return remote(block(jz, jx), block(jz, jx), bn_sems, jz * xn + jx, core_peer)

    def cross_y():
        for jy in ys:
            by_copy(jy).start()

    def to_planes():
        for jy in range(yn):
            if jy != 0:
                by_copy(jy).wait_recv()

            @pl.when(plane(jy) != z)
            def _():
                bz_copy(jy).start()

            @pl.when(plane(jy) == z)
            def _():
                stay_copy(jy).start()
                stay_copy(jy).wait()

    def across():
        @pl.when(hosts)
        def _():
            for jz in z_order:
                if jz != 0:
                    remote(block(jz), block(jz), bz_sems, jz, z_peers[jz]).wait_recv()
                for jx in xs:
                    bx_copy(jz, jx).start()
                bn_copy(jz, 0).start()

    def end():
        @pl.when(hosts)
        def _():
            for jz in z_order:
                for jx in xs:
                    view = block(jz, jx)
                    index = jz * (xn - 1) + jx - 1
                    remote(view, view, bx_sems, index, x_peers[jx]).wait_recv()
                    bn_copy(jz, jx).start()
            for jz in z_order:
                for jx in xs:
                    bx_copy(jz, jx).wait_send()
                for jx in range(xn):
                    bn_copy(jz, jx).wait_send()

        @pl.when(jnp.logical_not(hosts))
        def _():
            for jz in range(zn):
                for jx in range(xn):
                    bn_copy(jz, jx).wait_recv()

        for jy in range(yn):

            @pl.when(plane(jy) != z)
            def _():
                bz_copy(jy).wait_send()

        for jy in ys:
            by_copy(jy).wait_send()

    return [cross_y, to_planes, across, end]


def spread_kernel(sizes, own, pack, every, gathered, crossed, *sems):
    peers, steps = spread_steps(sizes, own, every, sems[:7])
    cross_y, to_planes, across, end = block_steps(sizes[:3], pack, gathered, crossed, sems[7:])
    greet(peers)
    steps[0]()
    cross_y()
    for step in steps[1:-4]:
        step()
    to_planes()
    steps[-4]()
    across()
    steps[-3]()
    steps[-2]()
    end()
    steps[-1]()


def reduce_steps(sizes, grads, total_out, refs):
    zn, xn, yn, slots, lead, count, part = sizes
    held, near, xd, yd, xs_in, ys_in, zs_in = refs[:7]
    load_sems, near_sems, xd_sems, yd_sems, xs_sems, ys_sems, zs_sems = refs[7:14]
    rest = count - part
    z, x = lax.axis_index("a"), lax.axis_index("b")
    y, core = lax.axis_index("y"), lax.axis_index("core")
    core_peer = {"core": 1 - core}
    xs, ys = range(1, xn), range(1, yn)
    y_peers = [{"y": lax.rem(y + k, yn)} for k in ys]
    x_peers = [{"b": lax.rem(x + k, xn)} for k in xs]
    z_peers = [{"a": lax.rem(z + k, zn)} for k in range(1, zn)]
    def flat(jz, jx, jy):
        return (jz * xn + jx) * yn + jy

    def chip_rows(jz, jx, jy, which):
        chip = (lax.rem(z + jz, zn) * xn + lax.rem(x + jx, xn)) * yn + lax.rem(y + jy, yn)
        return grads.at[pl.ds((chip * 2 + which) * slots + lead, count)]

    def near_copy(jz, jx, jy):
        index = flat(jz, jx, jy)
        return remote(chip_rows(jz, jx, jy, 1 - core), near.at[index], near_sems, index, core_peer)

    def load_copy(jz, jx, jy):
        index = flat(jz, jx, jy)
        return pltpu.make_async_copy(
            chip_rows(jz, jx, jy, core), held.at[index], load_sems.at[index]
        )

    def whole(jz, jx, jy):
        return held.at[flat(jz, jx, jy)]

    def first(jz, jx, jy):
        return held.at[flat(jz, jx, jy), pl.ds(0, part)]

    def second(jz, jx, jy):
        return held.at[flat(jz, jx, jy), pl.ds(part, rest)]

    def cross(jz, jx, jy):
        return (jz * (xn - 1) + jx - 1) * (yn - 1) + jy - 1

    def yd_copy(jz, jx, jy):
        index = cross(jz, jx, jy)
        return remote(first(jz, jx, jy), yd.at[index], yd_sems, index, y_peers[jy - 1])

    def xd_copy(jz, jx, jy):
        index = cross(jz, jx, jy)
        return remote(second(jz, jx, jy), xd.at[index], xd_sems, index, x_peers[jx - 1])

    def halves(low_half):
        return pl.ds(0, part) if low_half else pl.ds(part, rest)

    def xs_copy(jz, jx, low_half):
        index = jz * (xn - 1) + jx - 1
        return remote(
            held.at[flat(jz, jx, 0), halves(low_half)],
            xs_in.at[index, halves(low_half)],
            xs_sems,
            index * 2 + int(low_half),
            x_peers[jx - 1],
        )

    def ys_copy(jz, jy, low_half):
        index = jz * (yn - 1) + jy - 1
        return remote(
            held.at[flat(jz, 0, jy), halves(low_half)],
            ys_in.at[index, halves(low_half)],
            ys_sems,
            index * 2 + int(low_half),
            y_peers[jy - 1],
        )

    def zs_copy(jz):
        return remote(whole(jz, 0, 0), zs_in.at[jz - 1], zs_sems, jz - 1, z_peers[jz - 1])

    z_order = z_order_of(zn)[::-1]
    started = []

    def launch(copy):
        copy.start()
        started.append(copy)

    def plane(jz):
        return (
            [(jz, jx, jy) for jx in xs for jy in ys]
            + [(jz, jx, 0) for jx in xs]
            + [(jz, 0, jy) for jy in ys]
            + [(jz, 0, 0)]
        )

    def fetch(jz):
        for chip in plane(jz):
            launch(near_copy(*chip))
            load_copy(*chip).start()

    def prepare(index):
        for chip in plane(z_order[index]):
            load_copy(*chip).wait()
            near_copy(*chip).wait_recv()
            add_low(whole(*chip), near.at[flat(*chip)], count)
        if index + 1 < zn:
            fetch(z_order[index + 1])

    stages = [(index, stage) for index in range(zn) for stage in range(3)]

    def send_stage(number):
        index, stage = stages[number]
        jz = z_order[index]
        for jx in xs:
            if stage == 0:
                for jy in ys:
                    launch(xd_copy(jz, jx, jy))
            else:
                launch(xs_copy(jz, jx, stage == 2))
        for jy in ys:
            if stage == 0:
                for jx in xs:
                    launch(yd_copy(jz, jx, jy))
            else:
                launch(ys_copy(jz, jy, stage == 1))

    def take_stage(number):
        index, stage = stages[number]
        jz = z_order[index]
        if stage == 0:
            for jx in xs:
                for jy in ys:
                    yd_copy(jz, jx, jy).wait_recv()
                    add_low(first(jz, jx, 0), yd.at[cross(jz, jx, jy)], part)
                    xd_copy(jz, jx, jy).wait_recv()
                    add_low(second(jz, 0, jy), xd.at[cross(jz, jx, jy)], rest)
        else:
            for jx in xs:
                xs_copy(jz, jx, stage == 2).wait_recv()
            for jy in ys:
                ys_copy(jz, jy, stage == 1).wait_recv()

    def side_in(index):
        jz = z_order[index]

        def one(i, carry):
            total = held[flat(jz, 0, 0), i].astype(F32)
            for jx in xs:
                total = total + xs_in[jz * (xn - 1) + jx - 1, i].astype(F32)
            for jy in ys:
                total = total + ys_in[jz * (yn - 1) + jy - 1, i].astype(F32)
            if jz != 0:
                held[flat(jz, 0, 0), i] = total.astype(BF16)
            else:
                total_out[i] = total
            return carry

        lax.fori_loop(0, count, one, None)
        if jz != 0:
            launch(zs_copy(jz))

    ahead = 2

    def begin():
        fetch(z_order[0])

    def begin_stages():
        prepare(0)
        for number in range(ahead):
            send_stage(number)

    def one_stage(number):
        take_stage(number)
        later = number + ahead
        if later < len(stages):
            if stages[later][1] == 0:
                prepare(stages[later][0])
            send_stage(later)
        if stages[number][1] == 2:
            side_in(stages[number][0])

    def end():
        for jz in range(1, zn):
            zs_copy(jz).wait_recv()

        def last(i, carry):
            total = total_out[i]
            for jz in range(1, zn):
                total = total + zs_in[jz - 1, i].astype(F32)
            total_out[i] = total
            return carry

        lax.fori_loop(0, count, last, None)
        for copy in started:
            copy.wait_send()

    steps = [begin, begin_stages]
    steps += [functools.partial(one_stage, number) for number in range(len(stages))]
    steps.append(end)
    return [core_peer] + y_peers + x_peers + z_peers, steps


def norm_steps(dims, norm_in, norm_out, refs):
    zn, xn, yn = dims
    norm_core, norm_y, norm_x, norm_z, norm_sum, sems = refs
    z, x = lax.axis_index("a"), lax.axis_index("b")
    y, core = lax.axis_index("y"), lax.axis_index("core")
    rounds = [
        (norm_core, [{"core": 1 - core}]),
        (norm_y, [{"y": lax.rem(y + k, yn)} for k in range(1, yn)]),
        (norm_x, [{"b": lax.rem(x + k, xn)} for k in range(1, xn)]),
        (norm_z, [{"a": lax.rem(z + k, zn)} for k in range(1, zn)]),
    ]
    first = [sum(len(peers) for _, peers in rounds[:i]) for i in range(len(rounds))]

    def copies(i):
        buffer, peers = rounds[i]
        return [
            remote(norm_sum.at[i], buffer.at[k], sems, first[i] + k, peer)
            for k, peer in enumerate(peers)
        ]

    def begin():
        norm_sum[0] = norm_in[...]
        for copy in copies(0):
            copy.start()

    def turn_round(i):
        total = norm_sum[i]
        for k, copy in enumerate(copies(i)):
            copy.wait()
            total = total + rounds[i][0][k]
        if i + 1 == len(rounds):
            norm_out[...] = total
            return
        norm_sum[i + 1] = total
        for copy in copies(i + 1):
            copy.start()

    return [begin] + [functools.partial(turn_round, i) for i in range(len(rounds))]


def reduce_kernel(
    sizes, grads, norm_in, tokens_in, total_out, norm_out, tokens_out, *refs
):
    peers, steps = reduce_steps(sizes, grads, total_out, refs[:14])
    norms = norm_steps(sizes[:3], norm_in, norm_out, refs[14:20])
    turn_sems = refs[20]
    greet(peers, True)
    turn_refs = (tokens_in, tokens_out, turn_sems.at[0], turn_sems.at[1])
    steps[0]()
    start_turn(*turn_refs)
    for number, step in enumerate(steps[1:]):
        step()
        if number % 2 == 0 and norms:
            norms.pop(0)()
    for step in norms:
        step()
    finish_turn(*turn_refs)


def vmem():
    return pl.BlockSpec(memory_space=pltpu.VMEM)


def smem():
    return pl.BlockSpec(memory_space=pltpu.SMEM)


def anywhere():
    return pl.BlockSpec(memory_space=pl.ANY)


def shape_of(dims, kind):
    return jax.ShapeDtypeStruct(dims, kind)


def params(collective=None):
    if collective is None:
        return pltpu.CompilerParams(vmem_limit_bytes=VMEM_LIMIT)
    return pltpu.CompilerParams(
        vmem_limit_bytes=VMEM_LIMIT, collective_id=collective, has_side_effects=True
    )


def pair(count):
    return pltpu.SemaphoreType.DMA((2, max(count, 1)))


def spread_scratch(zn, xn, yn):
    return [
        pair(zn - 1),
        pair(zn * (xn - 1)),
        pair(zn * (yn - 1)),
        pair(zn * (xn - 1) * (yn - 1)),
        pair(zn * (xn - 1) * (yn - 1)),
        pair(zn * xn * yn),
        pltpu.SemaphoreType.DMA,
    ]


def reduce_scratch(zn, xn, yn, count, part, piece, width):
    def chunks(number, rows):
        return pltpu.VMEM((max(number, 1), rows, piece, width), BF16)

    n_chips, crossing = zn * xn * yn, zn * (xn - 1) * (yn - 1)
    return [
        chunks(n_chips, count),
        chunks(n_chips, count),
        chunks(crossing, count - part),
        chunks(crossing, part),
        chunks(zn * (xn - 1), count),
        chunks(zn * (yn - 1), count),
        chunks(zn - 1, count),
        pltpu.SemaphoreType.DMA((n_chips,)),
        pair(n_chips),
        pair(crossing),
        pair(crossing),
        pair(2 * zn * (xn - 1)),
        pair(2 * zn * (yn - 1)),
        pair(zn - 1),
    ]


def run_layer(dims, early, collective, own_low, pack, cotangent, location, norm_params):
    n_seq, n_dp = dims
    reps = n_seq // n_dp
    splits = n_seq // GROUPS
    slots, piece, width = own_low.shape
    tok = cotangent.shape[0]
    length = tok * n_seq
    hidden_units = (location.shape[0] * piece - 4 * width) // 3
    head = width // HEADS
    kind_pieces = width // piece
    hidden_pieces = hidden_units // piece
    chunk = hidden_units // CHUNKS
    zn, xn, yn = n_dp, reps, n_dp // 2
    all_slots = n_seq * n_dp * slots
    first_count = early if early else slots
    late = slots - first_count
    turn = [(i * n_dp + j, j * n_dp + i) for i in range(n_dp) for j in range(n_dp)]
    slopes = jnp.asarray(head_slopes(HEADS, tok, n_seq))

    first_part = first_count * 2 // 3 if early else first_count * 9 // 16
    weights, gathered, _ = pl.pallas_call(
        functools.partial(spread_kernel, (zn, xn, yn, slots, 0, first_count, first_part)),
        out_shape=(
            shape_of((all_slots, piece, width), BF16),
            shape_of((n_seq,) + pack.shape, BF16),
            shape_of((max(yn - 1, 1),) + pack.shape, BF16),
        ),
        in_specs=[anywhere(), anywhere()],
        out_specs=(anywhere(),) * 3,
        scratch_shapes=spread_scratch(zn, xn, yn)
        + [
            pair(yn - 1),
            pair(zn),
            pair(zn * (xn - 1)),
            pair(zn * xn),
            pltpu.SemaphoreType.DMA,
        ],
        compiler_params=params(collective),
    )(own_low, pack)
    weights, cotangent = lax.optimization_barrier((weights, cotangent))
    cotangent = lax.ppermute(cotangent, ("a", "y", "core"), turn)
    order = my_order(n_dp)
    tokens = lax.dynamic_index_in_dim(gathered, order, axis=0, keepdims=False)[:tok]

    attend_sizes = (n_dp, reps, splits, tok, head, n_seq)
    q_ext, k_ext, k_turned, v_rows, v_turned = pl.pallas_call(
        functools.partial(project_kernel, (n_dp, splits, tok, head, n_seq)),
        out_shape=(
            shape_of((TRIO, GROUPS * tok, 128), BF16),
            shape_of((TRIO, length, 128), BF16),
            shape_of((TRIO, head, length), BF16),
            shape_of((TRIO, length, head), BF16),
            shape_of((TRIO, head, length), BF16),
        ),
        in_specs=[smem(), vmem(), anywhere()],
        out_specs=(vmem(),) * 5,
        scratch_shapes=[
            pltpu.VMEM((3 * TRIO, 128, width), BF16),
            pltpu.SemaphoreType.DMA((3 * TRIO * (head // piece),)),
        ],
        compiler_params=params(),
    )(location, gathered, weights)

    spread_late = (zn, xn, yn, slots, first_count, late, late // 2) if late else None
    blocks_low = shape_of((GROUPS, TRIO, head, tok), BF16)
    blocks_full = shape_of((GROUPS, TRIO, head, tok), F32)
    outs = pl.pallas_call(
        functools.partial(attend_forward_kernel, attend_sizes, spread_late),
        out_shape=(blocks_full, shape_of((GROUPS, TRIO, 1, tok), F32), blocks_low)
        + ((shape_of(weights.shape, BF16),) if late else ()),
        in_specs=[smem(), vmem(), vmem(), vmem()] + [anywhere()] * (2 if late else 0),
        out_specs=(vmem(), vmem(), vmem()) + ((anywhere(),) if late else ()),
        scratch_shapes=[
            pltpu.VMEM((3 * TRIO, tok, tok), F32),
            pltpu.VMEM((n_seq, tok, tok), F32),
            pltpu.VMEM((GROUPS, TRIO, head, tok), BF16),
            pair(GROUPS - 1),
        ]
        + (spread_scratch(zn, xn, yn) if late else []),
        input_output_aliases={5: 3} if late else {},
        compiler_params=params(collective + 1),
    )(slopes, q_ext, k_ext, v_turned, *((own_low, weights) if late else ()))
    mixed_full, log_total, mixed_own = outs[:3]
    weights = outs[3] if late else weights

    out_low, d_pre_one, d_mixed, norm_part, grads = pl.pallas_call(
        functools.partial(
            dense_kernel, (tok, piece, kind_pieces, chunk // piece, hidden_pieces)
        ),
        out_shape=(
            shape_of((tok, width), BF16),
            shape_of((tok, width), F32),
            shape_of((width, tok), BF16),
            shape_of((8, width), F32),
            shape_of((all_slots, piece, width), BF16),
        ),
        in_specs=[smem(), vmem(), vmem(), vmem(), vmem(), anywhere()],
        out_specs=(vmem(), vmem(), vmem(), vmem(), anywhere()),
        scratch_shapes=[
            pltpu.VMEM((width, width), BF16),
            pltpu.VMEM((CHUNKS, chunk, width), BF16),
            pltpu.VMEM((CHUNKS, chunk, width), BF16),
            pltpu.VMEM((CHUNKS, chunk, width), BF16),
            pltpu.VMEM((CHUNKS, tok, chunk), F32),
            pltpu.VMEM((CHUNKS, tok, chunk), F32),
            pltpu.VMEM((CHUNKS, tok, chunk), BF16),
            pltpu.VMEM((2, 3, chunk, width), BF16),
            pltpu.VMEM((width, width), BF16),
            pltpu.SemaphoreType.DMA((3 * CHUNKS + 1,)),
            pltpu.SemaphoreType.DMA((7,)),
        ],
        compiler_params=params(),
    )(location, tokens, cotangent, mixed_own.reshape(width, tok), norm_params, weights)

    late_sizes = (zn, xn, yn, slots, first_count, late, late // 2) if late else None
    outs = pl.pallas_call(
        functools.partial(attend_backward_kernel, attend_sizes, late_sizes),
        out_shape=(
            shape_of((GROUPS, 3, TRIO, head, tok), BF16),
            shape_of(out_low.shape, BF16),
        )
        + ((shape_of((late, piece, width), F32),) if late else ()),
        in_specs=[smem()] + [vmem()] * 7 + [anywhere()] * (2 if late else 1),
        out_specs=(vmem(), anywhere()) + ((vmem(),) if late else ()),
        scratch_shapes=[
            pltpu.VMEM((length, 128), F32),
            pltpu.VMEM((length, head), F32),
            pltpu.VMEM((3 * TRIO, tok, tok), F32),
            pltpu.VMEM((GROUPS, TRIO, head, tok), BF16),
            pltpu.VMEM((GROUPS, 3, TRIO, head, tok), BF16),
            pltpu.VMEM((TRIO, splits, GROUPS, 2, head, tok), BF16),
            pltpu.VMEM((TRIO, splits - 1, GROUPS, 2, head, tok), BF16),
            pair(GROUPS - 1),
            pair(TRIO * (GROUPS - 1)),
            pair(TRIO * (splits - 1)),
            pair(TRIO * (GROUPS - 1)),
            pltpu.SemaphoreType.DMA((2,)),
        ]
        + (reduce_scratch(zn, xn, yn, late, late // 2, piece, width) if late else []),
        compiler_params=params(collective + 2),
    )(
        slopes,
        q_ext,
        k_ext,
        k_turned,
        v_rows,
        mixed_full,
        log_total,
        d_mixed.reshape(GROUPS, TRIO, head, tok),
        out_low,
        *((grads,) if late else ()),
    )
    d_own, result = outs[:2]

    trio_rows = TRIO * head
    d_tokens, grads = pl.pallas_call(
        functools.partial(project_grad_kernel, (piece, kind_pieces)),
        out_shape=(shape_of((tok, width), BF16), shape_of(grads.shape, BF16)),
        in_specs=[smem(), vmem(), vmem(), vmem()] + [anywhere()] * 2,
        out_specs=(vmem(), anywhere()),
        scratch_shapes=[
            pltpu.VMEM((GROUPS, 3 * trio_rows, width), BF16),
            pltpu.VMEM((GROUPS, 3 * trio_rows, width), BF16),
            pltpu.SemaphoreType.DMA((GROUPS,)),
            pltpu.SemaphoreType.DMA((GROUPS,)),
        ],
        input_output_aliases={5: 1},
        compiler_params=params(),
    )(location, tokens, d_own.reshape(GROUPS, 3 * trio_rows, tok), d_pre_one, weights, grads)

    def norm_rows(count):
        return pltpu.VMEM((max(count, 1), 8, width), F32)

    half = first_count // 2
    own_grad, norm_total, d_turned = pl.pallas_call(
        functools.partial(reduce_kernel, (zn, xn, yn, slots, 0, first_count, half)),
        out_shape=(
            shape_of((first_count, piece, width), F32),
            shape_of((8, width), F32),
            shape_of(d_tokens.shape, BF16),
        ),
        in_specs=[anywhere(), vmem(), anywhere()],
        out_specs=(vmem(), vmem(), anywhere()),
        scratch_shapes=reduce_scratch(zn, xn, yn, first_count, half, piece, width)
        + [
            norm_rows(1),
            norm_rows(yn - 1),
            norm_rows(xn - 1),
            norm_rows(zn - 1),
            norm_rows(4),
            pair(1 + (yn - 1) + (xn - 1) + (zn - 1)),
            pltpu.SemaphoreType.DMA((2,)),
        ],
        compiler_params=params(collective + 3),
    )(grads, norm_part, d_tokens)
    if late:
        own_grad = jnp.concatenate([own_grad, outs[2]], axis=0)
    return own_grad, norm_total, d_turned, result


def per_device(
    dims,
    layer_input,
    out_cotangent,
    segment_ids,
    piece_owner,
    weight_master,
    weight_first,
    weight_second,
    norm_params,
    norm_first,
    norm_second,
):
    slots, piece, width = weight_master.shape
    pieces = piece_owner.shape[0]
    tok = layer_input.shape[1]
    hidden_units = (pieces * piece - 4 * width) // 3
    location = locate_pieces(piece_owner, slots)
    own_low = weight_master.astype(BF16)
    seg_row = jnp.zeros((16, width), BF16).at[0, :tok].set(segment_ids[0].astype(BF16))
    pack = jnp.concatenate([layer_input[0], seg_row], axis=0)

    early = max(2, slots * 3 // 8)
    first_pieces = location[: 3 * width // piece]
    fits = jnp.max(first_pieces % slots) < early
    own_grad, norm_total, d_turned, result = lax.cond(
        fits,
        functools.partial(run_layer, dims, early, 1),
        functools.partial(run_layer, dims, 0, 5),
        own_low,
        pack,
        out_cotangent[0],
        location,
        norm_params,
    )

    numbers = jnp.arange(pieces, dtype=jnp.int32) + 1
    own_slots = lax.axis_index(("a", "b", "y", "core")) * slots + jnp.arange(slots)
    inverse = jnp.sum(jnp.where(location[None, :] == own_slots[:, None], numbers[None, :], 0), axis=1)
    own_grad = jnp.where((inverse > 0)[:, None, None], own_grad, 0.0)
    norm_grad = norm_total[:4]
    rates = slot_rates(inverse, piece, width, hidden_units)
    first_new, second_new, weight_new = adamw_step(
        weight_master, weight_first, weight_second, own_grad, rates[:, None, None], STEP
    )
    norm_first_new, norm_second_new, norm_new = adamw_step(
        norm_params, norm_first, norm_second, norm_grad, NORM_RATE, STEP
    )
    return (
        result[None],
        d_turned.astype(F32)[None],
        own_grad,
        first_new,
        second_new,
        weight_new,
        weight_new.astype(BF16),
        norm_grad,
        norm_first_new,
        norm_second_new,
        norm_new,
    )


def solution(mesh):
    n_seq, n_dp = mesh.shape["seq"], mesh.shape["dp"]
    inner = Mesh(
        mesh.devices.reshape(n_dp, n_seq // n_dp, n_dp // 2, 2), ("a", "b", "y", "core")
    )
    seq, dp, every = ("a", "b"), ("y", "core"), ("a", "b", "y", "core")
    block = P(dp, seq, None)
    owned = P(every, None, None)
    in_specs = (block, block, P(dp, seq), P(), owned, owned, owned, P(), P(), P())
    out_specs = (block, block, owned, owned, owned, owned, owned, P(), P(), P(), P())
    return jax.shard_map(
        functools.partial(per_device, (n_seq, n_dp)),
        mesh=inner,
        in_specs=in_specs,
        out_specs=out_specs,
        check_vma=False,
    )
```

```python
import functools

import jax
import jax.numpy as jnp
import numpy as np
from jax import lax
from jax.experimental import pallas as pl
from jax.experimental.pallas import tpu as pltpu
from jax.sharding import Mesh
from jax.sharding import PartitionSpec as P

HEADS = 12
GROUPS = 4
TRIO = HEADS // GROUPS
STEP = 4

NORM_EPS = 1e-06
BETA_ONE = 0.5
BETA_TWO = 0.5
DECAY = 0.01
ADAM_EPS = 1e-08
NORM_RATE = 0.3
OUT_RATE = 0.35
MASKED = -1e30
CHUNKS = 6
VMEM_LIMIT = 60 * 1024 * 1024
MESH_IDS = pl.DeviceIdType.MESH
F32 = jnp.float32
BF16 = jnp.bfloat16


def head_slopes(head_count, tok_rows, seq_devices):
    head_order = np.arange(head_count, dtype=np.float64)
    slopes = 8.0 / tok_rows * np.power(8.0 * seq_devices, -head_order / (head_count - 1))
    return slopes.astype(np.float32)


def locate_pieces(owners, slot_count):
    pieces = owners.shape[0]
    numbers = jnp.arange(pieces, dtype=jnp.int32)
    earlier = (owners[None, :] == owners[:, None]) & (numbers[None, :] < numbers[:, None])
    return owners * slot_count + jnp.sum(earlier.astype(jnp.int32), axis=1)


def slot_rates(inverse, piece_rows, model_width, hidden_units):
    first_row = (inverse - 1) * piece_rows
    narrow = model_width ** (-0.5)
    step_rate = jnp.where(
        first_row < 3 * model_width,
        narrow,
        jnp.where(
            first_row < 4 * model_width,
            OUT_RATE,
            jnp.where(
                first_row < 4 * model_width + 2 * hidden_units, narrow, hidden_units ** (-0.5)
            ),
        ),
    )
    return jnp.where(inverse > 0, step_rate, narrow).astype(jnp.float32)


def adamw_step(weight, first_moment, second, gradient, step_rate, step_count):
    first_moment = BETA_ONE * first_moment + (1.0 - BETA_ONE) * gradient
    second = BETA_TWO * second + (1.0 - BETA_TWO) * gradient * gradient
    mean_hat = first_moment / (1.0 - BETA_ONE**step_count)
    square_hat = second / (1.0 - BETA_TWO**step_count)
    weight = weight - step_rate * (mean_hat / (jnp.sqrt(square_hat) + ADAM_EPS) + DECAY * weight)
    return (first_moment, second, weight)


def dot_nt(left_side, right_side):
    return lax.dot_general(
        left_side, right_side, (((1,), (1,)), ((), ())), preferred_element_type=F32
    )


def dot_nn(left_side, right_side):
    return lax.dot_general(
        left_side, right_side, (((1,), (0,)), ((), ())), preferred_element_type=F32
    )


def dot_tn(left_side, right_side):
    return lax.dot_general(
        left_side, right_side, (((0,), (0,)), ((), ())), preferred_element_type=F32
    )


def fetch_piece(place, piece, weights, dst, sem):
    pltpu.make_async_copy(weights.at[place[piece]], dst, sem).start()


def fill_tables(table, slopes, group, tok):
    apart = lax.broadcasted_iota(jnp.int32, (tok, tok), 0) - lax.broadcasted_iota(
        jnp.int32, (tok, tok), 1
    )
    apart = apart.astype(F32)
    for h in range(TRIO):
        slope = slopes[group * TRIO + h]
        table[h * 3 + 0] = -slope * apart
        table[h * 3 + 1] = slope * jnp.abs(apart)
        table[h * 3 + 2] = slope * apart


def block_place(order, n_dp, reps):
    return (order % n_dp) * reps + order // n_dp


def bias_of(key_block, query_place, slope, h, tok, n_dp, reps):
    key_place = block_place(key_block, n_dp, reps)
    which = jnp.where(key_place > query_place, 2, jnp.where(key_place < query_place, 0, 1))
    shift = slope * (tok * jnp.abs(key_place - query_place)).astype(F32)
    return h * 3 + which, shift


def holder(order, n_dp):
    dp = lax.rem(order, n_dp)
    return {"b": lax.div(order, n_dp), "y": lax.div(dp, 2), "core": lax.rem(dp, 2)}


def turn_to():
    z, dp = lax.axis_index("a"), lax.axis_index("y") * 2 + lax.axis_index("core")
    return {"a": dp, "y": lax.div(z, 2), "core": lax.rem(z, 2)}, dp != z


def start_turn(src, dst, send_sem, recv_sem):
    peer, moves = turn_to()

    @pl.when(moves)
    def _():
        pltpu.make_async_remote_copy(
            src_ref=src,
            dst_ref=dst,
            send_sem=send_sem,
            recv_sem=recv_sem,
            device_id=peer,
            device_id_type=MESH_IDS,
        ).start()

    @pl.when(jnp.logical_not(moves))
    def _():
        pltpu.make_async_copy(src, dst, recv_sem).start()


def finish_turn(src, dst, send_sem, recv_sem):
    peer, moves = turn_to()

    @pl.when(moves)
    def _():
        pltpu.make_async_remote_copy(
            src_ref=src,
            dst_ref=dst,
            send_sem=send_sem,
            recv_sem=recv_sem,
            device_id=peer,
            device_id_type=MESH_IDS,
        ).wait()

    @pl.when(jnp.logical_not(moves))
    def _():
        pltpu.make_async_copy(src, dst, recv_sem).wait()


def greet(peers, turning=False):
    barrier = pltpu.get_barrier_semaphore()
    for peer in peers:
        pl.semaphore_signal(barrier, inc=1, device_id=peer, device_id_type=MESH_IDS)
    if not turning:
        pl.semaphore_wait(barrier, len(peers))
        return
    turn_peer, moves = turn_to()

    @pl.when(moves)
    def _():
        pl.semaphore_signal(barrier, inc=1, device_id=turn_peer, device_id_type=MESH_IDS)

    pl.semaphore_wait(barrier, len(peers) + moves.astype(jnp.int32))


def my_order(n_dp):
    return lax.axis_index("b") * n_dp + lax.axis_index("y") * 2 + lax.axis_index("core")


def remote(src, dst, sems, index, peer):
    return pltpu.make_async_remote_copy(
        src_ref=src,
        dst_ref=dst,
        send_sem=sems.at[0, index],
        recv_sem=sems.at[1, index],
        device_id=peer,
        device_id_type=MESH_IDS,
    )


def project_kernel(
    sizes,
    place,
    x_ref,
    weights,
    q_out,
    k_out,
    kt_out,
    v_out,
    vt_out,
    wpad,
    sems,
):
    n_dp, splits, tok, head, blocks = sizes
    order = my_order(n_dp)
    group, split = lax.div(order, splits), lax.rem(order, splits)
    per_head = head // 16
    width = x_ref.shape[2]
    kind_pieces = width // 16

    def spot(step):
        kind = lax.div(step, TRIO * per_head)
        rest = lax.rem(step, TRIO * per_head)
        dst = wpad.at[
            kind * TRIO + lax.div(rest, per_head), pl.ds(lax.rem(rest, per_head) * 16, 16)
        ]
        return kind * kind_pieces + group * (TRIO * per_head) + rest, dst

    def start(step, carry):
        number, dst = spot(step)
        fetch_piece(place, number, weights, dst, sems.at[step])
        return carry

    def finish(step, carry):
        pltpu.make_async_copy(weights.at[0], spot(step)[1], sems.at[step]).wait()
        return carry

    lax.fori_loop(0, 3 * TRIO * per_head, start, None, unroll=6)
    for row in range(3 * TRIO):
        wpad[row, head:, :] = jnp.zeros((wpad.shape[1] - head, width), BF16)
    lax.fori_loop(0, 3 * TRIO * per_head, finish, None)

    w_query = wpad[0:TRIO].reshape(TRIO * 128, width)
    w_key = wpad[TRIO : 2 * TRIO].reshape(TRIO * 128, width)
    w_value = wpad[2 * TRIO : 3 * TRIO].reshape(TRIO * 128, width)

    def marks_of(block):
        segs = x_ref[block, tok : tok + 1, 0:tok].astype(F32)
        number = lax.broadcasted_iota(jnp.int32, (128, tok), 0) - head
        same = segs == number.astype(F32)
        used = (number >= 0) & (number < 3)
        query_marks = jnp.where(same & used, 1.0, 0.0)
        key_marks = jnp.where(used & jnp.logical_not(same), MASKED, 0.0)
        return query_marks.T.astype(BF16), key_marks.T.astype(BF16)

    def project(block, carry):
        rows = pl.ds(pl.multiple_of(block * tok, tok), tok)
        xb = x_ref[block, 0:tok, :]
        keys = dot_nt(xb, w_key)
        values = dot_nt(xb, w_value)
        marks = marks_of(block)[1]
        for h in range(TRIO):
            key = keys[:, h * 128 : (h + 1) * 128]
            value = values[:, h * 128 : (h + 1) * 128]
            k_out[h, rows, :] = key.astype(BF16) + marks
            v_out[h, rows, :] = value[:, 0:head].astype(BF16)
            kt_out[h, :, rows] = key.T[0:head].astype(BF16)
            vt_out[h, :, rows] = value.T[0:head].astype(BF16)
        return carry

    lax.fori_loop(0, blocks, project, None)

    def project_query(index, carry):
        block = index * splits + split
        rows = pl.ds(pl.multiple_of(index * tok, tok), tok)
        xb = x_ref[block, 0:tok, :]
        queries = dot_nt(xb, w_query).astype(BF16) * jnp.asarray(head**-0.5, BF16)
        marks = marks_of(block)[0]
        for h in range(TRIO):
            q_out[h, rows, :] = queries[:, h * 128 : (h + 1) * 128] + marks
        return carry

    lax.fori_loop(0, GROUPS, project_query, None)


def attend_forward_kernel(
    sizes,
    slopes,
    q_ref,
    k_ref,
    vt_ref,
    mixed_full,
    log_out,
    mixed_own,
    table,
    scores,
    mixed_low,
    swap_sems,
):
    n_dp, reps, splits, tok, head, blocks = sizes
    order = my_order(n_dp)
    group, split = lax.div(order, splits), lax.rem(order, splits)
    others = [lax.rem(group + k, GROUPS) for k in range(1, GROUPS)]
    peers = [holder(other * splits + split, n_dp) for other in others]
    started = []
    greet(peers)
    fill_tables(table, slopes, group, tok)

    def attend(index, h):
        place_order = index * splits + split
        query_place = lax.rem(place_order, n_dp) * reps + lax.div(place_order, n_dp)
        slope = slopes[group * TRIO + h]
        qh = q_ref[h, pl.ds(pl.multiple_of(index * tok, tok), tok), :]
        top = None
        shifts = []
        for kb in range(blocks):
            which, shift = bias_of(kb, query_place, slope, h, tok, n_dp, reps)
            now = dot_nt(k_ref[h, kb * tok : (kb + 1) * tok, :], qh) - table[which]
            scores[kb] = now
            here = jnp.max(now, axis=0, keepdims=True) - shift
            top = here if top is None else jnp.maximum(top, here)
            shifts.append(shift)
        total = jnp.zeros((1, tok), F32)
        for kb in range(blocks):
            grown = jnp.exp(scores[kb] - (top + shifts[kb]))
            total = total + jnp.sum(grown, axis=0, keepdims=True)
            scores[kb] = grown
        inverse = 1.0 / total
        mixed = jnp.zeros((head, tok), F32)
        for kb in range(blocks):
            prob = (scores[kb] * inverse).astype(BF16)
            mixed = mixed + dot_nn(vt_ref[h, :, kb * tok : (kb + 1) * tok], prob)
        mixed_full[index, h] = mixed
        mixed_low[index, h] = mixed.astype(BF16)
        log_out[index, h] = top + jnp.log(total)

    for k in list(range(GROUPS - 1)) + [None]:
        index = group if k is None else others[k]

        def one(h, carry, index=index):
            attend(index, h)
            return carry

        lax.fori_loop(0, TRIO, one, None)
        if k is not None:
            copy = swap_copy(mixed_low, mixed_own, index, group, swap_sems, k, peers[k])
            copy.start()
            started.append(copy)
        else:
            mixed_own[group] = mixed_low[group]
    for copy in started:
        copy.wait()


def swap_copy(src, dst, there, here, sems, index, peer):
    return pltpu.make_async_remote_copy(
        src_ref=src.at[there],
        dst_ref=dst.at[here],
        send_sem=sems.at[0, index],
        recv_sem=sems.at[1, index],
        device_id=peer,
        device_id_type=MESH_IDS,
    )


def attend_backward_kernel(
    sizes,
    slopes,
    q_ref,
    k_ref,
    kt_ref,
    v_ref,
    mixed_full,
    log_in,
    d_mixed,
    low_in,
    own_ref,
    low_out,
    dk_sum,
    dv_sum,
    table,
    d_blocks,
    shared,
    pairs,
    landed,
    swap_sems,
    query_sems,
    pair_sems,
    value_sems,
    turn_sems,
):
    n_dp, reps, splits, tok, head, blocks = sizes
    order = my_order(n_dp)
    group, split = lax.div(order, splits), lax.rem(order, splits)
    twins = [lax.rem(split + k, splits) for k in range(1, splits)]
    twin_ids = [holder(group * splits + other, n_dp) for other in twins]
    others = [lax.rem(group + k, GROUPS) for k in range(1, GROUPS)]
    peers = [holder(other * splits + split, n_dp) for other in others]
    greet(twin_ids + peers, True)
    turn_refs = (low_in, low_out, turn_sems.at[0], turn_sems.at[1])
    started = []

    def launch(copy):
        copy.start()
        started.append(copy)

    for k in range(GROUPS - 1):
        launch(remote(d_mixed.at[others[k]], d_blocks.at[group], swap_sems, k, peers[k]))
    start_turn(*turn_refs)
    d_blocks[group] = d_mixed[group]
    fill_tables(table, slopes, group, tok)
    dk_sum[...] = jnp.zeros_like(dk_sum)
    dv_sum[...] = jnp.zeros_like(dv_sum)

    def step_fn(h, step):
        index = lax.rem(group + GROUPS - step, GROUPS)
        if h == 0:

            @pl.when(step > 0)
            def _():
                view = d_blocks.at[index]
                remote(view, view, swap_sems, step - 1, peers[0]).wait_recv()

        place_order = index * splits + split
        query_place = lax.rem(place_order, n_dp) * reps + lax.div(place_order, n_dp)
        slope = slopes[group * TRIO + h]
        qh = q_ref[h, pl.ds(pl.multiple_of(index * tok, tok), tok), :]
        dt = d_blocks[index, h]
        row_dot = jnp.sum(dt.astype(F32) * mixed_full[index, h], axis=0, keepdims=True)
        log_total = log_in[index, h]
        dq = jnp.zeros((head, tok), F32)
        for kb in range(blocks):
            rows = slice(kb * tok, (kb + 1) * tok)
            which, shift = bias_of(kb, query_place, slope, h, tok, n_dp, reps)
            now = dot_nt(k_ref[h, rows, :], qh) - table[which]
            prob = jnp.exp(now - (log_total + shift))
            d_prob = dot_nn(v_ref[h, rows, :], dt)
            d_score = (prob * (d_prob - row_dot)).astype(BF16)
            dv_sum[rows, :] += dot_nt(prob.astype(BF16), dt)
            dk_sum[rows, :] += dot_nn(d_score, qh)
            dq = dq + dot_nn(kt_ref[h, :, rows], d_score)
        shared[index, 0, h] = (dq * (head**-0.5)).astype(BF16)

    def pair_copy(h, k):
        return remote(
            pairs.at[h, twins[k]], landed.at[h, k], pair_sems, h * (splits - 1) + k, twin_ids[k]
        )

    def take_pairs(h):
        for k in range(splits - 1):
            pair_copy(h, k).wait_recv()
        for index in range(GROUPS):
            for kind in range(2):
                total = pairs[h, split, index, kind].astype(F32)
                for k in range(splits - 1):
                    total = total + landed[h, k, index, kind].astype(F32)
                shared[index, kind + 1, h] = total.astype(BF16)
        for k in range(GROUPS - 1):
            launch(
                remote(
                    shared.at[others[k], pl.ds(1, 2), h],
                    own_ref.at[group, pl.ds(1, 2), h],
                    value_sems,
                    h * (GROUPS - 1) + k,
                    peers[k],
                )
            )

    for h in range(TRIO):

        def one(step, carry, h=h):
            step_fn(h, step)
            return carry

        lax.fori_loop(0, GROUPS, one, None)
        for k in range(GROUPS - 1):
            launch(
                remote(
                    shared.at[others[k], 0, h],
                    own_ref.at[group, 0, h],
                    query_sems,
                    h * (GROUPS - 1) + k,
                    peers[k],
                )
            )

        def flip(index, carry, h=h):
            for part in range(splits):
                rows = pl.ds(pl.multiple_of((index * splits + part) * tok, tok), tok)
                pairs[h, part, index, 0] = dk_sum[rows, :].T[0:head].astype(BF16)
                pairs[h, part, index, 1] = dv_sum[rows, :].T.astype(BF16)
            return carry

        lax.fori_loop(0, GROUPS, flip, None)
        if h + 1 < TRIO:
            dk_sum[...] = jnp.zeros_like(dk_sum)
            dv_sum[...] = jnp.zeros_like(dv_sum)
        for k in range(splits - 1):
            launch(pair_copy(h, k))
        if h > 0:
            take_pairs(h - 1)
    take_pairs(TRIO - 1)
    own_ref[group] = shared[group]
    for h in range(TRIO):
        for k in range(GROUPS - 1):
            view = own_ref.at[others[k], 0, h]
            remote(view, view, query_sems, h * (GROUPS - 1) + k, peers[k]).wait_recv()
            view = own_ref.at[others[k], pl.ds(1, 2), h]
            remote(view, view, value_sems, h * (GROUPS - 1) + k, peers[k]).wait_recv()
    finish_turn(*turn_refs)
    for copy in started:
        copy.wait_send()


def norm_stats(values_in):
    mean = jnp.mean(values_in, axis=-1, keepdims=True)
    centred = values_in - mean
    spread = jnp.mean(centred * centred, axis=-1, keepdims=True)
    scale = lax.rsqrt(spread + NORM_EPS)
    return centred * scale, scale


def norm_back(unit, scale, gain, cotangent):
    d_unit = cotangent * gain
    first = jnp.mean(d_unit, axis=-1, keepdims=True)
    second = jnp.mean(d_unit * unit, axis=-1, keepdims=True)
    d_in = scale * (d_unit - first - unit * second)
    d_gain = jnp.sum(cotangent * unit, axis=0, keepdims=True)
    d_bias = jnp.sum(cotangent, axis=0, keepdims=True)
    return d_in, d_gain, d_bias


def dense_kernel(
    sizes,
    place,
    gathered,
    cot_ref,
    mixed_ref,
    norm_ref,
    weights,
    out_ref,
    d_pre_one_ref,
    d_mixed_ref,
    norm_grad,
    grads,
    w_out,
    w_gate,
    w_up,
    w_down,
    keep_gate,
    keep_up,
    keep_hidden,
    stage,
    stage_out,
    x_ref,
    load_sems,
    store_sems,
    own_sem,
):
    n_dp, tok, piece, kind_pieces, chunk_pieces, hidden_pieces = sizes
    own_copy = pltpu.make_async_copy(
        gathered.at[my_order(n_dp), pl.ds(0, tok)], x_ref, own_sem
    )
    own_copy.start()
    first_gate = 4 * kind_pieces
    first_up = first_gate + hidden_pieces
    first_down = first_up + hidden_pieces
    bases = (first_gate, first_up, first_down)
    buffers = (w_gate, w_up, w_down)
    chunk = chunk_pieces * piece

    def load_out(step, carry):
        fetch_piece(
            place,
            3 * kind_pieces + step,
            weights,
            w_out.at[pl.ds(step * piece, piece)],
            load_sems.at[3 * CHUNKS],
        )
        return carry

    def load_chunk(c):
        def one(step, carry):
            for kind in range(3):
                fetch_piece(
                    place,
                    bases[kind] + c * chunk_pieces + step,
                    weights,
                    buffers[kind].at[c, pl.ds(step * piece, piece)],
                    load_sems.at[kind * CHUNKS + c],
                )
            return carry

        lax.fori_loop(0, chunk_pieces, one, None, unroll=4)

    def wait_chunk(c):
        for kind in range(3):
            view = buffers[kind].at[c]
            pltpu.make_async_copy(view, view, load_sems.at[kind * CHUNKS + c]).wait()

    lax.fori_loop(0, kind_pieces, load_out, None, unroll=8)
    load_chunk(0)
    load_chunk(1)
    mixed = mixed_ref[...].T
    pltpu.make_async_copy(w_out, w_out, load_sems.at[3 * CHUNKS]).wait()
    own_copy.wait()
    pre_one = x_ref[...].astype(F32) + dot_nt(mixed, w_out[...])
    unit_one, scale_one = norm_stats(pre_one)
    h_one = unit_one * norm_ref[0:1, :] + norm_ref[1:2, :]
    h_low = h_one.astype(BF16)

    def forward(c, pre_two):
        @pl.when(c + 2 < CHUNKS)
        def _():
            load_chunk(c + 2)

        wait_chunk(c)
        gate = dot_nt(h_low, w_gate[c])
        up = dot_nt(h_low, w_up[c])
        below = 0.5 * (1.0 + lax.erf(gate * (0.5**0.5)))
        gelu = gate * below
        slope = below + gate * (jnp.exp(-0.5 * gate * gate) * (0.5 / jnp.pi) ** 0.5)
        hidden = (gelu * up).astype(BF16)
        keep_gate[c] = up * slope
        keep_up[c] = gelu
        keep_hidden[c] = hidden
        return pre_two + dot_nn(hidden, w_down[c])

    pre_two = lax.fori_loop(0, CHUNKS, forward, h_one)
    unit_two, scale_two = norm_stats(pre_two)
    out_ref[...] = (unit_two * norm_ref[2:3, :] + norm_ref[3:4, :]).astype(BF16)
    d_pre_two, d_gain_two, d_bias_two = norm_back(
        unit_two, scale_two, norm_ref[2:3, :], cot_ref[...].astype(F32)
    )
    d_branch = d_pre_two.astype(BF16)

    def drain(slot):
        for kind in range(3):
            view = stage.at[slot, kind]
            pltpu.make_async_copy(view, view, store_sems.at[slot * 3 + kind]).wait()

    def backward(c, d_h):
        slot = lax.rem(c, 2)

        @pl.when(c >= 2)
        def _():
            drain(slot)

        d_hidden = dot_nt(d_branch, w_down[c])
        d_gate = (d_hidden * keep_gate[c]).astype(BF16)
        d_up = (d_hidden * keep_up[c]).astype(BF16)
        stage[slot, 0] = dot_tn(d_gate, h_low).astype(BF16)
        stage[slot, 1] = dot_tn(d_up, h_low).astype(BF16)
        stage[slot, 2] = dot_tn(keep_hidden[c], d_branch).astype(BF16)

        def store(step, carry):
            for kind in range(3):
                pltpu.make_async_copy(
                    stage.at[slot, kind, pl.ds(step * piece, piece)],
                    grads.at[place[bases[kind] + c * chunk_pieces + step]],
                    store_sems.at[slot * 3 + kind],
                ).start()
            return carry

        lax.fori_loop(0, chunk_pieces, store, None, unroll=4)
        return d_h + dot_nn(d_gate, w_gate[c]) + dot_nn(d_up, w_up[c])

    d_h = lax.fori_loop(0, CHUNKS, backward, d_pre_two)
    d_pre_one, d_gain_one, d_bias_one = norm_back(unit_one, scale_one, norm_ref[0:1, :], d_h)
    d_pre_one_ref[...] = d_pre_one
    d_proj = d_pre_one.astype(BF16)
    d_mixed_ref[...] = lax.dot_general(
        w_out[...], d_proj, (((0,), (1,)), ((), ())), preferred_element_type=F32
    ).astype(BF16)
    stage_out[...] = dot_tn(d_proj, mixed).astype(BF16)

    def store_out(step, carry):
        pltpu.make_async_copy(
            stage_out.at[pl.ds(step * piece, piece)],
            grads.at[place[3 * kind_pieces + step]],
            store_sems.at[6],
        ).start()
        return carry

    lax.fori_loop(0, kind_pieces, store_out, None, unroll=8)
    norm_grad[...] = jnp.concatenate(
        [
            d_gain_one,
            d_bias_one,
            d_gain_two,
            d_bias_two,
            jnp.zeros((4, d_gain_one.shape[1]), F32),
        ],
        axis=0,
    )
    drain(CHUNKS % 2)
    drain((CHUNKS + 1) % 2)
    pltpu.make_async_copy(stage_out, stage_out, store_sems.at[6]).wait()


def project_grad_kernel(
    sizes,
    place,
    gathered,
    d_own,
    d_pre_one,
    weights,
    grads_in,
    d_input,
    grads,
    w_all,
    stage,
    x_ref,
    load_sems,
    store_sems,
    own_sem,
):
    n_dp, tok, piece, kind_pieces = sizes
    own_copy = pltpu.make_async_copy(
        gathered.at[my_order(n_dp), pl.ds(0, tok)], x_ref, own_sem
    )
    own_copy.start()
    group_pieces = kind_pieces // GROUPS
    rows = 3 * group_pieces * piece
    del grads_in

    def each(group, act):
        def one(step, carry):
            for kind in range(3):
                act(kind * kind_pieces + group * group_pieces + step, kind * group_pieces + step)
            return carry

        lax.fori_loop(0, group_pieces, one, None, unroll=4)

    for group in range(GROUPS):

        def load(number, row, group=group):
            dst = w_all.at[group, pl.ds(row * piece, piece)]
            fetch_piece(place, number, weights, dst, load_sems.at[group])

        each(group, load)
    own_copy.wait()
    x_own = x_ref[...]
    for group in range(GROUPS):
        stage[group] = dot_nn(d_own[group], x_own).astype(BF16)

        def store(number, row, group=group):
            src = stage.at[group, pl.ds(row * piece, piece)]
            pltpu.make_async_copy(src, grads.at[place[number]], store_sems.at[group]).start()

        each(group, store)
    total = d_pre_one[...]
    for group in range(GROUPS):
        view = w_all.at[group]
        pltpu.make_async_copy(view, view, load_sems.at[group]).wait()
        total = total + dot_tn(d_own[group], w_all[group])
    d_input[...] = total.astype(BF16)
    for group in range(GROUPS):
        view = stage.at[group]
        pltpu.make_async_copy(view, view, store_sems.at[group]).wait()


def add_low(dst, src, rows):
    def one(i, carry):
        dst[i] = (dst[i].astype(F32) + src[i].astype(F32)).astype(BF16)
        return carry

    lax.fori_loop(0, rows, one, None)


def z_order_of(count):
    order = [0]
    for k in range(1, count):
        for far in (k, count - k):
            if far not in order:
                order.append(far)
    return order


def spread_steps(sizes, own, every, sems):
    zn, xn, yn, slots, last = sizes
    z_sems, xs_sems, ys_sems, xf_sems, yf_sems, near_sems, own_sem = sems[:7]
    xb_sems, yb_sems, zb_sems, nb_sems = sems[7:11]
    count = slots - last
    part = count * 9 // 16
    rest = count - part
    z, x = lax.axis_index("a"), lax.axis_index("b")
    y, core = lax.axis_index("y"), lax.axis_index("core")
    core_peer = {"core": 1 - core}
    xs, ys, z_order = range(1, xn), range(1, yn), z_order_of(zn)
    x_peers = {k: {"b": lax.rem(x + k, xn)} for k in xs}
    y_peers = {k: {"y": lax.rem(y + k, yn)} for k in ys}
    z_peers = {k: {"a": lax.rem(z + k, zn)} for k in range(1, zn)}
    source = own.at[pl.ds(0, count)]

    def number(jz, jx, jy):
        chip = (lax.rem(z + zn - jz, zn) * xn + lax.rem(x + xn - jx, xn)) * yn + lax.rem(
            y + yn - jy, yn
        )
        return chip * 2 + core

    def shard(jz, jx, jy, lead=0, rows=count):
        return every.at[pl.ds(number(jz, jx, jy) * slots + lead, rows)]

    def tail(jz, jx, jy):
        return shard(jz, jx, jy, count, last)

    def tail_held(jz, jx, jy):
        return own.at[pl.ds(count, last)] if (jz, jx, jy) == (0, 0, 0) else tail(jz, jx, jy)

    def xb_copy(jx, jy):
        index = (jx - 1) * yn + jy
        return remote(tail_held(0, 0, jy), tail(0, 0, jy), xb_sems, index, x_peers[jx])

    def yb_copy(jy):
        return remote(tail_held(0, 0, 0), tail(0, 0, 0), yb_sems, jy - 1, y_peers[jy])

    def zb_copy(jz, jx, jy):
        index = ((jz - 1) * xn + jx) * yn + jy
        return remote(tail_held(0, jx, jy), tail(0, jx, jy), zb_sems, index, z_peers[jz])

    def nb_copy(jz, jx, jy):
        index = (jz * xn + jx) * yn + jy
        return remote(tail_held(jz, jx, jy), tail(jz, jx, jy), nb_sems, index, core_peer)

    def tail_begin():
        for jy in ys:
            launch(yb_copy(jy))
        for jx in xs:
            launch(xb_copy(jx, 0))
        launch(nb_copy(0, 0, 0))

    def tail_across():
        for jy in ys:
            view = tail(0, 0, jy)
            remote(view, view, yb_sems, jy - 1, y_peers[jy]).wait_recv()
            for jx in xs:
                launch(xb_copy(jx, jy))
            launch(nb_copy(0, 0, jy))

    def tail_planes():
        for jx in xs:
            for jy in range(yn):
                view = tail(0, jx, jy)
                remote(view, view, xb_sems, (jx - 1) * yn + jy, x_peers[jx]).wait_recv()
                launch(nb_copy(0, jx, jy))
        for jz in z_order[1:]:
            for jx in range(xn):
                for jy in range(yn):
                    launch(zb_copy(jz, jx, jy))

    def tail_end():
        for jz in z_order[1:]:
            for jx in range(xn):
                for jy in range(yn):
                    view = tail(jz, jx, jy)
                    index = ((jz - 1) * xn + jx) * yn + jy
                    remote(view, view, zb_sems, index, z_peers[jz]).wait_recv()
                    launch(nb_copy(jz, jx, jy))

    def tail_settle():
        for jz in range(zn):
            for jx in range(xn):
                for jy in range(yn):
                    chip = lax.div(number(jz, jx, jy), 2)
                    view = every.at[pl.ds((chip * 2 + 1 - core) * slots + count, last)]
                    index = (jz * xn + jx) * yn + jy
                    remote(view, view, nb_sems, index, core_peer).wait_recv()

    def held(jz, jx, jy):
        return source if (jz, jx, jy) == (0, 0, 0) else shard(jz, jx, jy)

    def z_copy(jz):
        return remote(source, shard(0, 0, 0), z_sems, jz - 1, z_peers[jz])

    def xs_copy(jz, jx):
        return remote(
            held(jz, 0, 0), shard(jz, 0, 0), xs_sems, jz * (xn - 1) + jx - 1, x_peers[jx]
        )

    def ys_copy(jz, jy):
        return remote(
            held(jz, 0, 0), shard(jz, 0, 0), ys_sems, jz * (yn - 1) + jy - 1, y_peers[jy]
        )

    def cross(jz, jx, jy):
        return (jz * (xn - 1) + jx - 1) * (yn - 1) + jy - 1

    def xf_copy(jz, jx, jy):
        view = shard(jz, 0, jy, part, rest)
        return remote(view, view, xf_sems, cross(jz, jx, jy), x_peers[jx])

    def yf_copy(jz, jx, jy):
        view = shard(jz, jx, 0, 0, part)
        return remote(view, view, yf_sems, cross(jz, jx, jy), y_peers[jy])

    def near_copy(jz, jx, jy):
        return remote(
            held(jz, jx, jy),
            shard(jz, jx, jy),
            near_sems,
            (jz * xn + jx) * yn + jy,
            core_peer,
        )

    started = []

    def launch(copy):
        copy.start()
        started.append(copy)

    def send_own(jz):
        for jx in xs:
            launch(xs_copy(jz, jx))
        for jy in ys:
            launch(ys_copy(jz, jy))
        launch(near_copy(jz, 0, 0))

    def ys_copy_in(jz, jy):
        view = shard(jz, 0, jy)
        remote(view, view, ys_sems, jz * (yn - 1) + jy - 1, y_peers[jy]).wait_recv()

    def xs_copy_in(jz, jx):
        view = shard(jz, jx, 0)
        remote(view, view, xs_sems, jz * (xn - 1) + jx - 1, x_peers[jx]).wait_recv()

    def forward(jz):
        for jy in ys:
            ys_copy_in(jz, jy)
            for jx in xs:
                launch(xf_copy(jz, jx, jy))
        for jx in xs:
            xs_copy_in(jz, jx)
            for jy in ys:
                launch(yf_copy(jz, jx, jy))
        for jy in ys:
            launch(near_copy(jz, 0, jy))
        for jx in xs:
            launch(near_copy(jz, jx, 0))

    def finish(jz):
        for jx in xs:
            for jy in ys:
                view = shard(jz, jx, jy, part, rest)
                remote(view, view, xf_sems, cross(jz, jx, jy), x_peers[jx]).wait_recv()
                view = shard(jz, jx, jy, 0, part)
                remote(view, view, yf_sems, cross(jz, jx, jy), y_peers[jy]).wait_recv()
                launch(near_copy(jz, jx, jy))

    def z_in(index):
        jz = z_order[index]
        view = shard(jz, 0, 0)
        remote(view, view, z_sems, jz - 1, z_peers[jz]).wait_recv()
        if index + 1 < zn:
            launch(z_copy(z_order[index + 1]))

    own_local = pltpu.make_async_copy(own, shard(0, 0, 0, 0, slots), own_sem)

    def begin():
        launch(z_copy(z_order[1]))
        send_own(0)
        own_local.start()
        if last:
            tail_begin()

    def advance(index):
        z_in(index)
        send_own(z_order[index])
        if last and index == 1:
            tail_across()

    def forward_step(index):
        forward(z_order[index])
        if last and index == zn - 2:
            tail_planes()

    def end():
        finish(z_order[zn - 1])
        if last:
            tail_end()
            tail_settle()
        for jz in range(zn):
            for jx in range(xn):
                for jy in range(yn):
                    chip = lax.div(number(jz, jx, jy), 2)
                    view = every.at[pl.ds((chip * 2 + 1 - core) * slots, count)]
                    remote(
                        view, view, near_sems, (jz * xn + jx) * yn + jy, core_peer
                    ).wait_recv()

    def settle():
        own_local.wait()
        for copy in started:
            copy.wait_send()

    steps = [begin]
    for index in range(1, zn):
        steps.append(functools.partial(advance, index))
        steps.append(functools.partial(forward_step, index - 1))
        if index >= 2:
            steps.append(functools.partial(finish, z_order[index - 2]))
    steps.append(functools.partial(forward_step, zn - 1))
    steps.append(functools.partial(finish, z_order[zn - 2]))
    steps.append(end)
    steps.append(settle)
    return [core_peer, *x_peers.values(), *y_peers.values(), *z_peers.values()], steps


def block_steps(sizes, pack, gathered, crossed, sems):
    zn, xn, yn = sizes
    by_sems, bz_sems, bx_sems, bn_sems, stay_sem = sems
    z, x = lax.axis_index("a"), lax.axis_index("b")
    y, core = lax.axis_index("y"), lax.axis_index("core")
    core_peer = {"core": 1 - core}
    xs, ys, z_order = range(1, xn), range(1, yn), z_order_of(zn)
    x_peers = {k: {"b": lax.rem(x + k, xn)} for k in xs}
    y_peers = {k: {"y": lax.rem(y + k, yn)} for k in ys}
    z_peers = {k: {"a": lax.rem(z + k, zn)} for k in range(1, zn)}
    hosts = lax.rem(z, 2) == core

    def block(jz, jx=0):
        return gathered.at[lax.rem(x + xn - jx, xn) * zn + lax.rem(z + zn - jz, zn)]

    def by_copy(jy):
        return remote(pack, crossed.at[jy - 1], by_sems, jy - 1, y_peers[jy])

    def plane(jy):
        return lax.rem(y + yn - jy, yn) * 2 + core

    def bz_copy(jy):
        src = pack if jy == 0 else crossed.at[jy - 1]
        far = lax.rem(plane(jy) + zn - z, zn)
        return remote(src, block(0), bz_sems, far, {"a": plane(jy)})

    def stay_copy(jy):
        src = pack if jy == 0 else crossed.at[jy - 1]
        return pltpu.make_async_copy(src, block(0), stay_sem)

    def bx_copy(jz, jx):
        return remote(block(jz), block(jz), bx_sems, jz * (xn - 1) + jx - 1, x_peers[jx])

    def bn_copy(jz, jx):
        return remote(block(jz, jx), block(jz, jx), bn_sems, jz * xn + jx, core_peer)

    def cross_y():
        for jy in ys:
            by_copy(jy).start()

    def to_planes():
        for jy in range(yn):
            if jy != 0:
                by_copy(jy).wait_recv()

            @pl.when(plane(jy) != z)
            def _():
                bz_copy(jy).start()

            @pl.when(plane(jy) == z)
            def _():
                stay_copy(jy).start()
                stay_copy(jy).wait()

    def across():
        @pl.when(hosts)
        def _():
            for jz in z_order:
                if jz != 0:
                    remote(block(jz), block(jz), bz_sems, jz, z_peers[jz]).wait_recv()
                for jx in xs:
                    bx_copy(jz, jx).start()
                bn_copy(jz, 0).start()

    def end():
        @pl.when(hosts)
        def _():
            for jz in z_order:
                for jx in xs:
                    view = block(jz, jx)
                    index = jz * (xn - 1) + jx - 1
                    remote(view, view, bx_sems, index, x_peers[jx]).wait_recv()
                    bn_copy(jz, jx).start()
            for jz in z_order:
                for jx in xs:
                    bx_copy(jz, jx).wait_send()
                for jx in range(xn):
                    bn_copy(jz, jx).wait_send()

        @pl.when(jnp.logical_not(hosts))
        def _():
            for jz in range(zn):
                for jx in range(xn):
                    bn_copy(jz, jx).wait_recv()

        for jy in range(yn):

            @pl.when(plane(jy) != z)
            def _():
                bz_copy(jy).wait_send()

        for jy in ys:
            by_copy(jy).wait_send()

    return [cross_y, to_planes, across, end]


def spread_kernel(sizes, own, pack, every, gathered, crossed, *sems):
    peers, steps = spread_steps(sizes, own, every, sems[:11])
    cross_y, to_planes, across, end = block_steps(sizes[:3], pack, gathered, crossed, sems[11:])
    greet(peers)
    steps[0]()
    cross_y()
    for step in steps[1:-7]:
        step()
    to_planes()
    for step in steps[-7:-3]:
        step()
    across()
    steps[-3]()
    steps[-2]()
    end()
    steps[-1]()


def reduce_steps(sizes, grads, total_out, refs):
    zn, xn, yn, slots, last = sizes
    held, near, xd, yd, xs_in, ys_in, zs_in, xb, yb, zb = refs[:10]
    load_sems, near_sems, xd_sems, yd_sems, xs_sems, ys_sems, zs_sems = refs[10:17]
    xb_sems, yb_sems, zb_sems = refs[17:20]
    count = slots - last
    part = count // 2
    rest = count - part
    tail = pl.ds(count, last)
    z, x = lax.axis_index("a"), lax.axis_index("b")
    y, core = lax.axis_index("y"), lax.axis_index("core")
    core_peer = {"core": 1 - core}
    xs, ys = range(1, xn), range(1, yn)
    y_peers = [{"y": lax.rem(y + k, yn)} for k in ys]
    x_peers = [{"b": lax.rem(x + k, xn)} for k in xs]
    z_peers = [{"a": lax.rem(z + k, zn)} for k in range(1, zn)]
    def flat(jz, jx, jy):
        return (jz * xn + jx) * yn + jy

    def chip_rows(jz, jx, jy, which):
        chip = (lax.rem(z + jz, zn) * xn + lax.rem(x + jx, xn)) * yn + lax.rem(y + jy, yn)
        return grads.at[pl.ds((chip * 2 + which) * slots, slots)]

    def near_copy(jz, jx, jy):
        index = flat(jz, jx, jy)
        return remote(chip_rows(jz, jx, jy, 1 - core), near.at[index], near_sems, index, core_peer)

    def load_copy(jz, jx, jy):
        index = flat(jz, jx, jy)
        return pltpu.make_async_copy(
            chip_rows(jz, jx, jy, core), held.at[index], load_sems.at[index]
        )

    def whole(jz, jx, jy):
        return held.at[flat(jz, jx, jy)]

    def first(jz, jx, jy):
        return held.at[flat(jz, jx, jy), pl.ds(0, part)]

    def second(jz, jx, jy):
        return held.at[flat(jz, jx, jy), pl.ds(part, rest)]

    def cross(jz, jx, jy):
        return (jz * (xn - 1) + jx - 1) * (yn - 1) + jy - 1

    def yd_copy(jz, jx, jy):
        index = cross(jz, jx, jy)
        return remote(first(jz, jx, jy), yd.at[index], yd_sems, index, y_peers[jy - 1])

    def xd_copy(jz, jx, jy):
        index = cross(jz, jx, jy)
        return remote(second(jz, jx, jy), xd.at[index], xd_sems, index, x_peers[jx - 1])

    def halves(low_half):
        return pl.ds(0, part) if low_half else pl.ds(part, rest)

    def xs_copy(jz, jx, low_half):
        index = jz * (xn - 1) + jx - 1
        return remote(
            held.at[flat(jz, jx, 0), halves(low_half)],
            xs_in.at[index, halves(low_half)],
            xs_sems,
            index * 2 + int(low_half),
            x_peers[jx - 1],
        )

    def ys_copy(jz, jy, low_half):
        index = jz * (yn - 1) + jy - 1
        return remote(
            held.at[flat(jz, 0, jy), halves(low_half)],
            ys_in.at[index, halves(low_half)],
            ys_sems,
            index * 2 + int(low_half),
            y_peers[jy - 1],
        )

    def zs_copy(jz):
        src = held.at[flat(jz, 0, 0), pl.ds(0, count)]
        return remote(src, zs_in.at[jz - 1], zs_sems, jz - 1, z_peers[jz - 1])

    def zb_copy(jz):
        src = held.at[pl.ds(jz * xn * yn, xn * yn), tail]
        return remote(src, zb.at[jz - 1], zb_sems, jz - 1, z_peers[jz - 1])

    def xb_copy(jx):
        src = held.at[pl.ds(jx * yn, yn), tail]
        return remote(src, xb.at[jx - 1], xb_sems, jx - 1, x_peers[jx - 1])

    def yb_copy(jy):
        return remote(held.at[jy, tail], yb.at[jy - 1], yb_sems, jy - 1, y_peers[jy - 1])

    def tail_planes():
        for jz in range(1, zn):
            zb_copy(jz).wait_recv()

        def one(i, carry):
            for chip in range(xn * yn):
                total = held[chip, count + i].astype(F32)
                for jz in range(1, zn):
                    total = total + zb[jz - 1, chip, i].astype(F32)
                held[chip, count + i] = total.astype(BF16)
            return carry

        lax.fori_loop(0, last, one, None)
        for jx in xs:
            launch(xb_copy(jx))

    def tail_columns():
        for jx in xs:
            xb_copy(jx).wait_recv()
            for jy in range(yn):
                add_low(held.at[jy, tail], xb.at[jx - 1, jy], last)
        for jy in ys:
            launch(yb_copy(jy))

    def tail_end():
        for jy in ys:
            yb_copy(jy).wait_recv()

        def one(i, carry):
            total = held[0, count + i].astype(F32)
            for jy in ys:
                total = total + yb[jy - 1, i].astype(F32)
            total_out[count + i] = total
            return carry

        lax.fori_loop(0, last, one, None)

    z_order = z_order_of(zn)[::-1]
    started = []

    def launch(copy):
        copy.start()
        started.append(copy)

    def plane(jz):
        return (
            [(jz, jx, jy) for jx in xs for jy in ys]
            + [(jz, jx, 0) for jx in xs]
            + [(jz, 0, jy) for jy in ys]
            + [(jz, 0, 0)]
        )

    def fetch(jz):
        for chip in plane(jz):
            launch(near_copy(*chip))
            load_copy(*chip).start()

    def prepare(index):
        for chip in plane(z_order[index]):
            load_copy(*chip).wait()
            near_copy(*chip).wait_recv()
            add_low(whole(*chip), near.at[flat(*chip)], slots)
        if index + 1 < zn:
            fetch(z_order[index + 1])
        if last and z_order[index] != 0:
            launch(zb_copy(z_order[index]))

    stages = [(index, stage) for index in range(zn) for stage in range(3)]

    def send_stage(number):
        index, stage = stages[number]
        jz = z_order[index]
        for jx in xs:
            if stage == 0:
                for jy in ys:
                    launch(xd_copy(jz, jx, jy))
            else:
                launch(xs_copy(jz, jx, stage == 2))
        for jy in ys:
            if stage == 0:
                for jx in xs:
                    launch(yd_copy(jz, jx, jy))
            else:
                launch(ys_copy(jz, jy, stage == 1))

    def take_stage(number):
        index, stage = stages[number]
        jz = z_order[index]
        if stage == 0:
            for jx in xs:
                for jy in ys:
                    yd_copy(jz, jx, jy).wait_recv()
                    add_low(first(jz, jx, 0), yd.at[cross(jz, jx, jy)], part)
                    xd_copy(jz, jx, jy).wait_recv()
                    add_low(second(jz, 0, jy), xd.at[cross(jz, jx, jy)], rest)
        else:
            for jx in xs:
                xs_copy(jz, jx, stage == 2).wait_recv()
            for jy in ys:
                ys_copy(jz, jy, stage == 1).wait_recv()

    def side_in(index):
        jz = z_order[index]

        def one(i, carry):
            total = held[flat(jz, 0, 0), i].astype(F32)
            for jx in xs:
                total = total + xs_in[jz * (xn - 1) + jx - 1, i].astype(F32)
            for jy in ys:
                total = total + ys_in[jz * (yn - 1) + jy - 1, i].astype(F32)
            if jz != 0:
                held[flat(jz, 0, 0), i] = total.astype(BF16)
            else:
                total_out[i] = total
            return carry

        lax.fori_loop(0, count, one, None)
        if jz != 0:
            launch(zs_copy(jz))

    ahead = 2

    def begin():
        fetch(z_order[0])

    def begin_stages():
        prepare(0)
        for number in range(ahead):
            send_stage(number)

    def one_stage(number):
        for index in range(1, zn):
            if number == (index - 1 if index < 3 else 3 * (index - 2)):
                prepare(index)
        take_stage(number)
        later = number + ahead
        if later < len(stages):
            send_stage(later)
        if stages[number][1] == 2:
            side_in(stages[number][0])
        if last and number == len(stages) - 4:
            tail_planes()
        if last and number == len(stages) - 2:
            tail_columns()

    def end():
        for jz in range(1, zn):
            zs_copy(jz).wait_recv()

        def add_planes(i, carry):
            total = total_out[i]
            for jz in range(1, zn):
                total = total + zs_in[jz - 1, i].astype(F32)
            total_out[i] = total
            return carry

        lax.fori_loop(0, count, add_planes, None)
        if last:
            tail_end()
        for copy in started:
            copy.wait_send()

    steps = [begin, begin_stages]
    steps += [functools.partial(one_stage, number) for number in range(len(stages))]
    steps.append(end)
    return [core_peer] + y_peers + x_peers + z_peers, steps


def norm_steps(dims, norm_in, norm_out, refs):
    zn, xn, yn = dims
    norm_core, norm_y, norm_x, norm_z, norm_sum, sems = refs
    z, x = lax.axis_index("a"), lax.axis_index("b")
    y, core = lax.axis_index("y"), lax.axis_index("core")
    rounds = [
        (norm_core, [{"core": 1 - core}]),
        (norm_y, [{"y": lax.rem(y + k, yn)} for k in range(1, yn)]),
        (norm_x, [{"b": lax.rem(x + k, xn)} for k in range(1, xn)]),
        (norm_z, [{"a": lax.rem(z + k, zn)} for k in range(1, zn)]),
    ]
    first = [sum(len(peers) for _, peers in rounds[:i]) for i in range(len(rounds))]

    def copies(i):
        buffer, peers = rounds[i]
        return [
            remote(norm_sum.at[i], buffer.at[k], sems, first[i] + k, peer)
            for k, peer in enumerate(peers)
        ]

    def begin():
        norm_sum[0] = norm_in[...]
        for copy in copies(0):
            copy.start()

    def turn_round(i):
        total = norm_sum[i]
        for k, copy in enumerate(copies(i)):
            copy.wait()
            total = total + rounds[i][0][k]
        if i + 1 == len(rounds):
            norm_out[...] = total
            return
        norm_sum[i + 1] = total
        for copy in copies(i + 1):
            copy.start()

    return [begin] + [functools.partial(turn_round, i) for i in range(len(rounds))]


def reduce_kernel(
    sizes, grads, norm_in, tokens_in, total_out, norm_out, tokens_out, *refs
):
    peers, steps = reduce_steps(sizes, grads, total_out, refs[:20])
    norms = norm_steps(sizes[:3], norm_in, norm_out, refs[20:26])
    turn_sems = refs[26]
    greet(peers, True)
    turn_refs = (tokens_in, tokens_out, turn_sems.at[0], turn_sems.at[1])
    steps[0]()
    start_turn(*turn_refs)
    for number, step in enumerate(steps[1:]):
        step()
        if number % 2 == 0 and norms:
            norms.pop(0)()
    for step in norms:
        step()
    finish_turn(*turn_refs)


def vmem():
    return pl.BlockSpec(memory_space=pltpu.VMEM)


def smem():
    return pl.BlockSpec(memory_space=pltpu.SMEM)


def anywhere():
    return pl.BlockSpec(memory_space=pl.ANY)


def shape_of(dims, kind):
    return jax.ShapeDtypeStruct(dims, kind)


def params(collective=None):
    if collective is None:
        return pltpu.CompilerParams(vmem_limit_bytes=VMEM_LIMIT)
    return pltpu.CompilerParams(
        vmem_limit_bytes=VMEM_LIMIT, collective_id=collective, has_side_effects=True
    )


def pair(count):
    return pltpu.SemaphoreType.DMA((2, max(count, 1)))


def spread_scratch(zn, xn, yn):
    return [
        pair(zn - 1),
        pair(zn * (xn - 1)),
        pair(zn * (yn - 1)),
        pair(zn * (xn - 1) * (yn - 1)),
        pair(zn * (xn - 1) * (yn - 1)),
        pair(zn * xn * yn),
        pltpu.SemaphoreType.DMA,
        pair((xn - 1) * yn),
        pair(yn - 1),
        pair((zn - 1) * xn * yn),
        pair(zn * xn * yn),
    ]


def reduce_scratch(zn, xn, yn, slots, last, piece, width):
    def chunks(*dims):
        return pltpu.VMEM(tuple(max(dim, 1) for dim in dims) + (piece, width), BF16)

    n_chips, crossing = zn * xn * yn, zn * (xn - 1) * (yn - 1)
    count = slots - last
    part = count // 2
    return [
        chunks(n_chips, slots),
        chunks(n_chips, slots),
        chunks(crossing, count - part),
        chunks(crossing, part),
        chunks(zn * (xn - 1), count),
        chunks(zn * (yn - 1), count),
        chunks(zn - 1, count),
        chunks(xn - 1, yn, last),
        chunks(yn - 1, last),
        chunks(zn - 1, xn * yn, last),
        pltpu.SemaphoreType.DMA((n_chips,)),
        pair(n_chips),
        pair(crossing),
        pair(crossing),
        pair(2 * zn * (xn - 1)),
        pair(2 * zn * (yn - 1)),
        pair(zn - 1),
        pair(xn - 1),
        pair(yn - 1),
        pair(zn - 1),
    ]


def run_layer(dims, own_low, pack, cotangent, location, norm_params):
    n_seq, n_dp = dims
    reps = n_seq // n_dp
    splits = n_seq // GROUPS
    slots, piece, width = own_low.shape
    tok = cotangent.shape[0]
    length = tok * n_seq
    hidden_units = (location.shape[0] * piece - 4 * width) // 3
    head = width // HEADS
    kind_pieces = width // piece
    hidden_pieces = hidden_units // piece
    chunk = hidden_units // CHUNKS
    zn, xn, yn = n_dp, reps, n_dp // 2
    all_slots = n_seq * n_dp * slots
    last = slots // 8
    turn = [(i * n_dp + j, j * n_dp + i) for i in range(n_dp) for j in range(n_dp)]
    slopes = jnp.asarray(head_slopes(HEADS, tok, n_seq))

    weights, gathered, _ = pl.pallas_call(
        functools.partial(spread_kernel, (zn, xn, yn, slots, last)),
        out_shape=(
            shape_of((all_slots, piece, width), BF16),
            shape_of((n_seq,) + pack.shape, BF16),
            shape_of((max(yn - 1, 1),) + pack.shape, BF16),
        ),
        in_specs=[anywhere(), anywhere()],
        out_specs=(anywhere(),) * 3,
        scratch_shapes=spread_scratch(zn, xn, yn)
        + [
            pair(yn - 1),
            pair(zn),
            pair(zn * (xn - 1)),
            pair(zn * xn),
            pltpu.SemaphoreType.DMA,
        ],
        compiler_params=params(1),
    )(own_low, pack)
    weights, cotangent = lax.optimization_barrier((weights, cotangent))
    cotangent = lax.ppermute(cotangent, ("a", "y", "core"), turn)
    attend_sizes = (n_dp, reps, splits, tok, head, n_seq)
    q_ext, k_ext, k_turned, v_rows, v_turned = pl.pallas_call(
        functools.partial(project_kernel, (n_dp, splits, tok, head, n_seq)),
        out_shape=(
            shape_of((TRIO, GROUPS * tok, 128), BF16),
            shape_of((TRIO, length, 128), BF16),
            shape_of((TRIO, head, length), BF16),
            shape_of((TRIO, length, head), BF16),
            shape_of((TRIO, head, length), BF16),
        ),
        in_specs=[smem(), vmem(), anywhere()],
        out_specs=(vmem(),) * 5,
        scratch_shapes=[
            pltpu.VMEM((3 * TRIO, 128, width), BF16),
            pltpu.SemaphoreType.DMA((3 * TRIO * (head // piece),)),
        ],
        compiler_params=params(),
    )(location, gathered, weights)

    mixed_full, log_total, mixed_own = pl.pallas_call(
        functools.partial(attend_forward_kernel, attend_sizes),
        out_shape=(
            shape_of((GROUPS, TRIO, head, tok), F32),
            shape_of((GROUPS, TRIO, 1, tok), F32),
            shape_of((GROUPS, TRIO, head, tok), BF16),
        ),
        in_specs=[smem(), vmem(), vmem(), vmem()],
        out_specs=(vmem(),) * 3,
        scratch_shapes=[
            pltpu.VMEM((3 * TRIO, tok, tok), F32),
            pltpu.VMEM((n_seq, tok, tok), F32),
            pltpu.VMEM((GROUPS, TRIO, head, tok), BF16),
            pair(GROUPS - 1),
        ],
        compiler_params=params(2),
    )(slopes, q_ext, k_ext, v_turned)

    out_low, d_pre_one, d_mixed, norm_part, grads = pl.pallas_call(
        functools.partial(
            dense_kernel, (n_dp, tok, piece, kind_pieces, chunk // piece, hidden_pieces)
        ),
        out_shape=(
            shape_of((tok, width), BF16),
            shape_of((tok, width), F32),
            shape_of((width, tok), BF16),
            shape_of((8, width), F32),
            shape_of((all_slots, piece, width), BF16),
        ),
        in_specs=[smem(), anywhere(), vmem(), vmem(), vmem(), anywhere()],
        out_specs=(vmem(), vmem(), vmem(), vmem(), anywhere()),
        scratch_shapes=[
            pltpu.VMEM((width, width), BF16),
            pltpu.VMEM((CHUNKS, chunk, width), BF16),
            pltpu.VMEM((CHUNKS, chunk, width), BF16),
            pltpu.VMEM((CHUNKS, chunk, width), BF16),
            pltpu.VMEM((CHUNKS, tok, chunk), F32),
            pltpu.VMEM((CHUNKS, tok, chunk), F32),
            pltpu.VMEM((CHUNKS, tok, chunk), BF16),
            pltpu.VMEM((2, 3, chunk, width), BF16),
            pltpu.VMEM((width, width), BF16),
            pltpu.VMEM((tok, width), BF16),
            pltpu.SemaphoreType.DMA((3 * CHUNKS + 1,)),
            pltpu.SemaphoreType.DMA((7,)),
            pltpu.SemaphoreType.DMA,
        ],
        compiler_params=params(),
    )(location, gathered, cotangent, mixed_own.reshape(width, tok), norm_params, weights)

    d_own, result = pl.pallas_call(
        functools.partial(attend_backward_kernel, attend_sizes),
        out_shape=(
            shape_of((GROUPS, 3, TRIO, head, tok), BF16),
            shape_of(out_low.shape, BF16),
        ),
        in_specs=[smem()] + [vmem()] * 7 + [anywhere()],
        out_specs=(vmem(), anywhere()),
        scratch_shapes=[
            pltpu.VMEM((length, 128), F32),
            pltpu.VMEM((length, head), F32),
            pltpu.VMEM((3 * TRIO, tok, tok), F32),
            pltpu.VMEM((GROUPS, TRIO, head, tok), BF16),
            pltpu.VMEM((GROUPS, 3, TRIO, head, tok), BF16),
            pltpu.VMEM((TRIO, splits, GROUPS, 2, head, tok), BF16),
            pltpu.VMEM((TRIO, splits - 1, GROUPS, 2, head, tok), BF16),
            pair(GROUPS - 1),
            pair(TRIO * (GROUPS - 1)),
            pair(TRIO * (splits - 1)),
            pair(TRIO * (GROUPS - 1)),
            pltpu.SemaphoreType.DMA((2,)),
        ],
        compiler_params=params(3),
    )(
        slopes,
        q_ext,
        k_ext,
        k_turned,
        v_rows,
        mixed_full,
        log_total,
        d_mixed.reshape(GROUPS, TRIO, head, tok),
        out_low,
    )

    trio_rows = TRIO * head
    d_tokens, grads = pl.pallas_call(
        functools.partial(project_grad_kernel, (n_dp, tok, piece, kind_pieces)),
        out_shape=(shape_of((tok, width), BF16), shape_of(grads.shape, BF16)),
        in_specs=[smem(), anywhere(), vmem(), vmem()] + [anywhere()] * 2,
        out_specs=(vmem(), anywhere()),
        scratch_shapes=[
            pltpu.VMEM((GROUPS, 3 * trio_rows, width), BF16),
            pltpu.VMEM((GROUPS, 3 * trio_rows, width), BF16),
            pltpu.VMEM((tok, width), BF16),
            pltpu.SemaphoreType.DMA((GROUPS,)),
            pltpu.SemaphoreType.DMA((GROUPS,)),
            pltpu.SemaphoreType.DMA,
        ],
        input_output_aliases={5: 1},
        compiler_params=params(),
    )(location, gathered, d_own.reshape(GROUPS, 3 * trio_rows, tok), d_pre_one, weights, grads)

    def norm_rows(count):
        return pltpu.VMEM((max(count, 1), 8, width), F32)

    own_grad, norm_total, d_turned = pl.pallas_call(
        functools.partial(reduce_kernel, (zn, xn, yn, slots, last)),
        out_shape=(
            shape_of((slots, piece, width), F32),
            shape_of((8, width), F32),
            shape_of(d_tokens.shape, BF16),
        ),
        in_specs=[anywhere(), vmem(), anywhere()],
        out_specs=(vmem(), vmem(), anywhere()),
        scratch_shapes=reduce_scratch(zn, xn, yn, slots, last, piece, width)
        + [
            norm_rows(1),
            norm_rows(yn - 1),
            norm_rows(xn - 1),
            norm_rows(zn - 1),
            norm_rows(4),
            pair(1 + (yn - 1) + (xn - 1) + (zn - 1)),
            pltpu.SemaphoreType.DMA((2,)),
        ],
        compiler_params=params(4),
    )(grads, norm_part, d_tokens)
    return own_grad, norm_total, d_turned, result


def per_device(
    dims,
    layer_input,
    out_cotangent,
    segment_ids,
    piece_owner,
    weight_master,
    weight_first,
    weight_second,
    norm_params,
    norm_first,
    norm_second,
):
    slots, piece, width = weight_master.shape
    pieces = piece_owner.shape[0]
    tok = layer_input.shape[1]
    hidden_units = (pieces * piece - 4 * width) // 3
    location = locate_pieces(piece_owner, slots)
    own_low = weight_master.astype(BF16)
    seg_row = jnp.zeros((16, width), BF16).at[0, :tok].set(segment_ids[0].astype(BF16))
    pack = jnp.concatenate([layer_input[0], seg_row], axis=0)

    own_grad, norm_total, d_turned, result = run_layer(
        dims, own_low, pack, out_cotangent[0], location, norm_params
    )

    numbers = jnp.arange(pieces, dtype=jnp.int32) + 1
    own_slots = lax.axis_index(("a", "b", "y", "core")) * slots + jnp.arange(slots)
    inverse = jnp.sum(jnp.where(location[None, :] == own_slots[:, None], numbers[None, :], 0), axis=1)
    own_grad = jnp.where((inverse > 0)[:, None, None], own_grad, 0.0)
    norm_grad = norm_total[:4]
    rates = slot_rates(inverse, piece, width, hidden_units)
    first_new, second_new, weight_new = adamw_step(
        weight_master, weight_first, weight_second, own_grad, rates[:, None, None], STEP
    )
    norm_first_new, norm_second_new, norm_new = adamw_step(
        norm_params, norm_first, norm_second, norm_grad, NORM_RATE, STEP
    )
    return (
        result[None],
        d_turned.astype(F32)[None],
        own_grad,
        first_new,
        second_new,
        weight_new,
        weight_new.astype(BF16),
        norm_grad,
        norm_first_new,
        norm_second_new,
        norm_new,
    )


def solution(mesh):
    n_seq, n_dp = mesh.shape["seq"], mesh.shape["dp"]
    inner = Mesh(
        mesh.devices.reshape(n_dp, n_seq // n_dp, n_dp // 2, 2), ("a", "b", "y", "core")
    )
    seq, dp, every = ("a", "b"), ("y", "core"), ("a", "b", "y", "core")
    block = P(dp, seq, None)
    owned = P(every, None, None)
    in_specs = (block, block, P(dp, seq), P(), owned, owned, owned, P(), P(), P())
    out_specs = (block, block, owned, owned, owned, owned, owned, P(), P(), P(), P())
    return jax.shard_map(
        functools.partial(per_device, (n_seq, n_dp)),
        mesh=inner,
        in_specs=in_specs,
        out_specs=out_specs,
        check_vma=False,
    )
```

```python
import functools

import jax
import jax.numpy as jnp
import numpy as np
from jax import lax
from jax.experimental import pallas as pl
from jax.experimental.pallas import tpu as pltpu
from jax.sharding import Mesh
from jax.sharding import PartitionSpec as P

HEADS = 12
GROUPS = 4
TRIO = HEADS // GROUPS
STEP = 4

NORM_EPS = 1e-06
BETA_ONE = 0.5
BETA_TWO = 0.5
DECAY = 0.01
ADAM_EPS = 1e-08
NORM_RATE = 0.3
OUT_RATE = 0.35
MASKED = -1e30
CHUNKS = 6
VMEM_LIMIT = 60 * 1024 * 1024
MESH_IDS = pl.DeviceIdType.MESH
F32 = jnp.float32
BF16 = jnp.bfloat16


def head_slopes(head_count, tok_rows, seq_devices):
    head_order = np.arange(head_count, dtype=np.float64)
    slopes = 8.0 / tok_rows * np.power(8.0 * seq_devices, -head_order / (head_count - 1))
    return slopes.astype(np.float32)


def locate_pieces(owners, slot_count):
    pieces = owners.shape[0]
    numbers = jnp.arange(pieces, dtype=jnp.int32)
    earlier = (owners[None, :] == owners[:, None]) & (numbers[None, :] < numbers[:, None])
    return owners * slot_count + jnp.sum(earlier.astype(jnp.int32), axis=1)


def slot_rates(inverse, piece_rows, model_width, hidden_units):
    first_row = (inverse - 1) * piece_rows
    narrow = model_width ** (-0.5)
    step_rate = jnp.where(
        first_row < 3 * model_width,
        narrow,
        jnp.where(
            first_row < 4 * model_width,
            OUT_RATE,
            jnp.where(
                first_row < 4 * model_width + 2 * hidden_units, narrow, hidden_units ** (-0.5)
            ),
        ),
    )
    return jnp.where(inverse > 0, step_rate, narrow).astype(jnp.float32)


def adamw_step(weight, first_moment, second, gradient, step_rate, step_count):
    first_moment = BETA_ONE * first_moment + (1.0 - BETA_ONE) * gradient
    second = BETA_TWO * second + (1.0 - BETA_TWO) * gradient * gradient
    mean_hat = first_moment / (1.0 - BETA_ONE**step_count)
    square_hat = second / (1.0 - BETA_TWO**step_count)
    weight = weight - step_rate * (mean_hat / (jnp.sqrt(square_hat) + ADAM_EPS) + DECAY * weight)
    return (first_moment, second, weight)


def dot_nt(left_side, right_side):
    return lax.dot_general(
        left_side, right_side, (((1,), (1,)), ((), ())), preferred_element_type=F32
    )


def dot_nn(left_side, right_side):
    return lax.dot_general(
        left_side, right_side, (((1,), (0,)), ((), ())), preferred_element_type=F32
    )


def dot_tn(left_side, right_side):
    return lax.dot_general(
        left_side, right_side, (((0,), (0,)), ((), ())), preferred_element_type=F32
    )


def fetch_piece(place, piece, weights, dst, sem):
    pltpu.make_async_copy(weights.at[place[piece]], dst, sem).start()


def fill_tables(table, slopes, group, tok):
    apart = lax.broadcasted_iota(jnp.int32, (tok, tok), 0) - lax.broadcasted_iota(
        jnp.int32, (tok, tok), 1
    )
    apart = apart.astype(F32)
    for h in range(TRIO):
        slope = slopes[group * TRIO + h]
        table[h * 3 + 0] = -slope * apart
        table[h * 3 + 1] = slope * jnp.abs(apart)
        table[h * 3 + 2] = slope * apart


def block_place(order, n_dp, reps):
    return (order % n_dp) * reps + order // n_dp


def bias_of(key_block, query_place, slope, h, tok, n_dp, reps):
    key_place = block_place(key_block, n_dp, reps)
    which = jnp.where(key_place > query_place, 2, jnp.where(key_place < query_place, 0, 1))
    shift = slope * (tok * jnp.abs(key_place - query_place)).astype(F32)
    return h * 3 + which, shift


def holder(order, n_dp):
    dp = lax.rem(order, n_dp)
    return {"b": lax.div(order, n_dp), "y": lax.div(dp, 2), "core": lax.rem(dp, 2)}


def turn_to():
    z, dp = lax.axis_index("a"), lax.axis_index("y") * 2 + lax.axis_index("core")
    return {"a": dp, "y": lax.div(z, 2), "core": lax.rem(z, 2)}, dp != z


def start_turn(src, dst, send_sem, recv_sem):
    peer, moves = turn_to()

    @pl.when(moves)
    def _():
        pltpu.make_async_remote_copy(
            src_ref=src,
            dst_ref=dst,
            send_sem=send_sem,
            recv_sem=recv_sem,
            device_id=peer,
            device_id_type=MESH_IDS,
        ).start()

    @pl.when(jnp.logical_not(moves))
    def _():
        pltpu.make_async_copy(src, dst, recv_sem).start()


def finish_turn(src, dst, send_sem, recv_sem):
    peer, moves = turn_to()

    @pl.when(moves)
    def _():
        pltpu.make_async_remote_copy(
            src_ref=src,
            dst_ref=dst,
            send_sem=send_sem,
            recv_sem=recv_sem,
            device_id=peer,
            device_id_type=MESH_IDS,
        ).wait()

    @pl.when(jnp.logical_not(moves))
    def _():
        pltpu.make_async_copy(src, dst, recv_sem).wait()


def greet(peers, turning=False):
    barrier = pltpu.get_barrier_semaphore()
    for peer in peers:
        pl.semaphore_signal(barrier, inc=1, device_id=peer, device_id_type=MESH_IDS)
    if not turning:
        pl.semaphore_wait(barrier, len(peers))
        return
    turn_peer, moves = turn_to()

    @pl.when(moves)
    def _():
        pl.semaphore_signal(barrier, inc=1, device_id=turn_peer, device_id_type=MESH_IDS)

    pl.semaphore_wait(barrier, len(peers) + moves.astype(jnp.int32))


def my_order(n_dp):
    return lax.axis_index("b") * n_dp + lax.axis_index("y") * 2 + lax.axis_index("core")


def remote(src, dst, sems, index, peer):
    return pltpu.make_async_remote_copy(
        src_ref=src,
        dst_ref=dst,
        send_sem=sems.at[0, index],
        recv_sem=sems.at[1, index],
        device_id=peer,
        device_id_type=MESH_IDS,
    )


def project_kernel(
    sizes,
    place,
    x_ref,
    weights,
    q_out,
    k_out,
    kt_out,
    v_out,
    vt_out,
    wpad,
    sems,
):
    n_dp, splits, tok, head, blocks = sizes
    order = my_order(n_dp)
    group, split = lax.div(order, splits), lax.rem(order, splits)
    per_head = head // 16
    width = x_ref.shape[2]
    kind_pieces = width // 16

    def spot(step):
        kind = lax.div(step, TRIO * per_head)
        rest = lax.rem(step, TRIO * per_head)
        dst = wpad.at[
            kind * TRIO + lax.div(rest, per_head), pl.ds(lax.rem(rest, per_head) * 16, 16)
        ]
        return kind * kind_pieces + group * (TRIO * per_head) + rest, dst

    def start(step, carry):
        number, dst = spot(step)
        fetch_piece(place, number, weights, dst, sems.at[step])
        return carry

    def finish(step, carry):
        pltpu.make_async_copy(weights.at[0], spot(step)[1], sems.at[step]).wait()
        return carry

    lax.fori_loop(0, 3 * TRIO * per_head, start, None, unroll=6)
    for row in range(3 * TRIO):
        wpad[row, head:, :] = jnp.zeros((wpad.shape[1] - head, width), BF16)
    lax.fori_loop(0, 3 * TRIO * per_head, finish, None)

    w_query = wpad[0:TRIO].reshape(TRIO * 128, width)
    w_key = wpad[TRIO : 2 * TRIO].reshape(TRIO * 128, width)
    w_value = wpad[2 * TRIO : 3 * TRIO].reshape(TRIO * 128, width)

    def marks_of(block):
        segs = x_ref[block, tok : tok + 1, 0:tok].astype(F32)
        number = lax.broadcasted_iota(jnp.int32, (128, tok), 0) - head
        same = segs == number.astype(F32)
        used = (number >= 0) & (number < 3)
        query_marks = jnp.where(same & used, 1.0, 0.0)
        key_marks = jnp.where(used & jnp.logical_not(same), MASKED, 0.0)
        return query_marks.T.astype(BF16), key_marks.T.astype(BF16)

    def project(block, carry):
        rows = pl.ds(pl.multiple_of(block * tok, tok), tok)
        xb = x_ref[block, 0:tok, :]
        keys = dot_nt(xb, w_key)
        values = dot_nt(xb, w_value)
        marks = marks_of(block)[1]
        for h in range(TRIO):
            key = keys[:, h * 128 : (h + 1) * 128]
            value = values[:, h * 128 : (h + 1) * 128]
            k_out[h, rows, :] = key.astype(BF16) + marks
            v_out[h, rows, :] = value[:, 0:head].astype(BF16)
            kt_out[h, :, rows] = key.T[0:head].astype(BF16)
            vt_out[h, :, rows] = value.T[0:head].astype(BF16)
        return carry

    lax.fori_loop(0, blocks, project, None)

    def project_query(index, carry):
        block = index * splits + split
        rows = pl.ds(pl.multiple_of(index * tok, tok), tok)
        xb = x_ref[block, 0:tok, :]
        queries = dot_nt(xb, w_query).astype(BF16) * jnp.asarray(head**-0.5, BF16)
        marks = marks_of(block)[0]
        for h in range(TRIO):
            q_out[h, rows, :] = queries[:, h * 128 : (h + 1) * 128] + marks
        return carry

    lax.fori_loop(0, GROUPS, project_query, None)


def attend_forward_kernel(
    sizes,
    slopes,
    q_ref,
    k_ref,
    vt_ref,
    cot_in,
    mixed_full,
    log_out,
    mixed_own,
    cot_out,
    table,
    scores,
    mixed_low,
    swap_sems,
    turn_sems,
):
    n_dp, reps, splits, tok, head, blocks = sizes
    order = my_order(n_dp)
    group, split = lax.div(order, splits), lax.rem(order, splits)
    others = [lax.rem(group + k, GROUPS) for k in range(1, GROUPS)]
    peers = [holder(other * splits + split, n_dp) for other in others]
    started = []
    greet(peers, True)
    turn_refs = (cot_in, cot_out, turn_sems.at[0], turn_sems.at[1])
    start_turn(*turn_refs)
    fill_tables(table, slopes, group, tok)

    def attend(index, h):
        place_order = index * splits + split
        query_place = lax.rem(place_order, n_dp) * reps + lax.div(place_order, n_dp)
        slope = slopes[group * TRIO + h]
        qh = q_ref[h, pl.ds(pl.multiple_of(index * tok, tok), tok), :]
        top = None
        shifts = []
        for kb in range(blocks):
            which, shift = bias_of(kb, query_place, slope, h, tok, n_dp, reps)
            now = dot_nt(k_ref[h, kb * tok : (kb + 1) * tok, :], qh) - table[which]
            scores[kb] = now
            here = jnp.max(now, axis=0, keepdims=True) - shift
            top = here if top is None else jnp.maximum(top, here)
            shifts.append(shift)
        total = jnp.zeros((1, tok), F32)
        for kb in range(blocks):
            grown = jnp.exp(scores[kb] - (top + shifts[kb]))
            total = total + jnp.sum(grown, axis=0, keepdims=True)
            scores[kb] = grown
        inverse = 1.0 / total
        mixed = jnp.zeros((head, tok), F32)
        for kb in range(blocks):
            prob = (scores[kb] * inverse).astype(BF16)
            mixed = mixed + dot_nn(vt_ref[h, :, kb * tok : (kb + 1) * tok], prob)
        mixed_full[index, h] = mixed
        mixed_low[index, h] = mixed.astype(BF16)
        log_out[index, h] = top + jnp.log(total)

    for k in list(range(GROUPS - 1)) + [None]:
        index = group if k is None else others[k]

        def one(h, carry, index=index):
            attend(index, h)
            return carry

        lax.fori_loop(0, TRIO, one, None)
        if k is not None:
            copy = swap_copy(mixed_low, mixed_own, index, group, swap_sems, k, peers[k])
            copy.start()
            started.append(copy)
        else:
            mixed_own[group] = mixed_low[group]
    for copy in started:
        copy.wait()
    finish_turn(*turn_refs)


def swap_copy(src, dst, there, here, sems, index, peer):
    return pltpu.make_async_remote_copy(
        src_ref=src.at[there],
        dst_ref=dst.at[here],
        send_sem=sems.at[0, index],
        recv_sem=sems.at[1, index],
        device_id=peer,
        device_id_type=MESH_IDS,
    )


def attend_backward_kernel(
    sizes,
    slopes,
    q_ref,
    k_ref,
    kt_ref,
    v_ref,
    mixed_full,
    log_in,
    d_mixed,
    low_in,
    own_ref,
    low_out,
    dk_sum,
    dv_sum,
    table,
    d_blocks,
    shared,
    pairs,
    landed,
    swap_sems,
    query_sems,
    pair_sems,
    value_sems,
    turn_sems,
):
    n_dp, reps, splits, tok, head, blocks = sizes
    order = my_order(n_dp)
    group, split = lax.div(order, splits), lax.rem(order, splits)
    twins = [lax.rem(split + k, splits) for k in range(1, splits)]
    twin_ids = [holder(group * splits + other, n_dp) for other in twins]
    others = [lax.rem(group + k, GROUPS) for k in range(1, GROUPS)]
    peers = [holder(other * splits + split, n_dp) for other in others]
    greet(twin_ids + peers, True)
    turn_refs = (low_in, low_out, turn_sems.at[0], turn_sems.at[1])
    started = []

    def launch(copy):
        copy.start()
        started.append(copy)

    for k in range(GROUPS - 1):
        launch(remote(d_mixed.at[others[k]], d_blocks.at[group], swap_sems, k, peers[k]))
    d_blocks[group] = d_mixed[group]
    fill_tables(table, slopes, group, tok)
    dk_sum[...] = jnp.zeros_like(dk_sum)
    dv_sum[...] = jnp.zeros_like(dv_sum)

    def step_fn(h, step):
        index = lax.rem(group + GROUPS - step, GROUPS)
        if h == 0:

            @pl.when(step > 0)
            def _():
                view = d_blocks.at[index]
                remote(view, view, swap_sems, step - 1, peers[0]).wait_recv()

        place_order = index * splits + split
        query_place = lax.rem(place_order, n_dp) * reps + lax.div(place_order, n_dp)
        slope = slopes[group * TRIO + h]
        qh = q_ref[h, pl.ds(pl.multiple_of(index * tok, tok), tok), :]
        dt = d_blocks[index, h]
        row_dot = jnp.sum(dt.astype(F32) * mixed_full[index, h], axis=0, keepdims=True)
        log_total = log_in[index, h]
        dq = jnp.zeros((head, tok), F32)
        for kb in range(blocks):
            rows = slice(kb * tok, (kb + 1) * tok)
            which, shift = bias_of(kb, query_place, slope, h, tok, n_dp, reps)
            now = dot_nt(k_ref[h, rows, :], qh) - table[which]
            prob = jnp.exp(now - (log_total + shift))
            d_prob = dot_nn(v_ref[h, rows, :], dt)
            d_score = (prob * (d_prob - row_dot)).astype(BF16)
            dv_sum[rows, :] += dot_nt(prob.astype(BF16), dt)
            dk_sum[rows, :] += dot_nn(d_score, qh)
            dq = dq + dot_nn(kt_ref[h, :, rows], d_score)
        shared[index, 0, h] = (dq * (head**-0.5)).astype(BF16)

    def pair_copy(h, k):
        return remote(
            pairs.at[h, twins[k]], landed.at[h, k], pair_sems, h * (splits - 1) + k, twin_ids[k]
        )

    def take_pairs(h):
        for k in range(splits - 1):
            pair_copy(h, k).wait_recv()
        for index in range(GROUPS):
            for kind in range(2):
                total = pairs[h, split, index, kind].astype(F32)
                for k in range(splits - 1):
                    total = total + landed[h, k, index, kind].astype(F32)
                shared[index, kind + 1, h] = total.astype(BF16)
        for k in range(GROUPS - 1):
            launch(
                remote(
                    shared.at[others[k], pl.ds(1, 2), h],
                    own_ref.at[group, pl.ds(1, 2), h],
                    value_sems,
                    h * (GROUPS - 1) + k,
                    peers[k],
                )
            )

    for h in range(TRIO):

        def one(step, carry, h=h):
            step_fn(h, step)
            return carry

        lax.fori_loop(0, GROUPS, one, None)
        if h == 0:
            start_turn(*turn_refs)
        for k in range(GROUPS - 1):
            launch(
                remote(
                    shared.at[others[k], 0, h],
                    own_ref.at[group, 0, h],
                    query_sems,
                    h * (GROUPS - 1) + k,
                    peers[k],
                )
            )

        def flip(index, carry, h=h):
            for part in range(splits):
                rows = pl.ds(pl.multiple_of((index * splits + part) * tok, tok), tok)
                pairs[h, part, index, 0] = dk_sum[rows, :].T[0:head].astype(BF16)
                pairs[h, part, index, 1] = dv_sum[rows, :].T.astype(BF16)
            return carry

        lax.fori_loop(0, GROUPS, flip, None)
        if h + 1 < TRIO:
            dk_sum[...] = jnp.zeros_like(dk_sum)
            dv_sum[...] = jnp.zeros_like(dv_sum)
        for k in range(splits - 1):
            launch(pair_copy(h, k))
        if h > 0:
            take_pairs(h - 1)
    take_pairs(TRIO - 1)
    own_ref[group] = shared[group]
    for h in range(TRIO):
        for k in range(GROUPS - 1):
            view = own_ref.at[others[k], 0, h]
            remote(view, view, query_sems, h * (GROUPS - 1) + k, peers[k]).wait_recv()
            view = own_ref.at[others[k], pl.ds(1, 2), h]
            remote(view, view, value_sems, h * (GROUPS - 1) + k, peers[k]).wait_recv()
    finish_turn(*turn_refs)
    for copy in started:
        copy.wait_send()


def norm_stats(values_in):
    mean = jnp.mean(values_in, axis=-1, keepdims=True)
    centred = values_in - mean
    spread = jnp.mean(centred * centred, axis=-1, keepdims=True)
    scale = lax.rsqrt(spread + NORM_EPS)
    return centred * scale, scale


def norm_back(unit, scale, gain, cotangent):
    d_unit = cotangent * gain
    first = jnp.mean(d_unit, axis=-1, keepdims=True)
    second = jnp.mean(d_unit * unit, axis=-1, keepdims=True)
    d_in = scale * (d_unit - first - unit * second)
    d_gain = jnp.sum(cotangent * unit, axis=0, keepdims=True)
    d_bias = jnp.sum(cotangent, axis=0, keepdims=True)
    return d_in, d_gain, d_bias


def dense_kernel(
    sizes,
    place,
    gathered,
    cot_ref,
    mixed_ref,
    norm_ref,
    weights,
    out_ref,
    d_pre_one_ref,
    d_mixed_ref,
    norm_grad,
    grads,
    w_out,
    w_gate,
    w_up,
    w_down,
    keep_gate,
    keep_up,
    keep_hidden,
    stage,
    stage_out,
    x_ref,
    load_sems,
    store_sems,
    own_sem,
):
    n_dp, tok, piece, kind_pieces, chunk_pieces, hidden_pieces = sizes
    own_copy = pltpu.make_async_copy(
        gathered.at[my_order(n_dp), pl.ds(0, tok)], x_ref, own_sem
    )
    own_copy.start()
    first_gate = 4 * kind_pieces
    first_up = first_gate + hidden_pieces
    first_down = first_up + hidden_pieces
    bases = (first_gate, first_up, first_down)
    buffers = (w_gate, w_up, w_down)
    chunk = chunk_pieces * piece

    for step in range(kind_pieces):
        dst = w_out.at[pl.ds(step * piece, piece)]
        fetch_piece(place, 3 * kind_pieces + step, weights, dst, load_sems.at[3 * CHUNKS])

    def load_chunk(c):
        for step in range(chunk_pieces):
            for kind in range(3):
                dst = buffers[kind].at[c, pl.ds(step * piece, piece)]
                number = bases[kind] + c * chunk_pieces + step
                fetch_piece(place, number, weights, dst, load_sems.at[kind * CHUNKS + c])

    def wait_chunk(c):
        for kind in range(3):
            view = buffers[kind].at[c]
            pltpu.make_async_copy(view, view, load_sems.at[kind * CHUNKS + c]).wait()

    load_chunk(0)
    mixed = mixed_ref[...].T
    own_copy.wait()
    pltpu.make_async_copy(w_out, w_out, load_sems.at[3 * CHUNKS]).wait()
    pre_one = x_ref[...].astype(F32) + dot_nt(mixed, w_out[...])
    load_chunk(1)
    unit_one, scale_one = norm_stats(pre_one)
    h_one = unit_one * norm_ref[0:1, :] + norm_ref[1:2, :]
    h_low = h_one.astype(BF16)

    pre_two = h_one
    for c in range(CHUNKS):
        wait_chunk(c)
        gate = dot_nt(w_gate[c], h_low)
        up = dot_nt(w_up[c], h_low)
        if c + 2 < CHUNKS:
            load_chunk(c + 2)
        below = 0.5 * (1.0 + lax.erf(gate * (0.5**0.5)))
        gelu = gate * below
        slope = below + gate * (jnp.exp(-0.5 * gate * gate) * (0.5 / jnp.pi) ** 0.5)
        hidden = (gelu * up).astype(BF16)
        keep_gate[c] = up * slope
        keep_up[c] = gelu
        keep_hidden[c] = hidden
        pre_two = pre_two + dot_tn(hidden, w_down[c])

    unit_two, scale_two = norm_stats(pre_two)
    out_ref[...] = (unit_two * norm_ref[2:3, :] + norm_ref[3:4, :]).astype(BF16)
    d_pre_two, d_gain_two, d_bias_two = norm_back(
        unit_two, scale_two, norm_ref[2:3, :], cot_ref[...].astype(F32)
    )
    d_branch = d_pre_two.astype(BF16)

    def drain(slot):
        for kind in range(3):
            view = stage.at[slot, kind]
            pltpu.make_async_copy(view, view, store_sems.at[slot * 3 + kind]).wait()

    d_h = d_pre_two
    for c in range(CHUNKS):
        slot = c % 2
        if c >= 2:
            drain(slot)
        d_hidden = dot_nt(w_down[c], d_branch)
        d_gate = (d_hidden * keep_gate[c]).astype(BF16)
        d_up = (d_hidden * keep_up[c]).astype(BF16)
        stage[slot, 0] = dot_nn(d_gate, h_low).astype(BF16)
        stage[slot, 1] = dot_nn(d_up, h_low).astype(BF16)
        stage[slot, 2] = dot_nn(keep_hidden[c], d_branch).astype(BF16)
        for step in range(chunk_pieces):
            for kind in range(3):
                pltpu.make_async_copy(
                    stage.at[slot, kind, pl.ds(step * piece, piece)],
                    grads.at[place[bases[kind] + c * chunk_pieces + step]],
                    store_sems.at[slot * 3 + kind],
                ).start()
        d_h = d_h + dot_tn(d_gate, w_gate[c]) + dot_tn(d_up, w_up[c])

    d_pre_one, d_gain_one, d_bias_one = norm_back(unit_one, scale_one, norm_ref[0:1, :], d_h)
    d_pre_one_ref[...] = d_pre_one
    d_proj = d_pre_one.astype(BF16)
    stage_out[...] = dot_tn(d_proj, mixed).astype(BF16)
    for step in range(kind_pieces):
        pltpu.make_async_copy(
            stage_out.at[pl.ds(step * piece, piece)],
            grads.at[place[3 * kind_pieces + step]],
            store_sems.at[6],
        ).start()
    d_mixed_ref[...] = lax.dot_general(
        w_out[...], d_proj, (((0,), (1,)), ((), ())), preferred_element_type=F32
    ).astype(BF16)
    norm_grad[...] = jnp.concatenate(
        [
            d_gain_one,
            d_bias_one,
            d_gain_two,
            d_bias_two,
            jnp.zeros((4, d_gain_one.shape[1]), F32),
        ],
        axis=0,
    )
    drain(CHUNKS % 2)
    drain((CHUNKS + 1) % 2)
    pltpu.make_async_copy(stage_out, stage_out, store_sems.at[6]).wait()


def project_grad_kernel(
    sizes,
    place,
    gathered,
    d_own,
    d_pre_one,
    weights,
    grads_in,
    d_input,
    grads,
    w_all,
    stage,
    x_ref,
    load_sems,
    store_sems,
    own_sem,
):
    n_dp, tok, piece, kind_pieces = sizes
    own_copy = pltpu.make_async_copy(
        gathered.at[my_order(n_dp), pl.ds(0, tok)], x_ref, own_sem
    )
    own_copy.start()
    group_pieces = kind_pieces // GROUPS
    rows = 3 * group_pieces * piece
    del grads_in

    def each(group, act):
        def one(step, carry):
            for kind in range(3):
                act(kind * kind_pieces + group * group_pieces + step, kind * group_pieces + step)
            return carry

        lax.fori_loop(0, group_pieces, one, None, unroll=4)

    for group in range(GROUPS):

        def load(number, row, group=group):
            dst = w_all.at[group, pl.ds(row * piece, piece)]
            fetch_piece(place, number, weights, dst, load_sems.at[group])

        each(group, load)
    own_copy.wait()
    x_own = x_ref[...]
    for group in range(GROUPS):
        stage[group] = dot_nn(d_own[group], x_own).astype(BF16)

        def store(number, row, group=group):
            src = stage.at[group, pl.ds(row * piece, piece)]
            pltpu.make_async_copy(src, grads.at[place[number]], store_sems.at[group]).start()

        each(group, store)
    total = d_pre_one[...]
    for group in range(GROUPS):
        view = w_all.at[group]
        pltpu.make_async_copy(view, view, load_sems.at[group]).wait()
        total = total + dot_tn(d_own[group], w_all[group])
    d_input[...] = total.astype(BF16)
    for group in range(GROUPS):
        view = stage.at[group]
        pltpu.make_async_copy(view, view, store_sems.at[group]).wait()


def add_low(dst, src, rows):
    def one(i, carry):
        dst[i] = (dst[i].astype(F32) + src[i].astype(F32)).astype(BF16)
        return carry

    lax.fori_loop(0, rows, one, None)


def z_order_of(count):
    order = [0]
    for k in range(1, count):
        for far in (k, count - k):
            if far not in order:
                order.append(far)
    return order


def spread_steps(sizes, own, every, sems):
    zn, xn, yn, slots, last = sizes
    z_sems, xs_sems, ys_sems, xf_sems, yf_sems, near_sems, own_sem = sems[:7]
    xb_sems, yb_sems, zb_sems, nb_sems = sems[7:11]
    count = slots - last
    part = count * 9 // 16
    rest = count - part
    z, x = lax.axis_index("a"), lax.axis_index("b")
    y, core = lax.axis_index("y"), lax.axis_index("core")
    core_peer = {"core": 1 - core}
    xs, ys, z_order = range(1, xn), range(1, yn), z_order_of(zn)
    x_peers = {k: {"b": lax.rem(x + k, xn)} for k in xs}
    y_peers = {k: {"y": lax.rem(y + k, yn)} for k in ys}
    z_peers = {k: {"a": lax.rem(z + k, zn)} for k in range(1, zn)}
    source = own.at[pl.ds(0, count)]

    def number(jz, jx, jy):
        chip = (lax.rem(z + zn - jz, zn) * xn + lax.rem(x + xn - jx, xn)) * yn + lax.rem(
            y + yn - jy, yn
        )
        return chip * 2 + core

    def shard(jz, jx, jy, lead=0, rows=count):
        return every.at[pl.ds(number(jz, jx, jy) * slots + lead, rows)]

    def tail(jz, jx, jy):
        return shard(jz, jx, jy, count, last)

    def tail_held(jz, jx, jy):
        return own.at[pl.ds(count, last)] if (jz, jx, jy) == (0, 0, 0) else tail(jz, jx, jy)

    def xb_copy(jx, jy):
        index = (jx - 1) * yn + jy
        return remote(tail_held(0, 0, jy), tail(0, 0, jy), xb_sems, index, x_peers[jx])

    def yb_copy(jy):
        return remote(tail_held(0, 0, 0), tail(0, 0, 0), yb_sems, jy - 1, y_peers[jy])

    def zb_copy(jz, jx, jy):
        index = ((jz - 1) * xn + jx) * yn + jy
        return remote(tail_held(0, jx, jy), tail(0, jx, jy), zb_sems, index, z_peers[jz])

    def nb_copy(jz, jx, jy):
        index = (jz * xn + jx) * yn + jy
        return remote(tail_held(jz, jx, jy), tail(jz, jx, jy), nb_sems, index, core_peer)

    def tail_begin():
        for jy in ys:
            launch(yb_copy(jy))
        for jx in xs:
            launch(xb_copy(jx, 0))
        launch(nb_copy(0, 0, 0))

    def tail_across():
        for jy in ys:
            view = tail(0, 0, jy)
            remote(view, view, yb_sems, jy - 1, y_peers[jy]).wait_recv()
            for jx in xs:
                launch(xb_copy(jx, jy))
            launch(nb_copy(0, 0, jy))

    def tail_planes():
        for jx in xs:
            for jy in range(yn):
                view = tail(0, jx, jy)
                remote(view, view, xb_sems, (jx - 1) * yn + jy, x_peers[jx]).wait_recv()
                launch(nb_copy(0, jx, jy))
        for jz in z_order[1:]:
            for jx in range(xn):
                for jy in range(yn):
                    launch(zb_copy(jz, jx, jy))

    def tail_end():
        for jz in z_order[1:]:
            for jx in range(xn):
                for jy in range(yn):
                    view = tail(jz, jx, jy)
                    index = ((jz - 1) * xn + jx) * yn + jy
                    remote(view, view, zb_sems, index, z_peers[jz]).wait_recv()
                    launch(nb_copy(jz, jx, jy))

    def tail_settle():
        for jz in range(zn):
            for jx in range(xn):
                for jy in range(yn):
                    chip = lax.div(number(jz, jx, jy), 2)
                    view = every.at[pl.ds((chip * 2 + 1 - core) * slots + count, last)]
                    index = (jz * xn + jx) * yn + jy
                    remote(view, view, nb_sems, index, core_peer).wait_recv()

    def held(jz, jx, jy):
        return source if (jz, jx, jy) == (0, 0, 0) else shard(jz, jx, jy)

    def z_copy(jz):
        return remote(source, shard(0, 0, 0), z_sems, jz - 1, z_peers[jz])

    def xs_copy(jz, jx):
        return remote(
            held(jz, 0, 0), shard(jz, 0, 0), xs_sems, jz * (xn - 1) + jx - 1, x_peers[jx]
        )

    def ys_copy(jz, jy):
        return remote(
            held(jz, 0, 0), shard(jz, 0, 0), ys_sems, jz * (yn - 1) + jy - 1, y_peers[jy]
        )

    def cross(jz, jx, jy):
        return (jz * (xn - 1) + jx - 1) * (yn - 1) + jy - 1

    def xf_copy(jz, jx, jy):
        view = shard(jz, 0, jy, part, rest)
        return remote(view, view, xf_sems, cross(jz, jx, jy), x_peers[jx])

    def yf_copy(jz, jx, jy):
        view = shard(jz, jx, 0, 0, part)
        return remote(view, view, yf_sems, cross(jz, jx, jy), y_peers[jy])

    def near_copy(jz, jx, jy):
        return remote(
            held(jz, jx, jy),
            shard(jz, jx, jy),
            near_sems,
            (jz * xn + jx) * yn + jy,
            core_peer,
        )

    started = []

    def launch(copy):
        copy.start()
        started.append(copy)

    def send_own(jz):
        for jx in xs:
            launch(xs_copy(jz, jx))
        for jy in ys:
            launch(ys_copy(jz, jy))
        launch(near_copy(jz, 0, 0))

    def ys_copy_in(jz, jy):
        view = shard(jz, 0, jy)
        remote(view, view, ys_sems, jz * (yn - 1) + jy - 1, y_peers[jy]).wait_recv()

    def xs_copy_in(jz, jx):
        view = shard(jz, jx, 0)
        remote(view, view, xs_sems, jz * (xn - 1) + jx - 1, x_peers[jx]).wait_recv()

    def forward(jz):
        for jy in ys:
            ys_copy_in(jz, jy)
            for jx in xs:
                launch(xf_copy(jz, jx, jy))
        for jx in xs:
            xs_copy_in(jz, jx)
            for jy in ys:
                launch(yf_copy(jz, jx, jy))
        for jy in ys:
            launch(near_copy(jz, 0, jy))
        for jx in xs:
            launch(near_copy(jz, jx, 0))

    def finish(jz):
        for jx in xs:
            for jy in ys:
                view = shard(jz, jx, jy, part, rest)
                remote(view, view, xf_sems, cross(jz, jx, jy), x_peers[jx]).wait_recv()
                view = shard(jz, jx, jy, 0, part)
                remote(view, view, yf_sems, cross(jz, jx, jy), y_peers[jy]).wait_recv()
                launch(near_copy(jz, jx, jy))

    def z_in(index):
        jz = z_order[index]
        view = shard(jz, 0, 0)
        remote(view, view, z_sems, jz - 1, z_peers[jz]).wait_recv()
        if index + 1 < zn:
            launch(z_copy(z_order[index + 1]))

    own_local = pltpu.make_async_copy(own, shard(0, 0, 0, 0, slots), own_sem)

    def begin():
        launch(z_copy(z_order[1]))
        send_own(0)
        own_local.start()
        if last:
            tail_begin()

    def advance(index):
        z_in(index)
        send_own(z_order[index])
        if last and index == 1:
            tail_across()

    def forward_step(index):
        forward(z_order[index])
        if last and index == zn - 2:
            tail_planes()

    def end():
        finish(z_order[zn - 1])
        if last:
            tail_end()
            tail_settle()
        for jz in range(zn):
            for jx in range(xn):
                for jy in range(yn):
                    chip = lax.div(number(jz, jx, jy), 2)
                    view = every.at[pl.ds((chip * 2 + 1 - core) * slots, count)]
                    remote(
                        view, view, near_sems, (jz * xn + jx) * yn + jy, core_peer
                    ).wait_recv()

    def settle():
        own_local.wait()
        for copy in started:
            copy.wait_send()

    steps = [begin]
    for index in range(1, zn):
        steps.append(functools.partial(advance, index))
        steps.append(functools.partial(forward_step, index - 1))
        if index >= 2:
            steps.append(functools.partial(finish, z_order[index - 2]))
    steps.append(functools.partial(forward_step, zn - 1))
    steps.append(functools.partial(finish, z_order[zn - 2]))
    steps.append(end)
    steps.append(settle)
    return [core_peer, *x_peers.values(), *y_peers.values(), *z_peers.values()], steps


def block_steps(sizes, pack, gathered, crossed, sems):
    zn, xn, yn = sizes
    by_sems, bz_sems, bx_sems, bn_sems, stay_sem = sems
    z, x = lax.axis_index("a"), lax.axis_index("b")
    y, core = lax.axis_index("y"), lax.axis_index("core")
    core_peer = {"core": 1 - core}
    xs, ys, z_order = range(1, xn), range(1, yn), z_order_of(zn)
    x_peers = {k: {"b": lax.rem(x + k, xn)} for k in xs}
    y_peers = {k: {"y": lax.rem(y + k, yn)} for k in ys}
    z_peers = {k: {"a": lax.rem(z + k, zn)} for k in range(1, zn)}
    hosts = lax.rem(z, 2) == core

    def block(jz, jx=0):
        return gathered.at[lax.rem(x + xn - jx, xn) * zn + lax.rem(z + zn - jz, zn)]

    def by_copy(jy):
        return remote(pack, crossed.at[jy - 1], by_sems, jy - 1, y_peers[jy])

    def plane(jy):
        return lax.rem(y + yn - jy, yn) * 2 + core

    def bz_copy(jy):
        src = pack if jy == 0 else crossed.at[jy - 1]
        far = lax.rem(plane(jy) + zn - z, zn)
        return remote(src, block(0), bz_sems, far, {"a": plane(jy)})

    def stay_copy(jy):
        src = pack if jy == 0 else crossed.at[jy - 1]
        return pltpu.make_async_copy(src, block(0), stay_sem)

    def bx_copy(jz, jx):
        return remote(block(jz), block(jz), bx_sems, jz * (xn - 1) + jx - 1, x_peers[jx])

    def bn_copy(jz, jx):
        return remote(block(jz, jx), block(jz, jx), bn_sems, jz * xn + jx, core_peer)

    def cross_y():
        for jy in ys:
            by_copy(jy).start()

    def to_planes():
        for jy in range(yn):
            if jy != 0:
                by_copy(jy).wait_recv()

            @pl.when(plane(jy) != z)
            def _():
                bz_copy(jy).start()

            @pl.when(plane(jy) == z)
            def _():
                stay_copy(jy).start()
                stay_copy(jy).wait()

    def across():
        @pl.when(hosts)
        def _():
            for jz in z_order:
                if jz != 0:
                    remote(block(jz), block(jz), bz_sems, jz, z_peers[jz]).wait_recv()
                for jx in xs:
                    bx_copy(jz, jx).start()
                bn_copy(jz, 0).start()

    def end():
        @pl.when(hosts)
        def _():
            for jz in z_order:
                for jx in xs:
                    view = block(jz, jx)
                    index = jz * (xn - 1) + jx - 1
                    remote(view, view, bx_sems, index, x_peers[jx]).wait_recv()
                    bn_copy(jz, jx).start()
            for jz in z_order:
                for jx in xs:
                    bx_copy(jz, jx).wait_send()
                for jx in range(xn):
                    bn_copy(jz, jx).wait_send()

        @pl.when(jnp.logical_not(hosts))
        def _():
            for jz in range(zn):
                for jx in range(xn):
                    bn_copy(jz, jx).wait_recv()

        for jy in range(yn):

            @pl.when(plane(jy) != z)
            def _():
                bz_copy(jy).wait_send()

        for jy in ys:
            by_copy(jy).wait_send()

    return [cross_y, to_planes, across, end]


def spread_kernel(sizes, own, pack, every, gathered, crossed, *sems):
    peers, steps = spread_steps(sizes, own, every, sems[:11])
    cross_y, to_planes, across, end = block_steps(sizes[:3], pack, gathered, crossed, sems[11:])
    greet(peers)
    steps[0]()
    cross_y()
    for step in steps[1:-7]:
        step()
    to_planes()
    for step in steps[-7:-3]:
        step()
    across()
    steps[-3]()
    steps[-2]()
    end()
    steps[-1]()


def reduce_steps(sizes, grads, total_out, refs):
    zn, xn, yn, slots = sizes
    held, near, xd, yd, xs_in, ys_in, zs_in = refs[:7]
    load_sems, near_sems, xd_sems, yd_sems, xs_sems, ys_sems, zs_sems = refs[7:14]
    part = slots // 2
    rest = slots - part
    z, x = lax.axis_index("a"), lax.axis_index("b")
    y, core = lax.axis_index("y"), lax.axis_index("core")
    core_peer = {"core": 1 - core}
    xs, ys = range(1, xn), range(1, yn)
    y_peers = [{"y": lax.rem(y + k, yn)} for k in ys]
    x_peers = [{"b": lax.rem(x + k, xn)} for k in xs]
    z_peers = [{"a": lax.rem(z + k, zn)} for k in range(1, zn)]
    def flat(jz, jx, jy):
        return (jz * xn + jx) * yn + jy

    def chip_rows(jz, jx, jy, which):
        chip = (lax.rem(z + jz, zn) * xn + lax.rem(x + jx, xn)) * yn + lax.rem(y + jy, yn)
        return grads.at[pl.ds((chip * 2 + which) * slots, slots)]

    def near_copy(jz, jx, jy):
        index = flat(jz, jx, jy)
        return remote(chip_rows(jz, jx, jy, 1 - core), near.at[index], near_sems, index, core_peer)

    def load_copy(jz, jx, jy):
        index = flat(jz, jx, jy)
        return pltpu.make_async_copy(
            chip_rows(jz, jx, jy, core), held.at[index], load_sems.at[index]
        )

    def whole(jz, jx, jy):
        return held.at[flat(jz, jx, jy)]

    def first(jz, jx, jy):
        return held.at[flat(jz, jx, jy), pl.ds(0, part)]

    def second(jz, jx, jy):
        return held.at[flat(jz, jx, jy), pl.ds(part, rest)]

    def cross(jz, jx, jy):
        return (jz * (xn - 1) + jx - 1) * (yn - 1) + jy - 1

    def yd_copy(jz, jx, jy):
        index = cross(jz, jx, jy)
        return remote(first(jz, jx, jy), yd.at[index], yd_sems, index, y_peers[jy - 1])

    def xd_copy(jz, jx, jy):
        index = cross(jz, jx, jy)
        return remote(second(jz, jx, jy), xd.at[index], xd_sems, index, x_peers[jx - 1])

    def halves(low_half):
        return pl.ds(0, part) if low_half else pl.ds(part, rest)

    def xs_copy(jz, jx, low_half):
        index = jz * (xn - 1) + jx - 1
        return remote(
            held.at[flat(jz, jx, 0), halves(low_half)],
            xs_in.at[index, halves(low_half)],
            xs_sems,
            index * 2 + int(low_half),
            x_peers[jx - 1],
        )

    def ys_copy(jz, jy, low_half):
        index = jz * (yn - 1) + jy - 1
        return remote(
            held.at[flat(jz, 0, jy), halves(low_half)],
            ys_in.at[index, halves(low_half)],
            ys_sems,
            index * 2 + int(low_half),
            y_peers[jy - 1],
        )

    def zs_copy(jz):
        return remote(whole(jz, 0, 0), zs_in.at[jz - 1], zs_sems, jz - 1, z_peers[jz - 1])

    z_order = z_order_of(zn)[::-1]
    started = []

    def launch(copy):
        copy.start()
        started.append(copy)

    def plane(jz):
        return (
            [(jz, jx, jy) for jx in xs for jy in ys]
            + [(jz, jx, 0) for jx in xs]
            + [(jz, 0, jy) for jy in ys]
            + [(jz, 0, 0)]
        )

    def fetch(jz):
        for chip in plane(jz):
            launch(near_copy(*chip))
            load_copy(*chip).start()

    def prepare(index):
        for chip in plane(z_order[index]):
            load_copy(*chip).wait()
            near_copy(*chip).wait_recv()
            add_low(whole(*chip), near.at[flat(*chip)], slots)
        if index + 1 < zn:
            fetch(z_order[index + 1])

    stages = [(index, stage) for index in range(zn) for stage in range(3)]

    def send_stage(number):
        index, stage = stages[number]
        jz = z_order[index]
        for jx in xs:
            if stage == 0:
                for jy in ys:
                    launch(xd_copy(jz, jx, jy))
            else:
                launch(xs_copy(jz, jx, stage == 2))
        for jy in ys:
            if stage == 0:
                for jx in xs:
                    launch(yd_copy(jz, jx, jy))
            else:
                launch(ys_copy(jz, jy, stage == 1))

    def take_stage(number):
        index, stage = stages[number]
        jz = z_order[index]
        if stage == 0:
            for jx in xs:
                for jy in ys:
                    yd_copy(jz, jx, jy).wait_recv()
                    add_low(first(jz, jx, 0), yd.at[cross(jz, jx, jy)], part)
                    xd_copy(jz, jx, jy).wait_recv()
                    add_low(second(jz, 0, jy), xd.at[cross(jz, jx, jy)], rest)
        else:
            for jx in xs:
                xs_copy(jz, jx, stage == 2).wait_recv()
            for jy in ys:
                ys_copy(jz, jy, stage == 1).wait_recv()

    def side_in(index):
        jz = z_order[index]

        def one(i, carry):
            total = held[flat(jz, 0, 0), i].astype(F32)
            for jx in xs:
                total = total + xs_in[jz * (xn - 1) + jx - 1, i].astype(F32)
            for jy in ys:
                total = total + ys_in[jz * (yn - 1) + jy - 1, i].astype(F32)
            if jz != 0:
                held[flat(jz, 0, 0), i] = total.astype(BF16)
            else:
                total_out[i] = total
            return carry

        lax.fori_loop(0, slots, one, None)
        if jz != 0:
            launch(zs_copy(jz))

    ahead = 2

    def begin():
        fetch(z_order[0])

    def begin_stages():
        prepare(0)
        for number in range(ahead):
            send_stage(number)

    def one_stage(number):
        take_stage(number)
        later = number + ahead
        if later < len(stages):
            if stages[later][1] == 0:
                prepare(stages[later][0])
            send_stage(later)
        if stages[number][1] == 2:
            side_in(stages[number][0])

    def end():
        for jz in range(1, zn):
            zs_copy(jz).wait_recv()

        def add_planes(i, carry):
            total = total_out[i]
            for jz in range(1, zn):
                total = total + zs_in[jz - 1, i].astype(F32)
            total_out[i] = total
            return carry

        lax.fori_loop(0, slots, add_planes, None)
        for copy in started:
            copy.wait_send()

    steps = [begin, begin_stages]
    steps += [functools.partial(one_stage, number) for number in range(len(stages))]
    steps.append(end)
    return [core_peer] + y_peers + x_peers + z_peers, steps


def norm_steps(dims, norm_in, norm_out, refs):
    zn, xn, yn = dims
    norm_core, norm_y, norm_x, norm_z, norm_sum, sems = refs
    z, x = lax.axis_index("a"), lax.axis_index("b")
    y, core = lax.axis_index("y"), lax.axis_index("core")
    rounds = [
        (norm_core, [{"core": 1 - core}]),
        (norm_y, [{"y": lax.rem(y + k, yn)} for k in range(1, yn)]),
        (norm_x, [{"b": lax.rem(x + k, xn)} for k in range(1, xn)]),
        (norm_z, [{"a": lax.rem(z + k, zn)} for k in range(1, zn)]),
    ]
    first = [sum(len(peers) for _, peers in rounds[:i]) for i in range(len(rounds))]

    def copies(i):
        buffer, peers = rounds[i]
        return [
            remote(norm_sum.at[i], buffer.at[k], sems, first[i] + k, peer)
            for k, peer in enumerate(peers)
        ]

    def begin():
        norm_sum[0] = norm_in[...]
        for copy in copies(0):
            copy.start()

    def turn_round(i):
        total = norm_sum[i]
        for k, copy in enumerate(copies(i)):
            copy.wait()
            total = total + rounds[i][0][k]
        if i + 1 == len(rounds):
            norm_out[...] = total
            return
        norm_sum[i + 1] = total
        for copy in copies(i + 1):
            copy.start()

    return [begin] + [functools.partial(turn_round, i) for i in range(len(rounds))]


def reduce_kernel(
    sizes, grads, norm_in, tokens_in, total_out, norm_out, tokens_out, *refs
):
    peers, steps = reduce_steps(sizes, grads, total_out, refs[:14])
    norms = norm_steps(sizes[:3], norm_in, norm_out, refs[14:20])
    turn_sems = refs[20]
    greet(peers, True)
    turn_refs = (tokens_in, tokens_out, turn_sems.at[0], turn_sems.at[1])
    steps[0]()
    start_turn(*turn_refs)
    for number, step in enumerate(steps[1:]):
        step()
        if number % 2 == 0 and norms:
            norms.pop(0)()
    for step in norms:
        step()
    finish_turn(*turn_refs)


def vmem():
    return pl.BlockSpec(memory_space=pltpu.VMEM)


def smem():
    return pl.BlockSpec(memory_space=pltpu.SMEM)


def anywhere():
    return pl.BlockSpec(memory_space=pl.ANY)


def shape_of(dims, kind):
    return jax.ShapeDtypeStruct(dims, kind)


def params(collective=None):
    if collective is None:
        return pltpu.CompilerParams(vmem_limit_bytes=VMEM_LIMIT)
    return pltpu.CompilerParams(
        vmem_limit_bytes=VMEM_LIMIT, collective_id=collective, has_side_effects=True
    )


def pair(count):
    return pltpu.SemaphoreType.DMA((2, max(count, 1)))


def spread_scratch(zn, xn, yn):
    return [
        pair(zn - 1),
        pair(zn * (xn - 1)),
        pair(zn * (yn - 1)),
        pair(zn * (xn - 1) * (yn - 1)),
        pair(zn * (xn - 1) * (yn - 1)),
        pair(zn * xn * yn),
        pltpu.SemaphoreType.DMA,
        pair((xn - 1) * yn),
        pair(yn - 1),
        pair((zn - 1) * xn * yn),
        pair(zn * xn * yn),
    ]


def reduce_scratch(zn, xn, yn, slots, piece, width):
    def chunks(number, rows):
        return pltpu.VMEM((max(number, 1), rows, piece, width), BF16)

    n_chips, crossing = zn * xn * yn, zn * (xn - 1) * (yn - 1)
    part = slots // 2
    return [
        chunks(n_chips, slots),
        chunks(n_chips, slots),
        chunks(crossing, slots - part),
        chunks(crossing, part),
        chunks(zn * (xn - 1), slots),
        chunks(zn * (yn - 1), slots),
        chunks(zn - 1, slots),
        pltpu.SemaphoreType.DMA((n_chips,)),
        pair(n_chips),
        pair(crossing),
        pair(crossing),
        pair(2 * zn * (xn - 1)),
        pair(2 * zn * (yn - 1)),
        pair(zn - 1),
    ]


def run_layer(dims, own_low, pack, cotangent, location, norm_params):
    n_seq, n_dp = dims
    reps = n_seq // n_dp
    splits = n_seq // GROUPS
    slots, piece, width = own_low.shape
    tok = cotangent.shape[0]
    length = tok * n_seq
    hidden_units = (location.shape[0] * piece - 4 * width) // 3
    head = width // HEADS
    kind_pieces = width // piece
    hidden_pieces = hidden_units // piece
    chunk = hidden_units // CHUNKS
    zn, xn, yn = n_dp, reps, n_dp // 2
    all_slots = n_seq * n_dp * slots
    last = slots // 8
    slopes = jnp.asarray(head_slopes(HEADS, tok, n_seq))

    weights, gathered, _ = pl.pallas_call(
        functools.partial(spread_kernel, (zn, xn, yn, slots, last)),
        out_shape=(
            shape_of((all_slots, piece, width), BF16),
            shape_of((n_seq,) + pack.shape, BF16),
            shape_of((max(yn - 1, 1),) + pack.shape, BF16),
        ),
        in_specs=[anywhere(), anywhere()],
        out_specs=(anywhere(),) * 3,
        scratch_shapes=spread_scratch(zn, xn, yn)
        + [
            pair(yn - 1),
            pair(zn),
            pair(zn * (xn - 1)),
            pair(zn * xn),
            pltpu.SemaphoreType.DMA,
        ],
        compiler_params=params(1),
    )(own_low, pack)
    attend_sizes = (n_dp, reps, splits, tok, head, n_seq)
    q_ext, k_ext, k_turned, v_rows, v_turned = pl.pallas_call(
        functools.partial(project_kernel, (n_dp, splits, tok, head, n_seq)),
        out_shape=(
            shape_of((TRIO, GROUPS * tok, 128), BF16),
            shape_of((TRIO, length, 128), BF16),
            shape_of((TRIO, head, length), BF16),
            shape_of((TRIO, length, head), BF16),
            shape_of((TRIO, head, length), BF16),
        ),
        in_specs=[smem(), vmem(), anywhere()],
        out_specs=(vmem(),) * 5,
        scratch_shapes=[
            pltpu.VMEM((3 * TRIO, 128, width), BF16),
            pltpu.SemaphoreType.DMA((3 * TRIO * (head // piece),)),
        ],
        compiler_params=params(),
    )(location, gathered, weights)

    mixed_full, log_total, mixed_own, cotangent = pl.pallas_call(
        functools.partial(attend_forward_kernel, attend_sizes),
        out_shape=(
            shape_of((GROUPS, TRIO, head, tok), F32),
            shape_of((GROUPS, TRIO, 1, tok), F32),
            shape_of((GROUPS, TRIO, head, tok), BF16),
            shape_of(cotangent.shape, BF16),
        ),
        in_specs=[smem(), vmem(), vmem(), vmem(), anywhere()],
        out_specs=(vmem(), vmem(), vmem(), anywhere()),
        scratch_shapes=[
            pltpu.VMEM((3 * TRIO, tok, tok), F32),
            pltpu.VMEM((n_seq, tok, tok), F32),
            pltpu.VMEM((GROUPS, TRIO, head, tok), BF16),
            pair(GROUPS - 1),
            pltpu.SemaphoreType.DMA((2,)),
        ],
        compiler_params=params(2),
    )(slopes, q_ext, k_ext, v_turned, cotangent)

    out_low, d_pre_one, d_mixed, norm_part, grads = pl.pallas_call(
        functools.partial(
            dense_kernel, (n_dp, tok, piece, kind_pieces, chunk // piece, hidden_pieces)
        ),
        out_shape=(
            shape_of((tok, width), BF16),
            shape_of((tok, width), F32),
            shape_of((width, tok), BF16),
            shape_of((8, width), F32),
            shape_of((all_slots, piece, width), BF16),
        ),
        in_specs=[smem(), anywhere(), vmem(), vmem(), vmem(), anywhere()],
        out_specs=(vmem(), vmem(), vmem(), vmem(), anywhere()),
        scratch_shapes=[
            pltpu.VMEM((width, width), BF16),
            pltpu.VMEM((CHUNKS, chunk, width), BF16),
            pltpu.VMEM((CHUNKS, chunk, width), BF16),
            pltpu.VMEM((CHUNKS, chunk, width), BF16),
            pltpu.VMEM((CHUNKS, chunk, tok), F32),
            pltpu.VMEM((CHUNKS, chunk, tok), F32),
            pltpu.VMEM((CHUNKS, chunk, tok), BF16),
            pltpu.VMEM((2, 3, chunk, width), BF16),
            pltpu.VMEM((width, width), BF16),
            pltpu.VMEM((tok, width), BF16),
            pltpu.SemaphoreType.DMA((3 * CHUNKS + 1,)),
            pltpu.SemaphoreType.DMA((7,)),
            pltpu.SemaphoreType.DMA,
        ],
        compiler_params=params(),
    )(location, gathered, cotangent, mixed_own.reshape(width, tok), norm_params, weights)

    d_own, result = pl.pallas_call(
        functools.partial(attend_backward_kernel, attend_sizes),
        out_shape=(
            shape_of((GROUPS, 3, TRIO, head, tok), BF16),
            shape_of(out_low.shape, BF16),
        ),
        in_specs=[smem()] + [vmem()] * 7 + [anywhere()],
        out_specs=(vmem(), anywhere()),
        scratch_shapes=[
            pltpu.VMEM((length, 128), F32),
            pltpu.VMEM((length, head), F32),
            pltpu.VMEM((3 * TRIO, tok, tok), F32),
            pltpu.VMEM((GROUPS, TRIO, head, tok), BF16),
            pltpu.VMEM((GROUPS, 3, TRIO, head, tok), BF16),
            pltpu.VMEM((TRIO, splits, GROUPS, 2, head, tok), BF16),
            pltpu.VMEM((TRIO, splits - 1, GROUPS, 2, head, tok), BF16),
            pair(GROUPS - 1),
            pair(TRIO * (GROUPS - 1)),
            pair(TRIO * (splits - 1)),
            pair(TRIO * (GROUPS - 1)),
            pltpu.SemaphoreType.DMA((2,)),
        ],
        compiler_params=params(3),
    )(
        slopes,
        q_ext,
        k_ext,
        k_turned,
        v_rows,
        mixed_full,
        log_total,
        d_mixed.reshape(GROUPS, TRIO, head, tok),
        out_low,
    )

    trio_rows = TRIO * head
    d_tokens, grads = pl.pallas_call(
        functools.partial(project_grad_kernel, (n_dp, tok, piece, kind_pieces)),
        out_shape=(shape_of((tok, width), BF16), shape_of(grads.shape, BF16)),
        in_specs=[smem(), anywhere(), vmem(), vmem()] + [anywhere()] * 2,
        out_specs=(vmem(), anywhere()),
        scratch_shapes=[
            pltpu.VMEM((GROUPS, 3 * trio_rows, width), BF16),
            pltpu.VMEM((GROUPS, 3 * trio_rows, width), BF16),
            pltpu.VMEM((tok, width), BF16),
            pltpu.SemaphoreType.DMA((GROUPS,)),
            pltpu.SemaphoreType.DMA((GROUPS,)),
            pltpu.SemaphoreType.DMA,
        ],
        input_output_aliases={5: 1},
        compiler_params=params(),
    )(location, gathered, d_own.reshape(GROUPS, 3 * trio_rows, tok), d_pre_one, weights, grads)

    def norm_rows(count):
        return pltpu.VMEM((max(count, 1), 8, width), F32)

    own_grad, norm_total, d_turned = pl.pallas_call(
        functools.partial(reduce_kernel, (zn, xn, yn, slots)),
        out_shape=(
            shape_of((slots, piece, width), F32),
            shape_of((8, width), F32),
            shape_of(d_tokens.shape, BF16),
        ),
        in_specs=[anywhere(), vmem(), anywhere()],
        out_specs=(vmem(), vmem(), anywhere()),
        scratch_shapes=reduce_scratch(zn, xn, yn, slots, piece, width)
        + [
            norm_rows(1),
            norm_rows(yn - 1),
            norm_rows(xn - 1),
            norm_rows(zn - 1),
            norm_rows(4),
            pair(1 + (yn - 1) + (xn - 1) + (zn - 1)),
            pltpu.SemaphoreType.DMA((2,)),
        ],
        compiler_params=params(4),
    )(grads, norm_part, d_tokens)
    return own_grad, norm_total, d_turned, result


def per_device(
    dims,
    layer_input,
    out_cotangent,
    segment_ids,
    piece_owner,
    weight_master,
    weight_first,
    weight_second,
    norm_params,
    norm_first,
    norm_second,
):
    slots, piece, width = weight_master.shape
    pieces = piece_owner.shape[0]
    tok = layer_input.shape[1]
    hidden_units = (pieces * piece - 4 * width) // 3
    location = locate_pieces(piece_owner, slots)
    own_low = weight_master.astype(BF16)
    seg_row = jnp.zeros((16, width), BF16).at[0, :tok].set(segment_ids[0].astype(BF16))
    pack = jnp.concatenate([layer_input[0], seg_row], axis=0)

    own_grad, norm_total, d_turned, result = run_layer(
        dims, own_low, pack, out_cotangent[0], location, norm_params
    )

    numbers = jnp.arange(pieces, dtype=jnp.int32) + 1
    own_slots = lax.axis_index(("a", "b", "y", "core")) * slots + jnp.arange(slots)
    inverse = jnp.sum(jnp.where(location[None, :] == own_slots[:, None], numbers[None, :], 0), axis=1)
    own_grad = jnp.where((inverse > 0)[:, None, None], own_grad, 0.0)
    norm_grad = norm_total[:4]
    rates = slot_rates(inverse, piece, width, hidden_units)
    first_new, second_new, weight_new = adamw_step(
        weight_master, weight_first, weight_second, own_grad, rates[:, None, None], STEP
    )
    norm_first_new, norm_second_new, norm_new = adamw_step(
        norm_params, norm_first, norm_second, norm_grad, NORM_RATE, STEP
    )
    return (
        result[None],
        d_turned.astype(F32)[None],
        own_grad,
        first_new,
        second_new,
        weight_new,
        weight_new.astype(BF16),
        norm_grad,
        norm_first_new,
        norm_second_new,
        norm_new,
    )


def solution(mesh):
    n_seq, n_dp = mesh.shape["seq"], mesh.shape["dp"]
    inner = Mesh(
        mesh.devices.reshape(n_dp, n_seq // n_dp, n_dp // 2, 2), ("a", "b", "y", "core")
    )
    seq, dp, every = ("a", "b"), ("y", "core"), ("a", "b", "y", "core")
    block = P(dp, seq, None)
    owned = P(every, None, None)
    in_specs = (block, block, P(dp, seq), P(), owned, owned, owned, P(), P(), P())
    out_specs = (block, block, owned, owned, owned, owned, owned, P(), P(), P(), P())
    return jax.shard_map(
        functools.partial(per_device, (n_seq, n_dp)),
        mesh=inner,
        in_specs=in_specs,
        out_specs=out_specs,
        check_vma=False,
    )
```

```python
import functools

import jax
import jax.numpy as jnp
import numpy as np
from jax import lax
from jax.experimental import pallas as pl
from jax.experimental.pallas import tpu as pltpu
from jax.sharding import Mesh
from jax.sharding import PartitionSpec as P

HEADS = 12
GROUPS = 4
TRIO = HEADS // GROUPS
STEP = 4

NORM_EPS = 1e-06
BETA_ONE = 0.5
BETA_TWO = 0.5
DECAY = 0.01
ADAM_EPS = 1e-08
NORM_RATE = 0.3
OUT_RATE = 0.35
MASKED = -1e30
CHUNKS = 6
VMEM_LIMIT = 60 * 1024 * 1024
MESH_IDS = pl.DeviceIdType.MESH
F32 = jnp.float32
BF16 = jnp.bfloat16


def head_slopes(head_count, tok_rows, seq_devices):
    head_order = np.arange(head_count, dtype=np.float64)
    slopes = 8.0 / tok_rows * np.power(8.0 * seq_devices, -head_order / (head_count - 1))
    return slopes.astype(np.float32)


def locate_pieces(owners, slot_count):
    pieces = owners.shape[0]
    numbers = jnp.arange(pieces, dtype=jnp.int32)
    earlier = (owners[None, :] == owners[:, None]) & (numbers[None, :] < numbers[:, None])
    return owners * slot_count + jnp.sum(earlier.astype(jnp.int32), axis=1)


def slot_rates(inverse, piece_rows, model_width, hidden_units):
    first_row = (inverse - 1) * piece_rows
    narrow = model_width ** (-0.5)
    step_rate = jnp.where(
        first_row < 3 * model_width,
        narrow,
        jnp.where(
            first_row < 4 * model_width,
            OUT_RATE,
            jnp.where(
                first_row < 4 * model_width + 2 * hidden_units, narrow, hidden_units ** (-0.5)
            ),
        ),
    )
    return jnp.where(inverse > 0, step_rate, narrow).astype(jnp.float32)


def adamw_step(weight, first_moment, second, gradient, step_rate, step_count):
    first_moment = BETA_ONE * first_moment + (1.0 - BETA_ONE) * gradient
    second = BETA_TWO * second + (1.0 - BETA_TWO) * gradient * gradient
    mean_hat = first_moment / (1.0 - BETA_ONE**step_count)
    square_hat = second / (1.0 - BETA_TWO**step_count)
    weight = weight - step_rate * (mean_hat / (jnp.sqrt(square_hat) + ADAM_EPS) + DECAY * weight)
    return (first_moment, second, weight)


def dot_nt(left_side, right_side):
    return lax.dot_general(
        left_side, right_side, (((1,), (1,)), ((), ())), preferred_element_type=F32
    )


def dot_nn(left_side, right_side):
    return lax.dot_general(
        left_side, right_side, (((1,), (0,)), ((), ())), preferred_element_type=F32
    )


def dot_tn(left_side, right_side):
    return lax.dot_general(
        left_side, right_side, (((0,), (0,)), ((), ())), preferred_element_type=F32
    )


def fetch_piece(place, piece, weights, dst, sem):
    pltpu.make_async_copy(weights.at[place[piece]], dst, sem).start()


def fill_tables(table, slopes, group, tok):
    apart = lax.broadcasted_iota(jnp.int32, (tok, tok), 0) - lax.broadcasted_iota(
        jnp.int32, (tok, tok), 1
    )
    apart = apart.astype(F32)
    for h in range(TRIO):
        slope = slopes[group * TRIO + h]
        table[h * 3 + 0] = -slope * apart
        table[h * 3 + 1] = slope * jnp.abs(apart)
        table[h * 3 + 2] = slope * apart


def block_place(order, n_dp, reps):
    return (order % n_dp) * reps + order // n_dp


def bias_of(key_block, query_place, slope, h, tok, n_dp, reps):
    key_place = block_place(key_block, n_dp, reps)
    which = jnp.where(key_place > query_place, 2, jnp.where(key_place < query_place, 0, 1))
    shift = slope * (tok * jnp.abs(key_place - query_place)).astype(F32)
    return h * 3 + which, shift


def holder(order, n_dp):
    dp = lax.rem(order, n_dp)
    return {"b": lax.div(order, n_dp), "y": lax.div(dp, 2), "core": lax.rem(dp, 2)}


def turn_to():
    z, dp = lax.axis_index("a"), lax.axis_index("y") * 2 + lax.axis_index("core")
    return {"a": dp, "y": lax.div(z, 2), "core": lax.rem(z, 2)}, dp != z


def start_turn(src, dst, send_sem, recv_sem):
    peer, moves = turn_to()

    @pl.when(moves)
    def _():
        pltpu.make_async_remote_copy(
            src_ref=src,
            dst_ref=dst,
            send_sem=send_sem,
            recv_sem=recv_sem,
            device_id=peer,
            device_id_type=MESH_IDS,
        ).start()

    @pl.when(jnp.logical_not(moves))
    def _():
        pltpu.make_async_copy(src, dst, recv_sem).start()


def finish_turn(src, dst, send_sem, recv_sem):
    peer, moves = turn_to()

    @pl.when(moves)
    def _():
        pltpu.make_async_remote_copy(
            src_ref=src,
            dst_ref=dst,
            send_sem=send_sem,
            recv_sem=recv_sem,
            device_id=peer,
            device_id_type=MESH_IDS,
        ).wait()

    @pl.when(jnp.logical_not(moves))
    def _():
        pltpu.make_async_copy(src, dst, recv_sem).wait()


def greet(peers, turning=False, meanwhile=None):
    barrier = pltpu.get_barrier_semaphore()
    for peer in peers:
        pl.semaphore_signal(barrier, inc=1, device_id=peer, device_id_type=MESH_IDS)
    if meanwhile is not None:
        meanwhile()
    if not turning:
        pl.semaphore_wait(barrier, len(peers))
        return
    turn_peer, moves = turn_to()

    @pl.when(moves)
    def _():
        pl.semaphore_signal(barrier, inc=1, device_id=turn_peer, device_id_type=MESH_IDS)

    pl.semaphore_wait(barrier, len(peers) + moves.astype(jnp.int32))


def my_order(n_dp):
    return lax.axis_index("b") * n_dp + lax.axis_index("y") * 2 + lax.axis_index("core")


def remote(src, dst, sems, index, peer):
    return pltpu.make_async_remote_copy(
        src_ref=src,
        dst_ref=dst,
        send_sem=sems.at[0, index],
        recv_sem=sems.at[1, index],
        device_id=peer,
        device_id_type=MESH_IDS,
    )


def project_kernel(
    sizes,
    place,
    x_ref,
    weights,
    q_out,
    k_out,
    kt_out,
    v_out,
    vt_out,
    wpad,
    sems,
):
    n_dp, splits, tok, head, blocks = sizes
    order = my_order(n_dp)
    group, split = lax.div(order, splits), lax.rem(order, splits)
    per_head = head // 16
    width = x_ref.shape[2]
    kind_pieces = width // 16

    def spot(step):
        kind = lax.div(step, TRIO * per_head)
        rest = lax.rem(step, TRIO * per_head)
        dst = wpad.at[
            kind * TRIO + lax.div(rest, per_head), pl.ds(lax.rem(rest, per_head) * 16, 16)
        ]
        return kind * kind_pieces + group * (TRIO * per_head) + rest, dst

    def start(step, carry):
        number, dst = spot(step)
        fetch_piece(place, number, weights, dst, sems.at[step])
        return carry

    def finish(step, carry):
        pltpu.make_async_copy(weights.at[0], spot(step)[1], sems.at[step]).wait()
        return carry

    lax.fori_loop(0, 3 * TRIO * per_head, start, None, unroll=6)
    for row in range(3 * TRIO):
        wpad[row, head:, :] = jnp.zeros((wpad.shape[1] - head, width), BF16)
    lax.fori_loop(0, 3 * TRIO * per_head, finish, None)

    w_query = wpad[0:TRIO].reshape(TRIO * 128, width)
    w_key = wpad[TRIO : 2 * TRIO].reshape(TRIO * 128, width)
    w_value = wpad[2 * TRIO : 3 * TRIO].reshape(TRIO * 128, width)

    def marks_of(block):
        segs = x_ref[block, tok : tok + 1, 0:tok].astype(F32)
        number = lax.broadcasted_iota(jnp.int32, (128, tok), 0) - head
        same = segs == number.astype(F32)
        used = (number >= 0) & (number < 3)
        query_marks = jnp.where(same & used, 1.0, 0.0)
        key_marks = jnp.where(used & jnp.logical_not(same), MASKED, 0.0)
        return query_marks.T.astype(BF16), key_marks.T.astype(BF16)

    def project(block, carry):
        rows = pl.ds(pl.multiple_of(block * tok, tok), tok)
        xb = x_ref[block, 0:tok, :]
        keys = dot_nt(xb, w_key)
        values = dot_nt(xb, w_value)
        marks = marks_of(block)[1]
        for h in range(TRIO):
            key = keys[:, h * 128 : (h + 1) * 128]
            value = values[:, h * 128 : (h + 1) * 128]
            k_out[h, rows, :] = key.astype(BF16) + marks
            v_out[h, rows, :] = value[:, 0:head].astype(BF16)
            kt_out[h, :, rows] = key.T[0:head].astype(BF16)
            vt_out[h, :, rows] = value.T[0:head].astype(BF16)
        return carry

    lax.fori_loop(0, blocks, project, None)

    def project_query(index, carry):
        block = index * splits + split
        rows = pl.ds(pl.multiple_of(index * tok, tok), tok)
        xb = x_ref[block, 0:tok, :]
        queries = dot_nt(xb, w_query).astype(BF16) * jnp.asarray(head**-0.5, BF16)
        marks = marks_of(block)[0]
        for h in range(TRIO):
            q_out[h, rows, :] = queries[:, h * 128 : (h + 1) * 128] + marks
        return carry

    lax.fori_loop(0, GROUPS, project_query, None)


def attend_forward_kernel(
    sizes,
    slopes,
    q_ref,
    k_ref,
    vt_ref,
    cot_in,
    mixed_full,
    log_out,
    mixed_own,
    cot_out,
    table,
    scores,
    mixed_low,
    swap_sems,
    turn_sems,
):
    n_dp, reps, splits, tok, head, blocks = sizes
    order = my_order(n_dp)
    group, split = lax.div(order, splits), lax.rem(order, splits)
    others = [lax.rem(group + k, GROUPS) for k in range(1, GROUPS)]
    peers = [holder(other * splits + split, n_dp) for other in others]
    started = []
    greet(peers, True)
    turn_refs = (cot_in, cot_out, turn_sems.at[0], turn_sems.at[1])
    start_turn(*turn_refs)
    fill_tables(table, slopes, group, tok)

    def attend(index, h):
        place_order = index * splits + split
        query_place = lax.rem(place_order, n_dp) * reps + lax.div(place_order, n_dp)
        slope = slopes[group * TRIO + h]
        qh = q_ref[h, pl.ds(pl.multiple_of(index * tok, tok), tok), :]
        top = None
        shifts = []
        for kb in range(blocks):
            which, shift = bias_of(kb, query_place, slope, h, tok, n_dp, reps)
            now = dot_nt(k_ref[h, kb * tok : (kb + 1) * tok, :], qh) - table[which]
            scores[kb] = now
            here = jnp.max(now, axis=0, keepdims=True) - shift
            top = here if top is None else jnp.maximum(top, here)
            shifts.append(shift)
        total = jnp.zeros((1, tok), F32)
        for kb in range(blocks):
            grown = jnp.exp(scores[kb] - (top + shifts[kb]))
            total = total + jnp.sum(grown, axis=0, keepdims=True)
            scores[kb] = grown
        inverse = 1.0 / total
        mixed = jnp.zeros((head, tok), F32)
        for kb in range(blocks):
            prob = (scores[kb] * inverse).astype(BF16)
            mixed = mixed + dot_nn(vt_ref[h, :, kb * tok : (kb + 1) * tok], prob)
        mixed_full[index, h] = mixed
        mixed_low[index, h] = mixed.astype(BF16)
        log_out[index, h] = top + jnp.log(total)

    for k in list(range(GROUPS - 1)) + [None]:
        index = group if k is None else others[k]

        def one(h, carry, index=index):
            attend(index, h)
            return carry

        lax.fori_loop(0, TRIO, one, None)
        if k is not None:
            copy = swap_copy(mixed_low, mixed_own, index, group, swap_sems, k, peers[k])
            copy.start()
            started.append(copy)
        else:
            mixed_own[group] = mixed_low[group]
    for copy in started:
        copy.wait()
    finish_turn(*turn_refs)


def swap_copy(src, dst, there, here, sems, index, peer):
    return pltpu.make_async_remote_copy(
        src_ref=src.at[there],
        dst_ref=dst.at[here],
        send_sem=sems.at[0, index],
        recv_sem=sems.at[1, index],
        device_id=peer,
        device_id_type=MESH_IDS,
    )


def norm_steps(dims, norm_in, norm_out, refs):
    zn, xn, yn = dims
    norm_core, norm_y, norm_x, norm_z, norm_sum, sems = refs
    z, x = lax.axis_index("a"), lax.axis_index("b")
    y, core = lax.axis_index("y"), lax.axis_index("core")
    rounds = [
        (norm_core, [{"core": 1 - core}]),
        (norm_y, [{"y": lax.rem(y + k, yn)} for k in range(1, yn)]),
        (norm_x, [{"b": lax.rem(x + k, xn)} for k in range(1, xn)]),
        (norm_z, [{"a": lax.rem(z + k, zn)} for k in range(1, zn)]),
    ]
    first = [sum(len(peers) for _, peers in rounds[:i]) for i in range(len(rounds))]

    def copies(i):
        buffer, peers = rounds[i]
        return [
            remote(norm_sum.at[i], buffer.at[k], sems, first[i] + k, peer)
            for k, peer in enumerate(peers)
        ]

    def begin():
        norm_sum[0] = norm_in[...]
        for copy in copies(0):
            copy.start()

    def turn_round(i):
        total = norm_sum[i]
        for k, copy in enumerate(copies(i)):
            copy.wait()
            total = total + rounds[i][0][k]
        if i + 1 == len(rounds):
            norm_out[...] = total
            return
        norm_sum[i + 1] = total
        for copy in copies(i + 1):
            copy.start()

    peers = [peer for _, group in rounds for peer in group]
    return peers, [begin] + [functools.partial(turn_round, i) for i in range(len(rounds))]


def attend_backward_kernel(
    sizes,
    slopes,
    q_ref,
    k_ref,
    kt_ref,
    v_ref,
    mixed_full,
    log_in,
    d_mixed,
    low_in,
    norm_in,
    own_ref,
    low_out,
    norm_out,
    dk_sum,
    dv_sum,
    table,
    d_blocks,
    shared,
    pairs,
    landed,
    swap_sems,
    query_sems,
    pair_sems,
    value_sems,
    turn_sems,
    *norm_refs,
):
    n_dp, reps, splits, tok, head, blocks = sizes
    order = my_order(n_dp)
    group, split = lax.div(order, splits), lax.rem(order, splits)
    twins = [lax.rem(split + k, splits) for k in range(1, splits)]
    twin_ids = [holder(group * splits + other, n_dp) for other in twins]
    others = [lax.rem(group + k, GROUPS) for k in range(1, GROUPS)]
    peers = [holder(other * splits + split, n_dp) for other in others]
    norm_peers, norms = norm_steps((n_dp, reps, n_dp // 2), norm_in, norm_out, norm_refs)
    greet(twin_ids + peers + norm_peers, True)
    turn_refs = (low_in, low_out, turn_sems.at[0], turn_sems.at[1])
    started = []

    def launch(copy):
        copy.start()
        started.append(copy)

    for k in range(GROUPS - 1):
        launch(remote(d_mixed.at[others[k]], d_blocks.at[group], swap_sems, k, peers[k]))
    d_blocks[group] = d_mixed[group]
    norms.pop(0)()
    fill_tables(table, slopes, group, tok)
    dk_sum[...] = jnp.zeros_like(dk_sum)
    dv_sum[...] = jnp.zeros_like(dv_sum)

    def step_fn(h, step):
        index = lax.rem(group + GROUPS - step, GROUPS)
        if h == 0:

            @pl.when(step > 0)
            def _():
                view = d_blocks.at[index]
                remote(view, view, swap_sems, step - 1, peers[0]).wait_recv()

        place_order = index * splits + split
        query_place = lax.rem(place_order, n_dp) * reps + lax.div(place_order, n_dp)
        slope = slopes[group * TRIO + h]
        qh = q_ref[h, pl.ds(pl.multiple_of(index * tok, tok), tok), :]
        dt = d_blocks[index, h]
        row_dot = jnp.sum(dt.astype(F32) * mixed_full[index, h], axis=0, keepdims=True)
        log_total = log_in[index, h]
        dq = jnp.zeros((head, tok), F32)
        for kb in range(blocks):
            rows = slice(kb * tok, (kb + 1) * tok)
            which, shift = bias_of(kb, query_place, slope, h, tok, n_dp, reps)
            now = dot_nt(k_ref[h, rows, :], qh) - table[which]
            prob = jnp.exp(now - (log_total + shift))
            d_prob = dot_nn(v_ref[h, rows, :], dt)
            d_score = (prob * (d_prob - row_dot)).astype(BF16)
            dv_sum[rows, :] += dot_nt(prob.astype(BF16), dt)
            dk_sum[rows, :] += dot_nn(d_score, qh)
            dq = dq + dot_nn(kt_ref[h, :, rows], d_score)
        shared[index, 0, h] = (dq * (head**-0.5)).astype(BF16)

    def pair_copy(h, k):
        return remote(
            pairs.at[h, twins[k]], landed.at[h, k], pair_sems, h * (splits - 1) + k, twin_ids[k]
        )

    def take_pairs(h):
        for k in range(splits - 1):
            pair_copy(h, k).wait_recv()
        for index in range(GROUPS):
            for kind in range(2):
                total = pairs[h, split, index, kind].astype(F32)
                for k in range(splits - 1):
                    total = total + landed[h, k, index, kind].astype(F32)
                shared[index, kind + 1, h] = total.astype(BF16)
        for k in range(GROUPS - 1):
            launch(
                remote(
                    shared.at[others[k], pl.ds(1, 2), h],
                    own_ref.at[group, pl.ds(1, 2), h],
                    value_sems,
                    h * (GROUPS - 1) + k,
                    peers[k],
                )
            )

    for h in range(TRIO):

        def one(step, carry, h=h):
            step_fn(h, step)
            return carry

        lax.fori_loop(0, GROUPS, one, None)
        if h == 0:
            start_turn(*turn_refs)
        norms.pop(0)()
        for k in range(GROUPS - 1):
            launch(
                remote(
                    shared.at[others[k], 0, h],
                    own_ref.at[group, 0, h],
                    query_sems,
                    h * (GROUPS - 1) + k,
                    peers[k],
                )
            )

        def flip(index, carry, h=h):
            for part in range(splits):
                rows = pl.ds(pl.multiple_of((index * splits + part) * tok, tok), tok)
                pairs[h, part, index, 0] = dk_sum[rows, :].T[0:head].astype(BF16)
                pairs[h, part, index, 1] = dv_sum[rows, :].T.astype(BF16)
            return carry

        lax.fori_loop(0, GROUPS, flip, None)
        if h + 1 < TRIO:
            dk_sum[...] = jnp.zeros_like(dk_sum)
            dv_sum[...] = jnp.zeros_like(dv_sum)
        for k in range(splits - 1):
            launch(pair_copy(h, k))
        if h > 0:
            take_pairs(h - 1)
    for step in norms:
        step()
    take_pairs(TRIO - 1)
    own_ref[group] = shared[group]
    for h in range(TRIO):
        for k in range(GROUPS - 1):
            view = own_ref.at[others[k], 0, h]
            remote(view, view, query_sems, h * (GROUPS - 1) + k, peers[k]).wait_recv()
            view = own_ref.at[others[k], pl.ds(1, 2), h]
            remote(view, view, value_sems, h * (GROUPS - 1) + k, peers[k]).wait_recv()
    finish_turn(*turn_refs)
    for copy in started:
        copy.wait_send()


def norm_stats(values_in):
    mean = jnp.mean(values_in, axis=-1, keepdims=True)
    centred = values_in - mean
    spread = jnp.mean(centred * centred, axis=-1, keepdims=True)
    scale = lax.rsqrt(spread + NORM_EPS)
    return centred * scale, scale


def norm_back(unit, scale, gain, cotangent):
    d_unit = cotangent * gain
    first = jnp.mean(d_unit, axis=-1, keepdims=True)
    second = jnp.mean(d_unit * unit, axis=-1, keepdims=True)
    d_in = scale * (d_unit - first - unit * second)
    d_gain = jnp.sum(cotangent * unit, axis=0, keepdims=True)
    d_bias = jnp.sum(cotangent, axis=0, keepdims=True)
    return d_in, d_gain, d_bias


def dense_kernel(
    sizes,
    place,
    gathered,
    cot_ref,
    mixed_ref,
    norm_ref,
    weights,
    out_ref,
    d_pre_one_ref,
    d_mixed_ref,
    norm_grad,
    grads,
    w_out,
    w_gate,
    w_up,
    w_down,
    keep_gate,
    keep_up,
    keep_hidden,
    stage,
    stage_out,
    x_ref,
    load_sems,
    store_sems,
    own_sem,
):
    n_dp, tok, piece, kind_pieces, chunk_pieces, hidden_pieces = sizes
    own_copy = pltpu.make_async_copy(
        gathered.at[my_order(n_dp), pl.ds(0, tok)], x_ref, own_sem
    )
    own_copy.start()
    first_gate = 4 * kind_pieces
    first_up = first_gate + hidden_pieces
    first_down = first_up + hidden_pieces
    bases = (first_gate, first_up, first_down)
    buffers = (w_gate, w_up, w_down)
    chunk = chunk_pieces * piece

    for step in range(kind_pieces):
        dst = w_out.at[pl.ds(step * piece, piece)]
        fetch_piece(place, 3 * kind_pieces + step, weights, dst, load_sems.at[3 * CHUNKS])

    def load_chunk(c):
        for step in range(chunk_pieces):
            for kind in range(3):
                dst = buffers[kind].at[c, pl.ds(step * piece, piece)]
                number = bases[kind] + c * chunk_pieces + step
                fetch_piece(place, number, weights, dst, load_sems.at[kind * CHUNKS + c])

    def wait_chunk(c):
        for kind in range(3):
            view = buffers[kind].at[c]
            pltpu.make_async_copy(view, view, load_sems.at[kind * CHUNKS + c]).wait()

    load_chunk(0)
    mixed = mixed_ref[...].T
    own_copy.wait()
    pltpu.make_async_copy(w_out, w_out, load_sems.at[3 * CHUNKS]).wait()
    pre_one = x_ref[...].astype(F32) + dot_nt(mixed, w_out[...])
    load_chunk(1)
    unit_one, scale_one = norm_stats(pre_one)
    h_one = unit_one * norm_ref[0:1, :] + norm_ref[1:2, :]
    h_low = h_one.astype(BF16)

    pre_two = h_one
    for c in range(CHUNKS):
        wait_chunk(c)
        gate = dot_nt(w_gate[c], h_low)
        up = dot_nt(w_up[c], h_low)
        if c + 2 < CHUNKS:
            load_chunk(c + 2)
        below = 0.5 * (1.0 + lax.erf(gate * (0.5**0.5)))
        gelu = gate * below
        slope = below + gate * (jnp.exp(-0.5 * gate * gate) * (0.5 / jnp.pi) ** 0.5)
        hidden = (gelu * up).astype(BF16)
        keep_gate[c] = up * slope
        keep_up[c] = gelu
        keep_hidden[c] = hidden
        pre_two = pre_two + dot_tn(hidden, w_down[c])

    unit_two, scale_two = norm_stats(pre_two)
    out_ref[...] = (unit_two * norm_ref[2:3, :] + norm_ref[3:4, :]).astype(BF16)
    d_pre_two, d_gain_two, d_bias_two = norm_back(
        unit_two, scale_two, norm_ref[2:3, :], cot_ref[...].astype(F32)
    )
    d_branch = d_pre_two.astype(BF16)

    def drain(slot):
        for kind in range(3):
            view = stage.at[slot, kind]
            pltpu.make_async_copy(view, view, store_sems.at[slot * 3 + kind]).wait()

    d_h = d_pre_two
    for c in range(CHUNKS):
        slot = c % 2
        if c >= 2:
            drain(slot)
        d_hidden = dot_nt(w_down[c], d_branch)
        d_gate = (d_hidden * keep_gate[c]).astype(BF16)
        d_up = (d_hidden * keep_up[c]).astype(BF16)
        stage[slot, 0] = dot_nn(d_gate, h_low).astype(BF16)
        stage[slot, 1] = dot_nn(d_up, h_low).astype(BF16)
        stage[slot, 2] = dot_nn(keep_hidden[c], d_branch).astype(BF16)
        for step in range(chunk_pieces):
            for kind in range(3):
                pltpu.make_async_copy(
                    stage.at[slot, kind, pl.ds(step * piece, piece)],
                    grads.at[place[bases[kind] + c * chunk_pieces + step]],
                    store_sems.at[slot * 3 + kind],
                ).start()
        d_h = d_h + dot_tn(d_gate, w_gate[c]) + dot_tn(d_up, w_up[c])

    d_pre_one, d_gain_one, d_bias_one = norm_back(unit_one, scale_one, norm_ref[0:1, :], d_h)
    d_pre_one_ref[...] = d_pre_one
    d_proj = d_pre_one.astype(BF16)
    stage_out[...] = dot_tn(d_proj, mixed).astype(BF16)
    for step in range(kind_pieces):
        pltpu.make_async_copy(
            stage_out.at[pl.ds(step * piece, piece)],
            grads.at[place[3 * kind_pieces + step]],
            store_sems.at[6],
        ).start()
    d_mixed_ref[...] = lax.dot_general(
        w_out[...], d_proj, (((0,), (1,)), ((), ())), preferred_element_type=F32
    ).astype(BF16)
    norm_grad[...] = jnp.concatenate(
        [
            d_gain_one,
            d_bias_one,
            d_gain_two,
            d_bias_two,
            jnp.zeros((4, d_gain_one.shape[1]), F32),
        ],
        axis=0,
    )
    drain(CHUNKS % 2)
    drain((CHUNKS + 1) % 2)
    pltpu.make_async_copy(stage_out, stage_out, store_sems.at[6]).wait()


def project_grad_kernel(
    sizes,
    place,
    gathered,
    d_own,
    d_pre_one,
    weights,
    grads_in,
    d_input,
    grads,
    w_all,
    stage,
    x_ref,
    load_sems,
    store_sems,
    own_sem,
):
    n_dp, tok, piece, kind_pieces = sizes
    own_copy = pltpu.make_async_copy(
        gathered.at[my_order(n_dp), pl.ds(0, tok)], x_ref, own_sem
    )
    own_copy.start()
    group_pieces = kind_pieces // GROUPS
    del grads_in

    def each(group):
        for kind in range(3):
            for step in range(group_pieces):
                row = (kind * group_pieces + step) * piece
                yield kind * kind_pieces + group * group_pieces + step, pl.ds(row, piece)

    def load(group):
        for number, span in each(group):
            fetch_piece(place, number, weights, w_all.at[group, span], load_sems.at[group])

    load(0)
    load(1)
    own_copy.wait()
    x_own = x_ref[...]
    for group in range(GROUPS):
        stage[group] = dot_nn(d_own[group], x_own).astype(BF16)
        if group + 2 < GROUPS:
            load(group + 2)
        for number, span in each(group):
            pltpu.make_async_copy(
                stage.at[group, span], grads.at[place[number]], store_sems.at[group]
            ).start()
    total = d_pre_one[...]
    for group in range(GROUPS):
        view = w_all.at[group]
        pltpu.make_async_copy(view, view, load_sems.at[group]).wait()
        total = total + dot_tn(d_own[group], w_all[group])
    d_input[...] = total.astype(BF16)
    for group in range(GROUPS):
        view = stage.at[group]
        pltpu.make_async_copy(view, view, store_sems.at[group]).wait()


def add_low(dst, src, rows):
    def one(i, carry):
        dst[i] = (dst[i].astype(F32) + src[i].astype(F32)).astype(BF16)
        return carry

    lax.fori_loop(0, rows, one, None)


def z_order_of(count):
    order = [0]
    for k in range(1, count):
        for far in (k, count - k):
            if far not in order:
                order.append(far)
    return order


def spread_steps(sizes, own, every, sems):
    zn, xn, yn, slots, last = sizes
    z_sems, xs_sems, ys_sems, xf_sems, yf_sems, near_sems, own_sem = sems[:7]
    xb_sems, yb_sems, zb_sems, nb_sems = sems[7:11]
    count = slots - last
    part = count * 9 // 16
    rest = count - part
    z, x = lax.axis_index("a"), lax.axis_index("b")
    y, core = lax.axis_index("y"), lax.axis_index("core")
    core_peer = {"core": 1 - core}
    xs, ys, z_order = range(1, xn), range(1, yn), z_order_of(zn)
    x_peers = {k: {"b": lax.rem(x + k, xn)} for k in xs}
    y_peers = {k: {"y": lax.rem(y + k, yn)} for k in ys}
    z_peers = {k: {"a": lax.rem(z + k, zn)} for k in range(1, zn)}
    source = own.at[pl.ds(0, count)]

    def number(jz, jx, jy):
        chip = (lax.rem(z + zn - jz, zn) * xn + lax.rem(x + xn - jx, xn)) * yn + lax.rem(
            y + yn - jy, yn
        )
        return chip * 2 + core

    def shard(jz, jx, jy, lead=0, rows=count):
        return every.at[pl.ds(number(jz, jx, jy) * slots + lead, rows)]

    def tail(jz, jx, jy):
        return shard(jz, jx, jy, count, last)

    def tail_held(jz, jx, jy):
        return own.at[pl.ds(count, last)] if (jz, jx, jy) == (0, 0, 0) else tail(jz, jx, jy)

    def xb_copy(jx, jy):
        index = (jx - 1) * yn + jy
        return remote(tail_held(0, 0, jy), tail(0, 0, jy), xb_sems, index, x_peers[jx])

    def yb_copy(jy):
        return remote(tail_held(0, 0, 0), tail(0, 0, 0), yb_sems, jy - 1, y_peers[jy])

    def zb_copy(jz, jx, jy):
        index = ((jz - 1) * xn + jx) * yn + jy
        return remote(tail_held(0, jx, jy), tail(0, jx, jy), zb_sems, index, z_peers[jz])

    def nb_copy(jz, jx, jy):
        index = (jz * xn + jx) * yn + jy
        return remote(tail_held(jz, jx, jy), tail(jz, jx, jy), nb_sems, index, core_peer)

    def tail_begin():
        for jy in ys:
            launch(yb_copy(jy))
        for jx in xs:
            launch(xb_copy(jx, 0))
        launch(nb_copy(0, 0, 0))

    def tail_across():
        for jy in ys:
            view = tail(0, 0, jy)
            remote(view, view, yb_sems, jy - 1, y_peers[jy]).wait_recv()
            for jx in xs:
                launch(xb_copy(jx, jy))
            launch(nb_copy(0, 0, jy))

    def tail_planes():
        for jx in xs:
            for jy in range(yn):
                view = tail(0, jx, jy)
                remote(view, view, xb_sems, (jx - 1) * yn + jy, x_peers[jx]).wait_recv()
                launch(nb_copy(0, jx, jy))
        for jz in z_order[1:]:
            for jx in range(xn):
                for jy in range(yn):
                    launch(zb_copy(jz, jx, jy))

    def tail_end():
        for jz in z_order[1:]:
            for jx in range(xn):
                for jy in range(yn):
                    view = tail(jz, jx, jy)
                    index = ((jz - 1) * xn + jx) * yn + jy
                    remote(view, view, zb_sems, index, z_peers[jz]).wait_recv()
                    launch(nb_copy(jz, jx, jy))

    def tail_settle():
        for jz in range(zn):
            for jx in range(xn):
                for jy in range(yn):
                    chip = lax.div(number(jz, jx, jy), 2)
                    view = every.at[pl.ds((chip * 2 + 1 - core) * slots + count, last)]
                    index = (jz * xn + jx) * yn + jy
                    remote(view, view, nb_sems, index, core_peer).wait_recv()

    def held(jz, jx, jy):
        return source if (jz, jx, jy) == (0, 0, 0) else shard(jz, jx, jy)

    def z_copy(jz):
        return remote(source, shard(0, 0, 0), z_sems, jz - 1, z_peers[jz])

    def xs_copy(jz, jx):
        return remote(
            held(jz, 0, 0), shard(jz, 0, 0), xs_sems, jz * (xn - 1) + jx - 1, x_peers[jx]
        )

    def ys_copy(jz, jy):
        return remote(
            held(jz, 0, 0), shard(jz, 0, 0), ys_sems, jz * (yn - 1) + jy - 1, y_peers[jy]
        )

    def cross(jz, jx, jy):
        return (jz * (xn - 1) + jx - 1) * (yn - 1) + jy - 1

    def xf_copy(jz, jx, jy):
        view = shard(jz, 0, jy, part, rest)
        return remote(view, view, xf_sems, cross(jz, jx, jy), x_peers[jx])

    def yf_copy(jz, jx, jy):
        view = shard(jz, jx, 0, 0, part)
        return remote(view, view, yf_sems, cross(jz, jx, jy), y_peers[jy])

    def near_copy(jz, jx, jy):
        return remote(
            held(jz, jx, jy),
            shard(jz, jx, jy),
            near_sems,
            (jz * xn + jx) * yn + jy,
            core_peer,
        )

    started = []

    def launch(copy):
        copy.start()
        started.append(copy)

    def send_own(jz):
        for jx in xs:
            launch(xs_copy(jz, jx))
        for jy in ys:
            launch(ys_copy(jz, jy))
        launch(near_copy(jz, 0, 0))

    def ys_copy_in(jz, jy):
        view = shard(jz, 0, jy)
        remote(view, view, ys_sems, jz * (yn - 1) + jy - 1, y_peers[jy]).wait_recv()

    def xs_copy_in(jz, jx):
        view = shard(jz, jx, 0)
        remote(view, view, xs_sems, jz * (xn - 1) + jx - 1, x_peers[jx]).wait_recv()

    def forward(jz):
        for jy in ys:
            ys_copy_in(jz, jy)
            for jx in xs:
                launch(xf_copy(jz, jx, jy))
        for jx in xs:
            xs_copy_in(jz, jx)
            for jy in ys:
                launch(yf_copy(jz, jx, jy))
        for jy in ys:
            launch(near_copy(jz, 0, jy))
        for jx in xs:
            launch(near_copy(jz, jx, 0))

    def finish(jz):
        for jx in xs:
            for jy in ys:
                view = shard(jz, jx, jy, part, rest)
                remote(view, view, xf_sems, cross(jz, jx, jy), x_peers[jx]).wait_recv()
                view = shard(jz, jx, jy, 0, part)
                remote(view, view, yf_sems, cross(jz, jx, jy), y_peers[jy]).wait_recv()
                launch(near_copy(jz, jx, jy))

    def z_in(index):
        jz = z_order[index]
        view = shard(jz, 0, 0)
        remote(view, view, z_sems, jz - 1, z_peers[jz]).wait_recv()
        if index + 1 < zn:
            launch(z_copy(z_order[index + 1]))

    own_local = pltpu.make_async_copy(own, shard(0, 0, 0, 0, slots), own_sem)

    def begin():
        launch(z_copy(z_order[1]))
        send_own(0)
        own_local.start()
        if last:
            tail_begin()

    def advance(index):
        z_in(index)
        send_own(z_order[index])
        if last and index == 1:
            tail_across()

    def forward_step(index):
        forward(z_order[index])
        if last and index == zn - 2:
            tail_planes()

    def end():
        finish(z_order[zn - 1])
        if last:
            tail_end()
            tail_settle()
        for jz in range(zn):
            for jx in range(xn):
                for jy in range(yn):
                    chip = lax.div(number(jz, jx, jy), 2)
                    view = every.at[pl.ds((chip * 2 + 1 - core) * slots, count)]
                    remote(
                        view, view, near_sems, (jz * xn + jx) * yn + jy, core_peer
                    ).wait_recv()

    def settle():
        own_local.wait()
        for copy in started:
            copy.wait_send()

    steps = [begin]
    for index in range(1, zn):
        steps.append(functools.partial(advance, index))
        steps.append(functools.partial(forward_step, index - 1))
        if index >= 2:
            steps.append(functools.partial(finish, z_order[index - 2]))
    steps.append(functools.partial(forward_step, zn - 1))
    steps.append(functools.partial(finish, z_order[zn - 2]))
    steps.append(end)
    steps.append(settle)
    return [core_peer, *x_peers.values(), *y_peers.values(), *z_peers.values()], steps


def block_steps(sizes, pack, gathered, crossed, sems):
    zn, xn, yn = sizes
    by_sems, bz_sems, bx_sems, bn_sems, stay_sem = sems
    z, x = lax.axis_index("a"), lax.axis_index("b")
    y, core = lax.axis_index("y"), lax.axis_index("core")
    core_peer = {"core": 1 - core}
    xs, ys, z_order = range(1, xn), range(1, yn), z_order_of(zn)
    x_peers = {k: {"b": lax.rem(x + k, xn)} for k in xs}
    y_peers = {k: {"y": lax.rem(y + k, yn)} for k in ys}
    z_peers = {k: {"a": lax.rem(z + k, zn)} for k in range(1, zn)}
    hosts = lax.rem(z, 2) == core

    def block(jz, jx=0):
        return gathered.at[lax.rem(x + xn - jx, xn) * zn + lax.rem(z + zn - jz, zn)]

    def by_copy(jy):
        return remote(pack, crossed.at[jy - 1], by_sems, jy - 1, y_peers[jy])

    def plane(jy):
        return lax.rem(y + yn - jy, yn) * 2 + core

    def bz_copy(jy):
        src = pack if jy == 0 else crossed.at[jy - 1]
        far = lax.rem(plane(jy) + zn - z, zn)
        return remote(src, block(0), bz_sems, far, {"a": plane(jy)})

    def stay_copy(jy):
        src = pack if jy == 0 else crossed.at[jy - 1]
        return pltpu.make_async_copy(src, block(0), stay_sem)

    def bx_copy(jz, jx):
        return remote(block(jz), block(jz), bx_sems, jz * (xn - 1) + jx - 1, x_peers[jx])

    def bn_copy(jz, jx):
        return remote(block(jz, jx), block(jz, jx), bn_sems, jz * xn + jx, core_peer)

    def cross_y():
        for jy in ys:
            by_copy(jy).start()

    def to_planes():
        for jy in range(yn):
            if jy != 0:
                by_copy(jy).wait_recv()

            @pl.when(plane(jy) != z)
            def _():
                bz_copy(jy).start()

            @pl.when(plane(jy) == z)
            def _():
                stay_copy(jy).start()
                stay_copy(jy).wait()

    def across():
        @pl.when(hosts)
        def _():
            for jz in z_order:
                if jz != 0:
                    remote(block(jz), block(jz), bz_sems, jz, z_peers[jz]).wait_recv()
                for jx in xs:
                    bx_copy(jz, jx).start()
                bn_copy(jz, 0).start()

    def end():
        @pl.when(hosts)
        def _():
            for jz in z_order:
                for jx in xs:
                    view = block(jz, jx)
                    index = jz * (xn - 1) + jx - 1
                    remote(view, view, bx_sems, index, x_peers[jx]).wait_recv()
                    bn_copy(jz, jx).start()
            for jz in z_order:
                for jx in xs:
                    bx_copy(jz, jx).wait_send()
                for jx in range(xn):
                    bn_copy(jz, jx).wait_send()

        @pl.when(jnp.logical_not(hosts))
        def _():
            for jz in range(zn):
                for jx in range(xn):
                    bn_copy(jz, jx).wait_recv()

        for jy in range(yn):

            @pl.when(plane(jy) != z)
            def _():
                bz_copy(jy).wait_send()

        for jy in ys:
            by_copy(jy).wait_send()

    return [cross_y, to_planes, across, end]


def spread_kernel(
    sizes, master, x_in, seg_in, every, gathered, crossed, own, pack, *sems
):
    peers, steps = spread_steps(sizes, own, every, sems[:11])
    cross_y, to_planes, across, end = block_steps(sizes[:3], pack, gathered, crossed, sems[11:])
    tok, width = x_in.shape

    def prepare():
        own[...] = master[...].astype(BF16)
        pack[0:tok, :] = x_in[...]
        segs = jnp.concatenate(
            [seg_in[...].astype(F32), jnp.zeros((1, width - tok), F32)], axis=1
        )
        pack[tok:, :] = jnp.broadcast_to(segs, (pack.shape[0] - tok, width)).astype(BF16)

    greet(peers, meanwhile=prepare)
    steps[0]()
    cross_y()
    for step in steps[1:-7]:
        step()
    to_planes()
    for step in steps[-7:-3]:
        step()
    across()
    steps[-3]()
    steps[-2]()
    end()
    steps[-1]()


def reduce_steps(sizes, grads, total_out, refs):
    zn, xn, yn, slots = sizes
    held, near, xd, yd, xs_in, ys_in, zs_in = refs[:7]
    load_sems, near_sems, xd_sems, yd_sems, xs_sems, ys_sems, zs_sems = refs[7:14]
    part = slots // 2
    rest = slots - part
    z, x = lax.axis_index("a"), lax.axis_index("b")
    y, core = lax.axis_index("y"), lax.axis_index("core")
    core_peer = {"core": 1 - core}
    xs, ys = range(1, xn), range(1, yn)
    y_peers = [{"y": lax.rem(y + k, yn)} for k in ys]
    x_peers = [{"b": lax.rem(x + k, xn)} for k in xs]
    z_peers = [{"a": lax.rem(z + k, zn)} for k in range(1, zn)]
    def flat(jz, jx, jy):
        return (jz * xn + jx) * yn + jy

    def chip_rows(jz, jx, jy, which):
        chip = (lax.rem(z + jz, zn) * xn + lax.rem(x + jx, xn)) * yn + lax.rem(y + jy, yn)
        return grads.at[pl.ds((chip * 2 + which) * slots, slots)]

    def near_copy(jz, jx, jy):
        index = flat(jz, jx, jy)
        return remote(chip_rows(jz, jx, jy, 1 - core), near.at[index], near_sems, index, core_peer)

    def load_copy(jz, jx, jy):
        index = flat(jz, jx, jy)
        return pltpu.make_async_copy(
            chip_rows(jz, jx, jy, core), held.at[index], load_sems.at[index]
        )

    def whole(jz, jx, jy):
        return held.at[flat(jz, jx, jy)]

    def first(jz, jx, jy):
        return held.at[flat(jz, jx, jy), pl.ds(0, part)]

    def second(jz, jx, jy):
        return held.at[flat(jz, jx, jy), pl.ds(part, rest)]

    def cross(jz, jx, jy):
        return (jz * (xn - 1) + jx - 1) * (yn - 1) + jy - 1

    def yd_copy(jz, jx, jy):
        index = cross(jz, jx, jy)
        return remote(first(jz, jx, jy), yd.at[index], yd_sems, index, y_peers[jy - 1])

    def xd_copy(jz, jx, jy):
        index = cross(jz, jx, jy)
        return remote(second(jz, jx, jy), xd.at[index], xd_sems, index, x_peers[jx - 1])

    def halves(low_half):
        return pl.ds(0, part) if low_half else pl.ds(part, rest)

    def xs_copy(jz, jx, low_half):
        index = jz * (xn - 1) + jx - 1
        return remote(
            held.at[flat(jz, jx, 0), halves(low_half)],
            xs_in.at[index, halves(low_half)],
            xs_sems,
            index * 2 + int(low_half),
            x_peers[jx - 1],
        )

    def ys_copy(jz, jy, low_half):
        index = jz * (yn - 1) + jy - 1
        return remote(
            held.at[flat(jz, 0, jy), halves(low_half)],
            ys_in.at[index, halves(low_half)],
            ys_sems,
            index * 2 + int(low_half),
            y_peers[jy - 1],
        )

    def zs_copy(jz):
        return remote(whole(jz, 0, 0), zs_in.at[jz - 1], zs_sems, jz - 1, z_peers[jz - 1])

    z_order = z_order_of(zn)[::-1]
    started = []

    def launch(copy):
        copy.start()
        started.append(copy)

    def plane(jz):
        return (
            [(jz, jx, jy) for jx in xs for jy in ys]
            + [(jz, jx, 0) for jx in xs]
            + [(jz, 0, jy) for jy in ys]
            + [(jz, 0, 0)]
        )

    def fetch(jz):
        for chip in plane(jz):
            launch(near_copy(*chip))
            load_copy(*chip).start()

    def prepare(index):
        for chip in plane(z_order[index]):
            load_copy(*chip).wait()
            near_copy(*chip).wait_recv()
            add_low(whole(*chip), near.at[flat(*chip)], slots)
        if index + 1 < zn:
            fetch(z_order[index + 1])

    stages = [(index, stage) for index in range(zn) for stage in range(3)]

    def send_stage(number):
        index, stage = stages[number]
        jz = z_order[index]
        for jx in xs:
            if stage == 0:
                for jy in ys:
                    launch(xd_copy(jz, jx, jy))
            else:
                launch(xs_copy(jz, jx, stage == 2))
        for jy in ys:
            if stage == 0:
                for jx in xs:
                    launch(yd_copy(jz, jx, jy))
            else:
                launch(ys_copy(jz, jy, stage == 1))

    def take_stage(number):
        index, stage = stages[number]
        jz = z_order[index]
        if stage == 0:
            for jx in xs:
                for jy in ys:
                    yd_copy(jz, jx, jy).wait_recv()
                    add_low(first(jz, jx, 0), yd.at[cross(jz, jx, jy)], part)
                    xd_copy(jz, jx, jy).wait_recv()
                    add_low(second(jz, 0, jy), xd.at[cross(jz, jx, jy)], rest)
        else:
            for jx in xs:
                xs_copy(jz, jx, stage == 2).wait_recv()
            for jy in ys:
                ys_copy(jz, jy, stage == 1).wait_recv()

    def side_in(index):
        jz = z_order[index]

        def one(i, carry):
            total = held[flat(jz, 0, 0), i].astype(F32)
            for jx in xs:
                total = total + xs_in[jz * (xn - 1) + jx - 1, i].astype(F32)
            for jy in ys:
                total = total + ys_in[jz * (yn - 1) + jy - 1, i].astype(F32)
            if jz != 0:
                held[flat(jz, 0, 0), i] = total.astype(BF16)
            else:
                total_out[i] = total
            return carry

        lax.fori_loop(0, slots, one, None)
        if jz != 0:
            launch(zs_copy(jz))

    ahead = 2

    def begin():
        fetch(z_order[0])

    def begin_stages():
        prepare(0)
        for number in range(ahead):
            send_stage(number)

    def one_stage(number):
        take_stage(number)
        later = number + ahead
        if later < len(stages):
            if stages[later][1] == 0:
                prepare(stages[later][0])
            send_stage(later)
        if stages[number][1] == 2:
            side_in(stages[number][0])

    def end():
        for jz in range(1, zn):
            zs_copy(jz).wait_recv()

        def add_planes(i, carry):
            total = total_out[i]
            for jz in range(1, zn):
                total = total + zs_in[jz - 1, i].astype(F32)
            total_out[i] = total
            return carry

        lax.fori_loop(0, slots, add_planes, None)
        for copy in started:
            copy.wait_send()

    steps = [begin, begin_stages]
    steps += [functools.partial(one_stage, number) for number in range(len(stages))]
    steps.append(end)
    return [core_peer] + y_peers + x_peers + z_peers, steps


def reduce_kernel(sizes, grads, tokens_in, total_out, tokens_out, *refs):
    peers, steps = reduce_steps(sizes, grads, total_out, refs[:14])
    turn_sems = refs[14]
    greet(peers, True)
    turn_refs = (tokens_in, tokens_out, turn_sems.at[0], turn_sems.at[1])
    start_turn(*turn_refs)
    for step in steps:
        step()
    finish_turn(*turn_refs)


def vmem():
    return pl.BlockSpec(memory_space=pltpu.VMEM)


def smem():
    return pl.BlockSpec(memory_space=pltpu.SMEM)


def anywhere():
    return pl.BlockSpec(memory_space=pl.ANY)


def shape_of(dims, kind):
    return jax.ShapeDtypeStruct(dims, kind)


def params(collective=None):
    if collective is None:
        return pltpu.CompilerParams(vmem_limit_bytes=VMEM_LIMIT)
    return pltpu.CompilerParams(
        vmem_limit_bytes=VMEM_LIMIT, collective_id=collective, has_side_effects=True
    )


def pair(count):
    return pltpu.SemaphoreType.DMA((2, max(count, 1)))


def spread_scratch(zn, xn, yn):
    return [
        pair(zn - 1),
        pair(zn * (xn - 1)),
        pair(zn * (yn - 1)),
        pair(zn * (xn - 1) * (yn - 1)),
        pair(zn * (xn - 1) * (yn - 1)),
        pair(zn * xn * yn),
        pltpu.SemaphoreType.DMA,
        pair((xn - 1) * yn),
        pair(yn - 1),
        pair((zn - 1) * xn * yn),
        pair(zn * xn * yn),
    ]


def reduce_scratch(zn, xn, yn, slots, piece, width):
    def chunks(number, rows):
        return pltpu.VMEM((max(number, 1), rows, piece, width), BF16)

    n_chips, crossing = zn * xn * yn, zn * (xn - 1) * (yn - 1)
    part = slots // 2
    return [
        chunks(n_chips, slots),
        chunks(n_chips, slots),
        chunks(crossing, slots - part),
        chunks(crossing, part),
        chunks(zn * (xn - 1), slots),
        chunks(zn * (yn - 1), slots),
        chunks(zn - 1, slots),
        pltpu.SemaphoreType.DMA((n_chips,)),
        pair(n_chips),
        pair(crossing),
        pair(crossing),
        pair(2 * zn * (xn - 1)),
        pair(2 * zn * (yn - 1)),
        pair(zn - 1),
    ]


def run_layer(dims, weight_master, x_own, segments, cotangent, location, norm_params):
    n_seq, n_dp = dims
    reps = n_seq // n_dp
    splits = n_seq // GROUPS
    slots, piece, width = weight_master.shape
    tok = cotangent.shape[0]
    length = tok * n_seq
    hidden_units = (location.shape[0] * piece - 4 * width) // 3
    head = width // HEADS
    kind_pieces = width // piece
    hidden_pieces = hidden_units // piece
    chunk = hidden_units // CHUNKS
    zn, xn, yn = n_dp, reps, n_dp // 2
    all_slots = n_seq * n_dp * slots
    last = slots // 8
    slopes = jnp.asarray(head_slopes(HEADS, tok, n_seq))

    weights, gathered, _ = pl.pallas_call(
        functools.partial(spread_kernel, (zn, xn, yn, slots, last)),
        out_shape=(
            shape_of((all_slots, piece, width), BF16),
            shape_of((n_seq, tok + 16, width), BF16),
            shape_of((max(yn - 1, 1), tok + 16, width), BF16),
        ),
        in_specs=[vmem(), vmem(), vmem()],
        out_specs=(anywhere(),) * 3,
        scratch_shapes=[
            pltpu.VMEM((slots, piece, width), BF16),
            pltpu.VMEM((tok + 16, width), BF16),
        ]
        + spread_scratch(zn, xn, yn)
        + [
            pair(yn - 1),
            pair(zn),
            pair(zn * (xn - 1)),
            pair(zn * xn),
            pltpu.SemaphoreType.DMA,
        ],
        compiler_params=params(1),
    )(weight_master, x_own, segments)
    attend_sizes = (n_dp, reps, splits, tok, head, n_seq)
    q_ext, k_ext, k_turned, v_rows, v_turned = pl.pallas_call(
        functools.partial(project_kernel, (n_dp, splits, tok, head, n_seq)),
        out_shape=(
            shape_of((TRIO, GROUPS * tok, 128), BF16),
            shape_of((TRIO, length, 128), BF16),
            shape_of((TRIO, head, length), BF16),
            shape_of((TRIO, length, head), BF16),
            shape_of((TRIO, head, length), BF16),
        ),
        in_specs=[smem(), vmem(), anywhere()],
        out_specs=(vmem(),) * 5,
        scratch_shapes=[
            pltpu.VMEM((3 * TRIO, 128, width), BF16),
            pltpu.SemaphoreType.DMA((3 * TRIO * (head // piece),)),
        ],
        compiler_params=params(),
    )(location, gathered, weights)

    mixed_full, log_total, mixed_own, cotangent = pl.pallas_call(
        functools.partial(attend_forward_kernel, attend_sizes),
        out_shape=(
            shape_of((GROUPS, TRIO, head, tok), F32),
            shape_of((GROUPS, TRIO, 1, tok), F32),
            shape_of((GROUPS, TRIO, head, tok), BF16),
            shape_of(cotangent.shape, BF16),
        ),
        in_specs=[smem(), vmem(), vmem(), vmem(), anywhere()],
        out_specs=(vmem(), vmem(), vmem(), anywhere()),
        scratch_shapes=[
            pltpu.VMEM((3 * TRIO, tok, tok), F32),
            pltpu.VMEM((n_seq, tok, tok), F32),
            pltpu.VMEM((GROUPS, TRIO, head, tok), BF16),
            pair(GROUPS - 1),
            pltpu.SemaphoreType.DMA((2,)),
        ],
        compiler_params=params(2),
    )(slopes, q_ext, k_ext, v_turned, cotangent)

    out_low, d_pre_one, d_mixed, norm_part, grads = pl.pallas_call(
        functools.partial(
            dense_kernel, (n_dp, tok, piece, kind_pieces, chunk // piece, hidden_pieces)
        ),
        out_shape=(
            shape_of((tok, width), BF16),
            shape_of((tok, width), F32),
            shape_of((width, tok), BF16),
            shape_of((8, width), F32),
            shape_of((all_slots, piece, width), BF16),
        ),
        in_specs=[smem(), anywhere(), vmem(), vmem(), vmem(), anywhere()],
        out_specs=(vmem(), vmem(), vmem(), vmem(), anywhere()),
        scratch_shapes=[
            pltpu.VMEM((width, width), BF16),
            pltpu.VMEM((CHUNKS, chunk, width), BF16),
            pltpu.VMEM((CHUNKS, chunk, width), BF16),
            pltpu.VMEM((CHUNKS, chunk, width), BF16),
            pltpu.VMEM((CHUNKS, chunk, tok), F32),
            pltpu.VMEM((CHUNKS, chunk, tok), F32),
            pltpu.VMEM((CHUNKS, chunk, tok), BF16),
            pltpu.VMEM((2, 3, chunk, width), BF16),
            pltpu.VMEM((width, width), BF16),
            pltpu.VMEM((tok, width), BF16),
            pltpu.SemaphoreType.DMA((3 * CHUNKS + 1,)),
            pltpu.SemaphoreType.DMA((7,)),
            pltpu.SemaphoreType.DMA,
        ],
        compiler_params=params(),
    )(location, gathered, cotangent, mixed_own.reshape(width, tok), norm_params, weights)

    def norm_rows(count):
        return pltpu.VMEM((max(count, 1), 8, width), F32)

    d_own, result, norm_total = pl.pallas_call(
        functools.partial(attend_backward_kernel, attend_sizes),
        out_shape=(
            shape_of((GROUPS, 3, TRIO, head, tok), BF16),
            shape_of(out_low.shape, BF16),
            shape_of((8, width), F32),
        ),
        in_specs=[smem()] + [vmem()] * 7 + [anywhere(), vmem()],
        out_specs=(vmem(), anywhere(), vmem()),
        scratch_shapes=[
            pltpu.VMEM((length, 128), F32),
            pltpu.VMEM((length, head), F32),
            pltpu.VMEM((3 * TRIO, tok, tok), F32),
            pltpu.VMEM((GROUPS, TRIO, head, tok), BF16),
            pltpu.VMEM((GROUPS, 3, TRIO, head, tok), BF16),
            pltpu.VMEM((TRIO, splits, GROUPS, 2, head, tok), BF16),
            pltpu.VMEM((TRIO, splits - 1, GROUPS, 2, head, tok), BF16),
            pair(GROUPS - 1),
            pair(TRIO * (GROUPS - 1)),
            pair(TRIO * (splits - 1)),
            pair(TRIO * (GROUPS - 1)),
            pltpu.SemaphoreType.DMA((2,)),
            norm_rows(1),
            norm_rows(yn - 1),
            norm_rows(xn - 1),
            norm_rows(zn - 1),
            norm_rows(4),
            pair(1 + (yn - 1) + (xn - 1) + (zn - 1)),
        ],
        compiler_params=params(3),
    )(
        slopes,
        q_ext,
        k_ext,
        k_turned,
        v_rows,
        mixed_full,
        log_total,
        d_mixed.reshape(GROUPS, TRIO, head, tok),
        out_low,
        norm_part,
    )

    trio_rows = TRIO * head
    d_tokens, grads = pl.pallas_call(
        functools.partial(project_grad_kernel, (n_dp, tok, piece, kind_pieces)),
        out_shape=(shape_of((tok, width), BF16), shape_of(grads.shape, BF16)),
        in_specs=[smem(), anywhere(), vmem(), vmem()] + [anywhere()] * 2,
        out_specs=(vmem(), anywhere()),
        scratch_shapes=[
            pltpu.VMEM((GROUPS, 3 * trio_rows, width), BF16),
            pltpu.VMEM((GROUPS, 3 * trio_rows, width), BF16),
            pltpu.VMEM((tok, width), BF16),
            pltpu.SemaphoreType.DMA((GROUPS,)),
            pltpu.SemaphoreType.DMA((GROUPS,)),
            pltpu.SemaphoreType.DMA,
        ],
        input_output_aliases={5: 1},
        compiler_params=params(),
    )(location, gathered, d_own.reshape(GROUPS, 3 * trio_rows, tok), d_pre_one, weights, grads)

    own_grad, d_turned = pl.pallas_call(
        functools.partial(reduce_kernel, (zn, xn, yn, slots)),
        out_shape=(
            shape_of((slots, piece, width), F32),
            shape_of(d_tokens.shape, BF16),
        ),
        in_specs=[anywhere(), anywhere()],
        out_specs=(vmem(), anywhere()),
        scratch_shapes=reduce_scratch(zn, xn, yn, slots, piece, width)
        + [pltpu.SemaphoreType.DMA((2,))],
        compiler_params=params(4),
    )(grads, d_tokens)
    return own_grad, norm_total, d_turned, result


def per_device(
    dims,
    layer_input,
    out_cotangent,
    segment_ids,
    piece_owner,
    weight_master,
    weight_first,
    weight_second,
    norm_params,
    norm_first,
    norm_second,
):
    slots, piece, width = weight_master.shape
    pieces = piece_owner.shape[0]
    tok = layer_input.shape[1]
    hidden_units = (pieces * piece - 4 * width) // 3
    location = locate_pieces(piece_owner, slots)
    own_grad, norm_total, d_turned, result = run_layer(
        dims,
        weight_master,
        layer_input[0],
        segment_ids,
        out_cotangent[0],
        location,
        norm_params,
    )

    numbers = jnp.arange(pieces, dtype=jnp.int32) + 1
    own_slots = lax.axis_index(("a", "b", "y", "core")) * slots + jnp.arange(slots)
    inverse = jnp.sum(jnp.where(location[None, :] == own_slots[:, None], numbers[None, :], 0), axis=1)
    own_grad = jnp.where((inverse > 0)[:, None, None], own_grad, 0.0)
    norm_grad = norm_total[:4]
    rates = slot_rates(inverse, piece, width, hidden_units)
    first_new, second_new, weight_new = adamw_step(
        weight_master, weight_first, weight_second, own_grad, rates[:, None, None], STEP
    )
    norm_first_new, norm_second_new, norm_new = adamw_step(
        norm_params, norm_first, norm_second, norm_grad, NORM_RATE, STEP
    )
    return (
        result[None],
        d_turned.astype(F32)[None],
        own_grad,
        first_new,
        second_new,
        weight_new,
        weight_new.astype(BF16),
        norm_grad,
        norm_first_new,
        norm_second_new,
        norm_new,
    )


def solution(mesh):
    n_seq, n_dp = mesh.shape["seq"], mesh.shape["dp"]
    inner = Mesh(
        mesh.devices.reshape(n_dp, n_seq // n_dp, n_dp // 2, 2), ("a", "b", "y", "core")
    )
    seq, dp, every = ("a", "b"), ("y", "core"), ("a", "b", "y", "core")
    block = P(dp, seq, None)
    owned = P(every, None, None)
    in_specs = (block, block, P(dp, seq), P(), owned, owned, owned, P(), P(), P())
    out_specs = (block, block, owned, owned, owned, owned, owned, P(), P(), P(), P())
    return jax.shard_map(
        functools.partial(per_device, (n_seq, n_dp)),
        mesh=inner,
        in_specs=in_specs,
        out_specs=out_specs,
        check_vma=False,
    )
```

```python
import functools

import jax
import jax.numpy as jnp
import numpy as np
from jax import lax
from jax.experimental import pallas as pl
from jax.experimental.pallas import tpu as pltpu
from jax.sharding import Mesh
from jax.sharding import PartitionSpec as P

HEADS = 12
GROUPS = 4
TRIO = HEADS // GROUPS
STEP = 4

NORM_EPS = 1e-06
BETA_ONE = 0.5
BETA_TWO = 0.5
DECAY = 0.01
ADAM_EPS = 1e-08
NORM_RATE = 0.3
OUT_RATE = 0.35
MASKED = -1e30
CHUNKS = 6
VMEM_LIMIT = 60 * 1024 * 1024
MESH_IDS = pl.DeviceIdType.MESH
F32 = jnp.float32
BF16 = jnp.bfloat16


def head_slopes(head_count, tok_rows, seq_devices):
    head_order = np.arange(head_count, dtype=np.float64)
    slopes = 8.0 / tok_rows * np.power(8.0 * seq_devices, -head_order / (head_count - 1))
    return slopes.astype(np.float32)


def locate_pieces(owners, slot_count):
    pieces = owners.shape[0]
    numbers = jnp.arange(pieces, dtype=jnp.int32)
    earlier = (owners[None, :] == owners[:, None]) & (numbers[None, :] < numbers[:, None])
    return owners * slot_count + jnp.sum(earlier.astype(jnp.int32), axis=1)


def slot_rates(inverse, piece_rows, model_width, hidden_units):
    first_row = (inverse - 1) * piece_rows
    narrow = model_width ** (-0.5)
    step_rate = jnp.where(
        first_row < 3 * model_width,
        narrow,
        jnp.where(
            first_row < 4 * model_width,
            OUT_RATE,
            jnp.where(
                first_row < 4 * model_width + 2 * hidden_units, narrow, hidden_units ** (-0.5)
            ),
        ),
    )
    return jnp.where(inverse > 0, step_rate, narrow).astype(jnp.float32)


def adamw_step(weight, first_moment, second, gradient, step_rate, step_count):
    first_moment = BETA_ONE * first_moment + (1.0 - BETA_ONE) * gradient
    second = BETA_TWO * second + (1.0 - BETA_TWO) * gradient * gradient
    mean_hat = first_moment / (1.0 - BETA_ONE**step_count)
    square_hat = second / (1.0 - BETA_TWO**step_count)
    weight = weight - step_rate * (mean_hat / (jnp.sqrt(square_hat) + ADAM_EPS) + DECAY * weight)
    return (first_moment, second, weight)


def dot_nt(left_side, right_side):
    return lax.dot_general(
        left_side, right_side, (((1,), (1,)), ((), ())), preferred_element_type=F32
    )


def dot_nn(left_side, right_side):
    return lax.dot_general(
        left_side, right_side, (((1,), (0,)), ((), ())), preferred_element_type=F32
    )


def dot_tn(left_side, right_side):
    return lax.dot_general(
        left_side, right_side, (((0,), (0,)), ((), ())), preferred_element_type=F32
    )


def fetch_piece(place, piece, weights, dst, sem):
    pltpu.make_async_copy(weights.at[place[piece]], dst, sem).start()


def fill_tables(table, slopes, group, tok):
    apart = lax.broadcasted_iota(jnp.int32, (tok, tok), 0) - lax.broadcasted_iota(
        jnp.int32, (tok, tok), 1
    )
    apart = apart.astype(F32)
    for h in range(TRIO):
        slope = slopes[group * TRIO + h]
        table[h * 3 + 0] = -slope * apart
        table[h * 3 + 1] = slope * jnp.abs(apart)
        table[h * 3 + 2] = slope * apart


def block_place(order, n_dp, reps):
    return (order % n_dp) * reps + order // n_dp


def bias_of(key_block, query_place, slope, h, tok, n_dp, reps):
    key_place = block_place(key_block, n_dp, reps)
    which = jnp.where(key_place > query_place, 2, jnp.where(key_place < query_place, 0, 1))
    shift = slope * (tok * jnp.abs(key_place - query_place)).astype(F32)
    return h * 3 + which, shift


def holder(order, n_dp):
    dp = lax.rem(order, n_dp)
    return {"b": lax.div(order, n_dp), "y": lax.div(dp, 2), "core": lax.rem(dp, 2)}


def turn_to():
    z, dp = lax.axis_index("a"), lax.axis_index("y") * 2 + lax.axis_index("core")
    return {"a": dp, "y": lax.div(z, 2), "core": lax.rem(z, 2)}, dp != z


def start_turn(src, dst, send_sem, recv_sem):
    peer, moves = turn_to()

    @pl.when(moves)
    def _():
        pltpu.make_async_remote_copy(
            src_ref=src,
            dst_ref=dst,
            send_sem=send_sem,
            recv_sem=recv_sem,
            device_id=peer,
            device_id_type=MESH_IDS,
        ).start()

    @pl.when(jnp.logical_not(moves))
    def _():
        pltpu.make_async_copy(src, dst, recv_sem).start()


def finish_turn(src, dst, send_sem, recv_sem):
    peer, moves = turn_to()

    @pl.when(moves)
    def _():
        pltpu.make_async_remote_copy(
            src_ref=src,
            dst_ref=dst,
            send_sem=send_sem,
            recv_sem=recv_sem,
            device_id=peer,
            device_id_type=MESH_IDS,
        ).wait()

    @pl.when(jnp.logical_not(moves))
    def _():
        pltpu.make_async_copy(src, dst, recv_sem).wait()


def greet(peers, turning=False, meanwhile=None):
    barrier = pltpu.get_barrier_semaphore()
    for peer in peers:
        pl.semaphore_signal(barrier, inc=1, device_id=peer, device_id_type=MESH_IDS)
    if meanwhile is not None:
        meanwhile()
    if not turning:
        pl.semaphore_wait(barrier, len(peers))
        return
    turn_peer, moves = turn_to()

    @pl.when(moves)
    def _():
        pl.semaphore_signal(barrier, inc=1, device_id=turn_peer, device_id_type=MESH_IDS)

    pl.semaphore_wait(barrier, len(peers) + moves.astype(jnp.int32))


def my_order(n_dp):
    return lax.axis_index("b") * n_dp + lax.axis_index("y") * 2 + lax.axis_index("core")


def remote(src, dst, sems, index, peer):
    return pltpu.make_async_remote_copy(
        src_ref=src,
        dst_ref=dst,
        send_sem=sems.at[0, index],
        recv_sem=sems.at[1, index],
        device_id=peer,
        device_id_type=MESH_IDS,
    )


def project_kernel(
    sizes,
    place,
    x_ref,
    weights,
    q_out,
    k_out,
    kt_out,
    v_out,
    vt_out,
    wpad,
    sems,
):
    n_dp, splits, tok, head = sizes
    order = my_order(n_dp)
    group, split = lax.div(order, splits), lax.rem(order, splits)
    block = pl.program_id(0)
    per_head = head // 16
    width = x_ref.shape[2]
    kind_pieces = width // 16

    @pl.when(block == 0)
    def _():
        def spots():
            for kind in range(3):
                for rest in range(TRIO * per_head):
                    step = kind * TRIO * per_head + rest
                    rows = pl.ds(rest % per_head * 16, 16)
                    dst = wpad.at[kind * TRIO + rest // per_head, rows]
                    yield kind * kind_pieces + group * (TRIO * per_head) + rest, dst, sems.at[step]

        for number, dst, sem in spots():
            fetch_piece(place, number, weights, dst, sem)
        for row in range(3 * TRIO):
            wpad[row, head:, :] = jnp.zeros((wpad.shape[1] - head, width), BF16)
        for _, dst, sem in spots():
            pltpu.make_async_copy(weights.at[0], dst, sem).wait()

    segs = x_ref[0, tok : tok + 1, 0:tok].astype(F32)
    number = lax.broadcasted_iota(jnp.int32, (128, tok), 0) - head
    same = segs == number.astype(F32)
    used = (number >= 0) & (number < 3)
    xb = x_ref[0, 0:tok, :]
    keys = dot_nt(xb, wpad[TRIO : 2 * TRIO].reshape(TRIO * 128, width))
    values = dot_nt(xb, wpad[2 * TRIO : 3 * TRIO].reshape(TRIO * 128, width))
    marks = jnp.where(used & jnp.logical_not(same), MASKED, 0.0).T.astype(BF16)
    for h in range(TRIO):
        key = keys[:, h * 128 : (h + 1) * 128]
        value = values[:, h * 128 : (h + 1) * 128]
        k_out[h] = key.astype(BF16) + marks
        v_out[h] = value[:, 0:head].astype(BF16)
        kt_out[h] = key.T[0:head].astype(BF16)
        vt_out[h] = value.T[0:head].astype(BF16)

    @pl.when(lax.rem(block, splits) == split)
    def _():
        w_query = wpad[0:TRIO].reshape(TRIO * 128, width)
        queries = dot_nt(xb, w_query).astype(BF16) * jnp.asarray(head**-0.5, BF16)
        query_marks = jnp.where(same & used, 1.0, 0.0).T.astype(BF16)
        for h in range(TRIO):
            q_out[h] = queries[:, h * 128 : (h + 1) * 128] + query_marks


def attend_forward_kernel(
    sizes,
    slopes,
    q_ref,
    k_ref,
    vt_ref,
    cot_in,
    mixed_full,
    log_out,
    mixed_own,
    cot_out,
    table,
    scores,
    mixed_low,
    swap_sems,
    turn_sems,
):
    n_dp, reps, splits, tok, head, blocks = sizes
    order = my_order(n_dp)
    group, split = lax.div(order, splits), lax.rem(order, splits)
    others = [lax.rem(group + k, GROUPS) for k in range(1, GROUPS)]
    peers = [holder(other * splits + split, n_dp) for other in others]
    started = []
    greet(peers, True)
    turn_refs = (cot_in, cot_out, turn_sems.at[0], turn_sems.at[1])
    start_turn(*turn_refs)
    fill_tables(table, slopes, group, tok)

    def attend(index, h):
        place_order = index * splits + split
        query_place = lax.rem(place_order, n_dp) * reps + lax.div(place_order, n_dp)
        slope = slopes[group * TRIO + h]
        qh = q_ref[h, pl.ds(pl.multiple_of(index * tok, tok), tok), :]
        top = None
        shifts = []
        for kb in range(blocks):
            which, shift = bias_of(kb, query_place, slope, h, tok, n_dp, reps)
            now = dot_nt(k_ref[h, kb * tok : (kb + 1) * tok, :], qh) - table[which]
            scores[kb] = now
            here = jnp.max(now, axis=0, keepdims=True) - shift
            top = here if top is None else jnp.maximum(top, here)
            shifts.append(shift)
        total = jnp.zeros((1, tok), F32)
        for kb in range(blocks):
            grown = jnp.exp(scores[kb] - (top + shifts[kb]))
            total = total + jnp.sum(grown, axis=0, keepdims=True)
            scores[kb] = grown
        inverse = 1.0 / total
        mixed = jnp.zeros((head, tok), F32)
        for kb in range(blocks):
            prob = (scores[kb] * inverse).astype(BF16)
            mixed = mixed + dot_nn(vt_ref[h, :, kb * tok : (kb + 1) * tok], prob)
        mixed_full[index, h] = mixed
        mixed_low[index, h] = mixed.astype(BF16)
        log_out[index, h] = top + jnp.log(total)

    for k in list(range(GROUPS - 1)) + [None]:
        index = group if k is None else others[k]

        def one(h, carry, index=index):
            attend(index, h)
            return carry

        lax.fori_loop(0, TRIO, one, None)
        if k is not None:
            copy = swap_copy(mixed_low, mixed_own, index, group, swap_sems, k, peers[k])
            copy.start()
            started.append(copy)
        else:
            mixed_own[group] = mixed_low[group]
    for copy in started:
        copy.wait()
    finish_turn(*turn_refs)


def swap_copy(src, dst, there, here, sems, index, peer):
    return pltpu.make_async_remote_copy(
        src_ref=src.at[there],
        dst_ref=dst.at[here],
        send_sem=sems.at[0, index],
        recv_sem=sems.at[1, index],
        device_id=peer,
        device_id_type=MESH_IDS,
    )


def norm_steps(dims, norm_in, norm_out, refs):
    zn, xn, yn = dims
    norm_core, norm_y, norm_x, norm_z, norm_sum, sems = refs
    z, x = lax.axis_index("a"), lax.axis_index("b")
    y, core = lax.axis_index("y"), lax.axis_index("core")
    rounds = [
        (norm_core, [{"core": 1 - core}]),
        (norm_y, [{"y": lax.rem(y + k, yn)} for k in range(1, yn)]),
        (norm_x, [{"b": lax.rem(x + k, xn)} for k in range(1, xn)]),
        (norm_z, [{"a": lax.rem(z + k, zn)} for k in range(1, zn)]),
    ]
    first = [sum(len(peers) for _, peers in rounds[:i]) for i in range(len(rounds))]

    def copies(i):
        buffer, peers = rounds[i]
        return [
            remote(norm_sum.at[i], buffer.at[k], sems, first[i] + k, peer)
            for k, peer in enumerate(peers)
        ]

    def begin():
        norm_sum[0] = norm_in[...]
        for copy in copies(0):
            copy.start()

    def turn_round(i):
        total = norm_sum[i]
        for k, copy in enumerate(copies(i)):
            copy.wait()
            total = total + rounds[i][0][k]
        if i + 1 == len(rounds):
            norm_out[...] = total
            return
        norm_sum[i + 1] = total
        for copy in copies(i + 1):
            copy.start()

    peers = [peer for _, group in rounds for peer in group]
    return peers, [begin] + [functools.partial(turn_round, i) for i in range(len(rounds))]


def attend_backward_kernel(
    sizes,
    slopes,
    q_ref,
    k_ref,
    kt_ref,
    v_ref,
    mixed_full,
    log_in,
    d_mixed,
    low_in,
    norm_in,
    own_ref,
    low_out,
    norm_out,
    dk_sum,
    dv_sum,
    table,
    d_blocks,
    shared,
    pairs,
    landed,
    swap_sems,
    query_sems,
    pair_sems,
    value_sems,
    turn_sems,
    *norm_refs,
):
    n_dp, reps, splits, tok, head, blocks = sizes
    order = my_order(n_dp)
    group, split = lax.div(order, splits), lax.rem(order, splits)
    twins = [lax.rem(split + k, splits) for k in range(1, splits)]
    twin_ids = [holder(group * splits + other, n_dp) for other in twins]
    others = [lax.rem(group + k, GROUPS) for k in range(1, GROUPS)]
    peers = [holder(other * splits + split, n_dp) for other in others]
    norm_peers, norms = norm_steps((n_dp, reps, n_dp // 2), norm_in, norm_out, norm_refs)
    greet(twin_ids + peers + norm_peers, True)
    turn_refs = (low_in, low_out, turn_sems.at[0], turn_sems.at[1])
    started = []

    def launch(copy):
        copy.start()
        started.append(copy)

    for k in range(GROUPS - 1):
        launch(remote(d_mixed.at[others[k]], d_blocks.at[group], swap_sems, k, peers[k]))
    d_blocks[group] = d_mixed[group]
    norms.pop(0)()
    fill_tables(table, slopes, group, tok)
    dk_sum[...] = jnp.zeros_like(dk_sum)
    dv_sum[...] = jnp.zeros_like(dv_sum)

    def step_fn(h, step):
        index = lax.rem(group + GROUPS - step, GROUPS)
        if h == 0:

            @pl.when(step > 0)
            def _():
                view = d_blocks.at[index]
                remote(view, view, swap_sems, step - 1, peers[0]).wait_recv()

        place_order = index * splits + split
        query_place = lax.rem(place_order, n_dp) * reps + lax.div(place_order, n_dp)
        slope = slopes[group * TRIO + h]
        qh = q_ref[h, pl.ds(pl.multiple_of(index * tok, tok), tok), :]
        dt = d_blocks[index, h]
        row_dot = jnp.sum(dt.astype(F32) * mixed_full[index, h], axis=0, keepdims=True)
        log_total = log_in[index, h]
        dq = jnp.zeros((head, tok), F32)
        for kb in range(blocks):
            rows = slice(kb * tok, (kb + 1) * tok)
            which, shift = bias_of(kb, query_place, slope, h, tok, n_dp, reps)
            now = dot_nt(k_ref[h, rows, :], qh) - table[which]
            prob = jnp.exp(now - (log_total + shift))
            d_prob = dot_nn(v_ref[h, rows, :], dt)
            d_score = (prob * (d_prob - row_dot)).astype(BF16)
            dv_sum[rows, :] += dot_nt(prob.astype(BF16), dt)
            dk_sum[rows, :] += dot_nn(d_score, qh)
            dq = dq + dot_nn(kt_ref[h, :, rows], d_score)
        shared[index, 0, h] = (dq * (head**-0.5)).astype(BF16)

    def pair_copy(h, k):
        return remote(
            pairs.at[h, twins[k]], landed.at[h, k], pair_sems, h * (splits - 1) + k, twin_ids[k]
        )

    def take_pairs(h):
        for k in range(splits - 1):
            pair_copy(h, k).wait_recv()
        for index in range(GROUPS):
            for kind in range(2):
                total = pairs[h, split, index, kind].astype(F32)
                for k in range(splits - 1):
                    total = total + landed[h, k, index, kind].astype(F32)
                shared[index, kind + 1, h] = total.astype(BF16)
        for k in range(GROUPS - 1):
            launch(
                remote(
                    shared.at[others[k], pl.ds(1, 2), h],
                    own_ref.at[group, pl.ds(1, 2), h],
                    value_sems,
                    h * (GROUPS - 1) + k,
                    peers[k],
                )
            )

    for h in range(TRIO):

        def one(step, carry, h=h):
            step_fn(h, step)
            return carry

        lax.fori_loop(0, GROUPS, one, None)
        if h == 0:
            start_turn(*turn_refs)
        norms.pop(0)()
        for k in range(GROUPS - 1):
            launch(
                remote(
                    shared.at[others[k], 0, h],
                    own_ref.at[group, 0, h],
                    query_sems,
                    h * (GROUPS - 1) + k,
                    peers[k],
                )
            )

        def flip(index, carry, h=h):
            for part in range(splits):
                rows = pl.ds(pl.multiple_of((index * splits + part) * tok, tok), tok)
                pairs[h, part, index, 0] = dk_sum[rows, :].T[0:head].astype(BF16)
                pairs[h, part, index, 1] = dv_sum[rows, :].T.astype(BF16)
            return carry

        lax.fori_loop(0, GROUPS, flip, None)
        if h + 1 < TRIO:
            dk_sum[...] = jnp.zeros_like(dk_sum)
            dv_sum[...] = jnp.zeros_like(dv_sum)
        for k in range(splits - 1):
            launch(pair_copy(h, k))
        if h > 0:
            take_pairs(h - 1)
    for step in norms:
        step()
    take_pairs(TRIO - 1)
    own_ref[group] = shared[group]
    for h in range(TRIO):
        for k in range(GROUPS - 1):
            view = own_ref.at[others[k], 0, h]
            remote(view, view, query_sems, h * (GROUPS - 1) + k, peers[k]).wait_recv()
            view = own_ref.at[others[k], pl.ds(1, 2), h]
            remote(view, view, value_sems, h * (GROUPS - 1) + k, peers[k]).wait_recv()
    finish_turn(*turn_refs)
    for copy in started:
        copy.wait_send()


def norm_stats(values_in):
    mean = jnp.mean(values_in, axis=-1, keepdims=True)
    centred = values_in - mean
    spread = jnp.mean(centred * centred, axis=-1, keepdims=True)
    scale = lax.rsqrt(spread + NORM_EPS)
    return centred * scale, scale


def norm_back(unit, scale, gain, cotangent):
    d_unit = cotangent * gain
    first = jnp.mean(d_unit, axis=-1, keepdims=True)
    second = jnp.mean(d_unit * unit, axis=-1, keepdims=True)
    d_in = scale * (d_unit - first - unit * second)
    d_gain = jnp.sum(cotangent * unit, axis=0, keepdims=True)
    d_bias = jnp.sum(cotangent, axis=0, keepdims=True)
    return d_in, d_gain, d_bias


def dense_kernel(
    sizes,
    place,
    gathered,
    cot_ref,
    mixed_ref,
    norm_ref,
    weights,
    out_ref,
    d_pre_one_ref,
    d_mixed_ref,
    norm_grad,
    grads,
    w_out,
    w_gate,
    w_up,
    w_down,
    keep_gate,
    keep_up,
    keep_hidden,
    stage,
    stage_out,
    x_ref,
    load_sems,
    store_sems,
    own_sem,
):
    n_dp, tok, piece, kind_pieces, chunk_pieces, hidden_pieces = sizes
    own_copy = pltpu.make_async_copy(
        gathered.at[my_order(n_dp), pl.ds(0, tok)], x_ref, own_sem
    )
    own_copy.start()
    first_gate = 4 * kind_pieces
    first_up = first_gate + hidden_pieces
    first_down = first_up + hidden_pieces
    bases = (first_gate, first_up, first_down)
    buffers = (w_gate, w_up, w_down)
    chunk = chunk_pieces * piece

    for step in range(kind_pieces):
        dst = w_out.at[pl.ds(step * piece, piece)]
        fetch_piece(place, 3 * kind_pieces + step, weights, dst, load_sems.at[3 * CHUNKS])

    def load_chunk(c):
        for step in range(chunk_pieces):
            for kind in range(3):
                dst = buffers[kind].at[c, pl.ds(step * piece, piece)]
                number = bases[kind] + c * chunk_pieces + step
                fetch_piece(place, number, weights, dst, load_sems.at[kind * CHUNKS + c])

    def wait_chunk(c):
        for kind in range(3):
            view = buffers[kind].at[c]
            pltpu.make_async_copy(view, view, load_sems.at[kind * CHUNKS + c]).wait()

    load_chunk(0)
    mixed = mixed_ref[...].T
    own_copy.wait()
    pltpu.make_async_copy(w_out, w_out, load_sems.at[3 * CHUNKS]).wait()
    pre_one = x_ref[...].astype(F32) + dot_nt(mixed, w_out[...])
    load_chunk(1)
    unit_one, scale_one = norm_stats(pre_one)
    h_one = unit_one * norm_ref[0:1, :] + norm_ref[1:2, :]
    h_low = h_one.astype(BF16)

    pre_two = h_one
    for c in range(CHUNKS):
        wait_chunk(c)
        gate = dot_nt(w_gate[c], h_low)
        up = dot_nt(w_up[c], h_low)
        if c + 2 < CHUNKS:
            load_chunk(c + 2)
        below = 0.5 * (1.0 + lax.erf(gate * (0.5**0.5)))
        gelu = gate * below
        slope = below + gate * (jnp.exp(-0.5 * gate * gate) * (0.5 / jnp.pi) ** 0.5)
        hidden = (gelu * up).astype(BF16)
        keep_gate[c] = up * slope
        keep_up[c] = gelu
        keep_hidden[c] = hidden
        pre_two = pre_two + dot_tn(hidden, w_down[c])

    unit_two, scale_two = norm_stats(pre_two)
    out_ref[...] = (unit_two * norm_ref[2:3, :] + norm_ref[3:4, :]).astype(BF16)
    d_pre_two, d_gain_two, d_bias_two = norm_back(
        unit_two, scale_two, norm_ref[2:3, :], cot_ref[...].astype(F32)
    )
    d_branch = d_pre_two.astype(BF16)

    def drain(slot):
        for kind in range(3):
            view = stage.at[slot, kind]
            pltpu.make_async_copy(view, view, store_sems.at[slot * 3 + kind]).wait()

    d_h = d_pre_two
    for c in range(CHUNKS):
        slot = c % 2
        if c >= 2:
            drain(slot)
        d_hidden = dot_nt(w_down[c], d_branch)
        d_gate = (d_hidden * keep_gate[c]).astype(BF16)
        d_up = (d_hidden * keep_up[c]).astype(BF16)
        stage[slot, 0] = dot_nn(d_gate, h_low).astype(BF16)
        stage[slot, 1] = dot_nn(d_up, h_low).astype(BF16)
        stage[slot, 2] = dot_nn(keep_hidden[c], d_branch).astype(BF16)
        for step in range(chunk_pieces):
            for kind in range(3):
                pltpu.make_async_copy(
                    stage.at[slot, kind, pl.ds(step * piece, piece)],
                    grads.at[place[bases[kind] + c * chunk_pieces + step]],
                    store_sems.at[slot * 3 + kind],
                ).start()
        d_h = d_h + dot_tn(d_gate, w_gate[c]) + dot_tn(d_up, w_up[c])

    d_pre_one, d_gain_one, d_bias_one = norm_back(unit_one, scale_one, norm_ref[0:1, :], d_h)
    d_pre_one_ref[...] = d_pre_one
    d_proj = d_pre_one.astype(BF16)
    stage_out[...] = dot_tn(d_proj, mixed).astype(BF16)
    for step in range(kind_pieces):
        pltpu.make_async_copy(
            stage_out.at[pl.ds(step * piece, piece)],
            grads.at[place[3 * kind_pieces + step]],
            store_sems.at[6],
        ).start()
    d_mixed_ref[...] = lax.dot_general(
        w_out[...], d_proj, (((0,), (1,)), ((), ())), preferred_element_type=F32
    ).astype(BF16)
    norm_grad[...] = jnp.concatenate(
        [
            d_gain_one,
            d_bias_one,
            d_gain_two,
            d_bias_two,
            jnp.zeros((4, d_gain_one.shape[1]), F32),
        ],
        axis=0,
    )
    drain(CHUNKS % 2)
    drain((CHUNKS + 1) % 2)
    pltpu.make_async_copy(stage_out, stage_out, store_sems.at[6]).wait()


def project_grad_kernel(
    sizes,
    place,
    gathered,
    d_own,
    d_pre_one,
    weights,
    grads_in,
    d_input,
    grads,
    w_all,
    stage,
    x_ref,
    load_sems,
    store_sems,
    own_sem,
):
    n_dp, tok, piece, kind_pieces = sizes
    own_copy = pltpu.make_async_copy(
        gathered.at[my_order(n_dp), pl.ds(0, tok)], x_ref, own_sem
    )
    own_copy.start()
    group_pieces = kind_pieces // GROUPS
    del grads_in

    def each(group):
        for kind in range(3):
            for step in range(group_pieces):
                row = (kind * group_pieces + step) * piece
                yield kind * kind_pieces + group * group_pieces + step, pl.ds(row, piece)

    def load(group):
        for number, span in each(group):
            fetch_piece(place, number, weights, w_all.at[group, span], load_sems.at[group])

    load(0)
    load(1)
    own_copy.wait()
    x_own = x_ref[...]
    for group in range(GROUPS):
        stage[group] = dot_nn(d_own[group], x_own).astype(BF16)
        if group + 2 < GROUPS:
            load(group + 2)
        for number, span in each(group):
            pltpu.make_async_copy(
                stage.at[group, span], grads.at[place[number]], store_sems.at[group]
            ).start()
    total = d_pre_one[...]
    for group in range(GROUPS):
        view = w_all.at[group]
        pltpu.make_async_copy(view, view, load_sems.at[group]).wait()
        total = total + dot_tn(d_own[group], w_all[group])
    d_input[...] = total.astype(BF16)
    for group in range(GROUPS):
        view = stage.at[group]
        pltpu.make_async_copy(view, view, store_sems.at[group]).wait()


def add_low(dst, src, rows):
    def one(i, carry):
        dst[i] = (dst[i].astype(F32) + src[i].astype(F32)).astype(BF16)
        return carry

    lax.fori_loop(0, rows, one, None)


def z_order_of(count):
    order = [0]
    for k in range(1, count):
        for far in (k, count - k):
            if far not in order:
                order.append(far)
    return order


def spread_steps(sizes, own, every, sems):
    zn, xn, yn, slots, last = sizes
    z_sems, xs_sems, ys_sems, xf_sems, yf_sems, near_sems, own_sem = sems[:7]
    xb_sems, yb_sems, zb_sems, nb_sems = sems[7:11]
    count = slots - last
    part = count * 9 // 16
    rest = count - part
    z, x = lax.axis_index("a"), lax.axis_index("b")
    y, core = lax.axis_index("y"), lax.axis_index("core")
    core_peer = {"core": 1 - core}
    xs, ys, z_order = range(1, xn), range(1, yn), z_order_of(zn)
    x_peers = {k: {"b": lax.rem(x + k, xn)} for k in xs}
    y_peers = {k: {"y": lax.rem(y + k, yn)} for k in ys}
    z_peers = {k: {"a": lax.rem(z + k, zn)} for k in range(1, zn)}
    source = own.at[pl.ds(0, count)]

    def number(jz, jx, jy):
        chip = (lax.rem(z + zn - jz, zn) * xn + lax.rem(x + xn - jx, xn)) * yn + lax.rem(
            y + yn - jy, yn
        )
        return chip * 2 + core

    def shard(jz, jx, jy, lead=0, rows=count):
        return every.at[pl.ds(number(jz, jx, jy) * slots + lead, rows)]

    def tail(jz, jx, jy):
        return shard(jz, jx, jy, count, last)

    def tail_held(jz, jx, jy):
        return own.at[pl.ds(count, last)] if (jz, jx, jy) == (0, 0, 0) else tail(jz, jx, jy)

    def xb_copy(jx, jy):
        index = (jx - 1) * yn + jy
        return remote(tail_held(0, 0, jy), tail(0, 0, jy), xb_sems, index, x_peers[jx])

    def yb_copy(jy):
        return remote(tail_held(0, 0, 0), tail(0, 0, 0), yb_sems, jy - 1, y_peers[jy])

    def zb_copy(jz, jx, jy):
        index = ((jz - 1) * xn + jx) * yn + jy
        return remote(tail_held(0, jx, jy), tail(0, jx, jy), zb_sems, index, z_peers[jz])

    def nb_copy(jz, jx, jy):
        index = (jz * xn + jx) * yn + jy
        return remote(tail_held(jz, jx, jy), tail(jz, jx, jy), nb_sems, index, core_peer)

    def tail_begin():
        for jy in ys:
            launch(yb_copy(jy))
        for jx in xs:
            launch(xb_copy(jx, 0))
        launch(nb_copy(0, 0, 0))

    def tail_across():
        for jy in ys:
            view = tail(0, 0, jy)
            remote(view, view, yb_sems, jy - 1, y_peers[jy]).wait_recv()
            for jx in xs:
                launch(xb_copy(jx, jy))
            launch(nb_copy(0, 0, jy))

    def tail_planes():
        for jx in xs:
            for jy in range(yn):
                view = tail(0, jx, jy)
                remote(view, view, xb_sems, (jx - 1) * yn + jy, x_peers[jx]).wait_recv()
                launch(nb_copy(0, jx, jy))
        for jz in z_order[1:]:
            for jx in range(xn):
                for jy in range(yn):
                    launch(zb_copy(jz, jx, jy))

    def tail_end():
        for jz in z_order[1:]:
            for jx in range(xn):
                for jy in range(yn):
                    view = tail(jz, jx, jy)
                    index = ((jz - 1) * xn + jx) * yn + jy
                    remote(view, view, zb_sems, index, z_peers[jz]).wait_recv()
                    launch(nb_copy(jz, jx, jy))

    def tail_settle():
        for jz in range(zn):
            for jx in range(xn):
                for jy in range(yn):
                    chip = lax.div(number(jz, jx, jy), 2)
                    view = every.at[pl.ds((chip * 2 + 1 - core) * slots + count, last)]
                    index = (jz * xn + jx) * yn + jy
                    remote(view, view, nb_sems, index, core_peer).wait_recv()

    def held(jz, jx, jy):
        return source if (jz, jx, jy) == (0, 0, 0) else shard(jz, jx, jy)

    def z_copy(jz):
        return remote(source, shard(0, 0, 0), z_sems, jz - 1, z_peers[jz])

    def xs_copy(jz, jx):
        return remote(
            held(jz, 0, 0), shard(jz, 0, 0), xs_sems, jz * (xn - 1) + jx - 1, x_peers[jx]
        )

    def ys_copy(jz, jy):
        return remote(
            held(jz, 0, 0), shard(jz, 0, 0), ys_sems, jz * (yn - 1) + jy - 1, y_peers[jy]
        )

    def cross(jz, jx, jy):
        return (jz * (xn - 1) + jx - 1) * (yn - 1) + jy - 1

    def xf_copy(jz, jx, jy):
        view = shard(jz, 0, jy, part, rest)
        return remote(view, view, xf_sems, cross(jz, jx, jy), x_peers[jx])

    def yf_copy(jz, jx, jy):
        view = shard(jz, jx, 0, 0, part)
        return remote(view, view, yf_sems, cross(jz, jx, jy), y_peers[jy])

    def near_copy(jz, jx, jy):
        return remote(
            held(jz, jx, jy),
            shard(jz, jx, jy),
            near_sems,
            (jz * xn + jx) * yn + jy,
            core_peer,
        )

    started = []

    def launch(copy):
        copy.start()
        started.append(copy)

    def send_own(jz):
        for jx in xs:
            launch(xs_copy(jz, jx))
        for jy in ys:
            launch(ys_copy(jz, jy))
        launch(near_copy(jz, 0, 0))

    def ys_copy_in(jz, jy):
        view = shard(jz, 0, jy)
        remote(view, view, ys_sems, jz * (yn - 1) + jy - 1, y_peers[jy]).wait_recv()

    def xs_copy_in(jz, jx):
        view = shard(jz, jx, 0)
        remote(view, view, xs_sems, jz * (xn - 1) + jx - 1, x_peers[jx]).wait_recv()

    def forward(jz):
        for jy in ys:
            ys_copy_in(jz, jy)
            for jx in xs:
                launch(xf_copy(jz, jx, jy))
        for jx in xs:
            xs_copy_in(jz, jx)
            for jy in ys:
                launch(yf_copy(jz, jx, jy))
        for jy in ys:
            launch(near_copy(jz, 0, jy))
        for jx in xs:
            launch(near_copy(jz, jx, 0))

    def finish(jz):
        for jx in xs:
            for jy in ys:
                view = shard(jz, jx, jy, part, rest)
                remote(view, view, xf_sems, cross(jz, jx, jy), x_peers[jx]).wait_recv()
                view = shard(jz, jx, jy, 0, part)
                remote(view, view, yf_sems, cross(jz, jx, jy), y_peers[jy]).wait_recv()
                launch(near_copy(jz, jx, jy))

    def z_in(index):
        jz = z_order[index]
        view = shard(jz, 0, 0)
        remote(view, view, z_sems, jz - 1, z_peers[jz]).wait_recv()
        if index + 1 < zn:
            launch(z_copy(z_order[index + 1]))

    own_local = pltpu.make_async_copy(own, shard(0, 0, 0, 0, slots), own_sem)

    def begin():
        launch(z_copy(z_order[1]))
        send_own(0)
        own_local.start()
        if last:
            tail_begin()

    def advance(index):
        z_in(index)
        send_own(z_order[index])
        if last and index == 1:
            tail_across()

    def forward_step(index):
        forward(z_order[index])
        if last and index == zn - 2:
            tail_planes()

    def end():
        finish(z_order[zn - 1])
        if last:
            tail_end()
            tail_settle()
        for jz in range(zn):
            for jx in range(xn):
                for jy in range(yn):
                    chip = lax.div(number(jz, jx, jy), 2)
                    view = every.at[pl.ds((chip * 2 + 1 - core) * slots, count)]
                    remote(
                        view, view, near_sems, (jz * xn + jx) * yn + jy, core_peer
                    ).wait_recv()

    def settle():
        own_local.wait()
        for copy in started:
            copy.wait_send()

    steps = [begin]
    for index in range(1, zn):
        steps.append(functools.partial(advance, index))
        steps.append(functools.partial(forward_step, index - 1))
        if index >= 2:
            steps.append(functools.partial(finish, z_order[index - 2]))
    steps.append(functools.partial(forward_step, zn - 1))
    steps.append(functools.partial(finish, z_order[zn - 2]))
    steps.append(end)
    steps.append(settle)
    return [core_peer, *x_peers.values(), *y_peers.values(), *z_peers.values()], steps


def block_steps(sizes, pack, gathered, crossed, sems):
    zn, xn, yn = sizes
    by_sems, bz_sems, bx_sems, bn_sems, stay_sem = sems
    z, x = lax.axis_index("a"), lax.axis_index("b")
    y, core = lax.axis_index("y"), lax.axis_index("core")
    core_peer = {"core": 1 - core}
    xs, ys, z_order = range(1, xn), range(1, yn), z_order_of(zn)
    x_peers = {k: {"b": lax.rem(x + k, xn)} for k in xs}
    y_peers = {k: {"y": lax.rem(y + k, yn)} for k in ys}
    z_peers = {k: {"a": lax.rem(z + k, zn)} for k in range(1, zn)}
    hosts = lax.rem(z, 2) == core

    def block(jz, jx=0):
        return gathered.at[lax.rem(x + xn - jx, xn) * zn + lax.rem(z + zn - jz, zn)]

    def by_copy(jy):
        return remote(pack, crossed.at[jy - 1], by_sems, jy - 1, y_peers[jy])

    def plane(jy):
        return lax.rem(y + yn - jy, yn) * 2 + core

    def bz_copy(jy):
        src = pack if jy == 0 else crossed.at[jy - 1]
        far = lax.rem(plane(jy) + zn - z, zn)
        return remote(src, block(0), bz_sems, far, {"a": plane(jy)})

    def stay_copy(jy):
        src = pack if jy == 0 else crossed.at[jy - 1]
        return pltpu.make_async_copy(src, block(0), stay_sem)

    def bx_copy(jz, jx):
        return remote(block(jz), block(jz), bx_sems, jz * (xn - 1) + jx - 1, x_peers[jx])

    def bn_copy(jz, jx):
        return remote(block(jz, jx), block(jz, jx), bn_sems, jz * xn + jx, core_peer)

    def cross_y():
        for jy in ys:
            by_copy(jy).start()

    def to_planes():
        for jy in range(yn):
            if jy != 0:
                by_copy(jy).wait_recv()

            @pl.when(plane(jy) != z)
            def _():
                bz_copy(jy).start()

            @pl.when(plane(jy) == z)
            def _():
                stay_copy(jy).start()
                stay_copy(jy).wait()

    def across():
        @pl.when(hosts)
        def _():
            for jz in z_order:
                if jz != 0:
                    remote(block(jz), block(jz), bz_sems, jz, z_peers[jz]).wait_recv()
                for jx in xs:
                    bx_copy(jz, jx).start()
                bn_copy(jz, 0).start()

    def end():
        @pl.when(hosts)
        def _():
            for jz in z_order:
                for jx in xs:
                    view = block(jz, jx)
                    index = jz * (xn - 1) + jx - 1
                    remote(view, view, bx_sems, index, x_peers[jx]).wait_recv()
                    bn_copy(jz, jx).start()
            for jz in z_order:
                for jx in xs:
                    bx_copy(jz, jx).wait_send()
                for jx in range(xn):
                    bn_copy(jz, jx).wait_send()

        @pl.when(jnp.logical_not(hosts))
        def _():
            for jz in range(zn):
                for jx in range(xn):
                    bn_copy(jz, jx).wait_recv()

        for jy in range(yn):

            @pl.when(plane(jy) != z)
            def _():
                bz_copy(jy).wait_send()

        for jy in ys:
            by_copy(jy).wait_send()

    return [cross_y, to_planes, across, end]


def spread_kernel(
    sizes, master, x_in, seg_in, every, gathered, crossed, own, pack, *sems
):
    peers, steps = spread_steps(sizes, own, every, sems[:11])
    cross_y, to_planes, across, end = block_steps(sizes[:3], pack, gathered, crossed, sems[11:])
    tok, width = x_in.shape

    def prepare():
        own[...] = master[...].astype(BF16)
        pack[0:tok, :] = x_in[...]
        segs = jnp.concatenate(
            [seg_in[...].astype(F32), jnp.zeros((1, width - tok), F32)], axis=1
        )
        pack[tok:, :] = jnp.broadcast_to(segs, (pack.shape[0] - tok, width)).astype(BF16)

    greet(peers, meanwhile=prepare)
    steps[0]()
    cross_y()
    for step in steps[1:-7]:
        step()
    to_planes()
    for step in steps[-7:-3]:
        step()
    across()
    steps[-3]()
    steps[-2]()
    end()
    steps[-1]()


def reduce_steps(sizes, grads, total_out, refs):
    zn, xn, yn, slots, last = sizes
    held, near, xd, yd, xs_in, ys_in, zs_in, xb, yb, zb = refs[:10]
    load_sems, near_sems, xd_sems, yd_sems, xs_sems, ys_sems, zs_sems = refs[10:17]
    xb_sems, yb_sems, zb_sems = refs[17:20]
    count = slots - last
    part = count // 2
    rest = count - part
    tail = pl.ds(count, last)
    z, x = lax.axis_index("a"), lax.axis_index("b")
    y, core = lax.axis_index("y"), lax.axis_index("core")
    core_peer = {"core": 1 - core}
    xs, ys = range(1, xn), range(1, yn)
    y_peers = [{"y": lax.rem(y + k, yn)} for k in ys]
    x_peers = [{"b": lax.rem(x + k, xn)} for k in xs]
    z_peers = [{"a": lax.rem(z + k, zn)} for k in range(1, zn)]
    def flat(jz, jx, jy):
        return (jz * xn + jx) * yn + jy

    def chip_rows(jz, jx, jy, which):
        chip = (lax.rem(z + jz, zn) * xn + lax.rem(x + jx, xn)) * yn + lax.rem(y + jy, yn)
        return grads.at[pl.ds((chip * 2 + which) * slots, slots)]

    def near_copy(jz, jx, jy):
        index = flat(jz, jx, jy)
        return remote(chip_rows(jz, jx, jy, 1 - core), near.at[index], near_sems, index, core_peer)

    def load_copy(jz, jx, jy):
        index = flat(jz, jx, jy)
        return pltpu.make_async_copy(
            chip_rows(jz, jx, jy, core), held.at[index], load_sems.at[index]
        )

    def whole(jz, jx, jy):
        return held.at[flat(jz, jx, jy)]

    def first(jz, jx, jy):
        return held.at[flat(jz, jx, jy), pl.ds(0, part)]

    def second(jz, jx, jy):
        return held.at[flat(jz, jx, jy), pl.ds(part, rest)]

    def cross(jz, jx, jy):
        return (jz * (xn - 1) + jx - 1) * (yn - 1) + jy - 1

    def yd_copy(jz, jx, jy):
        index = cross(jz, jx, jy)
        return remote(first(jz, jx, jy), yd.at[index], yd_sems, index, y_peers[jy - 1])

    def xd_copy(jz, jx, jy):
        index = cross(jz, jx, jy)
        return remote(second(jz, jx, jy), xd.at[index], xd_sems, index, x_peers[jx - 1])

    def halves(low_half):
        return pl.ds(0, part) if low_half else pl.ds(part, rest)

    def xs_copy(jz, jx, low_half):
        index = jz * (xn - 1) + jx - 1
        return remote(
            held.at[flat(jz, jx, 0), halves(low_half)],
            xs_in.at[index, halves(low_half)],
            xs_sems,
            index * 2 + int(low_half),
            x_peers[jx - 1],
        )

    def ys_copy(jz, jy, low_half):
        index = jz * (yn - 1) + jy - 1
        return remote(
            held.at[flat(jz, 0, jy), halves(low_half)],
            ys_in.at[index, halves(low_half)],
            ys_sems,
            index * 2 + int(low_half),
            y_peers[jy - 1],
        )

    def zs_copy(jz):
        src = held.at[flat(jz, 0, 0), pl.ds(0, count)]
        return remote(src, zs_in.at[jz - 1], zs_sems, jz - 1, z_peers[jz - 1])

    def zb_copy(jz):
        src = held.at[pl.ds(jz * xn * yn, xn * yn), tail]
        return remote(src, zb.at[jz - 1], zb_sems, jz - 1, z_peers[jz - 1])

    def xb_copy(jx):
        src = held.at[pl.ds(jx * yn, yn), tail]
        return remote(src, xb.at[jx - 1], xb_sems, jx - 1, x_peers[jx - 1])

    def yb_copy(jy):
        return remote(held.at[jy, tail], yb.at[jy - 1], yb_sems, jy - 1, y_peers[jy - 1])

    def tail_planes():
        for jz in range(1, zn):
            zb_copy(jz).wait_recv()

        def one(i, carry):
            for chip in range(xn * yn):
                total = held[chip, count + i].astype(F32)
                for jz in range(1, zn):
                    total = total + zb[jz - 1, chip, i].astype(F32)
                held[chip, count + i] = total.astype(BF16)
            return carry

        lax.fori_loop(0, last, one, None)
        for jx in xs:
            launch(xb_copy(jx))

    def tail_columns():
        for jx in xs:
            xb_copy(jx).wait_recv()
            for jy in range(yn):
                add_low(held.at[jy, tail], xb.at[jx - 1, jy], last)
        for jy in ys:
            launch(yb_copy(jy))

    def tail_end():
        for jy in ys:
            yb_copy(jy).wait_recv()

        def one(i, carry):
            total = held[0, count + i].astype(F32)
            for jy in ys:
                total = total + yb[jy - 1, i].astype(F32)
            total_out[count + i] = total
            return carry

        lax.fori_loop(0, last, one, None)

    z_order = z_order_of(zn)[::-1]
    started = []

    def launch(copy):
        copy.start()
        started.append(copy)

    def plane(jz):
        return (
            [(jz, jx, jy) for jx in xs for jy in ys]
            + [(jz, jx, 0) for jx in xs]
            + [(jz, 0, jy) for jy in ys]
            + [(jz, 0, 0)]
        )

    def fetch(jz):
        for chip in plane(jz):
            launch(near_copy(*chip))
            load_copy(*chip).start()

    def prepare(index):
        for chip in plane(z_order[index]):
            load_copy(*chip).wait()
            near_copy(*chip).wait_recv()
            add_low(whole(*chip), near.at[flat(*chip)], slots)
        if index + 1 < zn:
            fetch(z_order[index + 1])
        if last and z_order[index] != 0:
            launch(zb_copy(z_order[index]))

    stages = [(index, stage) for index in range(zn) for stage in range(3)]

    def send_stage(number):
        index, stage = stages[number]
        jz = z_order[index]
        for jx in xs:
            if stage == 0:
                for jy in ys:
                    launch(xd_copy(jz, jx, jy))
            else:
                launch(xs_copy(jz, jx, stage == 2))
        for jy in ys:
            if stage == 0:
                for jx in xs:
                    launch(yd_copy(jz, jx, jy))
            else:
                launch(ys_copy(jz, jy, stage == 1))

    def take_stage(number):
        index, stage = stages[number]
        jz = z_order[index]
        if stage == 0:
            for jx in xs:
                for jy in ys:
                    yd_copy(jz, jx, jy).wait_recv()
                    add_low(first(jz, jx, 0), yd.at[cross(jz, jx, jy)], part)
                    xd_copy(jz, jx, jy).wait_recv()
                    add_low(second(jz, 0, jy), xd.at[cross(jz, jx, jy)], rest)
        else:
            for jx in xs:
                xs_copy(jz, jx, stage == 2).wait_recv()
            for jy in ys:
                ys_copy(jz, jy, stage == 1).wait_recv()

    def side_in(index):
        jz = z_order[index]

        def one(i, carry):
            total = held[flat(jz, 0, 0), i].astype(F32)
            for jx in xs:
                total = total + xs_in[jz * (xn - 1) + jx - 1, i].astype(F32)
            for jy in ys:
                total = total + ys_in[jz * (yn - 1) + jy - 1, i].astype(F32)
            if jz != 0:
                held[flat(jz, 0, 0), i] = total.astype(BF16)
            else:
                total_out[i] = total
            return carry

        lax.fori_loop(0, count, one, None)
        if jz != 0:
            launch(zs_copy(jz))

    ahead = 2

    def begin():
        fetch(z_order[0])

    def begin_stages():
        prepare(0)
        for number in range(ahead):
            send_stage(number)

    def one_stage(number):
        for index in range(1, zn):
            if number == (index - 1 if index < 3 else 3 * (index - 2)):
                prepare(index)
        take_stage(number)
        later = number + ahead
        if later < len(stages):
            send_stage(later)
        if stages[number][1] == 2:
            side_in(stages[number][0])
        if last and number == len(stages) - 4:
            tail_planes()
        if last and number == len(stages) - 2:
            tail_columns()

    def end():
        for jz in range(1, zn):
            zs_copy(jz).wait_recv()

        def add_planes(i, carry):
            total = total_out[i]
            for jz in range(1, zn):
                total = total + zs_in[jz - 1, i].astype(F32)
            total_out[i] = total
            return carry

        lax.fori_loop(0, count, add_planes, None)
        if last:
            tail_end()
        for copy in started:
            copy.wait_send()

    steps = [begin, begin_stages]
    steps += [functools.partial(one_stage, number) for number in range(len(stages))]
    steps.append(end)
    return [core_peer] + y_peers + x_peers + z_peers, steps


def reduce_kernel(sizes, grads, tokens_in, total_out, tokens_out, *refs):
    peers, steps = reduce_steps(sizes, grads, total_out, refs[:20])
    turn_sems = refs[20]
    greet(peers, True)
    turn_refs = (tokens_in, tokens_out, turn_sems.at[0], turn_sems.at[1])
    start_turn(*turn_refs)
    for step in steps:
        step()
    finish_turn(*turn_refs)


def vmem():
    return pl.BlockSpec(memory_space=pltpu.VMEM)


def smem():
    return pl.BlockSpec(memory_space=pltpu.SMEM)


def anywhere():
    return pl.BlockSpec(memory_space=pl.ANY)


def shape_of(dims, kind):
    return jax.ShapeDtypeStruct(dims, kind)


def params(collective=None):
    if collective is None:
        return pltpu.CompilerParams(vmem_limit_bytes=VMEM_LIMIT)
    return pltpu.CompilerParams(
        vmem_limit_bytes=VMEM_LIMIT, collective_id=collective, has_side_effects=True
    )


def pair(count):
    return pltpu.SemaphoreType.DMA((2, max(count, 1)))


def spread_scratch(zn, xn, yn):
    return [
        pair(zn - 1),
        pair(zn * (xn - 1)),
        pair(zn * (yn - 1)),
        pair(zn * (xn - 1) * (yn - 1)),
        pair(zn * (xn - 1) * (yn - 1)),
        pair(zn * xn * yn),
        pltpu.SemaphoreType.DMA,
        pair((xn - 1) * yn),
        pair(yn - 1),
        pair((zn - 1) * xn * yn),
        pair(zn * xn * yn),
    ]


def reduce_scratch(zn, xn, yn, slots, last, piece, width):
    def chunks(*dims):
        return pltpu.VMEM(tuple(max(dim, 1) for dim in dims) + (piece, width), BF16)

    n_chips, crossing = zn * xn * yn, zn * (xn - 1) * (yn - 1)
    count = slots - last
    part = count // 2
    return [
        chunks(n_chips, slots),
        chunks(n_chips, slots),
        chunks(crossing, count - part),
        chunks(crossing, part),
        chunks(zn * (xn - 1), count),
        chunks(zn * (yn - 1), count),
        chunks(zn - 1, count),
        chunks(xn - 1, yn, last),
        chunks(yn - 1, last),
        chunks(zn - 1, xn * yn, last),
        pltpu.SemaphoreType.DMA((n_chips,)),
        pair(n_chips),
        pair(crossing),
        pair(crossing),
        pair(2 * zn * (xn - 1)),
        pair(2 * zn * (yn - 1)),
        pair(zn - 1),
        pair(xn - 1),
        pair(yn - 1),
        pair(zn - 1),
    ]


def run_layer(dims, weight_master, x_own, segments, cotangent, location, norm_params):
    n_seq, n_dp = dims
    reps = n_seq // n_dp
    splits = n_seq // GROUPS
    slots, piece, width = weight_master.shape
    tok = cotangent.shape[0]
    length = tok * n_seq
    hidden_units = (location.shape[0] * piece - 4 * width) // 3
    head = width // HEADS
    kind_pieces = width // piece
    hidden_pieces = hidden_units // piece
    chunk = hidden_units // CHUNKS
    zn, xn, yn = n_dp, reps, n_dp // 2
    all_slots = n_seq * n_dp * slots
    last = slots // 8
    slopes = jnp.asarray(head_slopes(HEADS, tok, n_seq))

    weights, gathered, _ = pl.pallas_call(
        functools.partial(spread_kernel, (zn, xn, yn, slots, last)),
        out_shape=(
            shape_of((all_slots, piece, width), BF16),
            shape_of((n_seq, tok + 16, width), BF16),
            shape_of((max(yn - 1, 1), tok + 16, width), BF16),
        ),
        in_specs=[vmem(), vmem(), vmem()],
        out_specs=(anywhere(),) * 3,
        scratch_shapes=[
            pltpu.VMEM((slots, piece, width), BF16),
            pltpu.VMEM((tok + 16, width), BF16),
        ]
        + spread_scratch(zn, xn, yn)
        + [
            pair(yn - 1),
            pair(zn),
            pair(zn * (xn - 1)),
            pair(zn * xn),
            pltpu.SemaphoreType.DMA,
        ],
        compiler_params=params(1),
    )(weight_master, x_own, segments)
    attend_sizes = (n_dp, reps, splits, tok, head, n_seq)
    q_ext, k_ext, k_turned, v_rows, v_turned = pl.pallas_call(
        functools.partial(project_kernel, (n_dp, splits, tok, head)),
        grid=(n_seq,),
        out_shape=(
            shape_of((TRIO, GROUPS * tok, 128), BF16),
            shape_of((TRIO, length, 128), BF16),
            shape_of((TRIO, head, length), BF16),
            shape_of((TRIO, length, head), BF16),
            shape_of((TRIO, head, length), BF16),
        ),
        in_specs=[
            smem(),
            pl.BlockSpec((1, tok + 16, width), lambda i: (i, 0, 0)),
            anywhere(),
        ],
        out_specs=(
            pl.BlockSpec((TRIO, tok, 128), lambda i: (0, lax.div(i, splits), 0)),
            pl.BlockSpec((TRIO, tok, 128), lambda i: (0, i, 0)),
            pl.BlockSpec((TRIO, head, tok), lambda i: (0, 0, i)),
            pl.BlockSpec((TRIO, tok, head), lambda i: (0, i, 0)),
            pl.BlockSpec((TRIO, head, tok), lambda i: (0, 0, i)),
        ),
        scratch_shapes=[
            pltpu.VMEM((3 * TRIO, 128, width), BF16),
            pltpu.SemaphoreType.DMA((3 * TRIO * (head // piece),)),
        ],
        compiler_params=params(),
    )(location, gathered, weights)

    mixed_full, log_total, mixed_own, cotangent = pl.pallas_call(
        functools.partial(attend_forward_kernel, attend_sizes),
        out_shape=(
            shape_of((GROUPS, TRIO, head, tok), F32),
            shape_of((GROUPS, TRIO, 1, tok), F32),
            shape_of((GROUPS, TRIO, head, tok), BF16),
            shape_of(cotangent.shape, BF16),
        ),
        in_specs=[smem(), vmem(), vmem(), vmem(), anywhere()],
        out_specs=(vmem(), vmem(), vmem(), anywhere()),
        scratch_shapes=[
            pltpu.VMEM((3 * TRIO, tok, tok), F32),
            pltpu.VMEM((n_seq, tok, tok), F32),
            pltpu.VMEM((GROUPS, TRIO, head, tok), BF16),
            pair(GROUPS - 1),
            pltpu.SemaphoreType.DMA((2,)),
        ],
        compiler_params=params(2),
    )(slopes, q_ext, k_ext, v_turned, cotangent)

    out_low, d_pre_one, d_mixed, norm_part, grads = pl.pallas_call(
        functools.partial(
            dense_kernel, (n_dp, tok, piece, kind_pieces, chunk // piece, hidden_pieces)
        ),
        out_shape=(
            shape_of((tok, width), BF16),
            shape_of((tok, width), F32),
            shape_of((width, tok), BF16),
            shape_of((8, width), F32),
            shape_of((all_slots, piece, width), BF16),
        ),
        in_specs=[smem(), anywhere(), vmem(), vmem(), vmem(), anywhere()],
        out_specs=(vmem(), vmem(), vmem(), vmem(), anywhere()),
        scratch_shapes=[
            pltpu.VMEM((width, width), BF16),
            pltpu.VMEM((CHUNKS, chunk, width), BF16),
            pltpu.VMEM((CHUNKS, chunk, width), BF16),
            pltpu.VMEM((CHUNKS, chunk, width), BF16),
            pltpu.VMEM((CHUNKS, chunk, tok), F32),
            pltpu.VMEM((CHUNKS, chunk, tok), F32),
            pltpu.VMEM((CHUNKS, chunk, tok), BF16),
            pltpu.VMEM((2, 3, chunk, width), BF16),
            pltpu.VMEM((width, width), BF16),
            pltpu.VMEM((tok, width), BF16),
            pltpu.SemaphoreType.DMA((3 * CHUNKS + 1,)),
            pltpu.SemaphoreType.DMA((7,)),
            pltpu.SemaphoreType.DMA,
        ],
        compiler_params=params(),
    )(location, gathered, cotangent, mixed_own.reshape(width, tok), norm_params, weights)

    def norm_rows(count):
        return pltpu.VMEM((max(count, 1), 8, width), F32)

    d_own, result, norm_total = pl.pallas_call(
        functools.partial(attend_backward_kernel, attend_sizes),
        out_shape=(
            shape_of((GROUPS, 3, TRIO, head, tok), BF16),
            shape_of(out_low.shape, BF16),
            shape_of((8, width), F32),
        ),
        in_specs=[smem()] + [vmem()] * 7 + [anywhere(), vmem()],
        out_specs=(vmem(), anywhere(), vmem()),
        scratch_shapes=[
            pltpu.VMEM((length, 128), F32),
            pltpu.VMEM((length, head), F32),
            pltpu.VMEM((3 * TRIO, tok, tok), F32),
            pltpu.VMEM((GROUPS, TRIO, head, tok), BF16),
            pltpu.VMEM((GROUPS, 3, TRIO, head, tok), BF16),
            pltpu.VMEM((TRIO, splits, GROUPS, 2, head, tok), BF16),
            pltpu.VMEM((TRIO, splits - 1, GROUPS, 2, head, tok), BF16),
            pair(GROUPS - 1),
            pair(TRIO * (GROUPS - 1)),
            pair(TRIO * (splits - 1)),
            pair(TRIO * (GROUPS - 1)),
            pltpu.SemaphoreType.DMA((2,)),
            norm_rows(1),
            norm_rows(yn - 1),
            norm_rows(xn - 1),
            norm_rows(zn - 1),
            norm_rows(4),
            pair(1 + (yn - 1) + (xn - 1) + (zn - 1)),
        ],
        compiler_params=params(3),
    )(
        slopes,
        q_ext,
        k_ext,
        k_turned,
        v_rows,
        mixed_full,
        log_total,
        d_mixed.reshape(GROUPS, TRIO, head, tok),
        out_low,
        norm_part,
    )

    trio_rows = TRIO * head
    d_tokens, grads = pl.pallas_call(
        functools.partial(project_grad_kernel, (n_dp, tok, piece, kind_pieces)),
        out_shape=(shape_of((tok, width), BF16), shape_of(grads.shape, BF16)),
        in_specs=[smem(), anywhere(), vmem(), vmem()] + [anywhere()] * 2,
        out_specs=(vmem(), anywhere()),
        scratch_shapes=[
            pltpu.VMEM((GROUPS, 3 * trio_rows, width), BF16),
            pltpu.VMEM((GROUPS, 3 * trio_rows, width), BF16),
            pltpu.VMEM((tok, width), BF16),
            pltpu.SemaphoreType.DMA((GROUPS,)),
            pltpu.SemaphoreType.DMA((GROUPS,)),
            pltpu.SemaphoreType.DMA,
        ],
        input_output_aliases={5: 1},
        compiler_params=params(),
    )(location, gathered, d_own.reshape(GROUPS, 3 * trio_rows, tok), d_pre_one, weights, grads)

    own_grad, d_turned = pl.pallas_call(
        functools.partial(reduce_kernel, (zn, xn, yn, slots, last)),
        out_shape=(
            shape_of((slots, piece, width), F32),
            shape_of(d_tokens.shape, BF16),
        ),
        in_specs=[anywhere(), anywhere()],
        out_specs=(vmem(), anywhere()),
        scratch_shapes=reduce_scratch(zn, xn, yn, slots, last, piece, width)
        + [pltpu.SemaphoreType.DMA((2,))],
        compiler_params=params(4),
    )(grads, d_tokens)
    return own_grad, norm_total, d_turned, result


def per_device(
    dims,
    layer_input,
    out_cotangent,
    segment_ids,
    piece_owner,
    weight_master,
    weight_first,
    weight_second,
    norm_params,
    norm_first,
    norm_second,
):
    slots, piece, width = weight_master.shape
    pieces = piece_owner.shape[0]
    tok = layer_input.shape[1]
    hidden_units = (pieces * piece - 4 * width) // 3
    location = locate_pieces(piece_owner, slots)
    own_grad, norm_total, d_turned, result = run_layer(
        dims,
        weight_master,
        layer_input[0],
        segment_ids,
        out_cotangent[0],
        location,
        norm_params,
    )

    numbers = jnp.arange(pieces, dtype=jnp.int32) + 1
    own_slots = lax.axis_index(("a", "b", "y", "core")) * slots + jnp.arange(slots)
    inverse = jnp.sum(jnp.where(location[None, :] == own_slots[:, None], numbers[None, :], 0), axis=1)
    own_grad = jnp.where((inverse > 0)[:, None, None], own_grad, 0.0)
    norm_grad = norm_total[:4]
    rates = slot_rates(inverse, piece, width, hidden_units)
    first_new, second_new, weight_new = adamw_step(
        weight_master, weight_first, weight_second, own_grad, rates[:, None, None], STEP
    )
    norm_first_new, norm_second_new, norm_new = adamw_step(
        norm_params, norm_first, norm_second, norm_grad, NORM_RATE, STEP
    )
    return (
        result[None],
        d_turned.astype(F32)[None],
        own_grad,
        first_new,
        second_new,
        weight_new,
        weight_new.astype(BF16),
        norm_grad,
        norm_first_new,
        norm_second_new,
        norm_new,
    )


def solution(mesh):
    n_seq, n_dp = mesh.shape["seq"], mesh.shape["dp"]
    inner = Mesh(
        mesh.devices.reshape(n_dp, n_seq // n_dp, n_dp // 2, 2), ("a", "b", "y", "core")
    )
    seq, dp, every = ("a", "b"), ("y", "core"), ("a", "b", "y", "core")
    block = P(dp, seq, None)
    owned = P(every, None, None)
    in_specs = (block, block, P(dp, seq), P(), owned, owned, owned, P(), P(), P())
    out_specs = (block, block, owned, owned, owned, owned, owned, P(), P(), P(), P())
    return jax.shard_map(
        functools.partial(per_device, (n_seq, n_dp)),
        mesh=inner,
        in_specs=in_specs,
        out_specs=out_specs,
        check_vma=False,
    )
```

```python
import functools

import jax
import jax.numpy as jnp
import numpy as np
from jax import lax
from jax.experimental import pallas as pl
from jax.experimental.pallas import tpu as pltpu
from jax.sharding import Mesh
from jax.sharding import PartitionSpec as P

HEADS = 12
GROUPS = 4
TRIO = HEADS // GROUPS
STEP = 4

NORM_EPS = 1e-06
BETA_ONE = 0.5
BETA_TWO = 0.5
DECAY = 0.01
ADAM_EPS = 1e-08
NORM_RATE = 0.3
OUT_RATE = 0.35
MASKED = -1e30
CHUNKS = 6
VMEM_LIMIT = 60 * 1024 * 1024
MESH_IDS = pl.DeviceIdType.MESH
F32 = jnp.float32
BF16 = jnp.bfloat16


def head_slopes(head_count, tok_rows, seq_devices):
    head_order = np.arange(head_count, dtype=np.float64)
    slopes = 8.0 / tok_rows * np.power(8.0 * seq_devices, -head_order / (head_count - 1))
    return slopes.astype(np.float32)


def locate_pieces(owners, slot_count):
    pieces = owners.shape[0]
    numbers = jnp.arange(pieces, dtype=jnp.int32)
    earlier = (owners[None, :] == owners[:, None]) & (numbers[None, :] < numbers[:, None])
    return owners * slot_count + jnp.sum(earlier.astype(jnp.int32), axis=1)


def slot_rates(inverse, piece_rows, model_width, hidden_units):
    first_row = (inverse - 1) * piece_rows
    narrow = model_width ** (-0.5)
    step_rate = jnp.where(
        first_row < 3 * model_width,
        narrow,
        jnp.where(
            first_row < 4 * model_width,
            OUT_RATE,
            jnp.where(
                first_row < 4 * model_width + 2 * hidden_units, narrow, hidden_units ** (-0.5)
            ),
        ),
    )
    return jnp.where(inverse > 0, step_rate, narrow).astype(jnp.float32)


def adamw_step(weight, first_moment, second, gradient, step_rate, step_count):
    first_moment = BETA_ONE * first_moment + (1.0 - BETA_ONE) * gradient
    second = BETA_TWO * second + (1.0 - BETA_TWO) * gradient * gradient
    mean_hat = first_moment / (1.0 - BETA_ONE**step_count)
    square_hat = second / (1.0 - BETA_TWO**step_count)
    weight = weight - step_rate * (mean_hat / (jnp.sqrt(square_hat) + ADAM_EPS) + DECAY * weight)
    return (first_moment, second, weight)


def dot_nt(left_side, right_side):
    return lax.dot_general(
        left_side, right_side, (((1,), (1,)), ((), ())), preferred_element_type=F32
    )


def dot_nn(left_side, right_side):
    return lax.dot_general(
        left_side, right_side, (((1,), (0,)), ((), ())), preferred_element_type=F32
    )


def dot_tn(left_side, right_side):
    return lax.dot_general(
        left_side, right_side, (((0,), (0,)), ((), ())), preferred_element_type=F32
    )


def fetch_piece(place, piece, weights, dst, sem):
    pltpu.make_async_copy(weights.at[place[piece]], dst, sem).start()


def fill_tables(table, slopes, group, tok):
    apart = lax.broadcasted_iota(jnp.int32, (tok, tok), 0) - lax.broadcasted_iota(
        jnp.int32, (tok, tok), 1
    )
    apart = apart.astype(F32)
    for h in range(TRIO):
        slope = slopes[group * TRIO + h]
        table[h * 3 + 0] = -slope * apart
        table[h * 3 + 1] = slope * jnp.abs(apart)
        table[h * 3 + 2] = slope * apart


def block_place(order, n_dp, reps):
    return (order % n_dp) * reps + order // n_dp


def bias_of(key_block, query_place, slope, h, tok, n_dp, reps):
    key_place = block_place(key_block, n_dp, reps)
    which = jnp.where(key_place > query_place, 2, jnp.where(key_place < query_place, 0, 1))
    shift = slope * (tok * jnp.abs(key_place - query_place)).astype(F32)
    return h * 3 + which, shift


def holder(order, n_dp):
    dp = lax.rem(order, n_dp)
    return {"b": lax.div(order, n_dp), "y": lax.div(dp, 2), "core": lax.rem(dp, 2)}


def turn_to():
    z, dp = lax.axis_index("a"), lax.axis_index("y") * 2 + lax.axis_index("core")
    return {"a": dp, "y": lax.div(z, 2), "core": lax.rem(z, 2)}, dp != z


def start_turn(src, dst, send_sem, recv_sem):
    peer, moves = turn_to()

    @pl.when(moves)
    def _():
        pltpu.make_async_remote_copy(
            src_ref=src,
            dst_ref=dst,
            send_sem=send_sem,
            recv_sem=recv_sem,
            device_id=peer,
            device_id_type=MESH_IDS,
        ).start()

    @pl.when(jnp.logical_not(moves))
    def _():
        pltpu.make_async_copy(src, dst, recv_sem).start()


def finish_turn(src, dst, send_sem, recv_sem):
    peer, moves = turn_to()

    @pl.when(moves)
    def _():
        pltpu.make_async_remote_copy(
            src_ref=src,
            dst_ref=dst,
            send_sem=send_sem,
            recv_sem=recv_sem,
            device_id=peer,
            device_id_type=MESH_IDS,
        ).wait()

    @pl.when(jnp.logical_not(moves))
    def _():
        pltpu.make_async_copy(src, dst, recv_sem).wait()


def greet(peers, turning=False, meanwhile=None):
    barrier = pltpu.get_barrier_semaphore()
    for peer in peers:
        pl.semaphore_signal(barrier, inc=1, device_id=peer, device_id_type=MESH_IDS)
    if meanwhile is not None:
        meanwhile()
    if not turning:
        pl.semaphore_wait(barrier, len(peers))
        return
    turn_peer, moves = turn_to()

    @pl.when(moves)
    def _():
        pl.semaphore_signal(barrier, inc=1, device_id=turn_peer, device_id_type=MESH_IDS)

    pl.semaphore_wait(barrier, len(peers) + moves.astype(jnp.int32))


def my_order(n_dp):
    return lax.axis_index("b") * n_dp + lax.axis_index("y") * 2 + lax.axis_index("core")


def remote(src, dst, sems, index, peer):
    return pltpu.make_async_remote_copy(
        src_ref=src,
        dst_ref=dst,
        send_sem=sems.at[0, index],
        recv_sem=sems.at[1, index],
        device_id=peer,
        device_id_type=MESH_IDS,
    )


def project_kernel(
    sizes,
    place,
    x_ref,
    weights,
    q_out,
    k_out,
    kt_out,
    v_out,
    vt_out,
    wpad,
    sems,
):
    n_dp, splits, tok, head = sizes
    order = my_order(n_dp)
    group, split = lax.div(order, splits), lax.rem(order, splits)
    block = pl.program_id(0)
    per_head = head // 16
    width = x_ref.shape[2]
    kind_pieces = width // 16

    @pl.when(block == 0)
    def _():
        def spots():
            for kind in range(3):
                for rest in range(TRIO * per_head):
                    step = kind * TRIO * per_head + rest
                    rows = pl.ds(rest % per_head * 16, 16)
                    dst = wpad.at[kind * TRIO + rest // per_head, rows]
                    yield kind * kind_pieces + group * (TRIO * per_head) + rest, dst, sems.at[step]

        for number, dst, sem in spots():
            fetch_piece(place, number, weights, dst, sem)
        for row in range(3 * TRIO):
            wpad[row, head:, :] = jnp.zeros((wpad.shape[1] - head, width), BF16)
        for _, dst, sem in spots():
            pltpu.make_async_copy(weights.at[0], dst, sem).wait()

    segs = x_ref[0, tok : tok + 1, 0:tok].astype(F32)
    number = lax.broadcasted_iota(jnp.int32, (128, tok), 0) - head
    same = segs == number.astype(F32)
    used = (number >= 0) & (number < 3)
    xb = x_ref[0, 0:tok, :]
    keys = dot_nt(xb, wpad[TRIO : 2 * TRIO].reshape(TRIO * 128, width))
    values = dot_nt(xb, wpad[2 * TRIO : 3 * TRIO].reshape(TRIO * 128, width))
    marks = jnp.where(used & jnp.logical_not(same), MASKED, 0.0).T.astype(BF16)
    for h in range(TRIO):
        key = keys[:, h * 128 : (h + 1) * 128]
        value = values[:, h * 128 : (h + 1) * 128]
        k_out[h] = key.astype(BF16) + marks
        v_out[h] = value[:, 0:head].astype(BF16)
        kt_out[h] = key.T[0:head].astype(BF16)
        vt_out[h] = value.T[0:head].astype(BF16)

    @pl.when(lax.rem(block, splits) == split)
    def _():
        w_query = wpad[0:TRIO].reshape(TRIO * 128, width)
        queries = dot_nt(xb, w_query).astype(BF16) * jnp.asarray(head**-0.5, BF16)
        query_marks = jnp.where(same & used, 1.0, 0.0).T.astype(BF16)
        for h in range(TRIO):
            q_out[h] = queries[:, h * 128 : (h + 1) * 128] + query_marks


def attend_forward_kernel(
    sizes,
    slopes,
    q_ref,
    k_ref,
    vt_ref,
    cot_in,
    mixed_full,
    log_out,
    mixed_own,
    cot_out,
    table,
    scores,
    mixed_low,
    swap_sems,
    turn_sems,
):
    n_dp, reps, splits, tok, head, blocks = sizes
    order = my_order(n_dp)
    group, split = lax.div(order, splits), lax.rem(order, splits)
    others = [lax.rem(group + k, GROUPS) for k in range(1, GROUPS)]
    peers = [holder(other * splits + split, n_dp) for other in others]
    started = []
    greet(peers, True)
    turn_refs = (cot_in, cot_out, turn_sems.at[0], turn_sems.at[1])
    start_turn(*turn_refs)
    fill_tables(table, slopes, group, tok)

    def attend(index, h):
        place_order = index * splits + split
        query_place = lax.rem(place_order, n_dp) * reps + lax.div(place_order, n_dp)
        slope = slopes[group * TRIO + h]
        qh = q_ref[h, pl.ds(pl.multiple_of(index * tok, tok), tok), :]
        top = None
        shifts = []
        for kb in range(blocks):
            which, shift = bias_of(kb, query_place, slope, h, tok, n_dp, reps)
            now = dot_nt(k_ref[h, kb * tok : (kb + 1) * tok, :], qh) - table[which]
            scores[kb] = now
            here = jnp.max(now, axis=0, keepdims=True) - shift
            top = here if top is None else jnp.maximum(top, here)
            shifts.append(shift)
        total = jnp.zeros((1, tok), F32)
        for kb in range(blocks):
            grown = jnp.exp(scores[kb] - (top + shifts[kb]))
            total = total + jnp.sum(grown, axis=0, keepdims=True)
        log_total = top + jnp.log(total)
        mixed = jnp.zeros((head, tok), F32)
        for kb in range(blocks):
            prob = jnp.exp(scores[kb] - (log_total + shifts[kb])).astype(BF16)
            mixed = mixed + dot_nn(vt_ref[h, :, kb * tok : (kb + 1) * tok], prob)
        mixed_full[index, h] = mixed
        mixed_low[index, h] = mixed.astype(BF16)
        log_out[index, h] = log_total

    for k in list(range(GROUPS - 1)) + [None]:
        index = group if k is None else others[k]

        def one(h, carry, index=index):
            attend(index, h)
            return carry

        lax.fori_loop(0, TRIO, one, None)
        if k is not None:
            copy = swap_copy(mixed_low, mixed_own, index, group, swap_sems, k, peers[k])
            copy.start()
            started.append(copy)
        else:
            mixed_own[group] = mixed_low[group]
    for copy in started:
        copy.wait()
    finish_turn(*turn_refs)


def swap_copy(src, dst, there, here, sems, index, peer):
    return pltpu.make_async_remote_copy(
        src_ref=src.at[there],
        dst_ref=dst.at[here],
        send_sem=sems.at[0, index],
        recv_sem=sems.at[1, index],
        device_id=peer,
        device_id_type=MESH_IDS,
    )


def norm_steps(dims, norm_in, norm_out, refs):
    zn, xn, yn = dims
    norm_core, norm_y, norm_x, norm_z, norm_sum, sems = refs
    z, x = lax.axis_index("a"), lax.axis_index("b")
    y, core = lax.axis_index("y"), lax.axis_index("core")
    rounds = [
        (norm_core, [{"core": 1 - core}]),
        (norm_y, [{"y": lax.rem(y + k, yn)} for k in range(1, yn)]),
        (norm_x, [{"b": lax.rem(x + k, xn)} for k in range(1, xn)]),
        (norm_z, [{"a": lax.rem(z + k, zn)} for k in range(1, zn)]),
    ]
    first = [sum(len(peers) for _, peers in rounds[:i]) for i in range(len(rounds))]

    def copies(i):
        buffer, peers = rounds[i]
        return [
            remote(norm_sum.at[i], buffer.at[k], sems, first[i] + k, peer)
            for k, peer in enumerate(peers)
        ]

    def begin():
        norm_sum[0] = norm_in[...]
        for copy in copies(0):
            copy.start()

    def turn_round(i):
        total = norm_sum[i]
        for k, copy in enumerate(copies(i)):
            copy.wait()
            total = total + rounds[i][0][k]
        if i + 1 == len(rounds):
            norm_out[...] = total
            return
        norm_sum[i + 1] = total
        for copy in copies(i + 1):
            copy.start()

    peers = [peer for _, group in rounds for peer in group]
    return peers, [begin] + [functools.partial(turn_round, i) for i in range(len(rounds))]


def attend_backward_kernel(
    sizes,
    slopes,
    q_ref,
    k_ref,
    kt_ref,
    v_ref,
    mixed_full,
    log_in,
    d_mixed,
    low_in,
    norm_in,
    own_ref,
    low_out,
    norm_out,
    kv_sum,
    table,
    d_blocks,
    shared,
    pairs,
    landed,
    swap_sems,
    query_sems,
    pair_sems,
    value_sems,
    turn_sems,
    *norm_refs,
):
    n_dp, reps, splits, tok, head, blocks = sizes
    order = my_order(n_dp)
    group, split = lax.div(order, splits), lax.rem(order, splits)
    twins = [lax.rem(split + k, splits) for k in range(1, splits)]
    twin_ids = [holder(group * splits + other, n_dp) for other in twins]
    others = [lax.rem(group + k, GROUPS) for k in range(1, GROUPS)]
    peers = [holder(other * splits + split, n_dp) for other in others]
    norm_peers, norms = norm_steps((n_dp, reps, n_dp // 2), norm_in, norm_out, norm_refs)
    greet(twin_ids + peers + norm_peers, True)
    turn_refs = (low_in, low_out, turn_sems.at[0], turn_sems.at[1])
    started = []

    def launch(copy):
        copy.start()
        started.append(copy)

    for k in range(GROUPS - 1):
        launch(remote(d_mixed.at[others[k]], d_blocks.at[group], swap_sems, k, peers[k]))
    d_blocks[group] = d_mixed[group]
    norms.pop(0)()
    fill_tables(table, slopes, group, tok)
    kv_sum[...] = jnp.zeros_like(kv_sum)

    def step_fn(h, step):
        index = lax.rem(group + GROUPS - step, GROUPS)
        if h == 0:

            @pl.when(step > 0)
            def _():
                view = d_blocks.at[index]
                remote(view, view, swap_sems, step - 1, peers[0]).wait_recv()

        place_order = index * splits + split
        query_place = lax.rem(place_order, n_dp) * reps + lax.div(place_order, n_dp)
        slope = slopes[group * TRIO + h]
        qh = q_ref[h, pl.ds(pl.multiple_of(index * tok, tok), tok), :]
        dt = d_blocks[index, h]
        lane = lax.broadcasted_iota(jnp.int32, qh.shape, 1)
        wide = jnp.concatenate([jnp.zeros((128 - head, tok), BF16), dt], axis=0)
        both = jnp.concatenate([jnp.where(lane < head, qh, jnp.zeros_like(qh)), wide.T], axis=0)
        row_dot = jnp.sum(dt.astype(F32) * mixed_full[index, h], axis=0, keepdims=True)
        log_total = log_in[index, h]
        dq = jnp.zeros((head, tok), F32)
        for kb in range(blocks):
            rows = slice(kb * tok, (kb + 1) * tok)
            which, shift = bias_of(kb, query_place, slope, h, tok, n_dp, reps)
            now = dot_nt(k_ref[h, rows, :], qh) - table[which]
            prob = jnp.exp(now - (log_total + shift))
            d_prob = dot_nn(v_ref[h, rows, :], dt)
            d_score = (prob * (d_prob - row_dot)).astype(BF16)
            sides = jnp.concatenate([d_score, prob.astype(BF16)], axis=1)
            kv_sum[rows, :] += dot_nn(sides, both)
            dq = dq + dot_nn(kt_ref[h, :, rows], d_score)
        shared[index, 0, h] = (dq * (head**-0.5)).astype(BF16)

    def pair_copy(h, k):
        return remote(
            pairs.at[h, twins[k]], landed.at[h, k], pair_sems, h * (splits - 1) + k, twin_ids[k]
        )

    def take_pairs(h):
        for k in range(splits - 1):
            pair_copy(h, k).wait_recv()
        for index in range(GROUPS):
            for kind in range(2):
                total = pairs[h, split, index, kind].astype(F32)
                for k in range(splits - 1):
                    total = total + landed[h, k, index, kind].astype(F32)
                shared[index, kind + 1, h] = total.astype(BF16)
        for k in range(GROUPS - 1):
            launch(
                remote(
                    shared.at[others[k], pl.ds(1, 2), h],
                    own_ref.at[group, pl.ds(1, 2), h],
                    value_sems,
                    h * (GROUPS - 1) + k,
                    peers[k],
                )
            )

    for h in range(TRIO):

        def one(step, carry, h=h):
            step_fn(h, step)
            return carry

        lax.fori_loop(0, GROUPS, one, None)
        if h == 0:
            start_turn(*turn_refs)
        norms.pop(0)()
        for k in range(GROUPS - 1):
            launch(
                remote(
                    shared.at[others[k], 0, h],
                    own_ref.at[group, 0, h],
                    query_sems,
                    h * (GROUPS - 1) + k,
                    peers[k],
                )
            )

        def flip(index, carry, h=h):
            for part in range(splits):
                rows = pl.ds(pl.multiple_of((index * splits + part) * tok, tok), tok)
                flipped = kv_sum[rows, :].T.astype(BF16)
                pairs[h, part, index, 0] = flipped[0:head]
                pairs[h, part, index, 1] = flipped[128 - head :]
            return carry

        lax.fori_loop(0, GROUPS, flip, None)
        if h + 1 < TRIO:
            kv_sum[...] = jnp.zeros_like(kv_sum)
        for k in range(splits - 1):
            launch(pair_copy(h, k))
        if h > 0:
            take_pairs(h - 1)
    for step in norms:
        step()
    take_pairs(TRIO - 1)
    own_ref[group] = shared[group]
    for h in range(TRIO):
        for k in range(GROUPS - 1):
            view = own_ref.at[others[k], 0, h]
            remote(view, view, query_sems, h * (GROUPS - 1) + k, peers[k]).wait_recv()
            view = own_ref.at[others[k], pl.ds(1, 2), h]
            remote(view, view, value_sems, h * (GROUPS - 1) + k, peers[k]).wait_recv()
    finish_turn(*turn_refs)
    for copy in started:
        copy.wait_send()


def norm_stats(values_in):
    mean = jnp.mean(values_in, axis=-1, keepdims=True)
    centred = values_in - mean
    spread = jnp.mean(centred * centred, axis=-1, keepdims=True)
    scale = lax.rsqrt(spread + NORM_EPS)
    return centred * scale, scale


def norm_back(unit, scale, gain, cotangent):
    d_unit = cotangent * gain
    first = jnp.mean(d_unit, axis=-1, keepdims=True)
    second = jnp.mean(d_unit * unit, axis=-1, keepdims=True)
    d_in = scale * (d_unit - first - unit * second)
    d_gain = jnp.sum(cotangent * unit, axis=0, keepdims=True)
    d_bias = jnp.sum(cotangent, axis=0, keepdims=True)
    return d_in, d_gain, d_bias


def dense_kernel(
    sizes,
    place,
    gathered,
    cot_ref,
    mixed_ref,
    norm_ref,
    weights,
    out_ref,
    d_pre_one_ref,
    d_mixed_ref,
    norm_grad,
    grads,
    w_out,
    w_gate,
    w_up,
    w_down,
    keep_gate,
    keep_up,
    keep_hidden,
    stage,
    stage_out,
    x_ref,
    load_sems,
    store_sems,
    own_sem,
):
    n_dp, tok, piece, kind_pieces, chunk_pieces, hidden_pieces = sizes
    own_copy = pltpu.make_async_copy(
        gathered.at[my_order(n_dp), pl.ds(0, tok)], x_ref, own_sem
    )
    own_copy.start()
    first_gate = 4 * kind_pieces
    first_up = first_gate + hidden_pieces
    first_down = first_up + hidden_pieces
    bases = (first_gate, first_up, first_down)
    buffers = (w_gate, w_up, w_down)
    chunk = chunk_pieces * piece

    for step in range(kind_pieces):
        dst = w_out.at[pl.ds(step * piece, piece)]
        fetch_piece(place, 3 * kind_pieces + step, weights, dst, load_sems.at[3 * CHUNKS])

    def load_chunk(c):
        for step in range(chunk_pieces):
            for kind in range(3):
                dst = buffers[kind].at[c, pl.ds(step * piece, piece)]
                number = bases[kind] + c * chunk_pieces + step
                fetch_piece(place, number, weights, dst, load_sems.at[kind * CHUNKS + c])

    def wait_chunk(c):
        for kind in range(3):
            view = buffers[kind].at[c]
            pltpu.make_async_copy(view, view, load_sems.at[kind * CHUNKS + c]).wait()

    load_chunk(0)
    mixed = mixed_ref[...].T
    own_copy.wait()
    pltpu.make_async_copy(w_out, w_out, load_sems.at[3 * CHUNKS]).wait()
    pre_one = x_ref[...].astype(F32) + dot_nt(mixed, w_out[...])
    load_chunk(1)
    unit_one, scale_one = norm_stats(pre_one)
    h_one = unit_one * norm_ref[0:1, :] + norm_ref[1:2, :]
    h_low = h_one.astype(BF16)

    pre_two = h_one
    for c in range(CHUNKS):
        wait_chunk(c)
        gate = dot_nt(w_gate[c], h_low)
        up = dot_nt(w_up[c], h_low)
        if c + 2 < CHUNKS:
            load_chunk(c + 2)
        below = 0.5 * (1.0 + lax.erf(gate * (0.5**0.5)))
        gelu = gate * below
        slope = below + gate * (jnp.exp(-0.5 * gate * gate) * (0.5 / jnp.pi) ** 0.5)
        hidden = (gelu * up).astype(BF16)
        keep_gate[c] = up * slope
        keep_up[c] = gelu
        keep_hidden[c] = hidden
        pre_two = pre_two + dot_tn(hidden, w_down[c])

    unit_two, scale_two = norm_stats(pre_two)
    out_ref[...] = (unit_two * norm_ref[2:3, :] + norm_ref[3:4, :]).astype(BF16)
    d_pre_two, d_gain_two, d_bias_two = norm_back(
        unit_two, scale_two, norm_ref[2:3, :], cot_ref[...].astype(F32)
    )
    d_branch = d_pre_two.astype(BF16)

    def drain(slot):
        for kind in range(3):
            view = stage.at[slot, kind]
            pltpu.make_async_copy(view, view, store_sems.at[slot * 3 + kind]).wait()

    d_h = d_pre_two
    for c in range(CHUNKS):
        slot = c % 2
        if c >= 2:
            drain(slot)
        d_hidden = dot_nt(w_down[c], d_branch)
        d_gate = (d_hidden * keep_gate[c]).astype(BF16)
        d_up = (d_hidden * keep_up[c]).astype(BF16)
        stage[slot, 0] = dot_nn(d_gate, h_low).astype(BF16)
        stage[slot, 1] = dot_nn(d_up, h_low).astype(BF16)
        stage[slot, 2] = dot_nn(keep_hidden[c], d_branch).astype(BF16)
        for step in range(chunk_pieces):
            for kind in range(3):
                pltpu.make_async_copy(
                    stage.at[slot, kind, pl.ds(step * piece, piece)],
                    grads.at[place[bases[kind] + c * chunk_pieces + step]],
                    store_sems.at[slot * 3 + kind],
                ).start()
        d_h = d_h + dot_tn(d_gate, w_gate[c]) + dot_tn(d_up, w_up[c])

    d_pre_one, d_gain_one, d_bias_one = norm_back(unit_one, scale_one, norm_ref[0:1, :], d_h)
    d_pre_one_ref[...] = d_pre_one
    d_proj = d_pre_one.astype(BF16)
    stage_out[...] = dot_tn(d_proj, mixed).astype(BF16)
    for step in range(kind_pieces):
        pltpu.make_async_copy(
            stage_out.at[pl.ds(step * piece, piece)],
            grads.at[place[3 * kind_pieces + step]],
            store_sems.at[6],
        ).start()
    d_mixed_ref[...] = lax.dot_general(
        w_out[...], d_proj, (((0,), (1,)), ((), ())), preferred_element_type=F32
    ).astype(BF16)
    norm_grad[...] = jnp.concatenate(
        [
            d_gain_one,
            d_bias_one,
            d_gain_two,
            d_bias_two,
            jnp.zeros((4, d_gain_one.shape[1]), F32),
        ],
        axis=0,
    )
    drain(CHUNKS % 2)
    drain((CHUNKS + 1) % 2)
    pltpu.make_async_copy(stage_out, stage_out, store_sems.at[6]).wait()


def project_grad_kernel(
    sizes,
    place,
    gathered,
    d_own,
    d_pre_one,
    weights,
    grads_in,
    d_input,
    grads,
    w_all,
    stage,
    x_ref,
    load_sems,
    store_sems,
    own_sem,
):
    n_dp, tok, piece, kind_pieces = sizes
    own_copy = pltpu.make_async_copy(
        gathered.at[my_order(n_dp), pl.ds(0, tok)], x_ref, own_sem
    )
    own_copy.start()
    group_pieces = kind_pieces // GROUPS
    del grads_in

    def each(group):
        for kind in range(3):
            for step in range(group_pieces):
                row = (kind * group_pieces + step) * piece
                yield kind * kind_pieces + group * group_pieces + step, pl.ds(row, piece)

    def load(group):
        for number, span in each(group):
            fetch_piece(place, number, weights, w_all.at[group, span], load_sems.at[group])

    load(0)
    load(1)
    own_copy.wait()
    x_own = x_ref[...]
    for group in range(GROUPS):
        stage[group] = dot_nn(d_own[group], x_own).astype(BF16)
        if group + 2 < GROUPS:
            load(group + 2)
        for number, span in each(group):
            pltpu.make_async_copy(
                stage.at[group, span], grads.at[place[number]], store_sems.at[group]
            ).start()
    total = d_pre_one[...]
    for group in range(GROUPS):
        view = w_all.at[group]
        pltpu.make_async_copy(view, view, load_sems.at[group]).wait()
        total = total + dot_tn(d_own[group], w_all[group])
    d_input[...] = total.astype(BF16)
    for group in range(GROUPS):
        view = stage.at[group]
        pltpu.make_async_copy(view, view, store_sems.at[group]).wait()


def add_low(dst, src, rows):
    def one(i, carry):
        dst[i] = (dst[i].astype(F32) + src[i].astype(F32)).astype(BF16)
        return carry

    lax.fori_loop(0, rows, one, None)


def z_order_of(count):
    order = [0]
    for k in range(1, count):
        for far in (k, count - k):
            if far not in order:
                order.append(far)
    return order


def spread_steps(sizes, own, every, sems):
    zn, xn, yn, slots, last = sizes
    z_sems, xs_sems, ys_sems, xf_sems, yf_sems, near_sems, own_sem = sems[:7]
    xb_sems, yb_sems, zb_sems, nb_sems = sems[7:11]
    count = slots - last
    part = count * 9 // 16
    rest = count - part
    z, x = lax.axis_index("a"), lax.axis_index("b")
    y, core = lax.axis_index("y"), lax.axis_index("core")
    core_peer = {"core": 1 - core}
    xs, ys, z_order = range(1, xn), range(1, yn), z_order_of(zn)
    x_peers = {k: {"b": lax.rem(x + k, xn)} for k in xs}
    y_peers = {k: {"y": lax.rem(y + k, yn)} for k in ys}
    z_peers = {k: {"a": lax.rem(z + k, zn)} for k in range(1, zn)}
    source = own.at[pl.ds(0, count)]

    def number(jz, jx, jy):
        chip = (lax.rem(z + zn - jz, zn) * xn + lax.rem(x + xn - jx, xn)) * yn + lax.rem(
            y + yn - jy, yn
        )
        return chip * 2 + core

    def shard(jz, jx, jy, lead=0, rows=count):
        return every.at[pl.ds(number(jz, jx, jy) * slots + lead, rows)]

    def tail(jz, jx, jy):
        return shard(jz, jx, jy, count, last)

    def tail_held(jz, jx, jy):
        return own.at[pl.ds(count, last)] if (jz, jx, jy) == (0, 0, 0) else tail(jz, jx, jy)

    def xb_copy(jx, jy):
        index = (jx - 1) * yn + jy
        return remote(tail_held(0, 0, jy), tail(0, 0, jy), xb_sems, index, x_peers[jx])

    def yb_copy(jy):
        return remote(tail_held(0, 0, 0), tail(0, 0, 0), yb_sems, jy - 1, y_peers[jy])

    def zb_copy(jz, jx, jy):
        index = ((jz - 1) * xn + jx) * yn + jy
        return remote(tail_held(0, jx, jy), tail(0, jx, jy), zb_sems, index, z_peers[jz])

    def nb_copy(jz, jx, jy):
        index = (jz * xn + jx) * yn + jy
        return remote(tail_held(jz, jx, jy), tail(jz, jx, jy), nb_sems, index, core_peer)

    def tail_begin():
        for jy in ys:
            launch(yb_copy(jy))
        for jx in xs:
            launch(xb_copy(jx, 0))
        launch(nb_copy(0, 0, 0))

    def tail_across():
        for jy in ys:
            view = tail(0, 0, jy)
            remote(view, view, yb_sems, jy - 1, y_peers[jy]).wait_recv()
            for jx in xs:
                launch(xb_copy(jx, jy))
            launch(nb_copy(0, 0, jy))

    def tail_planes():
        for jx in xs:
            for jy in range(yn):
                view = tail(0, jx, jy)
                remote(view, view, xb_sems, (jx - 1) * yn + jy, x_peers[jx]).wait_recv()
                launch(nb_copy(0, jx, jy))
        for jz in z_order[1:]:
            for jx in range(xn):
                for jy in range(yn):
                    launch(zb_copy(jz, jx, jy))

    def tail_end():
        for jz in z_order[1:]:
            for jx in range(xn):
                for jy in range(yn):
                    view = tail(jz, jx, jy)
                    index = ((jz - 1) * xn + jx) * yn + jy
                    remote(view, view, zb_sems, index, z_peers[jz]).wait_recv()
                    launch(nb_copy(jz, jx, jy))

    def tail_settle():
        for jz in range(zn):
            for jx in range(xn):
                for jy in range(yn):
                    chip = lax.div(number(jz, jx, jy), 2)
                    view = every.at[pl.ds((chip * 2 + 1 - core) * slots + count, last)]
                    index = (jz * xn + jx) * yn + jy
                    remote(view, view, nb_sems, index, core_peer).wait_recv()

    def held(jz, jx, jy):
        return source if (jz, jx, jy) == (0, 0, 0) else shard(jz, jx, jy)

    def z_copy(jz):
        return remote(source, shard(0, 0, 0), z_sems, jz - 1, z_peers[jz])

    def xs_copy(jz, jx):
        return remote(
            held(jz, 0, 0), shard(jz, 0, 0), xs_sems, jz * (xn - 1) + jx - 1, x_peers[jx]
        )

    def ys_copy(jz, jy):
        return remote(
            held(jz, 0, 0), shard(jz, 0, 0), ys_sems, jz * (yn - 1) + jy - 1, y_peers[jy]
        )

    def cross(jz, jx, jy):
        return (jz * (xn - 1) + jx - 1) * (yn - 1) + jy - 1

    def xf_copy(jz, jx, jy):
        view = shard(jz, 0, jy, part, rest)
        return remote(view, view, xf_sems, cross(jz, jx, jy), x_peers[jx])

    def yf_copy(jz, jx, jy):
        view = shard(jz, jx, 0, 0, part)
        return remote(view, view, yf_sems, cross(jz, jx, jy), y_peers[jy])

    def near_copy(jz, jx, jy):
        return remote(
            held(jz, jx, jy),
            shard(jz, jx, jy),
            near_sems,
            (jz * xn + jx) * yn + jy,
            core_peer,
        )

    started = []

    def launch(copy):
        copy.start()
        started.append(copy)

    def send_own(jz):
        for jx in xs:
            launch(xs_copy(jz, jx))
        for jy in ys:
            launch(ys_copy(jz, jy))
        launch(near_copy(jz, 0, 0))

    def ys_copy_in(jz, jy):
        view = shard(jz, 0, jy)
        remote(view, view, ys_sems, jz * (yn - 1) + jy - 1, y_peers[jy]).wait_recv()

    def xs_copy_in(jz, jx):
        view = shard(jz, jx, 0)
        remote(view, view, xs_sems, jz * (xn - 1) + jx - 1, x_peers[jx]).wait_recv()

    def forward(jz):
        for jy in ys:
            ys_copy_in(jz, jy)
            for jx in xs:
                launch(xf_copy(jz, jx, jy))
        for jx in xs:
            xs_copy_in(jz, jx)
            for jy in ys:
                launch(yf_copy(jz, jx, jy))
        for jy in ys:
            launch(near_copy(jz, 0, jy))
        for jx in xs:
            launch(near_copy(jz, jx, 0))

    def finish(jz):
        for jx in xs:
            for jy in ys:
                view = shard(jz, jx, jy, part, rest)
                remote(view, view, xf_sems, cross(jz, jx, jy), x_peers[jx]).wait_recv()
                view = shard(jz, jx, jy, 0, part)
                remote(view, view, yf_sems, cross(jz, jx, jy), y_peers[jy]).wait_recv()
                launch(near_copy(jz, jx, jy))

    def z_in(index):
        jz = z_order[index]
        view = shard(jz, 0, 0)
        remote(view, view, z_sems, jz - 1, z_peers[jz]).wait_recv()
        if index + 1 < zn:
            launch(z_copy(z_order[index + 1]))

    own_local = pltpu.make_async_copy(own, shard(0, 0, 0, 0, slots), own_sem)

    def begin():
        launch(z_copy(z_order[1]))
        send_own(0)
        own_local.start()
        if last:
            tail_begin()

    def advance(index):
        z_in(index)
        send_own(z_order[index])
        if last and index == 1:
            tail_across()

    def forward_step(index):
        forward(z_order[index])
        if last and index == zn - 2:
            tail_planes()

    def end():
        finish(z_order[zn - 1])
        if last:
            tail_end()
            tail_settle()
        for jz in range(zn):
            for jx in range(xn):
                for jy in range(yn):
                    chip = lax.div(number(jz, jx, jy), 2)
                    view = every.at[pl.ds((chip * 2 + 1 - core) * slots, count)]
                    remote(
                        view, view, near_sems, (jz * xn + jx) * yn + jy, core_peer
                    ).wait_recv()

    def settle():
        own_local.wait()
        for copy in started:
            copy.wait_send()

    steps = [begin]
    for index in range(1, zn):
        steps.append(functools.partial(advance, index))
        steps.append(functools.partial(forward_step, index - 1))
        if index >= 2:
            steps.append(functools.partial(finish, z_order[index - 2]))
    steps.append(functools.partial(forward_step, zn - 1))
    steps.append(functools.partial(finish, z_order[zn - 2]))
    steps.append(end)
    steps.append(settle)
    return [core_peer, *x_peers.values(), *y_peers.values(), *z_peers.values()], steps


def block_steps(sizes, pack, gathered, crossed, sems):
    zn, xn, yn = sizes
    by_sems, bz_sems, bx_sems, bn_sems, stay_sem = sems
    z, x = lax.axis_index("a"), lax.axis_index("b")
    y, core = lax.axis_index("y"), lax.axis_index("core")
    core_peer = {"core": 1 - core}
    xs, ys, z_order = range(1, xn), range(1, yn), z_order_of(zn)
    x_peers = {k: {"b": lax.rem(x + k, xn)} for k in xs}
    y_peers = {k: {"y": lax.rem(y + k, yn)} for k in ys}
    z_peers = {k: {"a": lax.rem(z + k, zn)} for k in range(1, zn)}
    hosts = lax.rem(z, 2) == core

    def block(jz, jx=0):
        return gathered.at[lax.rem(x + xn - jx, xn) * zn + lax.rem(z + zn - jz, zn)]

    def by_copy(jy):
        return remote(pack, crossed.at[jy - 1], by_sems, jy - 1, y_peers[jy])

    def plane(jy):
        return lax.rem(y + yn - jy, yn) * 2 + core

    def bz_copy(jy):
        src = pack if jy == 0 else crossed.at[jy - 1]
        far = lax.rem(plane(jy) + zn - z, zn)
        return remote(src, block(0), bz_sems, far, {"a": plane(jy)})

    def stay_copy(jy):
        src = pack if jy == 0 else crossed.at[jy - 1]
        return pltpu.make_async_copy(src, block(0), stay_sem)

    def bx_copy(jz, jx):
        return remote(block(jz), block(jz), bx_sems, jz * (xn - 1) + jx - 1, x_peers[jx])

    def bn_copy(jz, jx):
        return remote(block(jz, jx), block(jz, jx), bn_sems, jz * xn + jx, core_peer)

    def cross_y():
        for jy in ys:
            by_copy(jy).start()

    def to_planes():
        for jy in range(yn):
            if jy != 0:
                by_copy(jy).wait_recv()

            @pl.when(plane(jy) != z)
            def _():
                bz_copy(jy).start()

            @pl.when(plane(jy) == z)
            def _():
                stay_copy(jy).start()
                stay_copy(jy).wait()

    def across():
        @pl.when(hosts)
        def _():
            for jz in z_order:
                if jz != 0:
                    remote(block(jz), block(jz), bz_sems, jz, z_peers[jz]).wait_recv()
                for jx in xs:
                    bx_copy(jz, jx).start()
                bn_copy(jz, 0).start()

    def end():
        @pl.when(hosts)
        def _():
            for jz in z_order:
                for jx in xs:
                    view = block(jz, jx)
                    index = jz * (xn - 1) + jx - 1
                    remote(view, view, bx_sems, index, x_peers[jx]).wait_recv()
                    bn_copy(jz, jx).start()
            for jz in z_order:
                for jx in xs:
                    bx_copy(jz, jx).wait_send()
                for jx in range(xn):
                    bn_copy(jz, jx).wait_send()

        @pl.when(jnp.logical_not(hosts))
        def _():
            for jz in range(zn):
                for jx in range(xn):
                    bn_copy(jz, jx).wait_recv()

        for jy in range(yn):

            @pl.when(plane(jy) != z)
            def _():
                bz_copy(jy).wait_send()

        for jy in ys:
            by_copy(jy).wait_send()

    return [cross_y, to_planes, across, end]


def spread_kernel(
    sizes, master, x_in, seg_in, every, gathered, crossed, own, pack, *sems
):
    peers, steps = spread_steps(sizes, own, every, sems[:11])
    cross_y, to_planes, across, end = block_steps(sizes[:3], pack, gathered, crossed, sems[11:])
    tok, width = x_in.shape

    def prepare():
        own[...] = master[...].astype(BF16)
        pack[0:tok, :] = x_in[...]
        segs = jnp.concatenate(
            [seg_in[...].astype(F32), jnp.zeros((1, width - tok), F32)], axis=1
        )
        pack[tok:, :] = jnp.broadcast_to(segs, (pack.shape[0] - tok, width)).astype(BF16)

    greet(peers, meanwhile=prepare)
    steps[0]()
    cross_y()
    for step in steps[1:-7]:
        step()
    to_planes()
    for step in steps[-7:-3]:
        step()
    across()
    steps[-3]()
    steps[-2]()
    end()
    steps[-1]()


def reduce_steps(sizes, grads, total_out, refs):
    zn, xn, yn, slots, last = sizes
    held, near, xd, yd, xs_in, ys_in, zs_in, xb, yb, zb = refs[:10]
    load_sems, near_sems, xd_sems, yd_sems, xs_sems, ys_sems, zs_sems = refs[10:17]
    xb_sems, yb_sems, zb_sems = refs[17:20]
    count = slots - last
    part = count // 2
    rest = count - part
    tail = pl.ds(count, last)
    z, x = lax.axis_index("a"), lax.axis_index("b")
    y, core = lax.axis_index("y"), lax.axis_index("core")
    core_peer = {"core": 1 - core}
    xs, ys = range(1, xn), range(1, yn)
    y_peers = [{"y": lax.rem(y + k, yn)} for k in ys]
    x_peers = [{"b": lax.rem(x + k, xn)} for k in xs]
    z_peers = [{"a": lax.rem(z + k, zn)} for k in range(1, zn)]
    def flat(jz, jx, jy):
        return (jz * xn + jx) * yn + jy

    def chip_rows(jz, jx, jy, which):
        chip = (lax.rem(z + jz, zn) * xn + lax.rem(x + jx, xn)) * yn + lax.rem(y + jy, yn)
        return grads.at[pl.ds((chip * 2 + which) * slots, slots)]

    def near_copy(jz, jx, jy):
        index = flat(jz, jx, jy)
        return remote(chip_rows(jz, jx, jy, 1 - core), near.at[index], near_sems, index, core_peer)

    def load_copy(jz, jx, jy):
        index = flat(jz, jx, jy)
        return pltpu.make_async_copy(
            chip_rows(jz, jx, jy, core), held.at[index], load_sems.at[index]
        )

    def whole(jz, jx, jy):
        return held.at[flat(jz, jx, jy)]

    def first(jz, jx, jy):
        return held.at[flat(jz, jx, jy), pl.ds(0, part)]

    def second(jz, jx, jy):
        return held.at[flat(jz, jx, jy), pl.ds(part, rest)]

    def cross(jz, jx, jy):
        return (jz * (xn - 1) + jx - 1) * (yn - 1) + jy - 1

    def yd_copy(jz, jx, jy):
        index = cross(jz, jx, jy)
        return remote(first(jz, jx, jy), yd.at[index], yd_sems, index, y_peers[jy - 1])

    def xd_copy(jz, jx, jy):
        index = cross(jz, jx, jy)
        return remote(second(jz, jx, jy), xd.at[index], xd_sems, index, x_peers[jx - 1])

    def halves(low_half):
        return pl.ds(0, part) if low_half else pl.ds(part, rest)

    def xs_copy(jz, jx, low_half):
        index = jz * (xn - 1) + jx - 1
        return remote(
            held.at[flat(jz, jx, 0), halves(low_half)],
            xs_in.at[index, halves(low_half)],
            xs_sems,
            index * 2 + int(low_half),
            x_peers[jx - 1],
        )

    def ys_copy(jz, jy, low_half):
        index = jz * (yn - 1) + jy - 1
        return remote(
            held.at[flat(jz, 0, jy), halves(low_half)],
            ys_in.at[index, halves(low_half)],
            ys_sems,
            index * 2 + int(low_half),
            y_peers[jy - 1],
        )

    def zs_copy(jz):
        src = held.at[flat(jz, 0, 0), pl.ds(0, count)]
        return remote(src, zs_in.at[jz - 1], zs_sems, jz - 1, z_peers[jz - 1])

    def zb_copy(jz):
        src = held.at[pl.ds(jz * xn * yn, xn * yn), tail]
        return remote(src, zb.at[jz - 1], zb_sems, jz - 1, z_peers[jz - 1])

    def xb_copy(jx):
        src = held.at[pl.ds(jx * yn, yn), tail]
        return remote(src, xb.at[jx - 1], xb_sems, jx - 1, x_peers[jx - 1])

    def yb_copy(jy):
        return remote(held.at[jy, tail], yb.at[jy - 1], yb_sems, jy - 1, y_peers[jy - 1])

    def tail_planes():
        for jz in range(1, zn):
            zb_copy(jz).wait_recv()

        def one(i, carry):
            for chip in range(xn * yn):
                total = held[chip, count + i].astype(F32)
                for jz in range(1, zn):
                    total = total + zb[jz - 1, chip, i].astype(F32)
                held[chip, count + i] = total.astype(BF16)
            return carry

        lax.fori_loop(0, last, one, None)
        for jx in xs:
            launch(xb_copy(jx))

    def tail_columns():
        for jx in xs:
            xb_copy(jx).wait_recv()
            for jy in range(yn):
                add_low(held.at[jy, tail], xb.at[jx - 1, jy], last)
        for jy in ys:
            launch(yb_copy(jy))

    def tail_end():
        for jy in ys:
            yb_copy(jy).wait_recv()

        def one(i, carry):
            total = held[0, count + i].astype(F32)
            for jy in ys:
                total = total + yb[jy - 1, i].astype(F32)
            total_out[count + i] = total
            return carry

        lax.fori_loop(0, last, one, None)

    z_order = z_order_of(zn)[::-1]
    started = []

    def launch(copy):
        copy.start()
        started.append(copy)

    def plane(jz):
        return (
            [(jz, jx, jy) for jx in xs for jy in ys]
            + [(jz, jx, 0) for jx in xs]
            + [(jz, 0, jy) for jy in ys]
            + [(jz, 0, 0)]
        )

    def fetch(jz):
        for chip in plane(jz):
            launch(near_copy(*chip))
            load_copy(*chip).start()

    def prepare(index):
        for chip in plane(z_order[index]):
            load_copy(*chip).wait()
            near_copy(*chip).wait_recv()
            add_low(whole(*chip), near.at[flat(*chip)], slots)
        if index + 1 < zn:
            fetch(z_order[index + 1])
        if last and z_order[index] != 0:
            launch(zb_copy(z_order[index]))

    stages = [(index, stage) for index in range(zn) for stage in range(3)]

    def send_stage(number):
        index, stage = stages[number]
        jz = z_order[index]
        for jx in xs:
            if stage == 0:
                for jy in ys:
                    launch(xd_copy(jz, jx, jy))
            else:
                launch(xs_copy(jz, jx, stage == 2))
        for jy in ys:
            if stage == 0:
                for jx in xs:
                    launch(yd_copy(jz, jx, jy))
            else:
                launch(ys_copy(jz, jy, stage == 1))

    def take_stage(number):
        index, stage = stages[number]
        jz = z_order[index]
        if stage == 0:
            for jx in xs:
                for jy in ys:
                    yd_copy(jz, jx, jy).wait_recv()
                    add_low(first(jz, jx, 0), yd.at[cross(jz, jx, jy)], part)
                    xd_copy(jz, jx, jy).wait_recv()
                    add_low(second(jz, 0, jy), xd.at[cross(jz, jx, jy)], rest)
        else:
            for jx in xs:
                xs_copy(jz, jx, stage == 2).wait_recv()
            for jy in ys:
                ys_copy(jz, jy, stage == 1).wait_recv()

    def side_in(index):
        jz = z_order[index]

        def one(i, carry):
            total = held[flat(jz, 0, 0), i].astype(F32)
            for jx in xs:
                total = total + xs_in[jz * (xn - 1) + jx - 1, i].astype(F32)
            for jy in ys:
                total = total + ys_in[jz * (yn - 1) + jy - 1, i].astype(F32)
            if jz != 0:
                held[flat(jz, 0, 0), i] = total.astype(BF16)
            else:
                total_out[i] = total
            return carry

        lax.fori_loop(0, count, one, None)
        if jz != 0:
            launch(zs_copy(jz))

    ahead = 2

    def begin():
        fetch(z_order[0])

    def begin_stages():
        prepare(0)
        for number in range(ahead):
            send_stage(number)

    def one_stage(number):
        for index in range(1, zn):
            if number == (index - 1 if index < 3 else 3 * (index - 2)):
                prepare(index)
        take_stage(number)
        later = number + ahead
        if later < len(stages):
            send_stage(later)
        if stages[number][1] == 2:
            side_in(stages[number][0])
        if last and number == len(stages) - 4:
            tail_planes()
        if last and number == len(stages) - 2:
            tail_columns()

    def end():
        for jz in range(1, zn):
            zs_copy(jz).wait_recv()

        def add_planes(i, carry):
            total = total_out[i]
            for jz in range(1, zn):
                total = total + zs_in[jz - 1, i].astype(F32)
            total_out[i] = total
            return carry

        lax.fori_loop(0, count, add_planes, None)
        if last:
            tail_end()
        for copy in started:
            copy.wait_send()

    steps = [begin, begin_stages]
    steps += [functools.partial(one_stage, number) for number in range(len(stages))]
    steps.append(end)
    return [core_peer] + y_peers + x_peers + z_peers, steps


def reduce_kernel(sizes, grads, tokens_in, total_out, tokens_out, *refs):
    peers, steps = reduce_steps(sizes, grads, total_out, refs[:20])
    turn_sems = refs[20]
    greet(peers, True)
    turn_refs = (tokens_in, tokens_out, turn_sems.at[0], turn_sems.at[1])
    start_turn(*turn_refs)
    for step in steps:
        step()
    finish_turn(*turn_refs)


def vmem():
    return pl.BlockSpec(memory_space=pltpu.VMEM)


def smem():
    return pl.BlockSpec(memory_space=pltpu.SMEM)


def anywhere():
    return pl.BlockSpec(memory_space=pl.ANY)


def shape_of(dims, kind):
    return jax.ShapeDtypeStruct(dims, kind)


def params(collective=None):
    if collective is None:
        return pltpu.CompilerParams(vmem_limit_bytes=VMEM_LIMIT)
    return pltpu.CompilerParams(
        vmem_limit_bytes=VMEM_LIMIT, collective_id=collective, has_side_effects=True
    )


def pair(count):
    return pltpu.SemaphoreType.DMA((2, max(count, 1)))


def spread_scratch(zn, xn, yn):
    return [
        pair(zn - 1),
        pair(zn * (xn - 1)),
        pair(zn * (yn - 1)),
        pair(zn * (xn - 1) * (yn - 1)),
        pair(zn * (xn - 1) * (yn - 1)),
        pair(zn * xn * yn),
        pltpu.SemaphoreType.DMA,
        pair((xn - 1) * yn),
        pair(yn - 1),
        pair((zn - 1) * xn * yn),
        pair(zn * xn * yn),
    ]


def reduce_scratch(zn, xn, yn, slots, last, piece, width):
    def chunks(*dims):
        return pltpu.VMEM(tuple(max(dim, 1) for dim in dims) + (piece, width), BF16)

    n_chips, crossing = zn * xn * yn, zn * (xn - 1) * (yn - 1)
    count = slots - last
    part = count // 2
    return [
        chunks(n_chips, slots),
        chunks(n_chips, slots),
        chunks(crossing, count - part),
        chunks(crossing, part),
        chunks(zn * (xn - 1), count),
        chunks(zn * (yn - 1), count),
        chunks(zn - 1, count),
        chunks(xn - 1, yn, last),
        chunks(yn - 1, last),
        chunks(zn - 1, xn * yn, last),
        pltpu.SemaphoreType.DMA((n_chips,)),
        pair(n_chips),
        pair(crossing),
        pair(crossing),
        pair(2 * zn * (xn - 1)),
        pair(2 * zn * (yn - 1)),
        pair(zn - 1),
        pair(xn - 1),
        pair(yn - 1),
        pair(zn - 1),
    ]


def run_layer(dims, weight_master, x_own, segments, cotangent, location, norm_params):
    n_seq, n_dp = dims
    reps = n_seq // n_dp
    splits = n_seq // GROUPS
    slots, piece, width = weight_master.shape
    tok = cotangent.shape[0]
    length = tok * n_seq
    hidden_units = (location.shape[0] * piece - 4 * width) // 3
    head = width // HEADS
    kind_pieces = width // piece
    hidden_pieces = hidden_units // piece
    chunk = hidden_units // CHUNKS
    zn, xn, yn = n_dp, reps, n_dp // 2
    all_slots = n_seq * n_dp * slots
    last = slots // 8
    slopes = jnp.asarray(head_slopes(HEADS, tok, n_seq))

    weights, gathered, _ = pl.pallas_call(
        functools.partial(spread_kernel, (zn, xn, yn, slots, last)),
        out_shape=(
            shape_of((all_slots, piece, width), BF16),
            shape_of((n_seq, tok + 16, width), BF16),
            shape_of((max(yn - 1, 1), tok + 16, width), BF16),
        ),
        in_specs=[vmem(), vmem(), vmem()],
        out_specs=(anywhere(),) * 3,
        scratch_shapes=[
            pltpu.VMEM((slots, piece, width), BF16),
            pltpu.VMEM((tok + 16, width), BF16),
        ]
        + spread_scratch(zn, xn, yn)
        + [
            pair(yn - 1),
            pair(zn),
            pair(zn * (xn - 1)),
            pair(zn * xn),
            pltpu.SemaphoreType.DMA,
        ],
        compiler_params=params(1),
    )(weight_master, x_own, segments)
    attend_sizes = (n_dp, reps, splits, tok, head, n_seq)
    q_ext, k_ext, k_turned, v_rows, v_turned = pl.pallas_call(
        functools.partial(project_kernel, (n_dp, splits, tok, head)),
        grid=(n_seq,),
        out_shape=(
            shape_of((TRIO, GROUPS * tok, 128), BF16),
            shape_of((TRIO, length, 128), BF16),
            shape_of((TRIO, head, length), BF16),
            shape_of((TRIO, length, head), BF16),
            shape_of((TRIO, head, length), BF16),
        ),
        in_specs=[
            smem(),
            pl.BlockSpec((1, tok + 16, width), lambda i: (i, 0, 0)),
            anywhere(),
        ],
        out_specs=(
            pl.BlockSpec((TRIO, tok, 128), lambda i: (0, lax.div(i, splits), 0)),
            pl.BlockSpec((TRIO, tok, 128), lambda i: (0, i, 0)),
            pl.BlockSpec((TRIO, head, tok), lambda i: (0, 0, i)),
            pl.BlockSpec((TRIO, tok, head), lambda i: (0, i, 0)),
            pl.BlockSpec((TRIO, head, tok), lambda i: (0, 0, i)),
        ),
        scratch_shapes=[
            pltpu.VMEM((3 * TRIO, 128, width), BF16),
            pltpu.SemaphoreType.DMA((3 * TRIO * (head // piece),)),
        ],
        compiler_params=params(),
    )(location, gathered, weights)

    mixed_full, log_total, mixed_own, cotangent = pl.pallas_call(
        functools.partial(attend_forward_kernel, attend_sizes),
        out_shape=(
            shape_of((GROUPS, TRIO, head, tok), F32),
            shape_of((GROUPS, TRIO, 1, tok), F32),
            shape_of((GROUPS, TRIO, head, tok), BF16),
            shape_of(cotangent.shape, BF16),
        ),
        in_specs=[smem(), vmem(), vmem(), vmem(), anywhere()],
        out_specs=(vmem(), vmem(), vmem(), anywhere()),
        scratch_shapes=[
            pltpu.VMEM((3 * TRIO, tok, tok), F32),
            pltpu.VMEM((n_seq, tok, tok), F32),
            pltpu.VMEM((GROUPS, TRIO, head, tok), BF16),
            pair(GROUPS - 1),
            pltpu.SemaphoreType.DMA((2,)),
        ],
        compiler_params=params(2),
    )(slopes, q_ext, k_ext, v_turned, cotangent)

    out_low, d_pre_one, d_mixed, norm_part, grads = pl.pallas_call(
        functools.partial(
            dense_kernel, (n_dp, tok, piece, kind_pieces, chunk // piece, hidden_pieces)
        ),
        out_shape=(
            shape_of((tok, width), BF16),
            shape_of((tok, width), F32),
            shape_of((width, tok), BF16),
            shape_of((8, width), F32),
            shape_of((all_slots, piece, width), BF16),
        ),
        in_specs=[smem(), anywhere(), vmem(), vmem(), vmem(), anywhere()],
        out_specs=(vmem(), vmem(), vmem(), vmem(), anywhere()),
        scratch_shapes=[
            pltpu.VMEM((width, width), BF16),
            pltpu.VMEM((CHUNKS, chunk, width), BF16),
            pltpu.VMEM((CHUNKS, chunk, width), BF16),
            pltpu.VMEM((CHUNKS, chunk, width), BF16),
            pltpu.VMEM((CHUNKS, chunk, tok), F32),
            pltpu.VMEM((CHUNKS, chunk, tok), F32),
            pltpu.VMEM((CHUNKS, chunk, tok), BF16),
            pltpu.VMEM((2, 3, chunk, width), BF16),
            pltpu.VMEM((width, width), BF16),
            pltpu.VMEM((tok, width), BF16),
            pltpu.SemaphoreType.DMA((3 * CHUNKS + 1,)),
            pltpu.SemaphoreType.DMA((7,)),
            pltpu.SemaphoreType.DMA,
        ],
        compiler_params=params(),
    )(location, gathered, cotangent, mixed_own.reshape(width, tok), norm_params, weights)

    def norm_rows(count):
        return pltpu.VMEM((max(count, 1), 8, width), F32)

    d_own, result, norm_total = pl.pallas_call(
        functools.partial(attend_backward_kernel, attend_sizes),
        out_shape=(
            shape_of((GROUPS, 3, TRIO, head, tok), BF16),
            shape_of(out_low.shape, BF16),
            shape_of((8, width), F32),
        ),
        in_specs=[smem()] + [vmem()] * 7 + [anywhere(), vmem()],
        out_specs=(vmem(), anywhere(), vmem()),
        scratch_shapes=[
            pltpu.VMEM((length, 128), F32),
            pltpu.VMEM((3 * TRIO, tok, tok), F32),
            pltpu.VMEM((GROUPS, TRIO, head, tok), BF16),
            pltpu.VMEM((GROUPS, 3, TRIO, head, tok), BF16),
            pltpu.VMEM((TRIO, splits, GROUPS, 2, head, tok), BF16),
            pltpu.VMEM((TRIO, splits - 1, GROUPS, 2, head, tok), BF16),
            pair(GROUPS - 1),
            pair(TRIO * (GROUPS - 1)),
            pair(TRIO * (splits - 1)),
            pair(TRIO * (GROUPS - 1)),
            pltpu.SemaphoreType.DMA((2,)),
            norm_rows(1),
            norm_rows(yn - 1),
            norm_rows(xn - 1),
            norm_rows(zn - 1),
            norm_rows(4),
            pair(1 + (yn - 1) + (xn - 1) + (zn - 1)),
        ],
        compiler_params=params(3),
    )(
        slopes,
        q_ext,
        k_ext,
        k_turned,
        v_rows,
        mixed_full,
        log_total,
        d_mixed.reshape(GROUPS, TRIO, head, tok),
        out_low,
        norm_part,
    )

    trio_rows = TRIO * head
    d_tokens, grads = pl.pallas_call(
        functools.partial(project_grad_kernel, (n_dp, tok, piece, kind_pieces)),
        out_shape=(shape_of((tok, width), BF16), shape_of(grads.shape, BF16)),
        in_specs=[smem(), anywhere(), vmem(), vmem()] + [anywhere()] * 2,
        out_specs=(vmem(), anywhere()),
        scratch_shapes=[
            pltpu.VMEM((GROUPS, 3 * trio_rows, width), BF16),
            pltpu.VMEM((GROUPS, 3 * trio_rows, width), BF16),
            pltpu.VMEM((tok, width), BF16),
            pltpu.SemaphoreType.DMA((GROUPS,)),
            pltpu.SemaphoreType.DMA((GROUPS,)),
            pltpu.SemaphoreType.DMA,
        ],
        input_output_aliases={5: 1},
        compiler_params=params(),
    )(location, gathered, d_own.reshape(GROUPS, 3 * trio_rows, tok), d_pre_one, weights, grads)

    own_grad, d_turned = pl.pallas_call(
        functools.partial(reduce_kernel, (zn, xn, yn, slots, last)),
        out_shape=(
            shape_of((slots, piece, width), F32),
            shape_of(d_tokens.shape, BF16),
        ),
        in_specs=[anywhere(), anywhere()],
        out_specs=(vmem(), anywhere()),
        scratch_shapes=reduce_scratch(zn, xn, yn, slots, last, piece, width)
        + [pltpu.SemaphoreType.DMA((2,))],
        compiler_params=params(4),
    )(grads, d_tokens)
    return own_grad, norm_total, d_turned, result


def per_device(
    dims,
    layer_input,
    out_cotangent,
    segment_ids,
    piece_owner,
    weight_master,
    weight_first,
    weight_second,
    norm_params,
    norm_first,
    norm_second,
):
    slots, piece, width = weight_master.shape
    pieces = piece_owner.shape[0]
    tok = layer_input.shape[1]
    hidden_units = (pieces * piece - 4 * width) // 3
    location = locate_pieces(piece_owner, slots)
    own_grad, norm_total, d_turned, result = run_layer(
        dims,
        weight_master,
        layer_input[0],
        segment_ids,
        out_cotangent[0],
        location,
        norm_params,
    )

    numbers = jnp.arange(pieces, dtype=jnp.int32) + 1
    own_slots = lax.axis_index(("a", "b", "y", "core")) * slots + jnp.arange(slots)
    inverse = jnp.sum(jnp.where(location[None, :] == own_slots[:, None], numbers[None, :], 0), axis=1)
    own_grad = jnp.where((inverse > 0)[:, None, None], own_grad, 0.0)
    norm_grad = norm_total[:4]
    rates = slot_rates(inverse, piece, width, hidden_units)
    first_new, second_new, weight_new = adamw_step(
        weight_master, weight_first, weight_second, own_grad, rates[:, None, None], STEP
    )
    norm_first_new, norm_second_new, norm_new = adamw_step(
        norm_params, norm_first, norm_second, norm_grad, NORM_RATE, STEP
    )
    return (
        result[None],
        d_turned.astype(F32)[None],
        own_grad,
        first_new,
        second_new,
        weight_new,
        weight_new.astype(BF16),
        norm_grad,
        norm_first_new,
        norm_second_new,
        norm_new,
    )


def solution(mesh):
    n_seq, n_dp = mesh.shape["seq"], mesh.shape["dp"]
    inner = Mesh(
        mesh.devices.reshape(n_dp, n_seq // n_dp, n_dp // 2, 2), ("a", "b", "y", "core")
    )
    seq, dp, every = ("a", "b"), ("y", "core"), ("a", "b", "y", "core")
    block = P(dp, seq, None)
    owned = P(every, None, None)
    in_specs = (block, block, P(dp, seq), P(), owned, owned, owned, P(), P(), P())
    out_specs = (block, block, owned, owned, owned, owned, owned, P(), P(), P(), P())
    return jax.shard_map(
        functools.partial(per_device, (n_seq, n_dp)),
        mesh=inner,
        in_specs=in_specs,
        out_specs=out_specs,
        check_vma=False,
    )
```

```python
import functools

import jax
import jax.numpy as jnp
import numpy as np
from jax import lax
from jax.experimental import pallas as pl
from jax.experimental.pallas import tpu as pltpu
from jax.sharding import Mesh
from jax.sharding import PartitionSpec as P

HEADS = 12
GROUPS = 4
TRIO = HEADS // GROUPS
STEP = 4

NORM_EPS = 1e-06
BETA_ONE = 0.5
BETA_TWO = 0.5
DECAY = 0.01
ADAM_EPS = 1e-08
NORM_RATE = 0.3
OUT_RATE = 0.35
MASKED = -1e30
CHUNKS = 6
VMEM_LIMIT = 60 * 1024 * 1024
MESH_IDS = pl.DeviceIdType.MESH
F32 = jnp.float32
BF16 = jnp.bfloat16


def head_slopes(head_count, tok_rows, seq_devices):
    head_order = np.arange(head_count, dtype=np.float64)
    slopes = 8.0 / tok_rows * np.power(8.0 * seq_devices, -head_order / (head_count - 1))
    return slopes.astype(np.float32)


def locate_pieces(owners, slot_count):
    pieces = owners.shape[0]
    numbers = jnp.arange(pieces, dtype=jnp.int32)
    earlier = (owners[None, :] == owners[:, None]) & (numbers[None, :] < numbers[:, None])
    return owners * slot_count + jnp.sum(earlier.astype(jnp.int32), axis=1)


def slot_rates(inverse, piece_rows, model_width, hidden_units):
    first_row = (inverse - 1) * piece_rows
    narrow = model_width ** (-0.5)
    step_rate = jnp.where(
        first_row < 3 * model_width,
        narrow,
        jnp.where(
            first_row < 4 * model_width,
            OUT_RATE,
            jnp.where(
                first_row < 4 * model_width + 2 * hidden_units, narrow, hidden_units ** (-0.5)
            ),
        ),
    )
    return jnp.where(inverse > 0, step_rate, narrow).astype(jnp.float32)


def adamw_step(weight, first_moment, second, gradient, step_rate, step_count):
    first_moment = BETA_ONE * first_moment + (1.0 - BETA_ONE) * gradient
    second = BETA_TWO * second + (1.0 - BETA_TWO) * gradient * gradient
    mean_hat = first_moment / (1.0 - BETA_ONE**step_count)
    square_hat = second / (1.0 - BETA_TWO**step_count)
    weight = weight - step_rate * (mean_hat / (jnp.sqrt(square_hat) + ADAM_EPS) + DECAY * weight)
    return (first_moment, second, weight)


def dot_nt(left_side, right_side):
    return lax.dot_general(
        left_side, right_side, (((1,), (1,)), ((), ())), preferred_element_type=F32
    )


def dot_nn(left_side, right_side):
    return lax.dot_general(
        left_side, right_side, (((1,), (0,)), ((), ())), preferred_element_type=F32
    )


def dot_tn(left_side, right_side):
    return lax.dot_general(
        left_side, right_side, (((0,), (0,)), ((), ())), preferred_element_type=F32
    )


def fetch_piece(place, piece, weights, dst, sem):
    pltpu.make_async_copy(weights.at[place[piece]], dst, sem).start()


def fill_tables(table, slopes, group, tok):
    apart = lax.broadcasted_iota(jnp.int32, (tok, tok), 0) - lax.broadcasted_iota(
        jnp.int32, (tok, tok), 1
    )
    apart = apart.astype(F32)
    for h in range(TRIO):
        slope = slopes[group * TRIO + h]
        table[h * 3 + 0] = -slope * apart
        table[h * 3 + 1] = slope * jnp.abs(apart)
        table[h * 3 + 2] = slope * apart


def block_place(order, n_dp, reps):
    return (order % n_dp) * reps + order // n_dp


def bias_of(key_block, query_place, slope, h, tok, n_dp, reps):
    key_place = block_place(key_block, n_dp, reps)
    which = jnp.where(key_place > query_place, 2, jnp.where(key_place < query_place, 0, 1))
    shift = slope * (tok * jnp.abs(key_place - query_place)).astype(F32)
    return h * 3 + which, shift


def holder(order, n_dp):
    dp = lax.rem(order, n_dp)
    return {"b": lax.div(order, n_dp), "y": lax.div(dp, 2), "core": lax.rem(dp, 2)}


def turn_to():
    z, dp = lax.axis_index("a"), lax.axis_index("y") * 2 + lax.axis_index("core")
    return {"a": dp, "y": lax.div(z, 2), "core": lax.rem(z, 2)}, dp != z


def start_turn(src, dst, send_sem, recv_sem):
    peer, moves = turn_to()

    @pl.when(moves)
    def _():
        pltpu.make_async_remote_copy(
            src_ref=src,
            dst_ref=dst,
            send_sem=send_sem,
            recv_sem=recv_sem,
            device_id=peer,
            device_id_type=MESH_IDS,
        ).start()

    @pl.when(jnp.logical_not(moves))
    def _():
        pltpu.make_async_copy(src, dst, recv_sem).start()


def finish_turn(src, dst, send_sem, recv_sem):
    peer, moves = turn_to()

    @pl.when(moves)
    def _():
        pltpu.make_async_remote_copy(
            src_ref=src,
            dst_ref=dst,
            send_sem=send_sem,
            recv_sem=recv_sem,
            device_id=peer,
            device_id_type=MESH_IDS,
        ).wait()

    @pl.when(jnp.logical_not(moves))
    def _():
        pltpu.make_async_copy(src, dst, recv_sem).wait()


def greet(peers, turning=False, meanwhile=None):
    barrier = pltpu.get_barrier_semaphore()
    for peer in peers:
        pl.semaphore_signal(barrier, inc=1, device_id=peer, device_id_type=MESH_IDS)
    if meanwhile is not None:
        meanwhile()
    if not turning:
        pl.semaphore_wait(barrier, len(peers))
        return
    turn_peer, moves = turn_to()

    @pl.when(moves)
    def _():
        pl.semaphore_signal(barrier, inc=1, device_id=turn_peer, device_id_type=MESH_IDS)

    pl.semaphore_wait(barrier, len(peers) + moves.astype(jnp.int32))


def my_order(n_dp):
    return lax.axis_index("b") * n_dp + lax.axis_index("y") * 2 + lax.axis_index("core")


def remote(src, dst, sems, index, peer):
    return pltpu.make_async_remote_copy(
        src_ref=src,
        dst_ref=dst,
        send_sem=sems.at[0, index],
        recv_sem=sems.at[1, index],
        device_id=peer,
        device_id_type=MESH_IDS,
    )


def project_kernel(
    sizes,
    place,
    x_ref,
    weights,
    q_out,
    k_out,
    kt_out,
    v_out,
    vt_out,
    wpad,
    sems,
):
    n_dp, splits, tok, head = sizes
    order = my_order(n_dp)
    group, split = lax.div(order, splits), lax.rem(order, splits)
    block = pl.program_id(0)
    per_head = head // 16
    width = x_ref.shape[2]
    kind_pieces = width // 16

    @pl.when(block == 0)
    def _():
        def spots():
            for kind in range(3):
                for rest in range(TRIO * per_head):
                    step = kind * TRIO * per_head + rest
                    rows = pl.ds(rest % per_head * 16, 16)
                    dst = wpad.at[kind * TRIO + rest // per_head, rows]
                    yield kind * kind_pieces + group * (TRIO * per_head) + rest, dst, sems.at[step]

        for number, dst, sem in spots():
            fetch_piece(place, number, weights, dst, sem)
        for row in range(3 * TRIO):
            wpad[row, head:, :] = jnp.zeros((wpad.shape[1] - head, width), BF16)
        for _, dst, sem in spots():
            pltpu.make_async_copy(weights.at[0], dst, sem).wait()

    segs = x_ref[0, tok : tok + 1, 0:tok].astype(F32)
    number = lax.broadcasted_iota(jnp.int32, (128, tok), 0) - head
    same = segs == number.astype(F32)
    used = (number >= 0) & (number < 3)
    xb = x_ref[0, 0:tok, :]
    keys = dot_nt(xb, wpad[TRIO : 2 * TRIO].reshape(TRIO * 128, width))
    values = dot_nt(xb, wpad[2 * TRIO : 3 * TRIO].reshape(TRIO * 128, width))
    marks = jnp.where(used & jnp.logical_not(same), MASKED, 0.0).T.astype(BF16)
    for h in range(TRIO):
        key = keys[:, h * 128 : (h + 1) * 128]
        value = values[:, h * 128 : (h + 1) * 128]
        k_out[h] = key.astype(BF16) + marks
        v_out[h] = value[:, 0:head].astype(BF16)
        kt_out[h] = key.T[0:head].astype(BF16)
        vt_out[h] = value.T[0:head].astype(BF16)

    @pl.when(lax.rem(block, splits) == split)
    def _():
        w_query = wpad[0:TRIO].reshape(TRIO * 128, width)
        queries = dot_nt(xb, w_query).astype(BF16) * jnp.asarray(head**-0.5, BF16)
        query_marks = jnp.where(same & used, 1.0, 0.0).T.astype(BF16)
        for h in range(TRIO):
            q_out[h] = queries[:, h * 128 : (h + 1) * 128] + query_marks


def attend_forward_kernel(
    sizes,
    slopes,
    q_ref,
    k_ref,
    vt_ref,
    cot_in,
    mixed_full,
    log_out,
    mixed_own,
    cot_out,
    table,
    scores,
    mixed_low,
    swap_sems,
    turn_sems,
):
    n_dp, reps, splits, tok, head, blocks = sizes
    order = my_order(n_dp)
    group, split = lax.div(order, splits), lax.rem(order, splits)
    others = [lax.rem(group + k, GROUPS) for k in range(1, GROUPS)]
    peers = [holder(other * splits + split, n_dp) for other in others]
    started = []
    greet(peers, True)
    turn_refs = (cot_in, cot_out, turn_sems.at[0], turn_sems.at[1])
    start_turn(*turn_refs)
    fill_tables(table, slopes, group, tok)

    def attend(index, h):
        place_order = index * splits + split
        query_place = lax.rem(place_order, n_dp) * reps + lax.div(place_order, n_dp)
        slope = slopes[group * TRIO + h]
        qh = q_ref[h, pl.ds(pl.multiple_of(index * tok, tok), tok), :]
        top = None
        shifts = []
        for kb in range(blocks):
            which, shift = bias_of(kb, query_place, slope, h, tok, n_dp, reps)
            now = dot_nt(k_ref[h, kb * tok : (kb + 1) * tok, :], qh) - table[which]
            scores[kb] = now
            here = jnp.max(now, axis=0, keepdims=True) - shift
            top = here if top is None else jnp.maximum(top, here)
            shifts.append(shift)
        total = jnp.zeros((1, tok), F32)
        for kb in range(blocks):
            grown = jnp.exp(scores[kb] - (top + shifts[kb]))
            total = total + jnp.sum(grown, axis=0, keepdims=True)
            scores[kb] = grown
        inverse = 1.0 / total
        mixed = jnp.zeros((head, tok), F32)
        for kb in range(blocks):
            prob = (scores[kb] * inverse).astype(BF16)
            mixed = mixed + dot_nn(vt_ref[h, :, kb * tok : (kb + 1) * tok], prob)
        mixed_full[index, h] = mixed
        mixed_low[index, h] = mixed.astype(BF16)
        log_out[index, h] = top + jnp.log(total)

    for k in list(range(GROUPS - 1)) + [None]:
        index = group if k is None else others[k]

        def one(h, carry, index=index):
            attend(index, h)
            return carry

        lax.fori_loop(0, TRIO, one, None)
        if k is not None:
            copy = swap_copy(mixed_low, mixed_own, index, group, swap_sems, k, peers[k])
            copy.start()
            started.append(copy)
        else:
            mixed_own[group] = mixed_low[group]
    for copy in started:
        copy.wait()
    finish_turn(*turn_refs)


def swap_copy(src, dst, there, here, sems, index, peer):
    return pltpu.make_async_remote_copy(
        src_ref=src.at[there],
        dst_ref=dst.at[here],
        send_sem=sems.at[0, index],
        recv_sem=sems.at[1, index],
        device_id=peer,
        device_id_type=MESH_IDS,
    )


def norm_steps(dims, norm_in, norm_out, refs):
    zn, xn, yn = dims
    norm_core, norm_y, norm_x, norm_z, norm_sum, sems = refs
    z, x = lax.axis_index("a"), lax.axis_index("b")
    y, core = lax.axis_index("y"), lax.axis_index("core")
    rounds = [
        (norm_core, [{"core": 1 - core}]),
        (norm_y, [{"y": lax.rem(y + k, yn)} for k in range(1, yn)]),
        (norm_x, [{"b": lax.rem(x + k, xn)} for k in range(1, xn)]),
        (norm_z, [{"a": lax.rem(z + k, zn)} for k in range(1, zn)]),
    ]
    first = [sum(len(peers) for _, peers in rounds[:i]) for i in range(len(rounds))]

    def copies(i):
        buffer, peers = rounds[i]
        return [
            remote(norm_sum.at[i], buffer.at[k], sems, first[i] + k, peer)
            for k, peer in enumerate(peers)
        ]

    def begin():
        norm_sum[0] = norm_in[...]
        for copy in copies(0):
            copy.start()

    def turn_round(i):
        total = norm_sum[i]
        for k, copy in enumerate(copies(i)):
            copy.wait()
            total = total + rounds[i][0][k]
        if i + 1 == len(rounds):
            norm_out[...] = total
            return
        norm_sum[i + 1] = total
        for copy in copies(i + 1):
            copy.start()

    peers = [peer for _, group in rounds for peer in group]
    return peers, [begin] + [functools.partial(turn_round, i) for i in range(len(rounds))]


def attend_backward_kernel(
    sizes,
    slopes,
    q_ref,
    k_ref,
    kt_ref,
    v_ref,
    mixed_full,
    log_in,
    d_mixed,
    low_in,
    norm_in,
    own_ref,
    low_out,
    norm_out,
    dk_sum,
    dv_sum,
    table,
    d_blocks,
    shared,
    pairs,
    landed,
    swap_sems,
    query_sems,
    pair_sems,
    value_sems,
    turn_sems,
    *norm_refs,
):
    n_dp, reps, splits, tok, head, blocks = sizes
    order = my_order(n_dp)
    group, split = lax.div(order, splits), lax.rem(order, splits)
    twins = [lax.rem(split + k, splits) for k in range(1, splits)]
    twin_ids = [holder(group * splits + other, n_dp) for other in twins]
    others = [lax.rem(group + k, GROUPS) for k in range(1, GROUPS)]
    peers = [holder(other * splits + split, n_dp) for other in others]
    norm_peers, norms = norm_steps((n_dp, reps, n_dp // 2), norm_in, norm_out, norm_refs)
    greet(twin_ids + peers + norm_peers, True)
    turn_refs = (low_in, low_out, turn_sems.at[0], turn_sems.at[1])
    started = []

    def launch(copy):
        copy.start()
        started.append(copy)

    for k in range(GROUPS - 1):
        launch(remote(d_mixed.at[others[k]], d_blocks.at[group], swap_sems, k, peers[k]))
    d_blocks[group] = d_mixed[group]
    norms.pop(0)()
    fill_tables(table, slopes, group, tok)
    dk_sum[...] = jnp.zeros_like(dk_sum)
    dv_sum[...] = jnp.zeros_like(dv_sum)

    def step_fn(h, step):
        index = lax.rem(group + GROUPS - step, GROUPS)
        if h == 0:

            @pl.when(step > 0)
            def _():
                view = d_blocks.at[index]
                remote(view, view, swap_sems, step - 1, peers[0]).wait_recv()

        place_order = index * splits + split
        query_place = lax.rem(place_order, n_dp) * reps + lax.div(place_order, n_dp)
        slope = slopes[group * TRIO + h]
        qh = q_ref[h, pl.ds(pl.multiple_of(index * tok, tok), tok), :]
        dt = d_blocks[index, h]
        row_dot = jnp.sum(dt.astype(F32) * mixed_full[index, h], axis=0, keepdims=True)
        log_total = log_in[index, h]
        dq = jnp.zeros((head, tok), F32)
        for kb in range(blocks):
            rows = slice(kb * tok, (kb + 1) * tok)
            which, shift = bias_of(kb, query_place, slope, h, tok, n_dp, reps)
            now = dot_nt(k_ref[h, rows, :], qh) - table[which]
            prob = jnp.exp(now - (log_total + shift))
            d_prob = dot_nn(v_ref[h, rows, :], dt)
            d_score = (prob * (d_prob - row_dot)).astype(BF16)
            dv_sum[rows, :] += dot_nt(prob.astype(BF16), dt)
            dk_sum[rows, :] += dot_nn(d_score, qh)
            dq = dq + dot_nn(kt_ref[h, :, rows], d_score)
        shared[index, 0, h] = (dq * (head**-0.5)).astype(BF16)

    def pair_copy(h, k):
        return remote(
            pairs.at[h, twins[k]], landed.at[h, k], pair_sems, h * (splits - 1) + k, twin_ids[k]
        )

    def take_pairs(h):
        for k in range(splits - 1):
            pair_copy(h, k).wait_recv()
        for index in range(GROUPS):
            for kind in range(2):
                total = pairs[h, split, index, kind].astype(F32)
                for k in range(splits - 1):
                    total = total + landed[h, k, index, kind].astype(F32)
                shared[index, kind + 1, h] = total.astype(BF16)
        for k in range(GROUPS - 1):
            launch(
                remote(
                    shared.at[others[k], pl.ds(1, 2), h],
                    own_ref.at[group, pl.ds(1, 2), h],
                    value_sems,
                    h * (GROUPS - 1) + k,
                    peers[k],
                )
            )

    for h in range(TRIO):

        def one(step, carry, h=h):
            step_fn(h, step)
            return carry

        lax.fori_loop(0, GROUPS, one, None)
        if h == 0:
            start_turn(*turn_refs)
        norms.pop(0)()
        for k in range(GROUPS - 1):
            launch(
                remote(
                    shared.at[others[k], 0, h],
                    own_ref.at[group, 0, h],
                    query_sems,
                    h * (GROUPS - 1) + k,
                    peers[k],
                )
            )

        def flip(index, carry, h=h):
            for part in range(splits):
                rows = pl.ds(pl.multiple_of((index * splits + part) * tok, tok), tok)
                pairs[h, part, index, 0] = dk_sum[rows, :].T[0:head].astype(BF16)
                pairs[h, part, index, 1] = dv_sum[rows, :].T.astype(BF16)
            return carry

        lax.fori_loop(0, GROUPS, flip, None)
        if h + 1 < TRIO:
            dk_sum[...] = jnp.zeros_like(dk_sum)
            dv_sum[...] = jnp.zeros_like(dv_sum)
        for k in range(splits - 1):
            launch(pair_copy(h, k))
        if h > 0:
            take_pairs(h - 1)
    for step in norms:
        step()
    take_pairs(TRIO - 1)
    own_ref[group] = shared[group]
    for h in range(TRIO):
        for k in range(GROUPS - 1):
            view = own_ref.at[others[k], 0, h]
            remote(view, view, query_sems, h * (GROUPS - 1) + k, peers[k]).wait_recv()
            view = own_ref.at[others[k], pl.ds(1, 2), h]
            remote(view, view, value_sems, h * (GROUPS - 1) + k, peers[k]).wait_recv()
    finish_turn(*turn_refs)
    for copy in started:
        copy.wait_send()


def norm_stats(values_in):
    mean = jnp.mean(values_in, axis=-1, keepdims=True)
    centred = values_in - mean
    spread = jnp.mean(centred * centred, axis=-1, keepdims=True)
    scale = lax.rsqrt(spread + NORM_EPS)
    return centred * scale, scale


def norm_back(unit, scale, gain, cotangent):
    d_unit = cotangent * gain
    first = jnp.mean(d_unit, axis=-1, keepdims=True)
    second = jnp.mean(d_unit * unit, axis=-1, keepdims=True)
    d_in = scale * (d_unit - first - unit * second)
    d_gain = jnp.sum(cotangent * unit, axis=0, keepdims=True)
    d_bias = jnp.sum(cotangent, axis=0, keepdims=True)
    return d_in, d_gain, d_bias


def dense_kernel(
    sizes,
    place,
    gathered,
    cot_ref,
    mixed_ref,
    norm_ref,
    weights,
    out_ref,
    d_pre_one_ref,
    d_mixed_ref,
    norm_grad,
    grads,
    w_out,
    w_gate,
    w_up,
    w_down,
    keep_gate,
    keep_up,
    keep_hidden,
    stage,
    stage_out,
    x_ref,
    load_sems,
    store_sems,
    own_sem,
):
    n_dp, tok, piece, kind_pieces, chunk_pieces, hidden_pieces = sizes
    own_copy = pltpu.make_async_copy(
        gathered.at[my_order(n_dp), pl.ds(0, tok)], x_ref, own_sem
    )
    own_copy.start()
    first_gate = 4 * kind_pieces
    first_up = first_gate + hidden_pieces
    first_down = first_up + hidden_pieces
    bases = (first_gate, first_up, first_down)
    buffers = (w_gate, w_up, w_down)
    chunk = chunk_pieces * piece

    for step in range(kind_pieces):
        dst = w_out.at[pl.ds(step * piece, piece)]
        fetch_piece(place, 3 * kind_pieces + step, weights, dst, load_sems.at[3 * CHUNKS])

    def load_chunk(c):
        for step in range(chunk_pieces):
            for kind in range(3):
                dst = buffers[kind].at[c, pl.ds(step * piece, piece)]
                number = bases[kind] + c * chunk_pieces + step
                fetch_piece(place, number, weights, dst, load_sems.at[kind * CHUNKS + c])

    def wait_chunk(c):
        for kind in range(3):
            view = buffers[kind].at[c]
            pltpu.make_async_copy(view, view, load_sems.at[kind * CHUNKS + c]).wait()

    load_chunk(0)
    mixed = mixed_ref[...].T
    own_copy.wait()
    pltpu.make_async_copy(w_out, w_out, load_sems.at[3 * CHUNKS]).wait()
    pre_one = x_ref[...].astype(F32) + dot_nt(mixed, w_out[...])
    load_chunk(1)
    unit_one, scale_one = norm_stats(pre_one)
    h_one = unit_one * norm_ref[0:1, :] + norm_ref[1:2, :]
    h_low = h_one.astype(BF16)

    pre_two = h_one
    for c in range(CHUNKS):
        wait_chunk(c)
        gate = dot_nt(w_gate[c], h_low)
        up = dot_nt(w_up[c], h_low)
        if c + 2 < CHUNKS:
            load_chunk(c + 2)
        below = 0.5 * (1.0 + lax.erf(gate * (0.5**0.5)))
        gelu = gate * below
        slope = below + gate * (jnp.exp(-0.5 * gate * gate) * (0.5 / jnp.pi) ** 0.5)
        hidden = (gelu * up).astype(BF16)
        keep_gate[c] = up * slope
        keep_up[c] = gelu
        keep_hidden[c] = hidden
        pre_two = pre_two + dot_tn(hidden, w_down[c])

    unit_two, scale_two = norm_stats(pre_two)
    out_ref[...] = (unit_two * norm_ref[2:3, :] + norm_ref[3:4, :]).astype(BF16)
    d_pre_two, d_gain_two, d_bias_two = norm_back(
        unit_two, scale_two, norm_ref[2:3, :], cot_ref[...].astype(F32)
    )
    d_branch = d_pre_two.astype(BF16)

    def drain(slot):
        for kind in range(3):
            view = stage.at[slot, kind]
            pltpu.make_async_copy(view, view, store_sems.at[slot * 3 + kind]).wait()

    d_h = d_pre_two
    for c in range(CHUNKS):
        slot = c % 2
        if c >= 2:
            drain(slot)
        d_hidden = dot_nt(w_down[c], d_branch)
        d_gate = (d_hidden * keep_gate[c]).astype(BF16)
        d_up = (d_hidden * keep_up[c]).astype(BF16)
        stage[slot, 0] = dot_nn(d_gate, h_low).astype(BF16)
        stage[slot, 1] = dot_nn(d_up, h_low).astype(BF16)
        stage[slot, 2] = dot_nn(keep_hidden[c], d_branch).astype(BF16)
        for step in range(chunk_pieces):
            for kind in range(3):
                pltpu.make_async_copy(
                    stage.at[slot, kind, pl.ds(step * piece, piece)],
                    grads.at[place[bases[kind] + c * chunk_pieces + step]],
                    store_sems.at[slot * 3 + kind],
                ).start()
        d_h = d_h + dot_tn(d_gate, w_gate[c]) + dot_tn(d_up, w_up[c])

    d_pre_one, d_gain_one, d_bias_one = norm_back(unit_one, scale_one, norm_ref[0:1, :], d_h)
    d_pre_one_ref[...] = d_pre_one
    d_proj = d_pre_one.astype(BF16)
    stage_out[...] = dot_tn(d_proj, mixed).astype(BF16)
    for step in range(kind_pieces):
        pltpu.make_async_copy(
            stage_out.at[pl.ds(step * piece, piece)],
            grads.at[place[3 * kind_pieces + step]],
            store_sems.at[6],
        ).start()
    d_mixed_ref[...] = lax.dot_general(
        w_out[...], d_proj, (((0,), (1,)), ((), ())), preferred_element_type=F32
    ).astype(BF16)
    norm_grad[...] = jnp.concatenate(
        [
            d_gain_one,
            d_bias_one,
            d_gain_two,
            d_bias_two,
            jnp.zeros((4, d_gain_one.shape[1]), F32),
        ],
        axis=0,
    )
    drain(CHUNKS % 2)
    drain((CHUNKS + 1) % 2)
    pltpu.make_async_copy(stage_out, stage_out, store_sems.at[6]).wait()


def project_grad_kernel(
    sizes,
    place,
    gathered,
    d_own,
    d_pre_one,
    weights,
    grads_in,
    d_input,
    grads,
    w_all,
    stage,
    x_ref,
    load_sems,
    store_sems,
    own_sem,
):
    n_dp, tok, piece, kind_pieces = sizes
    own_copy = pltpu.make_async_copy(
        gathered.at[my_order(n_dp), pl.ds(0, tok)], x_ref, own_sem
    )
    own_copy.start()
    group_pieces = kind_pieces // GROUPS
    del grads_in

    def each(group):
        for kind in range(3):
            for step in range(group_pieces):
                row = (kind * group_pieces + step) * piece
                yield kind * kind_pieces + group * group_pieces + step, pl.ds(row, piece)

    def load(group):
        for number, span in each(group):
            fetch_piece(place, number, weights, w_all.at[group, span], load_sems.at[group])

    load(0)
    load(1)
    own_copy.wait()
    x_own = x_ref[...]
    for group in range(GROUPS):
        stage[group] = dot_nn(d_own[group], x_own).astype(BF16)
        if group + 2 < GROUPS:
            load(group + 2)
        for number, span in each(group):
            pltpu.make_async_copy(
                stage.at[group, span], grads.at[place[number]], store_sems.at[group]
            ).start()
    total = d_pre_one[...]
    for group in range(GROUPS):
        view = w_all.at[group]
        pltpu.make_async_copy(view, view, load_sems.at[group]).wait()
        total = total + dot_tn(d_own[group], w_all[group])
    d_input[...] = total.astype(BF16)
    for group in range(GROUPS):
        view = stage.at[group]
        pltpu.make_async_copy(view, view, store_sems.at[group]).wait()


def add_low(dst, src, rows):
    def one(i, carry):
        dst[i] = (dst[i].astype(F32) + src[i].astype(F32)).astype(BF16)
        return carry

    lax.fori_loop(0, rows, one, None)


def z_order_of(count):
    order = [0]
    for k in range(1, count):
        for far in (k, count - k):
            if far not in order:
                order.append(far)
    return order


def spread_steps(sizes, own, every, sems):
    zn, xn, yn, slots, last = sizes
    z_sems, xs_sems, ys_sems, xf_sems, yf_sems, near_sems, own_sem = sems[:7]
    xb_sems, yb_sems, zb_sems, nb_sems = sems[7:11]
    count = slots - last
    part = count * 9 // 16
    rest = count - part
    z, x = lax.axis_index("a"), lax.axis_index("b")
    y, core = lax.axis_index("y"), lax.axis_index("core")
    core_peer = {"core": 1 - core}
    xs, ys, z_order = range(1, xn), range(1, yn), z_order_of(zn)
    x_peers = {k: {"b": lax.rem(x + k, xn)} for k in xs}
    y_peers = {k: {"y": lax.rem(y + k, yn)} for k in ys}
    z_peers = {k: {"a": lax.rem(z + k, zn)} for k in range(1, zn)}
    source = own.at[pl.ds(0, count)]

    def number(jz, jx, jy):
        chip = (lax.rem(z + zn - jz, zn) * xn + lax.rem(x + xn - jx, xn)) * yn + lax.rem(
            y + yn - jy, yn
        )
        return chip * 2 + core

    def shard(jz, jx, jy, lead=0, rows=count):
        return every.at[pl.ds(number(jz, jx, jy) * slots + lead, rows)]

    def tail(jz, jx, jy):
        return shard(jz, jx, jy, count, last)

    def tail_held(jz, jx, jy):
        return own.at[pl.ds(count, last)] if (jz, jx, jy) == (0, 0, 0) else tail(jz, jx, jy)

    def xb_copy(jx, jy):
        index = (jx - 1) * yn + jy
        return remote(tail_held(0, 0, jy), tail(0, 0, jy), xb_sems, index, x_peers[jx])

    def yb_copy(jy):
        return remote(tail_held(0, 0, 0), tail(0, 0, 0), yb_sems, jy - 1, y_peers[jy])

    def zb_copy(jz, jx, jy):
        index = ((jz - 1) * xn + jx) * yn + jy
        return remote(tail_held(0, jx, jy), tail(0, jx, jy), zb_sems, index, z_peers[jz])

    def nb_copy(jz, jx, jy):
        index = (jz * xn + jx) * yn + jy
        return remote(tail_held(jz, jx, jy), tail(jz, jx, jy), nb_sems, index, core_peer)

    def tail_begin():
        for jy in ys:
            launch(yb_copy(jy))
        for jx in xs:
            launch(xb_copy(jx, 0))
        launch(nb_copy(0, 0, 0))

    def tail_across():
        for jy in ys:
            view = tail(0, 0, jy)
            remote(view, view, yb_sems, jy - 1, y_peers[jy]).wait_recv()
            for jx in xs:
                launch(xb_copy(jx, jy))
            launch(nb_copy(0, 0, jy))

    def tail_planes():
        for jx in xs:
            for jy in range(yn):
                view = tail(0, jx, jy)
                remote(view, view, xb_sems, (jx - 1) * yn + jy, x_peers[jx]).wait_recv()
                launch(nb_copy(0, jx, jy))
        for jz in z_order[1:]:
            for jx in range(xn):
                for jy in range(yn):
                    launch(zb_copy(jz, jx, jy))

    def tail_end():
        for jz in z_order[1:]:
            for jx in range(xn):
                for jy in range(yn):
                    view = tail(jz, jx, jy)
                    index = ((jz - 1) * xn + jx) * yn + jy
                    remote(view, view, zb_sems, index, z_peers[jz]).wait_recv()
                    launch(nb_copy(jz, jx, jy))

    def tail_settle():
        for jz in range(zn):
            for jx in range(xn):
                for jy in range(yn):
                    chip = lax.div(number(jz, jx, jy), 2)
                    view = every.at[pl.ds((chip * 2 + 1 - core) * slots + count, last)]
                    index = (jz * xn + jx) * yn + jy
                    remote(view, view, nb_sems, index, core_peer).wait_recv()

    def held(jz, jx, jy):
        return source if (jz, jx, jy) == (0, 0, 0) else shard(jz, jx, jy)

    def z_copy(jz):
        return remote(source, shard(0, 0, 0), z_sems, jz - 1, z_peers[jz])

    def xs_copy(jz, jx):
        return remote(
            held(jz, 0, 0), shard(jz, 0, 0), xs_sems, jz * (xn - 1) + jx - 1, x_peers[jx]
        )

    def ys_copy(jz, jy):
        return remote(
            held(jz, 0, 0), shard(jz, 0, 0), ys_sems, jz * (yn - 1) + jy - 1, y_peers[jy]
        )

    def cross(jz, jx, jy):
        return (jz * (xn - 1) + jx - 1) * (yn - 1) + jy - 1

    def xf_copy(jz, jx, jy):
        view = shard(jz, 0, jy, part, rest)
        return remote(view, view, xf_sems, cross(jz, jx, jy), x_peers[jx])

    def yf_copy(jz, jx, jy):
        view = shard(jz, jx, 0, 0, part)
        return remote(view, view, yf_sems, cross(jz, jx, jy), y_peers[jy])

    def near_copy(jz, jx, jy):
        return remote(
            held(jz, jx, jy),
            shard(jz, jx, jy),
            near_sems,
            (jz * xn + jx) * yn + jy,
            core_peer,
        )

    started = []

    def launch(copy):
        copy.start()
        started.append(copy)

    def send_own(jz):
        for jx in xs:
            launch(xs_copy(jz, jx))
        for jy in ys:
            launch(ys_copy(jz, jy))
        launch(near_copy(jz, 0, 0))

    def ys_copy_in(jz, jy):
        view = shard(jz, 0, jy)
        remote(view, view, ys_sems, jz * (yn - 1) + jy - 1, y_peers[jy]).wait_recv()

    def xs_copy_in(jz, jx):
        view = shard(jz, jx, 0)
        remote(view, view, xs_sems, jz * (xn - 1) + jx - 1, x_peers[jx]).wait_recv()

    def forward(jz):
        for jy in ys:
            ys_copy_in(jz, jy)
            for jx in xs:
                launch(xf_copy(jz, jx, jy))
        for jx in xs:
            xs_copy_in(jz, jx)
            for jy in ys:
                launch(yf_copy(jz, jx, jy))
        for jy in ys:
            launch(near_copy(jz, 0, jy))
        for jx in xs:
            launch(near_copy(jz, jx, 0))

    def finish(jz):
        for jx in xs:
            for jy in ys:
                view = shard(jz, jx, jy, part, rest)
                remote(view, view, xf_sems, cross(jz, jx, jy), x_peers[jx]).wait_recv()
                view = shard(jz, jx, jy, 0, part)
                remote(view, view, yf_sems, cross(jz, jx, jy), y_peers[jy]).wait_recv()
                launch(near_copy(jz, jx, jy))

    def z_in(index):
        jz = z_order[index]
        view = shard(jz, 0, 0)
        remote(view, view, z_sems, jz - 1, z_peers[jz]).wait_recv()
        if index + 1 < zn:
            launch(z_copy(z_order[index + 1]))

    own_local = pltpu.make_async_copy(own, shard(0, 0, 0, 0, slots), own_sem)

    def begin():
        launch(z_copy(z_order[1]))
        send_own(0)
        own_local.start()
        if last:
            tail_begin()

    def advance(index):
        z_in(index)
        send_own(z_order[index])
        if last and index == 1:
            tail_across()

    def forward_step(index):
        forward(z_order[index])
        if last and index == zn - 2:
            tail_planes()

    def end():
        finish(z_order[zn - 1])
        if last:
            tail_end()
            tail_settle()
        for jz in range(zn):
            for jx in range(xn):
                for jy in range(yn):
                    chip = lax.div(number(jz, jx, jy), 2)
                    view = every.at[pl.ds((chip * 2 + 1 - core) * slots, count)]
                    remote(
                        view, view, near_sems, (jz * xn + jx) * yn + jy, core_peer
                    ).wait_recv()

    def settle():
        own_local.wait()
        for copy in started:
            copy.wait_send()

    steps = [begin]
    for index in range(1, zn):
        steps.append(functools.partial(advance, index))
        steps.append(functools.partial(forward_step, index - 1))
        if index >= 2:
            steps.append(functools.partial(finish, z_order[index - 2]))
    steps.append(functools.partial(forward_step, zn - 1))
    steps.append(functools.partial(finish, z_order[zn - 2]))
    steps.append(end)
    steps.append(settle)
    return [core_peer, *x_peers.values(), *y_peers.values(), *z_peers.values()], steps


def block_steps(sizes, pack, gathered, crossed, sems):
    zn, xn, yn = sizes
    by_sems, bz_sems, bx_sems, bn_sems, stay_sem = sems
    z, x = lax.axis_index("a"), lax.axis_index("b")
    y, core = lax.axis_index("y"), lax.axis_index("core")
    core_peer = {"core": 1 - core}
    xs, ys, z_order = range(1, xn), range(1, yn), z_order_of(zn)
    x_peers = {k: {"b": lax.rem(x + k, xn)} for k in xs}
    y_peers = {k: {"y": lax.rem(y + k, yn)} for k in ys}
    z_peers = {k: {"a": lax.rem(z + k, zn)} for k in range(1, zn)}
    hosts = lax.rem(z, 2) == core

    def block(jz, jx=0):
        return gathered.at[lax.rem(x + xn - jx, xn) * zn + lax.rem(z + zn - jz, zn)]

    def by_copy(jy):
        return remote(pack, crossed.at[jy - 1], by_sems, jy - 1, y_peers[jy])

    def plane(jy):
        return lax.rem(y + yn - jy, yn) * 2 + core

    def bz_copy(jy):
        src = pack if jy == 0 else crossed.at[jy - 1]
        far = lax.rem(plane(jy) + zn - z, zn)
        return remote(src, block(0), bz_sems, far, {"a": plane(jy)})

    def stay_copy(jy):
        src = pack if jy == 0 else crossed.at[jy - 1]
        return pltpu.make_async_copy(src, block(0), stay_sem)

    def bx_copy(jz, jx):
        return remote(block(jz), block(jz), bx_sems, jz * (xn - 1) + jx - 1, x_peers[jx])

    def bn_copy(jz, jx):
        return remote(block(jz, jx), block(jz, jx), bn_sems, jz * xn + jx, core_peer)

    def cross_y():
        for jy in ys:
            by_copy(jy).start()

    def to_planes():
        for jy in range(yn):
            if jy != 0:
                by_copy(jy).wait_recv()

            @pl.when(plane(jy) != z)
            def _():
                bz_copy(jy).start()

            @pl.when(plane(jy) == z)
            def _():
                stay_copy(jy).start()
                stay_copy(jy).wait()

    def across():
        @pl.when(hosts)
        def _():
            for jz in z_order:
                if jz != 0:
                    remote(block(jz), block(jz), bz_sems, jz, z_peers[jz]).wait_recv()
                for jx in xs:
                    bx_copy(jz, jx).start()
                bn_copy(jz, 0).start()

    def end():
        @pl.when(hosts)
        def _():
            for jz in z_order:
                for jx in xs:
                    view = block(jz, jx)
                    index = jz * (xn - 1) + jx - 1
                    remote(view, view, bx_sems, index, x_peers[jx]).wait_recv()
                    bn_copy(jz, jx).start()
            for jz in z_order:
                for jx in xs:
                    bx_copy(jz, jx).wait_send()
                for jx in range(xn):
                    bn_copy(jz, jx).wait_send()

        @pl.when(jnp.logical_not(hosts))
        def _():
            for jz in range(zn):
                for jx in range(xn):
                    bn_copy(jz, jx).wait_recv()

        for jy in range(yn):

            @pl.when(plane(jy) != z)
            def _():
                bz_copy(jy).wait_send()

        for jy in ys:
            by_copy(jy).wait_send()

    return [cross_y, to_planes, across, end]


def spread_kernel(
    sizes, master, x_in, seg_in, every, gathered, crossed, own, pack, *sems
):
    peers, steps = spread_steps(sizes, own, every, sems[:11])
    cross_y, to_planes, across, end = block_steps(sizes[:3], pack, gathered, crossed, sems[11:])
    tok, width = x_in.shape

    def prepare():
        own[...] = master[...].astype(BF16)
        pack[0:tok, :] = x_in[...]
        segs = jnp.concatenate(
            [seg_in[...].astype(F32), jnp.zeros((1, width - tok), F32)], axis=1
        )
        pack[tok:, :] = jnp.broadcast_to(segs, (pack.shape[0] - tok, width)).astype(BF16)

    greet(peers, meanwhile=prepare)
    steps[0]()
    cross_y()
    for step in steps[1:-7]:
        step()
    to_planes()
    for step in steps[-7:-3]:
        step()
    across()
    steps[-3]()
    steps[-2]()
    end()
    steps[-1]()


def reduce_steps(sizes, grads, total_out, refs):
    zn, xn, yn, slots, last = sizes
    held, near, xd, yd, xs_in, ys_in, zs_in, xb, yb, zb = refs[:10]
    load_sems, near_sems, xd_sems, yd_sems, xs_sems, ys_sems, zs_sems = refs[10:17]
    xb_sems, yb_sems, zb_sems = refs[17:20]
    count = slots - last
    part = count // 2
    rest = count - part
    tail = pl.ds(count, last)
    z, x = lax.axis_index("a"), lax.axis_index("b")
    y, core = lax.axis_index("y"), lax.axis_index("core")
    core_peer = {"core": 1 - core}
    xs, ys = range(1, xn), range(1, yn)
    y_peers = [{"y": lax.rem(y + k, yn)} for k in ys]
    x_peers = [{"b": lax.rem(x + k, xn)} for k in xs]
    z_peers = [{"a": lax.rem(z + k, zn)} for k in range(1, zn)]
    def flat(jz, jx, jy):
        return (jz * xn + jx) * yn + jy

    def chip_rows(jz, jx, jy, which):
        chip = (lax.rem(z + jz, zn) * xn + lax.rem(x + jx, xn)) * yn + lax.rem(y + jy, yn)
        return grads.at[pl.ds((chip * 2 + which) * slots, slots)]

    def near_copy(jz, jx, jy):
        index = flat(jz, jx, jy)
        return remote(chip_rows(jz, jx, jy, 1 - core), near.at[index], near_sems, index, core_peer)

    def load_copy(jz, jx, jy):
        index = flat(jz, jx, jy)
        return pltpu.make_async_copy(
            chip_rows(jz, jx, jy, core), held.at[index], load_sems.at[index]
        )

    def whole(jz, jx, jy):
        return held.at[flat(jz, jx, jy)]

    def first(jz, jx, jy):
        return held.at[flat(jz, jx, jy), pl.ds(0, part)]

    def second(jz, jx, jy):
        return held.at[flat(jz, jx, jy), pl.ds(part, rest)]

    def cross(jz, jx, jy):
        return (jz * (xn - 1) + jx - 1) * (yn - 1) + jy - 1

    def yd_copy(jz, jx, jy):
        index = cross(jz, jx, jy)
        return remote(first(jz, jx, jy), yd.at[index], yd_sems, index, y_peers[jy - 1])

    def xd_copy(jz, jx, jy):
        index = cross(jz, jx, jy)
        return remote(second(jz, jx, jy), xd.at[index], xd_sems, index, x_peers[jx - 1])

    def halves(low_half):
        return pl.ds(0, part) if low_half else pl.ds(part, rest)

    def xs_copy(jz, jx, low_half):
        index = jz * (xn - 1) + jx - 1
        return remote(
            held.at[flat(jz, jx, 0), halves(low_half)],
            xs_in.at[index, halves(low_half)],
            xs_sems,
            index * 2 + int(low_half),
            x_peers[jx - 1],
        )

    def ys_copy(jz, jy, low_half):
        index = jz * (yn - 1) + jy - 1
        return remote(
            held.at[flat(jz, 0, jy), halves(low_half)],
            ys_in.at[index, halves(low_half)],
            ys_sems,
            index * 2 + int(low_half),
            y_peers[jy - 1],
        )

    def zs_copy(jz):
        src = held.at[flat(jz, 0, 0), pl.ds(0, count)]
        return remote(src, zs_in.at[jz - 1], zs_sems, jz - 1, z_peers[jz - 1])

    def zb_copy(jz):
        src = held.at[pl.ds(jz * xn * yn, xn * yn), tail]
        return remote(src, zb.at[jz - 1], zb_sems, jz - 1, z_peers[jz - 1])

    def xb_copy(jx):
        src = held.at[pl.ds(jx * yn, yn), tail]
        return remote(src, xb.at[jx - 1], xb_sems, jx - 1, x_peers[jx - 1])

    def yb_copy(jy):
        return remote(held.at[jy, tail], yb.at[jy - 1], yb_sems, jy - 1, y_peers[jy - 1])

    def tail_planes():
        for jz in range(1, zn):
            zb_copy(jz).wait_recv()

        def one(i, carry):
            for chip in range(xn * yn):
                total = held[chip, count + i].astype(F32)
                for jz in range(1, zn):
                    total = total + zb[jz - 1, chip, i].astype(F32)
                held[chip, count + i] = total.astype(BF16)
            return carry

        lax.fori_loop(0, last, one, None)
        for jx in xs:
            launch(xb_copy(jx))

    def tail_columns():
        for jx in xs:
            xb_copy(jx).wait_recv()
            for jy in range(yn):
                add_low(held.at[jy, tail], xb.at[jx - 1, jy], last)
        for jy in ys:
            launch(yb_copy(jy))

    def tail_end():
        for jy in ys:
            yb_copy(jy).wait_recv()

        def one(i, carry):
            total = held[0, count + i].astype(F32)
            for jy in ys:
                total = total + yb[jy - 1, i].astype(F32)
            total_out[count + i] = total
            return carry

        lax.fori_loop(0, last, one, None)

    z_order = z_order_of(zn)[::-1]
    started = []

    def launch(copy):
        copy.start()
        started.append(copy)

    def plane(jz):
        return (
            [(jz, jx, jy) for jx in xs for jy in ys]
            + [(jz, jx, 0) for jx in xs]
            + [(jz, 0, jy) for jy in ys]
            + [(jz, 0, 0)]
        )

    def fetch(jz):
        for chip in plane(jz):
            launch(near_copy(*chip))
            load_copy(*chip).start()

    def prepare(index):
        for chip in plane(z_order[index]):
            load_copy(*chip).wait()
            near_copy(*chip).wait_recv()
            add_low(whole(*chip), near.at[flat(*chip)], slots)
        if index + 1 < zn:
            fetch(z_order[index + 1])
        if last and z_order[index] != 0:
            launch(zb_copy(z_order[index]))

    stages = [(index, stage) for index in range(zn) for stage in range(3)]

    def send_stage(number):
        index, stage = stages[number]
        jz = z_order[index]
        for jx in xs:
            if stage == 0:
                for jy in ys:
                    launch(xd_copy(jz, jx, jy))
            else:
                launch(xs_copy(jz, jx, stage == 2))
        for jy in ys:
            if stage == 0:
                for jx in xs:
                    launch(yd_copy(jz, jx, jy))
            else:
                launch(ys_copy(jz, jy, stage == 1))

    def take_stage(number):
        index, stage = stages[number]
        jz = z_order[index]
        if stage == 0:
            for jx in xs:
                for jy in ys:
                    yd_copy(jz, jx, jy).wait_recv()
                    add_low(first(jz, jx, 0), yd.at[cross(jz, jx, jy)], part)
                    xd_copy(jz, jx, jy).wait_recv()
                    add_low(second(jz, 0, jy), xd.at[cross(jz, jx, jy)], rest)
        else:
            for jx in xs:
                xs_copy(jz, jx, stage == 2).wait_recv()
            for jy in ys:
                ys_copy(jz, jy, stage == 1).wait_recv()

    def side_in(index):
        jz = z_order[index]

        def one(i, carry):
            total = held[flat(jz, 0, 0), i].astype(F32)
            for jx in xs:
                total = total + xs_in[jz * (xn - 1) + jx - 1, i].astype(F32)
            for jy in ys:
                total = total + ys_in[jz * (yn - 1) + jy - 1, i].astype(F32)
            if jz != 0:
                held[flat(jz, 0, 0), i] = total.astype(BF16)
            else:
                total_out[i] = total
            return carry

        lax.fori_loop(0, count, one, None)
        if jz != 0:
            launch(zs_copy(jz))

    ahead = 2

    def begin():
        fetch(z_order[0])

    def begin_stages():
        prepare(0)
        for number in range(ahead):
            send_stage(number)

    def one_stage(number):
        for index in range(1, zn):
            if number == (index - 1 if index < 3 else 3 * (index - 2)):
                prepare(index)
        take_stage(number)
        later = number + ahead
        if later < len(stages):
            send_stage(later)
        if stages[number][1] == 2:
            side_in(stages[number][0])
        if last and number == len(stages) - 4:
            tail_planes()
        if last and number == len(stages) - 2:
            tail_columns()

    def end():
        for jz in range(1, zn):
            zs_copy(jz).wait_recv()

        def add_planes(i, carry):
            total = total_out[i]
            for jz in range(1, zn):
                total = total + zs_in[jz - 1, i].astype(F32)
            total_out[i] = total
            return carry

        lax.fori_loop(0, count, add_planes, None)
        if last:
            tail_end()
        for copy in started:
            copy.wait_send()

    steps = [begin, begin_stages]
    steps += [functools.partial(one_stage, number) for number in range(len(stages))]
    steps.append(end)
    return [core_peer] + y_peers + x_peers + z_peers, steps


def reduce_kernel(sizes, grads, tokens_in, total_out, tokens_out, *refs):
    peers, steps = reduce_steps(sizes, grads, total_out, refs[:20])
    turn_sems = refs[20]
    greet(peers, True)
    turn_refs = (tokens_in, tokens_out, turn_sems.at[0], turn_sems.at[1])
    start_turn(*turn_refs)
    for step in steps:
        step()
    finish_turn(*turn_refs)


def vmem():
    return pl.BlockSpec(memory_space=pltpu.VMEM)


def smem():
    return pl.BlockSpec(memory_space=pltpu.SMEM)


def anywhere():
    return pl.BlockSpec(memory_space=pl.ANY)


def shape_of(dims, kind):
    return jax.ShapeDtypeStruct(dims, kind)


def params(collective=None):
    if collective is None:
        return pltpu.CompilerParams(vmem_limit_bytes=VMEM_LIMIT)
    return pltpu.CompilerParams(
        vmem_limit_bytes=VMEM_LIMIT, collective_id=collective, has_side_effects=True
    )


def pair(count):
    return pltpu.SemaphoreType.DMA((2, max(count, 1)))


def spread_scratch(zn, xn, yn):
    return [
        pair(zn - 1),
        pair(zn * (xn - 1)),
        pair(zn * (yn - 1)),
        pair(zn * (xn - 1) * (yn - 1)),
        pair(zn * (xn - 1) * (yn - 1)),
        pair(zn * xn * yn),
        pltpu.SemaphoreType.DMA,
        pair((xn - 1) * yn),
        pair(yn - 1),
        pair((zn - 1) * xn * yn),
        pair(zn * xn * yn),
    ]


def reduce_scratch(zn, xn, yn, slots, last, piece, width):
    def chunks(*dims):
        return pltpu.VMEM(tuple(max(dim, 1) for dim in dims) + (piece, width), BF16)

    n_chips, crossing = zn * xn * yn, zn * (xn - 1) * (yn - 1)
    count = slots - last
    part = count // 2
    return [
        chunks(n_chips, slots),
        chunks(n_chips, slots),
        chunks(crossing, count - part),
        chunks(crossing, part),
        chunks(zn * (xn - 1), count),
        chunks(zn * (yn - 1), count),
        chunks(zn - 1, count),
        chunks(xn - 1, yn, last),
        chunks(yn - 1, last),
        chunks(zn - 1, xn * yn, last),
        pltpu.SemaphoreType.DMA((n_chips,)),
        pair(n_chips),
        pair(crossing),
        pair(crossing),
        pair(2 * zn * (xn - 1)),
        pair(2 * zn * (yn - 1)),
        pair(zn - 1),
        pair(xn - 1),
        pair(yn - 1),
        pair(zn - 1),
    ]


def run_layer(dims, weight_master, x_own, segments, cotangent, location, norm_params):
    n_seq, n_dp = dims
    reps = n_seq // n_dp
    splits = n_seq // GROUPS
    slots, piece, width = weight_master.shape
    tok = cotangent.shape[0]
    length = tok * n_seq
    hidden_units = (location.shape[0] * piece - 4 * width) // 3
    head = width // HEADS
    kind_pieces = width // piece
    hidden_pieces = hidden_units // piece
    chunk = hidden_units // CHUNKS
    zn, xn, yn = n_dp, reps, n_dp // 2
    all_slots = n_seq * n_dp * slots
    last, reduce_last = slots // 8, slots * 3 // 32
    slopes = jnp.asarray(head_slopes(HEADS, tok, n_seq))

    weights, gathered, _ = pl.pallas_call(
        functools.partial(spread_kernel, (zn, xn, yn, slots, last)),
        out_shape=(
            shape_of((all_slots, piece, width), BF16),
            shape_of((n_seq, tok + 16, width), BF16),
            shape_of((max(yn - 1, 1), tok + 16, width), BF16),
        ),
        in_specs=[vmem(), vmem(), vmem()],
        out_specs=(anywhere(),) * 3,
        scratch_shapes=[
            pltpu.VMEM((slots, piece, width), BF16),
            pltpu.VMEM((tok + 16, width), BF16),
        ]
        + spread_scratch(zn, xn, yn)
        + [
            pair(yn - 1),
            pair(zn),
            pair(zn * (xn - 1)),
            pair(zn * xn),
            pltpu.SemaphoreType.DMA,
        ],
        compiler_params=params(1),
    )(weight_master, x_own, segments)
    attend_sizes = (n_dp, reps, splits, tok, head, n_seq)
    q_ext, k_ext, k_turned, v_rows, v_turned = pl.pallas_call(
        functools.partial(project_kernel, (n_dp, splits, tok, head)),
        grid=(n_seq,),
        out_shape=(
            shape_of((TRIO, GROUPS * tok, 128), BF16),
            shape_of((TRIO, length, 128), BF16),
            shape_of((TRIO, head, length), BF16),
            shape_of((TRIO, length, head), BF16),
            shape_of((TRIO, head, length), BF16),
        ),
        in_specs=[
            smem(),
            pl.BlockSpec((1, tok + 16, width), lambda i: (i, 0, 0)),
            anywhere(),
        ],
        out_specs=(
            pl.BlockSpec((TRIO, tok, 128), lambda i: (0, lax.div(i, splits), 0)),
            pl.BlockSpec((TRIO, tok, 128), lambda i: (0, i, 0)),
            pl.BlockSpec((TRIO, head, tok), lambda i: (0, 0, i)),
            pl.BlockSpec((TRIO, tok, head), lambda i: (0, i, 0)),
            pl.BlockSpec((TRIO, head, tok), lambda i: (0, 0, i)),
        ),
        scratch_shapes=[
            pltpu.VMEM((3 * TRIO, 128, width), BF16),
            pltpu.SemaphoreType.DMA((3 * TRIO * (head // piece),)),
        ],
        compiler_params=params(),
    )(location, gathered, weights)

    mixed_full, log_total, mixed_own, cotangent = pl.pallas_call(
        functools.partial(attend_forward_kernel, attend_sizes),
        out_shape=(
            shape_of((GROUPS, TRIO, head, tok), F32),
            shape_of((GROUPS, TRIO, 1, tok), F32),
            shape_of((GROUPS, TRIO, head, tok), BF16),
            shape_of(cotangent.shape, BF16),
        ),
        in_specs=[smem(), vmem(), vmem(), vmem(), anywhere()],
        out_specs=(vmem(), vmem(), vmem(), anywhere()),
        scratch_shapes=[
            pltpu.VMEM((3 * TRIO, tok, tok), F32),
            pltpu.VMEM((n_seq, tok, tok), F32),
            pltpu.VMEM((GROUPS, TRIO, head, tok), BF16),
            pair(GROUPS - 1),
            pltpu.SemaphoreType.DMA((2,)),
        ],
        compiler_params=params(2),
    )(slopes, q_ext, k_ext, v_turned, cotangent)

    out_low, d_pre_one, d_mixed, norm_part, grads = pl.pallas_call(
        functools.partial(
            dense_kernel, (n_dp, tok, piece, kind_pieces, chunk // piece, hidden_pieces)
        ),
        out_shape=(
            shape_of((tok, width), BF16),
            shape_of((tok, width), F32),
            shape_of((width, tok), BF16),
            shape_of((8, width), F32),
            shape_of((all_slots, piece, width), BF16),
        ),
        in_specs=[smem(), anywhere(), vmem(), vmem(), vmem(), anywhere()],
        out_specs=(vmem(), vmem(), vmem(), vmem(), anywhere()),
        scratch_shapes=[
            pltpu.VMEM((width, width), BF16),
            pltpu.VMEM((CHUNKS, chunk, width), BF16),
            pltpu.VMEM((CHUNKS, chunk, width), BF16),
            pltpu.VMEM((CHUNKS, chunk, width), BF16),
            pltpu.VMEM((CHUNKS, chunk, tok), F32),
            pltpu.VMEM((CHUNKS, chunk, tok), F32),
            pltpu.VMEM((CHUNKS, chunk, tok), BF16),
            pltpu.VMEM((2, 3, chunk, width), BF16),
            pltpu.VMEM((width, width), BF16),
            pltpu.VMEM((tok, width), BF16),
            pltpu.SemaphoreType.DMA((3 * CHUNKS + 1,)),
            pltpu.SemaphoreType.DMA((7,)),
            pltpu.SemaphoreType.DMA,
        ],
        compiler_params=params(),
    )(location, gathered, cotangent, mixed_own.reshape(width, tok), norm_params, weights)

    def norm_rows(count):
        return pltpu.VMEM((max(count, 1), 8, width), F32)

    d_own, result, norm_total = pl.pallas_call(
        functools.partial(attend_backward_kernel, attend_sizes),
        out_shape=(
            shape_of((GROUPS, 3, TRIO, head, tok), BF16),
            shape_of(out_low.shape, BF16),
            shape_of((8, width), F32),
        ),
        in_specs=[smem()] + [vmem()] * 7 + [anywhere(), vmem()],
        out_specs=(vmem(), anywhere(), vmem()),
        scratch_shapes=[
            pltpu.VMEM((length, 128), F32),
            pltpu.VMEM((length, head), F32),
            pltpu.VMEM((3 * TRIO, tok, tok), F32),
            pltpu.VMEM((GROUPS, TRIO, head, tok), BF16),
            pltpu.VMEM((GROUPS, 3, TRIO, head, tok), BF16),
            pltpu.VMEM((TRIO, splits, GROUPS, 2, head, tok), BF16),
            pltpu.VMEM((TRIO, splits - 1, GROUPS, 2, head, tok), BF16),
            pair(GROUPS - 1),
            pair(TRIO * (GROUPS - 1)),
            pair(TRIO * (splits - 1)),
            pair(TRIO * (GROUPS - 1)),
            pltpu.SemaphoreType.DMA((2,)),
            norm_rows(1),
            norm_rows(yn - 1),
            norm_rows(xn - 1),
            norm_rows(zn - 1),
            norm_rows(4),
            pair(1 + (yn - 1) + (xn - 1) + (zn - 1)),
        ],
        compiler_params=params(3),
    )(
        slopes,
        q_ext,
        k_ext,
        k_turned,
        v_rows,
        mixed_full,
        log_total,
        d_mixed.reshape(GROUPS, TRIO, head, tok),
        out_low,
        norm_part,
    )

    trio_rows = TRIO * head
    d_tokens, grads = pl.pallas_call(
        functools.partial(project_grad_kernel, (n_dp, tok, piece, kind_pieces)),
        out_shape=(shape_of((tok, width), BF16), shape_of(grads.shape, BF16)),
        in_specs=[smem(), anywhere(), vmem(), vmem()] + [anywhere()] * 2,
        out_specs=(vmem(), anywhere()),
        scratch_shapes=[
            pltpu.VMEM((GROUPS, 3 * trio_rows, width), BF16),
            pltpu.VMEM((GROUPS, 3 * trio_rows, width), BF16),
            pltpu.VMEM((tok, width), BF16),
            pltpu.SemaphoreType.DMA((GROUPS,)),
            pltpu.SemaphoreType.DMA((GROUPS,)),
            pltpu.SemaphoreType.DMA,
        ],
        input_output_aliases={5: 1},
        compiler_params=params(),
    )(location, gathered, d_own.reshape(GROUPS, 3 * trio_rows, tok), d_pre_one, weights, grads)

    own_grad, d_turned = pl.pallas_call(
        functools.partial(reduce_kernel, (zn, xn, yn, slots, reduce_last)),
        out_shape=(
            shape_of((slots, piece, width), F32),
            shape_of(d_tokens.shape, BF16),
        ),
        in_specs=[anywhere(), anywhere()],
        out_specs=(vmem(), anywhere()),
        scratch_shapes=reduce_scratch(zn, xn, yn, slots, reduce_last, piece, width)
        + [pltpu.SemaphoreType.DMA((2,))],
        compiler_params=params(4),
    )(grads, d_tokens)
    return own_grad, norm_total, d_turned, result


def per_device(
    dims,
    layer_input,
    out_cotangent,
    segment_ids,
    piece_owner,
    weight_master,
    weight_first,
    weight_second,
    norm_params,
    norm_first,
    norm_second,
):
    slots, piece, width = weight_master.shape
    pieces = piece_owner.shape[0]
    tok = layer_input.shape[1]
    hidden_units = (pieces * piece - 4 * width) // 3
    location = locate_pieces(piece_owner, slots)
    own_grad, norm_total, d_turned, result = run_layer(
        dims,
        weight_master,
        layer_input[0],
        segment_ids,
        out_cotangent[0],
        location,
        norm_params,
    )

    numbers = jnp.arange(pieces, dtype=jnp.int32) + 1
    own_slots = lax.axis_index(("a", "b", "y", "core")) * slots + jnp.arange(slots)
    inverse = jnp.sum(jnp.where(location[None, :] == own_slots[:, None], numbers[None, :], 0), axis=1)
    own_grad = jnp.where((inverse > 0)[:, None, None], own_grad, 0.0)
    norm_grad = norm_total[:4]
    rates = slot_rates(inverse, piece, width, hidden_units)
    first_new, second_new, weight_new = adamw_step(
        weight_master, weight_first, weight_second, own_grad, rates[:, None, None], STEP
    )
    norm_first_new, norm_second_new, norm_new = adamw_step(
        norm_params, norm_first, norm_second, norm_grad, NORM_RATE, STEP
    )
    return (
        result[None],
        d_turned.astype(F32)[None],
        own_grad,
        first_new,
        second_new,
        weight_new,
        weight_new.astype(BF16),
        norm_grad,
        norm_first_new,
        norm_second_new,
        norm_new,
    )


def solution(mesh):
    n_seq, n_dp = mesh.shape["seq"], mesh.shape["dp"]
    inner = Mesh(
        mesh.devices.reshape(n_dp, n_seq // n_dp, n_dp // 2, 2), ("a", "b", "y", "core")
    )
    seq, dp, every = ("a", "b"), ("y", "core"), ("a", "b", "y", "core")
    block = P(dp, seq, None)
    owned = P(every, None, None)
    in_specs = (block, block, P(dp, seq), P(), owned, owned, owned, P(), P(), P())
    out_specs = (block, block, owned, owned, owned, owned, owned, P(), P(), P(), P())
    return jax.shard_map(
        functools.partial(per_device, (n_seq, n_dp)),
        mesh=inner,
        in_specs=in_specs,
        out_specs=out_specs,
        check_vma=False,
    )
```
